128 devices in a mesh: dp: 4 (over x), blk: 4 (over y), heads: 8 (over z, core).
Axes of the slice: x: 4, y: 4, z: 4, core: 2. Of those that a mesh axis runs over, the one named last changes fastest.
Arguments:
- x_in: bfloat16 [16384, 2048], P(('dp', 'blk', 'heads')), may hold values from -7.5 to 7.5
- out_grad: bfloat16 [16384, 2048], P(('dp', 'blk', 'heads')), may hold values from -6 to 6
- norm_one: bfloat16 [2048], P(('dp', 'blk', 'heads')), may hold values from 0.5 to 1.5
- w_query: bfloat16 [2048, 1024], P(('dp', 'blk'), 'heads'), may hold values from -0.125 to 0.125
- w_key: bfloat16 [2048, 256], P(('dp', 'blk', 'heads')), may hold values from -0.125 to 0.125
- w_value: bfloat16 [2048, 256], P(('dp', 'blk', 'heads')), may hold values from -0.125 to 0.125
- output_gate_weight: bfloat16 [2048, 3072], P(('dp', 'blk'), 'heads'), may hold values from -0.125 to 0.125
- mixer_input_weight: bfloat16 [2048, 3072], P(('dp', 'blk'), 'heads'), may hold values from -0.125 to 0.125
- w_delta: bfloat16 [2048, 48], P(('dp', 'blk'), 'heads'), may hold values from -0.25 to 0.25
- w_bmat: bfloat16 [2048, 256], P(('dp', 'blk', 'heads')), may hold values from -0.03125 to 0.03125
- w_cmat: bfloat16 [2048, 256], P(('dp', 'blk', 'heads')), may hold values from -0.03125 to 0.03125
- delta_bias: float32 [48], P('heads'), may hold values from -1 to 1
- decay_log: float32 [48], P('heads'), may hold values from -9 to -3
- skip_gain: float32 [48], P('heads'), may hold values from 0 to 2
- w_attn_out: bfloat16 [1024, 2048], P('heads', ('dp', 'blk')), may hold values from -6 to 6
- mixer_output_weight: bfloat16 [3072, 2048], P('heads', ('dp', 'blk')), may hold values from -0.013671875 to 0.013671875
- norm_two: bfloat16 [2048], P(('dp', 'blk', 'heads')), may hold values from 0.5 to 1.5
- w_gate: bfloat16 [2048, 4096], P(('dp', 'blk'), 'heads'), may hold values from -0.125 to 0.125
- w_up: bfloat16 [2048, 4096], P(('dp', 'blk'), 'heads'), may hold values from -0.125 to 0.125
- w_down: bfloat16 [4096, 2048], P('heads', ('dp', 'blk')), may hold values from -0.09375 to 0.09375
Outputs:
- activations: bfloat16 [16384, 2048], P(('dp', 'blk', 'heads'))
- input_grad: float32 [16384, 2048], P(('dp', 'blk', 'heads'))
- grad_norm_one: float32 [2048], P(('dp', 'blk', 'heads'))
- grad_w_query: float32 [2048, 1024], P(('dp', 'blk'), 'heads')
- grad_w_key: float32 [2048, 256], P(('dp', 'blk', 'heads'))
- grad_w_value: float32 [2048, 256], P(('dp', 'blk', 'heads'))
- grad_w_gate_z: float32 [2048, 3072], P(('dp', 'blk'), 'heads')
- grad_w_ssm_x: float32 [2048, 3072], P(('dp', 'blk'), 'heads')
- grad_w_delta: float32 [2048, 48], P(('dp', 'blk'), 'heads')
- grad_w_bmat: float32 [2048, 256], P(('dp', 'blk', 'heads'))
- grad_w_cmat: float32 [2048, 256], P(('dp', 'blk', 'heads'))
- grad_delta_bias: float32 [48], P('heads')
- grad_decay_log: float32 [48], P('heads')
- grad_skip_gain: float32 [48], P('heads')
- grad_w_attn_out: float32 [1024, 2048], P('heads', ('dp', 'blk'))
- grad_w_ssm_out: float32 [3072, 2048], P('heads', ('dp', 'blk'))
- grad_norm_two: float32 [2048], P(('dp', 'blk', 'heads'))
- grad_w_gate: float32 [2048, 4096], P(('dp', 'blk'), 'heads')
- grad_w_up: float32 [2048, 4096], P(('dp', 'blk'), 'heads')
- grad_w_down: float32 [4096, 2048], P('heads', ('dp', 'blk'))
The draws below stay inside these ranges and needn't reach their ends.
All inputs are finite; a program needn't handle non-finite values.
Results may differ from the reference program's by a relative error of at most 0.014.
The reference program's roundings to bfloat16 on the way count: a program that leaves them out, or rounds other values in their place, can miss the bound.
Values may be sent and summed in bfloat16 or wider, within the bound.
No kernel may reach another device: no remote copies, remote signals or barrier semaphores. Data moves between devices by JAX's collectives and lax.ppermute only.
A program may use at most 320 MiB of HBM per device.

```python
import jax
import jax.numpy as jnp
from jax import lax

MODEL_WIDTH = 2048
QH = 8
KVH = 2
HD = 128
MIXER_HEADS = 48
MIXER_HEAD_SIZE = 64
STATE_SIZE = 256
FF = 4096
BLOCK = 256
SEQ = 4096
TOKENS = 16384
N_DP = 4
N_BLK = 4


def draw_x_in(key, part):
    key = jax.random.fold_in(key, 11)
    base_key, sign_key, level_key = jax.random.split(key, 3)
    base = jnp.clip(jax.random.normal(base_key, (TOKENS, MODEL_WIDTH), jnp.float32), -6.0, 6.0)
    pattern = jnp.where(jax.random.bernoulli(sign_key, 0.5, (MODEL_WIDTH,)), 1.0, -1.0).astype(jnp.float32)
    span_rows = SEQ // N_BLK
    levels = jax.random.uniform(level_key, (TOKENS // span_rows,), jnp.float32, -1.5, 1.5)
    row_levels = jnp.repeat(levels, span_rows, total_repeat_length=TOKENS)
    return (base + row_levels[:, None] * pattern[None, :]).astype(jnp.bfloat16)


def level_of(own_key, shape, cuts, least, top_value):
    loudness = 1.0
    for axis_at, shards_of in cuts:
        draws = jax.random.uniform(jax.random.fold_in(jax.random.fold_in(own_key, 6), axis_at), (shards_of,), jnp.float32, least / len(cuts), top_value / len(cuts))
        loudness = loudness * jnp.repeat(jnp.exp(draws), shape[axis_at] // shards_of).reshape((-1,) + (1,) * (len(shape) - 1 - axis_at))
    return loudness


def noise(key, extent, scale, most, cuts=(), kind=jnp.bfloat16):
    level = level_of(key, extent, cuts, -0.22, 0.18) if cuts else 1.0
    drawn = jax.random.normal(key, extent, jnp.float32) * scale * level
    return jnp.minimum(jnp.maximum(drawn, -most), most).astype(kind)


def setup_inputs(seed: int = 0) -> dict:
    key_list = jax.random.split(jax.random.key(seed), 21)
    return {
        "x_in": draw_x_in(jax.random.fold_in(key_list[20], 71), 0),
        "out_grad": noise(key_list[1], (TOKENS, MODEL_WIDTH), 1.0, 6.0, ((0, 128),)),
        "norm_one": jnp.clip(1.0 + 0.1 * jax.random.normal(key_list[2], (MODEL_WIDTH,), jnp.float32), 0.5, 1.5).astype(jnp.bfloat16),
        "w_query": noise(key_list[3], (MODEL_WIDTH, QH * HD), MODEL_WIDTH ** -0.5, 0.125, ((0, 16), (1, 8))),
        "w_key": noise(key_list[4], (MODEL_WIDTH, KVH * HD), MODEL_WIDTH ** -0.5, 0.125, ((0, 128),)),
        "w_value": noise(key_list[5], (MODEL_WIDTH, KVH * HD), MODEL_WIDTH ** -0.5, 0.125, ((0, 128),)),
        "output_gate_weight": noise(key_list[6], (MODEL_WIDTH, MIXER_HEADS * MIXER_HEAD_SIZE), MODEL_WIDTH ** -0.5, 0.125, ((0, 16), (1, 8))),
        "mixer_input_weight": noise(key_list[7], (MODEL_WIDTH, MIXER_HEADS * MIXER_HEAD_SIZE), MODEL_WIDTH ** -0.5, 0.125, ((0, 16), (1, 8))),
        "w_delta": noise(key_list[8], (MODEL_WIDTH, MIXER_HEADS), (MODEL_WIDTH // 4) ** -0.5, 0.25, ((0, 16), (1, 8))),
        "w_bmat": noise(key_list[9], (MODEL_WIDTH, STATE_SIZE), (MODEL_WIDTH * 16) ** -0.5, 0.03125, ((0, 128),)),
        "w_cmat": noise(key_list[10], (MODEL_WIDTH, STATE_SIZE), (MODEL_WIDTH * 16) ** -0.5, 0.03125, ((0, 128),)),
        "delta_bias": jnp.clip(jax.random.uniform(key_list[11], (MIXER_HEADS,), jnp.float32, -1.0, 1.0) * level_of(key_list[11], (MIXER_HEADS,), ((0, 8),), -0.4, 0.0), -1.0, 1.0),
        "decay_log": jnp.clip(-9.0 + 6.0 * jax.random.uniform(key_list[12], (MIXER_HEADS,), jnp.float32) ** level_of(key_list[12], (MIXER_HEADS,), ((0, 8),), -0.2, 0.2), -9.0, -3.0),
        "skip_gain": jnp.clip(2.0 * jax.random.uniform(key_list[13], (MIXER_HEADS,), jnp.float32) ** level_of(key_list[13], (MIXER_HEADS,), ((0, 8),), -0.2, 0.2), 0.0, 2.0),
        "w_attn_out": noise(key_list[14], (QH * HD, MODEL_WIDTH), (max(1, QH * HD // SEQ)) ** -0.5, 6.0, ((0, 8), (1, 16))),
        "mixer_output_weight": noise(key_list[15], (MIXER_HEADS * MIXER_HEAD_SIZE, MODEL_WIDTH), (MIXER_HEADS * MIXER_HEAD_SIZE * 64) ** -0.5, 0.013671875, ((0, 8), (1, 16))),
        "norm_two": jnp.clip(1.0 + 0.1 * jax.random.normal(key_list[16], (MODEL_WIDTH,), jnp.float32), 0.5, 1.5).astype(jnp.bfloat16),
        "w_gate": noise(key_list[17], (MODEL_WIDTH, FF), MODEL_WIDTH ** -0.5, 0.125, ((0, 16), (1, 8))),
        "w_up": noise(key_list[18], (MODEL_WIDTH, FF), MODEL_WIDTH ** -0.5, 0.125, ((0, 16), (1, 8))),
        "w_down": noise(key_list[19], (FF, MODEL_WIDTH), FF ** -0.5, 0.09375, ((0, 8), (1, 16))),
    }


HIGH_PRECISION = lax.Precision.HIGHEST
norm_eps = 1e-05
rope_base = 100000000000.0

@jax.custom_vjp
def low(v):
    return lax.optimization_barrier(v.astype(jnp.bfloat16)).astype(jnp.float32)

@jax.custom_vjp
def low_back(v):
    return v

def low_keep(v):
    return (low(v), None)

def low_pass(kept, grad):
    return (grad,)

def back_keep(v):
    return (v, None)

def back_low(kept, grad):
    return (low(grad),)
low.defvjp(low_keep, low_pass)
low_back.defvjp(back_keep, back_low)

def forward_and_reverse(value_in):
    return low(low_back(value_in))

def simple_product(left_side, right_side):
    return jnp.dot(left_side, right_side, precision=HIGH_PRECISION, preferred_element_type=jnp.float32)

def norm_apply(rows_in, gain_in):
    return rows_in * lax.rsqrt(lax.optimization_barrier(jnp.mean(rows_in * rows_in, axis=-1, keepdims=True)) + norm_eps) * gain_in

def rotate(values_in, positions, direction):
    half_width = values_in.shape[-1] // 2
    freqs = rope_base ** (-2.0 * jnp.arange(half_width, dtype=jnp.float32) / values_in.shape[-1])
    angles = positions.astype(jnp.float32)[:, None] * freqs[None, :]
    cosine = jnp.cos(angles)[:, None, :]
    sine = direction * jnp.sin(angles)[:, None, :]
    first_half = values_in[..., :half_width]
    second_half = values_in[..., half_width:]
    return jnp.concatenate([first_half * cosine - second_half * sine, second_half * cosine + first_half * sine], axis=-1)

def ssd_block(carry_state, block_inputs):
    block_x, block_b, block_c, block_delta, block_log = block_inputs
    cumulative = jnp.cumsum(block_log, axis=0)
    sequence_length = block_log.shape[0]
    lower_mask = jnp.arange(sequence_length)[:, None, None] >= jnp.arange(sequence_length)[None, :, None]
    spread = cumulative[:, None, :] - cumulative[None, :, :]
    decay_mat = jnp.where(lower_mask, jnp.exp(jnp.where(lower_mask, spread, 0.0)), 0.0)
    inner_prod = jnp.dot(block_c, block_b.T, precision=HIGH_PRECISION)
    mixing = inner_prod[:, :, None] * decay_mat * block_delta[None, :, :]
    output = jnp.einsum('ijh,jhp->ihp', mixing, block_x, precision=HIGH_PRECISION)
    output = output + jnp.exp(cumulative)[:, :, None] * jnp.einsum('in,hpn->ihp', block_c, carry_state, precision=HIGH_PRECISION)
    ending = cumulative[-1]
    weight_in = jnp.exp(ending[None, :] - cumulative) * block_delta
    weighted_x = weight_in[:, :, None] * block_x
    carry_state = jnp.exp(ending)[:, None, None] * carry_state + jnp.einsum('jhp,jn->hpn', weighted_x, block_b, precision=HIGH_PRECISION)
    return (carry_state, output)

def ssd_sequence(mixer_input, bmat, cmat, delta, log_step):
    sequence_length = mixer_input.shape[0]
    count_blocks = sequence_length // BLOCK

    def split_blocks(array_in):
        return array_in.reshape((count_blocks, BLOCK) + array_in.shape[1:])
    initial_state = jnp.zeros((MIXER_HEADS, MIXER_HEAD_SIZE, STATE_SIZE), jnp.float32)
    final_state, block_outputs = lax.scan(jax.checkpoint(ssd_block), initial_state, (split_blocks(mixer_input), split_blocks(bmat), split_blocks(cmat), split_blocks(delta), split_blocks(log_step)))
    return block_outputs.reshape(sequence_length, MIXER_HEADS, MIXER_HEAD_SIZE)

def attention(queries, key_set, value_set):
    sequence_length = queries.shape[0]
    row_block = min(512, sequence_length)
    group_size = QH // KVH
    keys_wide = jnp.repeat(key_set, group_size, axis=1)
    values_wide = jnp.repeat(value_set, group_size, axis=1)
    score_scale = HD ** (-0.5)
    key_pos = jnp.arange(sequence_length)

    def one_block(row_start):
        query_rows = lax.dynamic_slice_in_dim(queries, row_start, row_block, 0)
        scores = low_back(score_scale * jnp.einsum('rhd,khd->hrk', query_rows, keys_wide, precision=HIGH_PRECISION))
        allowed = (row_start + jnp.arange(row_block))[:, None] >= key_pos[None, :]
        scores = jnp.where(allowed[None], scores, -1e+30)
        log_total = jax.nn.logsumexp(scores, axis=-1, keepdims=True)
        probs_low = low(jnp.exp(scores - log_total))
        return jnp.einsum('hrk,khd->rhd', probs_low, values_wide, precision=HIGH_PRECISION)
    starts = (jnp.arange(sequence_length // row_block) * row_block).astype(jnp.int32)
    blocks = lax.map(jax.checkpoint(one_block), starts)
    return blocks.reshape(sequence_length, QH, HD)

def layer(x_float, norm_one, w_query, w_key, w_value, output_gate_weight, mixer_input_weight, w_delta, w_bmat, w_cmat, delta_bias, decay_log, skip_gain, w_attn_out, mixer_output_weight, norm_two, w_gate, w_up, w_down):
    sequence_length = x_float.shape[0]
    positions = jnp.arange(sequence_length)
    normed_input = low(norm_apply(x_float, norm_one))
    queries = low(rotate(low_back(simple_product(normed_input, w_query)).reshape(sequence_length, QH, HD), positions, 1.0))
    key_set = low(rotate(low_back(simple_product(normed_input, w_key)).reshape(sequence_length, KVH, HD), positions, 1.0))
    value_set = forward_and_reverse(simple_product(normed_input, w_value)).reshape(sequence_length, KVH, HD)
    attended = attention(queries, key_set, value_set)
    attn_part = forward_and_reverse(attended).reshape(sequence_length, QH * HD)
    output_gate = low_back(simple_product(normed_input, output_gate_weight)).reshape(sequence_length, MIXER_HEADS, MIXER_HEAD_SIZE)
    mixer_input = forward_and_reverse(simple_product(normed_input, mixer_input_weight)).reshape(sequence_length, MIXER_HEADS, MIXER_HEAD_SIZE)
    delta = jax.nn.softplus(low_back(simple_product(normed_input, w_delta)) + delta_bias[None, :])
    log_step = -delta * jnp.exp(decay_log)[None, :]
    bmat = forward_and_reverse(simple_product(normed_input, w_bmat))
    cmat = forward_and_reverse(simple_product(normed_input, w_cmat))
    scan_result = ssd_sequence(mixer_input, bmat, cmat, delta, log_step) + skip_gain[:, None] * mixer_input
    gated_output = forward_and_reverse((scan_result * jax.nn.silu(output_gate)).reshape(sequence_length, MIXER_HEADS * MIXER_HEAD_SIZE))
    mixed = low_back(simple_product(attn_part, w_attn_out) + simple_product(gated_output, mixer_output_weight))
    middle = x_float + mixed
    normed_two = low(norm_apply(middle, norm_two))
    gate = low_back(simple_product(normed_two, w_gate))
    upper = low_back(simple_product(normed_two, w_up))
    hidden = low(jax.nn.silu(gate) * upper)
    return middle + low_back(simple_product(hidden, w_down))

def reference(x_in, out_grad, norm_one, w_query, w_key, w_value, output_gate_weight, mixer_input_weight, w_delta, w_bmat, w_cmat, delta_bias, decay_log, skip_gain, w_attn_out, mixer_output_weight, norm_two, w_gate, w_up, w_down):
    params = tuple((array_in.astype(jnp.float32) for array_in in (norm_one, w_query, w_key, w_value, output_gate_weight, mixer_input_weight, w_delta, w_bmat, w_cmat, delta_bias, decay_log, skip_gain, w_attn_out, mixer_output_weight, norm_two, w_gate, w_up, w_down)))
    seq_rows = x_in.reshape(N_DP, SEQ, MODEL_WIDTH)
    seq_grads = out_grad.reshape(N_DP, SEQ, MODEL_WIDTH)
    start_totals = tuple((jnp.zeros_like(array_in) for array_in in params))

    def one_sequence(totals, pair_in):
        tokens_in, grad_in = pair_in
        block_outputs, pull_back = jax.vjp(layer, tokens_in.astype(jnp.float32), *params)
        grads_all = pull_back(grad_in.astype(jnp.float32))
        totals = jax.tree.map(lambda first_arg, second_arg: first_arg + second_arg, totals, tuple(grads_all[1:]))
        return (totals, (block_outputs.astype(jnp.bfloat16), grads_all[0]))
    totals, (acts_out, input_grads) = lax.scan(one_sequence, start_totals, (seq_rows, seq_grads))
    return (acts_out.reshape(TOKENS, MODEL_WIDTH), input_grads.reshape(TOKENS, MODEL_WIDTH), totals[0], totals[1], totals[2], totals[3], totals[4], totals[5], totals[6], totals[7], totals[8], totals[9], totals[10], totals[11], totals[12], totals[13], totals[14], totals[15], totals[16], totals[17])
```

```python
import jax
import jax.numpy as jnp
from jax import lax
from jax.sharding import PartitionSpec as P

QH = 8
KVH = 2
HD = 128
MIXER_HEAD_SIZE = 64
BLOCK = 256


HIGH_PRECISION = lax.Precision.HIGHEST
norm_eps = 1e-05
rope_base = 100000000000.0


def simple_product(left_side, right_side):
    return jnp.dot(left_side, right_side, preferred_element_type=jnp.float32)


def dot_last(left_side, right_side):
    return lax.dot_general(
        left_side, right_side, (((1,), (1,)), ((), ())), preferred_element_type=jnp.float32
    )


def dot_first(left_side, right_side):
    return lax.dot_general(
        left_side, right_side, (((0,), (0,)), ((), ())), preferred_element_type=jnp.float32
    )


def rotate(values_in, positions, direction):
    half_width = values_in.shape[-1] // 2
    freqs = rope_base ** (-2.0 * jnp.arange(half_width, dtype=jnp.float32) / values_in.shape[-1])
    angles = positions.astype(jnp.float32)[:, None] * freqs[None, :]
    cosine = jnp.cos(angles)[:, None, :]
    sine = direction * jnp.sin(angles)[:, None, :]
    first_half = values_in[..., :half_width]
    second_half = values_in[..., half_width:]
    return jnp.concatenate(
        [first_half * cosine - second_half * sine, second_half * cosine + first_half * sine],
        axis=-1,
    )


def ssd_block(carry_state, block_inputs):
    block_x, block_b, block_c, block_delta, block_log = block_inputs
    cumulative = jnp.cumsum(block_log, axis=0)
    sequence_length = block_log.shape[0]
    lower_mask = (
        jnp.arange(sequence_length)[:, None, None] >= jnp.arange(sequence_length)[None, :, None]
    )
    spread = cumulative[:, None, :] - cumulative[None, :, :]
    decay_mat = jnp.where(lower_mask, jnp.exp(jnp.where(lower_mask, spread, 0.0)), 0.0)
    inner_prod = dot_last(block_c.astype(jnp.bfloat16), block_b.astype(jnp.bfloat16))
    mixing = inner_prod[:, :, None] * decay_mat * block_delta[None, :, :]
    output = jnp.einsum("ijh,jhp->ihp", mixing, block_x, precision=HIGH_PRECISION)
    output = output + jnp.exp(cumulative)[:, :, None] * jnp.einsum(
        "in,hpn->ihp", block_c, carry_state, precision=HIGH_PRECISION
    )
    ending = cumulative[-1]
    weight_in = jnp.exp(ending[None, :] - cumulative) * block_delta
    weighted_x = weight_in[:, :, None] * block_x
    carry_state = jnp.exp(ending)[:, None, None] * carry_state + jnp.einsum(
        "jhp,jn->hpn", weighted_x, block_b, precision=HIGH_PRECISION
    )
    return (carry_state, output)


def ssd_local(mixer_input_single, bmat_float, cmat_float, delta, log_step):
    sequence_length, mixer_head_rows, head_size = mixer_input_single.shape
    count_blocks = sequence_length // BLOCK

    def split_blocks(array_in):
        return array_in.reshape((count_blocks, BLOCK) + array_in.shape[1:])

    initial_state = jnp.zeros(
        (mixer_head_rows, head_size, bmat_float.shape[1]), mixer_input_single.dtype
    )
    final_state, block_outputs = lax.scan(
        ssd_block,
        initial_state,
        (
            split_blocks(mixer_input_single),
            split_blocks(bmat_float),
            split_blocks(cmat_float),
            split_blocks(delta),
            split_blocks(log_step),
        ),
    )
    return (
        block_outputs.reshape(sequence_length, mixer_head_rows, head_size),
        jnp.sum(log_step, axis=0),
        final_state,
    )


def incoming(cmat_float, log_step, entry_state):
    cumulative = jnp.cumsum(log_step, axis=0)
    return jnp.exp(cumulative)[:, :, None] * jnp.einsum(
        "tn,hpn->thp", cmat_float, entry_state, precision=HIGH_PRECISION
    )


def score_block(query_rows, row_start, key_all, key_start, row_block):
    key_rows = lax.dynamic_slice_in_dim(key_all, key_start, row_block, 0)
    raw_scores = jnp.einsum(
        "rhd,kd->hrk", query_rows, key_rows, preferred_element_type=jnp.float32
    ) * key_rows.shape[1] ** (-0.5)
    allowed = (row_start + jnp.arange(row_block))[:, None] >= (key_start + jnp.arange(row_block))[
        None, :
    ]
    return (jnp.where(allowed[None], raw_scores, -1e30), key_rows)


def attend(queries, key_all, value_all, offset):
    span_length, query_heads, head_size = queries.shape
    row_block = min(512, span_length)

    def query_block(block_index):
        row_start = block_index * row_block
        query_rows = lax.dynamic_slice_in_dim(queries, row_start, row_block, 0)
        global_start = offset + row_start
        key_count = global_start // row_block + 1

        def peak_step(key_index, carried):
            running_top, running_sum = carried
            scores = score_block(
                query_rows, global_start, key_all, key_index * row_block, row_block
            )[0]
            new_top = jnp.maximum(running_top, jnp.max(scores, axis=-1))
            running_sum = running_sum * jnp.exp(running_top - new_top) + jnp.sum(
                jnp.exp(scores - new_top[:, :, None]), axis=-1
            )
            return (new_top, running_sum)

        start_top = jnp.full((query_heads, row_block), -1e30, jnp.float32)
        start_sum = jnp.zeros((query_heads, row_block), jnp.float32)
        running_top, running_sum = lax.fori_loop(0, key_count, peak_step, (start_top, start_sum))
        log_total = running_top + jnp.log(running_sum)

        def value_step(key_index, summed):
            scores = score_block(
                query_rows, global_start, key_all, key_index * row_block, row_block
            )[0]
            value_rows = lax.dynamic_slice_in_dim(value_all, key_index * row_block, row_block, 0)
            probs_low = jnp.exp(scores - log_total[:, :, None]).astype(jnp.bfloat16)
            return summed + jnp.einsum(
                "hrk,kd->rhd", probs_low, value_rows, preferred_element_type=jnp.float32
            )

        attended = lax.fori_loop(
            0, key_count, value_step, jnp.zeros((row_block, query_heads, head_size), jnp.float32)
        )
        return (attended, log_total)

    block_outputs, log_totals = lax.map(query_block, jnp.arange(span_length // row_block))
    return (block_outputs.reshape(span_length, query_heads, head_size), log_totals)


def attend_back(queries, key_all, value_all, attended, log_totals, d_attn, offset):
    span_length, query_heads, head_size = queries.shape
    row_block = min(512, span_length)
    score_scale = head_size ** (-0.5)

    def query_block(carried, block_index):
        d_keys, d_values = carried
        row_start = block_index * row_block
        query_rows = lax.dynamic_slice_in_dim(queries, row_start, row_block, 0)
        grad_rows = lax.dynamic_slice_in_dim(d_attn, row_start, row_block, 0)
        out_rows = lax.dynamic_slice_in_dim(attended, row_start, row_block, 0)
        log_total = lax.dynamic_index_in_dim(log_totals, block_index, 0, keepdims=False)
        delta_row = jnp.sum(grad_rows.astype(jnp.float32) * out_rows, axis=-1).T
        global_start = offset + row_start
        key_count = global_start // row_block + 1

        def key_step(key_index, inner):
            d_query, d_keys, d_values = inner
            key_start = key_index * row_block
            scores, key_rows = score_block(query_rows, global_start, key_all, key_start, row_block)
            value_rows = lax.dynamic_slice_in_dim(value_all, key_start, row_block, 0)
            probs = jnp.exp(scores - log_total[:, :, None])
            value_part = jnp.einsum(
                "hrk,rhd->kd",
                probs.astype(jnp.bfloat16),
                grad_rows,
                preferred_element_type=jnp.float32,
            )
            d_probs = jnp.einsum(
                "rhd,kd->hrk", grad_rows, value_rows, preferred_element_type=jnp.float32
            )
            d_scores = (probs * (d_probs - delta_row[:, :, None])).astype(jnp.bfloat16)
            d_query = (
                d_query
                + jnp.einsum("hrk,kd->rhd", d_scores, key_rows, preferred_element_type=jnp.float32)
                * score_scale
            )
            key_part = (
                jnp.einsum("hrk,rhd->kd", d_scores, query_rows, preferred_element_type=jnp.float32)
                * score_scale
            )
            d_keys = lax.dynamic_update_slice_in_dim(
                d_keys,
                lax.dynamic_slice_in_dim(d_keys, key_start, row_block, 0) + key_part,
                key_start,
                0,
            )
            d_values = lax.dynamic_update_slice_in_dim(
                d_values,
                lax.dynamic_slice_in_dim(d_values, key_start, row_block, 0) + value_part,
                key_start,
                0,
            )
            return (d_query, d_keys, d_values)

        start_query = jnp.zeros((row_block, query_heads, head_size), jnp.float32)
        d_query, d_keys, d_values = lax.fori_loop(
            0, key_count, key_step, (start_query, d_keys, d_values)
        )
        return ((d_keys, d_values), d_query)

    start_keys = jnp.zeros(key_all.shape, jnp.float32)
    (d_keys, d_values), d_queries = lax.scan(
        query_block,
        (start_keys, jnp.zeros(value_all.shape, jnp.float32)),
        jnp.arange(span_length // row_block),
    )
    return (d_queries.reshape(span_length, query_heads, head_size), d_keys, d_values)


def span_rows(value_in):
    return lax.all_gather(value_in, "heads", axis=0, tiled=True)


def row_sum(summed):
    return lax.psum_scatter(
        summed.astype(jnp.bfloat16), "heads", scatter_dimension=0, tiled=True
    ).astype(jnp.float32)


def weight_sum(parts):
    return lax.psum_scatter(
        jnp.concatenate(parts, axis=1), ("dp", "blk"), scatter_dimension=0, tiled=True
    ).astype(jnp.float32)


def low_first(left_side, right_side):
    return dot_first(left_side, right_side).astype(jnp.bfloat16)


def split_columns(value_in, widths):
    pieces, start = [], 0
    for width in widths:
        pieces.append(value_in[:, start : start + width])
        start += width
    return pieces


def inverse_rms(rows_in):
    return lax.rsqrt(jnp.mean(rows_in * rows_in, axis=-1, keepdims=True) + norm_eps)


def norm_back(rows_in, gain_in, cotangent):
    inverse = inverse_rms(rows_in)
    scaled = rows_in * inverse
    weighted = cotangent * gain_in
    return inverse * (weighted - scaled * jnp.mean(weighted * scaled, axis=-1, keepdims=True))


def shards(
    x_in,
    out_grad,
    norm_one,
    w_query,
    w_key,
    w_value,
    output_gate_weight,
    mixer_input_weight,
    w_delta,
    w_bmat,
    w_cmat,
    delta_bias,
    decay_log,
    skip_gain,
    w_attn_out,
    mixer_output_weight,
    norm_two,
    w_gate,
    w_up,
    w_down,
):
    heads_count = lax.axis_size("heads")
    head_rank = lax.axis_index("heads")
    block_rank = lax.axis_index("blk")
    own_rows = x_in.shape[0]
    span_length = own_rows * heads_count
    span_start = block_rank * span_length
    span_pos = span_start + jnp.arange(span_length)
    query_width = w_query.shape[1]
    query_heads = query_width // HD
    mixer_width = mixer_input_weight.shape[1]
    mixer_head_rows = mixer_width // MIXER_HEAD_SIZE
    state_size = w_bmat.shape[1]
    hidden_width = w_gate.shape[1]
    kv_index = head_rank * query_heads // (QH // KVH)

    shared = jnp.concatenate(
        [w_key, w_value, w_bmat, w_cmat, norm_one[:, None], norm_two[:, None]], axis=1
    )
    shared = lax.all_gather(shared, "heads", axis=0, tiled=True)
    key_part = lax.dynamic_slice_in_dim(shared, kv_index * HD, HD, 1)
    value_part = lax.dynamic_slice_in_dim(shared, KVH * HD + kv_index * HD, HD, 1)
    state_part = shared[:, 2 * KVH * HD : 2 * KVH * HD + 2 * state_size]
    gain_part = shared[:, 2 * KVH * HD + 2 * state_size :]
    rows_of = w_query.shape[0]
    misc_width = 128
    misc_part = jnp.concatenate(
        [
            w_delta,
            gain_part,
            jnp.zeros((rows_of, misc_width - mixer_head_rows - 2), w_delta.dtype),
        ],
        axis=1,
    )
    in_widths = (HD, HD, state_size, state_size, query_width, mixer_width, mixer_width, misc_width)
    in_full = lax.all_gather(
        jnp.concatenate(
            [
                key_part,
                value_part,
                state_part,
                w_query,
                output_gate_weight,
                mixer_input_weight,
                misc_part,
            ],
            axis=1,
        ),
        ("dp", "blk"),
        axis=0,
        tiled=True,
    )
    out_widths = (query_width, mixer_width, hidden_width, hidden_width, hidden_width)
    out_full = lax.all_gather(
        jnp.concatenate([w_attn_out.T, mixer_output_weight.T, w_gate, w_up, w_down.T], axis=1),
        ("dp", "blk"),
        axis=0,
        tiled=True,
    )
    misc_full = split_columns(in_full, in_widths)[-1]
    gain_one = misc_full[:, mixer_head_rows].astype(jnp.float32)
    gain_two = misc_full[:, mixer_head_rows + 1].astype(jnp.float32)
    attnout_t, ssmout_t, gate_full, up_full, down_t = split_columns(out_full, out_widths)

    x_float = x_in.astype(jnp.float32)
    x_span = span_rows(x_in).astype(jnp.float32)
    x_scaled = x_span * inverse_rms(x_span)
    normed_input = (x_scaled * gain_one).astype(jnp.bfloat16)
    ffn_grad = span_rows(out_grad)

    projected = simple_product(normed_input, in_full)
    key_raw, value_raw, bmat_raw, cmat_raw, query_raw, output_gate, ssm_raw, misc_raw = (
        split_columns(projected, in_widths)
    )
    keys_own = rotate(key_raw.reshape(span_length, 1, HD), span_pos, 1.0).astype(jnp.bfloat16)
    values_own = value_raw.astype(jnp.bfloat16)
    keys_values = lax.all_gather(
        jnp.concatenate([keys_own.reshape(span_length, HD), values_own], axis=1),
        "blk",
        axis=0,
        tiled=True,
    )
    key_all, value_all = (keys_values[:, :HD], keys_values[:, HD:])
    queries = rotate(
        query_raw.reshape(span_length, query_heads, HD), span_pos, 1.0
    ).astype(jnp.bfloat16)
    output_gate = output_gate.reshape(span_length, mixer_head_rows, MIXER_HEAD_SIZE)
    mixer_input_single = (
        ssm_raw.astype(jnp.bfloat16)
        .astype(jnp.float32)
        .reshape(span_length, mixer_head_rows, MIXER_HEAD_SIZE)
    )
    bmat_float = bmat_raw.astype(jnp.bfloat16).astype(jnp.float32)
    cmat_float = cmat_raw.astype(jnp.bfloat16).astype(jnp.float32)
    delta_pre = misc_raw[:, :mixer_head_rows] + delta_bias[None, :]
    delta = jax.nn.softplus(delta_pre)
    decay_rate = jnp.exp(decay_log)
    log_step = -delta * decay_rate[None, :]

    (local_out, local_log, local_state), ssd_pull = jax.vjp(
        ssd_local, mixer_input_single, bmat_float, cmat_float, delta, log_step
    )
    state_rows = mixer_head_rows * MIXER_HEAD_SIZE
    state_shape = local_state.shape

    def gather_states(state):
        log_rows = jnp.broadcast_to(
            jnp.pad(local_log, (0, 8 - mixer_head_rows))[:, None], (8, state_size)
        )
        both = lax.all_gather(
            jnp.concatenate([state.reshape(state_rows, state_size), log_rows], axis=0), "blk"
        )
        return (
            both[:, state_rows : state_rows + mixer_head_rows, 0],
            both[:, :state_rows].reshape((-1,) + state_shape),
        )

    def enter(logs, states, reverse):
        devices = logs.shape[0]
        before = jnp.zeros(state_shape, jnp.float32)
        for k in range(devices):
            at = devices - 1 - k if reverse else k
            reached = at > block_rank if reverse else at < block_rank
            new = jnp.exp(logs[at])[:, None, None] * before + states[at]
            before = jnp.where(reached, new, before)
        return before

    entry_state = enter(*gather_states(local_state), False)
    entry_out, entry_pull = jax.vjp(incoming, cmat_float, log_step, entry_state)
    attended, log_totals = attend(queries, key_all, value_all, span_start)
    attn_part = attended.astype(jnp.bfloat16).reshape(span_length, query_width)
    scan_result = local_out + entry_out + skip_gain[None, :, None] * mixer_input_single
    gate_sigmoid = jax.nn.sigmoid(output_gate)
    gated_output = (
        (scan_result * (output_gate * gate_sigmoid))
        .astype(jnp.bfloat16)
        .reshape(span_length, mixer_width)
    )
    mixed = row_sum(dot_last(attn_part, attnout_t) + dot_last(gated_output, ssmout_t))
    middle = x_float + mixed
    normed_two_own = (middle * inverse_rms(middle) * gain_two).astype(jnp.bfloat16)
    normed_two = span_rows(normed_two_own)
    ffn_gate = simple_product(normed_two, gate_full)
    ffn_up = simple_product(normed_two, up_full)
    ffn_sig = jax.nn.sigmoid(ffn_gate)
    hidden = (ffn_gate * ffn_sig * ffn_up).astype(jnp.bfloat16)
    ffn_out = row_sum(dot_last(hidden, down_t))
    activations = (middle + ffn_out).astype(jnp.bfloat16)

    d_hidden = simple_product(ffn_grad, down_t)
    d_ffn_gate = (d_hidden * ffn_up * (ffn_sig * (1.0 + ffn_gate * (1.0 - ffn_sig)))).astype(
        jnp.bfloat16
    )
    d_ffn_up = (d_hidden * (ffn_gate * ffn_sig)).astype(jnp.bfloat16)
    d_normed_two = row_sum(dot_last(d_ffn_gate, gate_full) + dot_last(d_ffn_up, up_full))
    ffn_sums = weight_sum(
        [
            low_first(normed_two, d_ffn_gate),
            low_first(normed_two, d_ffn_up),
            low_first(ffn_grad, hidden),
        ]
    )
    grad_gate, grad_up, grad_down_t = split_columns(ffn_sums, (hidden_width,) * 3)
    grad_two_part = jnp.sum(d_normed_two * (middle * inverse_rms(middle)), axis=0)
    d_middle = out_grad.astype(jnp.float32) + norm_back(middle, gain_two, d_normed_two)
    mix_grad = span_rows(d_middle.astype(jnp.bfloat16))
    d_attn = (
        simple_product(mix_grad, attnout_t)
        .astype(jnp.bfloat16)
        .reshape(span_length, query_heads, HD)
    )
    d_gated = (
        simple_product(mix_grad, ssmout_t)
        .astype(jnp.bfloat16)
        .astype(jnp.float32)
        .reshape(span_length, mixer_head_rows, MIXER_HEAD_SIZE)
    )
    out_sums = weight_sum([low_first(mix_grad, attn_part), low_first(mix_grad, gated_output)])
    grad_attnout_t, grad_ssmout_t = split_columns(out_sums, (query_width, mixer_width))

    d_scanned = d_gated * (output_gate * gate_sigmoid)
    d_gate_z = (
        (d_gated * scan_result * (gate_sigmoid * (1.0 + output_gate * (1.0 - gate_sigmoid))))
        .astype(jnp.bfloat16)
        .reshape(span_length, mixer_width)
    )
    d_cmat_entry, d_log_entry, d_entry_state = entry_pull(d_scanned)
    back_state = enter(*gather_states(d_entry_state), True)
    d_local_log = jnp.exp(local_log) * jnp.sum(entry_state * back_state, axis=(1, 2))
    d_ssm_local, d_bmat_f, d_cmat_f, d_delta_f, d_log_f = ssd_pull(
        (d_scanned, d_local_log, back_state)
    )
    d_ssm_in = (
        (d_ssm_local + skip_gain[None, :, None] * d_scanned)
        .astype(jnp.bfloat16)
        .reshape(span_length, mixer_width)
    )
    d_log_total = d_log_f + d_log_entry
    d_delta = d_delta_f - d_log_total * decay_rate[None, :]
    grad_decay_part = jnp.sum(d_log_total * log_step, axis=0)
    grad_skip_part = jnp.sum(d_scanned * mixer_input_single, axis=(0, 2))
    d_pre_f = d_delta * jax.nn.sigmoid(delta_pre)
    grad_bias_part = jnp.sum(d_pre_f, axis=0)
    d_pre = jnp.pad(d_pre_f.astype(jnp.bfloat16), ((0, 0), (0, misc_width - mixer_head_rows)))
    d_bmat = d_bmat_f.astype(jnp.bfloat16)
    d_cmat = (d_cmat_f + d_cmat_entry).astype(jnp.bfloat16)
    d_queries, d_keys_all, d_values_all = attend_back(
        queries, key_all, value_all, attended, log_totals, d_attn, span_start
    )
    d_keys_values = lax.psum_scatter(
        jnp.concatenate([d_keys_all, d_values_all], axis=1).astype(jnp.bfloat16),
        "blk",
        scatter_dimension=0,
        tiled=True,
    ).astype(jnp.float32)
    d_key = (
        rotate(d_keys_values[:, :HD].reshape(span_length, 1, HD), span_pos, -1.0)
        .astype(jnp.bfloat16)
        .reshape(span_length, HD)
    )
    d_value = d_keys_values[:, HD:].astype(jnp.bfloat16)
    d_query = (
        rotate(d_queries, span_pos, -1.0).astype(jnp.bfloat16).reshape(span_length, query_width)
    )
    d_projected = jnp.concatenate(
        [d_key, d_value, d_bmat, d_cmat, d_query, d_gate_z, d_ssm_in, d_pre], axis=1
    )
    d_normed_term = dot_last(d_projected, in_full)
    grad_one_part = jnp.sum(d_normed_term * x_scaled, axis=0)
    d_normed = row_sum(d_normed_term)
    in_grads = dot_first(normed_input, d_projected)
    small = jnp.stack([grad_bias_part, grad_decay_part, grad_skip_part])
    small = jnp.pad(small, ((0, 8 - small.shape[0]), (0, misc_width - mixer_head_rows)))
    small_sums = jnp.sum(lax.all_gather(small, ("dp", "blk")), axis=0)[:, :mixer_head_rows]
    column = jnp.arange(in_grads.shape[1])[None, :]
    misc_at = in_grads.shape[1] - misc_width + mixer_head_rows
    for k, value in enumerate((grad_one_part, grad_two_part)):
        in_grads = jnp.where(column == misc_at + k, value[:, None], in_grads)
    in_sums = weight_sum([in_grads.astype(jnp.bfloat16)])
    (
        grad_key_half,
        grad_value_half,
        grad_bmat_part,
        grad_cmat_part,
        grad_query,
        grad_gatez,
        grad_ssmx,
        misc_sums,
    ) = split_columns(in_sums, in_widths)
    kv_zeros = jnp.zeros((rows_of, KVH * HD), jnp.float32)
    shared_sums = lax.psum_scatter(
        jnp.concatenate(
            [
                lax.dynamic_update_slice_in_dim(kv_zeros, grad_key_half, kv_index * HD, 1),
                lax.dynamic_update_slice_in_dim(kv_zeros, grad_value_half, kv_index * HD, 1),
                grad_bmat_part,
                grad_cmat_part,
                misc_sums,
            ],
            axis=1,
        ),
        "heads",
        scatter_dimension=0,
        tiled=True,
    )
    grad_key, grad_value, grad_bmat, grad_cmat, gain_sums = split_columns(
        shared_sums, (KVH * HD, KVH * HD, state_size, state_size, misc_width)
    )
    input_grad = d_middle + norm_back(x_float, gain_one, d_normed)
    return (
        activations,
        input_grad,
        gain_sums[:, mixer_head_rows],
        grad_query,
        grad_key,
        grad_value,
        grad_gatez,
        grad_ssmx,
        misc_sums[:, :mixer_head_rows],
        grad_bmat,
        grad_cmat,
        small_sums[0],
        small_sums[1],
        small_sums[2],
        grad_attnout_t.T,
        grad_ssmout_t.T,
        gain_sums[:, mixer_head_rows + 1],
        grad_gate,
        grad_up,
        grad_down_t.T,
    )


def solution(mesh):
    placed = (
        P(("dp", "blk", "heads"), None),
        P(("dp", "blk", "heads"), None),
        P(("dp", "blk", "heads")),
        P(("dp", "blk"), "heads"),
        P(("dp", "blk", "heads"), None),
        P(("dp", "blk", "heads"), None),
        P(("dp", "blk"), "heads"),
        P(("dp", "blk"), "heads"),
        P(("dp", "blk"), "heads"),
        P(("dp", "blk", "heads"), None),
        P(("dp", "blk", "heads"), None),
        P("heads"),
        P("heads"),
        P("heads"),
        P("heads", ("dp", "blk")),
        P("heads", ("dp", "blk")),
        P(("dp", "blk", "heads")),
        P(("dp", "blk"), "heads"),
        P(("dp", "blk"), "heads"),
        P("heads", ("dp", "blk")),
    )
    return jax.shard_map(
        shards,
        mesh=mesh,
        in_specs=placed,
        out_specs=(
            P(("dp", "blk", "heads"), None),
            P(("dp", "blk", "heads"), None),
            P(("dp", "blk", "heads")),
            P(("dp", "blk"), "heads"),
            P(("dp", "blk", "heads"), None),
            P(("dp", "blk", "heads"), None),
            P(("dp", "blk"), "heads"),
            P(("dp", "blk"), "heads"),
            P(("dp", "blk"), "heads"),
            P(("dp", "blk", "heads"), None),
            P(("dp", "blk", "heads"), None),
            P("heads"),
            P("heads"),
            P("heads"),
            P("heads", ("dp", "blk")),
            P("heads", ("dp", "blk")),
            P(("dp", "blk", "heads")),
            P(("dp", "blk"), "heads"),
            P(("dp", "blk"), "heads"),
            P("heads", ("dp", "blk")),
        ),
        check_vma=False,
    )
```

```python
import functools

import jax
import jax.numpy as jnp
from jax import lax
from jax.experimental import pallas as pl
from jax.experimental.pallas import tpu as pltpu
from jax.sharding import PartitionSpec as P

QH = 8
KVH = 2
HD = 128
MIXER_HEAD_SIZE = 64
BLOCK = 256
LANES = 128
LOG2_E = 1.4426950408889634


HIGH_PRECISION = lax.Precision.HIGHEST
norm_eps = 1e-05
rope_base = 100000000000.0


def simple_product(left_side, right_side):
    return jnp.dot(left_side, right_side, preferred_element_type=jnp.float32)


def dot_last(left_side, right_side):
    return lax.dot_general(
        left_side, right_side, (((1,), (1,)), ((), ())), preferred_element_type=jnp.float32
    )


def dot_first(left_side, right_side):
    return lax.dot_general(
        left_side, right_side, (((0,), (0,)), ((), ())), preferred_element_type=jnp.float32
    )


def compiler_params():
    return pltpu.CompilerParams(vmem_limit_bytes=50 * 1024 * 1024)


def in_vmem(count):
    return [pl.BlockSpec(memory_space=pltpu.VMEM)] * count


def mul(left_side, right_side):
    return jnp.dot(left_side, right_side, preferred_element_type=jnp.float32)


def tile_scores(key_rows, query_rows, head_size):
    return dot_last(key_rows, query_rows) * (head_size**-0.5 * LOG2_E)


def causal(scores):
    key_at = lax.broadcasted_iota(jnp.int32, scores.shape, 0)
    query_at = lax.broadcasted_iota(jnp.int32, scores.shape, 1)
    return jnp.where(key_at <= query_at, scores, -1e30)


def rope_kernel(raw_ref, cos_ref, sin_ref, query_ref, kv_ref):
    head_size = query_ref.shape[1]
    cosine, sine = (cos_ref[...], sin_ref[...])

    def turn(value):
        return (value * cosine + pltpu.roll(value, head_size // 2, 1) * sine).astype(jnp.bfloat16)

    kv_ref[:, :head_size] = turn(raw_ref[:, :head_size])
    kv_ref[:, head_size:] = raw_ref[:, head_size : 2 * head_size].astype(jnp.bfloat16)
    query_ref[...] = turn(raw_ref[:, 2 * head_size :])


def rope(raw, cosine, sine):
    rows, head_size = cosine.shape
    by_block = lambda columns: pl.BlockSpec((BLOCK, columns), lambda c: (c, 0))
    return pl.pallas_call(
        rope_kernel,
        grid=(rows // BLOCK,),
        out_shape=(
            jax.ShapeDtypeStruct((rows, head_size), jnp.bfloat16),
            jax.ShapeDtypeStruct((rows, 2 * head_size), jnp.bfloat16),
        ),
        in_specs=[by_block(3 * head_size), by_block(head_size), by_block(head_size)],
        out_specs=(by_block(head_size), by_block(2 * head_size)),
        compiler_params=compiler_params(),
        cost_estimate=pl.CostEstimate(flops=1_000_000, bytes_accessed=8_000_000, transcendentals=0),
        name="rope",
    )(raw, cosine, sine)


def attend_kernel(rank_ref, query_ref, own_ref, *refs):
    pieces, (out_ref, low_ref, log_ref) = (refs[:-3], refs[-3:])
    span_length, head_size = query_ref.shape
    tile = own_ref.shape[0] // 2
    for block in range(span_length // tile):
        here = slice(block * tile, (block + 1) * tile)
        query_rows = query_ref[here, :]

        def step(kv_rows, carried, masked=False):
            top, total, summed = carried
            scores = tile_scores(kv_rows[:, :head_size], query_rows, head_size)
            if masked:
                scores = causal(scores)
            new_top = jnp.maximum(top, jnp.max(scores, axis=0, keepdims=True))
            probs = jnp.exp2(scores - new_top)
            scale = jnp.exp2(top - new_top)
            total = total * scale + jnp.sum(probs, axis=0, keepdims=True)
            summed = summed * scale + dot_first(kv_rows[:, head_size:], probs.astype(jnp.bfloat16))
            return (new_top, total, summed)

        carried = (
            jnp.full((1, tile), -1e30, jnp.float32),
            jnp.zeros((1, tile), jnp.float32),
            jnp.zeros((head_size, tile), jnp.float32),
        )
        carried = step(own_ref[here, :], carried, True)
        for earlier in range(block):
            carried = step(own_ref[earlier * tile : (earlier + 1) * tile, :], carried)
        for distance in range(1, 1 + len(pieces) // 2):
            pair = pieces[2 * distance - 2 : 2 * distance]

            def both(_, carried, pair=pair):
                return step(pair[1][...], step(pair[0][...], carried))

            valid = (rank_ref[0] >= distance).astype(jnp.int32)
            carried = lax.fori_loop(0, valid, both, carried)
        top, total, summed = carried
        result = summed / total
        out_ref[:, here] = result
        low_ref[here, :] = result.T.astype(jnp.bfloat16)
        log_ref[:, here] = top + jnp.log2(total)


def attend(rank, queries, own, pieces):
    span_length, head_size = queries.shape
    return pl.pallas_call(
        attend_kernel,
        out_shape=(
            jax.ShapeDtypeStruct((head_size, span_length), jnp.float32),
            jax.ShapeDtypeStruct((span_length, head_size), jnp.bfloat16),
            jax.ShapeDtypeStruct((1, span_length), jnp.float32),
        ),
        in_specs=[pl.BlockSpec(memory_space=pltpu.SMEM)] + in_vmem(2 + len(pieces)),
        out_specs=tuple(in_vmem(3)),
        compiler_params=compiler_params(),
        cost_estimate=pl.CostEstimate(
            flops=10_000_000_000, bytes_accessed=4_000_000, transcendentals=4_000_000
        ),
        name="attend",
    )(rank, queries, own, *pieces)


def attend_back_kernel(rank_ref, query_ref, own_ref, *refs):
    pieces, refs = (refs[:-9], refs[-9:])
    out_ref, log_ref, grad_ref, cos_ref, sin_ref, d_query_ref, d_own_ref, d_far_ref, sums_ref = refs
    span_length, head_size = query_ref.shape
    tile = own_ref.shape[0] // 2
    score_scale = head_size**-0.5
    sums_ref[...] = jnp.zeros_like(sums_ref)
    for block in range(span_length // tile):
        here = slice(block * tile, (block + 1) * tile)
        query_rows = query_ref[here, :]
        grad_rows = grad_ref[here, :head_size]
        log_total = log_ref[:, here]
        delta_row = jnp.sum(
            grad_rows.astype(jnp.float32).T * out_ref[:, here], axis=0, keepdims=True
        )

        def step(kv_ref, start, at, d_query, masked=False):
            key_rows = kv_ref[start : start + tile, :head_size]
            scores = tile_scores(key_rows, query_rows, head_size)
            if masked:
                scores = causal(scores)
            probs = jnp.exp2(scores - log_total)
            d_probs = dot_last(kv_ref[start : start + tile, head_size:], grad_rows)
            d_scores = (probs * (d_probs - delta_row)).astype(jnp.bfloat16)
            rows = slice(at * tile, (at + 1) * tile)
            sums_ref[rows, head_size:] += mul(probs.astype(jnp.bfloat16), grad_rows)
            sums_ref[rows, :head_size] += mul(d_scores, query_rows)
            return d_query + dot_first(key_rows, d_scores)

        d_query = jnp.zeros((head_size, tile), jnp.float32)
        d_query = step(own_ref, block * tile, block, d_query, True)
        for earlier in range(block):
            d_query = step(own_ref, earlier * tile, earlier, d_query)
        for distance in range(1, 1 + len(pieces) // 2):

            def both(_, d_query, distance=distance):
                for k in (2 * distance - 2, 2 * distance - 1):
                    d_query = step(pieces[k], 0, 2 + k, d_query)
                return d_query

            valid = (rank_ref[0] >= distance).astype(jnp.int32)
            d_query = lax.fori_loop(0, valid, both, d_query)
        turned = d_query.T * score_scale
        d_query_ref[here, :] = (
            turned * cos_ref[here, :] - pltpu.roll(turned, head_size // 2, 1) * sin_ref[here, :]
        ).astype(jnp.bfloat16)
    lane = lax.broadcasted_iota(jnp.int32, (tile, 2 * head_size), 1)
    scale = jnp.where(lane < head_size, score_scale, 1.0)
    for at in range(2):
        rows = slice(at * tile, (at + 1) * tile)
        d_own_ref[rows, :] = sums_ref[rows, :] * scale
    for k in range(len(pieces)):
        rows = slice((2 + k) * tile, (3 + k) * tile)
        into = (k % 2) * (len(pieces) // 2) + k // 2
        d_far_ref[into * tile : (into + 1) * tile, :] = (sums_ref[rows, :] * scale).astype(
            jnp.bfloat16
        )


def attend_back(rank, queries, own, pieces, attended, log_totals, d_attn, cosine, sine):
    tile = own.shape[0] // 2
    return pl.pallas_call(
        attend_back_kernel,
        out_shape=(
            jax.ShapeDtypeStruct(queries.shape, jnp.bfloat16),
            jax.ShapeDtypeStruct(own.shape, jnp.float32),
            jax.ShapeDtypeStruct((len(pieces) * tile, own.shape[1]), jnp.bfloat16),
        ),
        in_specs=[pl.BlockSpec(memory_space=pltpu.SMEM)] + in_vmem(7 + len(pieces)),
        out_specs=tuple(in_vmem(3)),
        scratch_shapes=[pltpu.VMEM(((2 + len(pieces)) * tile, own.shape[1]), jnp.float32)],
        compiler_params=compiler_params(),
        cost_estimate=pl.CostEstimate(
            flops=25_000_000_000, bytes_accessed=8_000_000, transcendentals=4_000_000
        ),
        name="attend_back",
    )(rank, queries, own, *pieces, attended, log_totals, d_attn, cosine, sine)


def reorder_kernel(ranks_ref, *refs):
    out_ref = refs[-1]
    start = 0
    for ref in refs[:-1]:
        out_ref[:, start : start + ref.shape[1]] = ref[...].astype(out_ref.dtype)
        start += ref.shape[1]


def reorder(ranks, pieces, inverse=False):
    count = ranks.shape[0]
    rows = pieces[0].shape[0] // count
    width = sum(piece.shape[1] for piece in pieces)
    there = lambda k, ranks: (ranks[k], 0)
    here = lambda k, ranks: (k, 0)
    return pl.pallas_call(
        reorder_kernel,
        grid_spec=pltpu.PrefetchScalarGridSpec(
            num_scalar_prefetch=1,
            grid=(count,),
            in_specs=[
                pl.BlockSpec((rows, piece.shape[1]), here if inverse else there)
                for piece in pieces
            ],
            out_specs=pl.BlockSpec((rows, width), there if inverse else here),
        ),
        out_shape=jax.ShapeDtypeStruct((count * rows, width), jnp.bfloat16),
        compiler_params=compiler_params(),
        cost_estimate=pl.CostEstimate(
            flops=0, bytes_accessed=4 * count * rows * width, transcendentals=0
        ),
        name="reorder",
    )(ranks, *pieces)


def lower_ones(size, dtype=jnp.float32):
    row = lax.broadcasted_iota(jnp.int32, (size, size), 0)
    column = lax.broadcasted_iota(jnp.int32, (size, size), 1)
    return (row >= column).astype(dtype)


def precise(left_side, right_side):
    return jnp.dot(
        left_side, right_side, precision=HIGH_PRECISION, preferred_element_type=jnp.float32
    )


def spread_heads(columns, head_size, width):
    lane = lax.broadcasted_iota(jnp.int32, (columns.shape[0], 2 * head_size), 1)
    pairs = [
        jnp.where(lane < head_size, columns[:, k : k + 1], columns[:, k + 1 : k + 2])
        for k in range(0, width // head_size, 2)
    ]
    return jnp.concatenate(pairs, axis=1)


def head_ones(width, head_size, lanes, dtype):
    at = lax.broadcasted_iota(jnp.int32, (width, lanes), 0)
    lane = lax.broadcasted_iota(jnp.int32, (width, lanes), 1)
    low = lane * head_size
    return ((at >= low) & (at < low + head_size)).astype(dtype)


def scan_first_kernel(
    pre_ref, bias_ref, rate_ref, x_ref, b_ref, delta_ref, cum_ref, delta_row_ref, cum_row_ref, state_ref, log_ref
):
    @pl.when(pl.program_id(0) == 0)
    def _():
        state_ref[...] = jnp.zeros_like(state_ref)
        log_ref[...] = jnp.zeros_like(log_ref)

    delta = jax.nn.softplus(pre_ref[...] + bias_ref[...])
    log_step = -delta * rate_ref[...]
    cumulative = precise(lower_ones(log_step.shape[0]), log_step)
    delta_ref[...] = delta
    cum_ref[...] = cumulative
    delta_row_ref[...] = delta.T[:8]
    cum_row_ref[...] = cumulative.T[:8]
    ending = cumulative[-1:, :]
    weight = jnp.exp(ending - cumulative + log_ref[...]) * delta
    width = x_ref.shape[1]
    x_low = x_ref[...].astype(jnp.bfloat16).astype(jnp.float32)
    weighted = (x_low * spread_heads(weight, MIXER_HEAD_SIZE, width)).astype(jnp.bfloat16)
    state_ref[...] += dot_first(b_ref[...].astype(jnp.bfloat16), weighted)
    log_ref[...] += ending


def part(projected, start, width, order=lambda c: c):
    at = start // width
    return (projected, pl.BlockSpec((BLOCK, width), lambda c: (order(c), at)))


def run_scan(kernel, chunks, operands, out_shape, out_specs, flops, name, scratch=()):
    return pl.pallas_call(
        kernel,
        grid=(chunks,),
        out_shape=out_shape,
        in_specs=[spec for _, spec in operands],
        out_specs=out_specs,
        scratch_shapes=list(scratch),
        compiler_params=compiler_params(),
        cost_estimate=pl.CostEstimate(
            flops=flops, bytes_accessed=8_000_000, transcendentals=1_000_000
        ),
        name=name,
    )(*[array for array, _ in operands])


def whole(array):
    return (array, pl.BlockSpec(array.shape, lambda c: (0,) * array.ndim))


def scan_first(projected, at, bias, rate):
    rows, lanes = (projected.shape[0], bias.shape[1])
    chunks = rows // BLOCK
    back = lambda c: chunks - 1 - c
    width, state_size = (at["x"][1], at["b"][1])
    by_chunk = pl.BlockSpec((BLOCK, lanes), lambda c: (back(c), 0))
    across = pl.BlockSpec((8, BLOCK), lambda c: (0, back(c)))
    shape = lambda *sizes: jax.ShapeDtypeStruct(sizes, jnp.float32)
    return run_scan(
        scan_first_kernel,
        chunks,
        [
            part(projected, *at["misc"], back),
            whole(bias),
            whole(rate),
            part(projected, *at["x"], back),
            part(projected, *at["b"], back),
        ],
        (
            shape(rows, lanes),
            shape(rows, lanes),
            shape(8, rows),
            shape(8, rows),
            shape(state_size, width),
            shape(1, lanes),
        ),
        (
            by_chunk,
            by_chunk,
            across,
            across,
            pl.BlockSpec((state_size, width), lambda c: (0, 0)),
            pl.BlockSpec((1, lanes), lambda c: (0, 0)),
        ),
        1_000_000_000,
        "scan_first",
    )


def scan_kernel(
    x_ref,
    z_ref,
    b_ref,
    c_ref,
    delta_ref,
    cum_ref,
    delta_row_ref,
    cum_row_ref,
    entry_ref,
    skip_ref,
    scanned_ref,
    gated_ref,
    states_ref,
    state_ref,
):
    @pl.when(pl.program_id(0) == 0)
    def _():
        state_ref[...] = entry_ref[...]

    head_size = MIXER_HEAD_SIZE
    pair = 2 * head_size
    size, width = x_ref.shape
    state = state_ref[...]
    states_ref[0] = state
    delta, cumulative = (delta_ref[...], cum_ref[...])
    delta_row, cum_row = (delta_row_ref[...], cum_row_ref[...])
    bmat, cmat = (b_ref[...].astype(jnp.bfloat16), c_ref[...].astype(jnp.bfloat16))
    x_all = x_ref[...].astype(jnp.bfloat16)
    inner = dot_last(cmat, bmat)
    row = lax.broadcasted_iota(jnp.int32, (size, size), 0)
    column = lax.broadcasted_iota(jnp.int32, (size, size), 1)
    allowed = row >= column
    lane = lax.broadcasted_iota(jnp.int32, (size, pair), 1)
    from_state = mul(cmat, state.astype(jnp.bfloat16))
    spread = spread_heads(jnp.exp(cumulative), head_size, width)
    for first in range(0, width // head_size, 2):
        here = slice(first * head_size, first * head_size + pair)
        x_pair = x_all[:, here]
        total = from_state[:, here] * spread[:, here]
        total += skip_ref[:, here] * x_pair.astype(jnp.float32)
        for head in (first, first + 1):
            gap = cumulative[:, head : head + 1] - cum_row[head : head + 1, :]
            decay = jnp.exp(jnp.where(allowed, gap, -1e30))
            mixing = inner * decay * delta_row[head : head + 1, :]
            x_head = jnp.where((lane >= head_size) == (head > first), x_pair, 0.0)
            total += mul(mixing.astype(jnp.bfloat16), x_head.astype(jnp.bfloat16))
        scanned_ref[:, here] = total
        gate = z_ref[:, here]
        gated_ref[:, here] = (total * (gate * jax.nn.sigmoid(gate))).astype(jnp.bfloat16)
    ending = cumulative[-1:, :]
    weight = spread_heads(jnp.exp(ending - cumulative) * delta, head_size, width)
    weighted = (x_all.astype(jnp.float32) * weight).astype(jnp.bfloat16)
    state_ref[...] = state * spread[-1:, :] + dot_first(bmat, weighted)


def scan(projected, at, delta, cumulative, delta_row, cum_row, entry, skip):
    rows = projected.shape[0]
    state_size, width = entry.shape
    chunks = rows // BLOCK
    by_chunk = pl.BlockSpec((BLOCK, width), lambda c: (c, 0))
    lanes = delta.shape[1]
    across = pl.BlockSpec((8, BLOCK), lambda c: (0, c))
    return run_scan(
        scan_kernel,
        chunks,
        [
            part(projected, *at["x"]),
            part(projected, *at["z"]),
            part(projected, *at["b"]),
            part(projected, *at["c"]),
            part(delta, 0, lanes),
            part(cumulative, 0, lanes),
            (delta_row, across),
            (cum_row, across),
            whole(entry),
            whole(skip),
        ],
        (
            jax.ShapeDtypeStruct((rows, width), jnp.float32),
            jax.ShapeDtypeStruct((rows, width), jnp.bfloat16),
            jax.ShapeDtypeStruct((chunks, state_size, width), jnp.float32),
        ),
        (by_chunk, by_chunk, pl.BlockSpec((1, state_size, width), lambda c: (c, 0, 0))),
        3_000_000_000,
        "scan",
        [pltpu.VMEM((state_size, width), jnp.float32)],
    )


def scan_back_first_kernel(
    grad_ref, z_ref, scanned_ref, c_ref, cum_ref, d_scanned_ref, d_gate_ref, state_ref, log_ref
):
    @pl.when(pl.program_id(0) == 0)
    def _():
        state_ref[...] = jnp.zeros_like(state_ref)
        log_ref[...] = jnp.zeros_like(log_ref)

    gate = z_ref[...]
    chance = jax.nn.sigmoid(gate)
    grad = grad_ref[:, grad_ref.shape[1] - z_ref.shape[1] :].astype(jnp.float32)
    d_scanned = grad * (gate * chance)
    d_scanned_ref[...] = d_scanned
    d_gate_ref[...] = (
        grad * scanned_ref[...] * (chance * (1.0 + gate * (1.0 - chance)))
    ).astype(jnp.bfloat16)
    cumulative = cum_ref[...]
    decay = spread_heads(jnp.exp(cumulative + log_ref[...]), MIXER_HEAD_SIZE, z_ref.shape[1])
    state_ref[...] += dot_first(
        c_ref[...].astype(jnp.bfloat16), (d_scanned * decay).astype(jnp.bfloat16)
    )
    log_ref[...] += cumulative[-1:, :]


def scan_back_first(grads, projected, at, scanned, cumulative):
    rows, width = scanned.shape
    state_size, lanes = (at["c"][1], cumulative.shape[1])
    by_chunk = pl.BlockSpec((BLOCK, width), lambda c: (c, 0))
    return run_scan(
        scan_back_first_kernel,
        rows // BLOCK,
        [
            part(grads, 0, grads.shape[1]),
            part(projected, *at["z"]),
            part(scanned, 0, width),
            part(projected, *at["c"]),
            part(cumulative, 0, lanes),
        ],
        (
            jax.ShapeDtypeStruct((rows, width), jnp.float32),
            jax.ShapeDtypeStruct((rows, width), jnp.bfloat16),
            jax.ShapeDtypeStruct((state_size, width), jnp.float32),
        ),
        (by_chunk, by_chunk, pl.BlockSpec((state_size, width), lambda c: (0, 0))),
        1_000_000_000,
        "scan_back_first",
        [pltpu.VMEM((1, lanes), jnp.float32)],
    )


def scan_back_kernel(
    x_ref,
    grad_ref,
    b_ref,
    c_ref,
    pre_ref,
    bias_ref,
    rate_ref,
    delta_ref,
    cum_ref,
    cum_row_ref,
    states_ref,
    entry_ref,
    skip_ref,
    d_x_ref,
    d_b_ref,
    d_c_ref,
    d_pre_ref,
    sums_ref,
    state_ref,
):
    @pl.when(pl.program_id(0) == 0)
    def _():
        state_ref[...] = entry_ref[...]
        sums_ref[...] = jnp.zeros_like(sums_ref)

    head_size = MIXER_HEAD_SIZE
    pair = 2 * head_size
    size, width = x_ref.shape
    lanes = delta_ref.shape[1]
    low = jnp.bfloat16
    delta, cumulative, cum_row = (delta_ref[...], cum_ref[...], cum_row_ref[...])
    bmat, cmat = (b_ref[...].astype(low), c_ref[...].astype(low))
    x_all = x_ref[...].astype(low)
    x_single = x_all.astype(jnp.float32)
    grad = grad_ref[...]
    grad_low = grad.astype(low)
    state = states_ref[0]
    state_low = state.astype(low)
    after = state_ref[...]
    after_low = after.astype(low)
    ending = cumulative[-1:, :]
    row = lax.broadcasted_iota(jnp.int32, (size, size), 0)
    column = lax.broadcasted_iota(jnp.int32, (size, size), 1)
    later = column >= row
    before = (row > column).astype(low)
    onward = later.astype(low)
    lane = lax.broadcasted_iota(jnp.int32, (size, pair), 1)
    head_lane = lax.broadcasted_iota(jnp.int32, (size, lanes), 1)
    sum_heads = head_ones(width, head_size, lanes, low)

    inner = dot_last(bmat, cmat)
    from_after = mul(bmat, after_low)
    weight = jnp.exp(ending - cumulative)
    spread_weight = spread_heads(weight * delta, head_size, width)
    spread = spread_heads(jnp.exp(cumulative), head_size, width)
    to_end = mul((x_single * from_after).astype(low), sum_heads)
    through = jnp.exp(cumulative) * mul((grad * mul(cmat, state_low)).astype(low), sum_heads)
    carried = jnp.sum(state * after, axis=0, keepdims=True) * spread[-1:, :]
    carried = precise(carried, sum_heads.astype(jnp.float32))
    d_delta = weight * to_end
    d_log = (
        mul(onward, through.astype(low)) + mul(before, (d_delta * delta).astype(low)) + carried
    )

    d_inner = jnp.zeros((size, size), jnp.float32)
    for first in range(0, width // head_size, 2):
        here = slice(first * head_size, first * head_size + pair)
        x_pair, grad_pair = (x_all[:, here], grad_low[:, here])
        d_x = from_after[:, here] * spread_weight[:, here] + skip_ref[:, here] * grad[:, here]
        for head in (first, first + 1):
            mine = (lane >= head_size) == (head > first)
            gap = cum_row[head : head + 1, :] - cumulative[:, head : head + 1]
            decay = jnp.exp(jnp.where(later, gap, -1e30))
            delta_column = delta[:, head : head + 1]
            d_mixing = dot_last(jnp.where(mine, x_pair, 0.0).astype(low), grad_pair) * decay
            d_inner += d_mixing * delta_column
            flow = d_mixing * inner
            mixing = inner * decay * delta_column
            d_x += mul(mixing.astype(low), jnp.where(mine, grad_pair, 0.0).astype(low))
            d_delta_head = jnp.sum(flow, axis=1, keepdims=True)
            passing = mul(before, (flow * delta_column).astype(low))
            d_log_head = jnp.sum(jnp.where(later, passing, 0.0), axis=1, keepdims=True)
            d_delta += jnp.where(head_lane == head, d_delta_head, 0.0)
            d_log += jnp.where(head_lane == head, d_log_head, 0.0)
        d_x_ref[:, here] = d_x.astype(low)

    d_inner_low = d_inner.astype(low)
    scaled_grad = (grad * spread).astype(low)
    weighted = (x_single * spread_weight).astype(low)
    d_b_ref[...] = (mul(d_inner_low, cmat) + dot_last(weighted, after_low)).astype(low)
    d_c_ref[...] = (dot_first(d_inner_low, bmat) + dot_last(scaled_grad, state_low)).astype(low)
    state_ref[...] = after * spread[-1:, :] + dot_first(cmat, scaled_grad)
    rate = rate_ref[...]
    d_pre = (d_delta - d_log * rate) * jax.nn.sigmoid(pre_ref[...] + bias_ref[...])
    d_pre = jnp.where(head_lane < width // head_size, d_pre, 0.0)
    d_pre_ref[...] = d_pre.astype(low)
    skip_sum = precise(
        jnp.sum(grad * x_single, axis=0, keepdims=True), sum_heads.astype(jnp.float32)
    )
    sums_ref[0:1, :] += jnp.sum(d_pre, axis=0, keepdims=True)
    sums_ref[1:2, :] += jnp.sum(d_log * (-delta * rate), axis=0, keepdims=True)
    sums_ref[2:3, :] += skip_sum


def scan_back(
    projected, at, d_scanned, bias, rate, delta, cumulative, cum_row, states, entry, skip
):
    rows, width = d_scanned.shape
    state_size, lanes = (entry.shape[0], delta.shape[1])
    chunks = rows // BLOCK
    back = lambda c: chunks - 1 - c
    by_chunk = lambda columns: pl.BlockSpec((BLOCK, columns), lambda c: (back(c), 0))
    shape = lambda columns: jax.ShapeDtypeStruct((rows, columns), jnp.bfloat16)
    return run_scan(
        scan_back_kernel,
        chunks,
        [
            part(projected, *at["x"], back),
            part(d_scanned, 0, width, back),
            part(projected, *at["b"], back),
            part(projected, *at["c"], back),
            part(projected, *at["misc"], back),
            whole(bias),
            whole(rate),
            part(delta, 0, lanes, back),
            part(cumulative, 0, lanes, back),
            (cum_row, pl.BlockSpec((8, BLOCK), lambda c: (0, back(c)))),
            (states, pl.BlockSpec((1, state_size, width), lambda c: (back(c), 0, 0))),
            whole(entry),
            whole(skip),
        ],
        (
            shape(width),
            shape(state_size),
            shape(state_size),
            shape(lanes),
            jax.ShapeDtypeStruct((8, lanes), jnp.float32),
        ),
        (
            by_chunk(width),
            by_chunk(state_size),
            by_chunk(state_size),
            by_chunk(lanes),
            pl.BlockSpec((8, lanes), lambda c: (0, 0)),
        ),
        6_000_000_000,
        "scan_back",
        [pltpu.VMEM((state_size, width), jnp.float32)],
    )


def on_heads(value, move):
    devices = lax.axis_size("heads")
    pairs = []
    for at in range(devices):
        z, core = move(at // 2, at % 2)
        pairs.append((at, 2 * (z % (devices // 2)) + core))
    return lax.ppermute(value, "heads", pairs)


def to_partner(value):
    return on_heads(value, lambda z, core: (z, 1 - core))


def along(value):
    return on_heads(value, lambda z, core: (z + 1 - 2 * core, core))


def against(value):
    return on_heads(value, lambda z, core: (z - 1 + 2 * core, core))


def chunk_ranks():
    devices = lax.axis_size("heads")
    z, core = (lax.axis_index("heads") // 2, lax.axis_index("heads") % 2)
    step, other = (1 - 2 * core, 1 - core)
    owners = (
        (z, core),
        (z + 2, core),
        (z - step, core),
        (z - step, other),
        (z, other),
        (z + 2, other),
        (z + step, other),
        (z + step, core),
    )
    return jnp.stack([2 * ((at + devices) % (devices // 2)) + side for at, side in owners])


def gather_rows(own):
    partner = to_partner(own)
    near = along(own)
    near_other = along(partner)
    far = along(near)
    mine = (own, far, near, near_other)
    theirs = (partner, to_partner(far), to_partner(near), to_partner(near_other))
    return jnp.concatenate(mine + theirs, axis=0)


def scatter_rows(product, rows):
    half = rows.shape[0] // 2
    chunk = half // 4
    got = to_partner(product(rows[half:]).astype(jnp.bfloat16))
    summed = product(rows[:half]) + got.astype(jnp.float32)
    low = summed[chunk:].astype(jnp.bfloat16)
    far = against(low[:chunk])
    near_other = against(low[2 * chunk :])
    near = against((low[chunk : 2 * chunk].astype(jnp.float32) + far).astype(jnp.bfloat16))
    return summed[:chunk] + near.astype(jnp.float32) + to_partner(near_other).astype(jnp.float32)


def on_blocks(value, step):
    devices = lax.axis_size("blk")
    pairs = [(at, at + step) for at in range(devices) if 0 <= at + step < devices]
    return lax.ppermute(value, "blk", pairs)


def from_earlier(value, step=1):
    near = on_blocks(value, step)
    return (near, on_blocks(near, step), on_blocks(value, 3 * step))


def pack_state(state, log_total):
    high = log_total.astype(jnp.bfloat16)
    rest = log_total - high.astype(jnp.float32)
    middle = rest.astype(jnp.bfloat16)
    low = (rest - middle.astype(jnp.float32)).astype(jnp.bfloat16)
    logs = jnp.concatenate([high, middle, low], axis=0)
    logs = jnp.pad(logs, ((0, 16 - logs.shape[0]), (0, state.shape[1] - logs.shape[1])))
    return jnp.concatenate([state.astype(jnp.bfloat16), logs], axis=0)


def chain(packed, step, heads):
    decays, states = [], []
    for part_in in from_earlier(packed, step):
        state, logs = (part_in[:-16].astype(jnp.float32), part_in[-16:].astype(jnp.float32))
        decays.append(jnp.repeat(jnp.exp(jnp.sum(logs[:3, :heads], axis=0)), MIXER_HEAD_SIZE)[None])
        states.append(state)
    return states[0] + decays[0] * (states[1] + decays[1] * states[2])


def sum_blocks(value):
    for axis in ("dp", "blk"):
        for bit in (1, 2):
            value = value + lax.ppermute(
                value, axis, [(at, at ^ bit) for at in range(lax.axis_size(axis))]
            )
    return value


def weight_sum(parts):
    return lax.psum_scatter(
        jnp.concatenate(parts, axis=1), ("dp", "blk"), scatter_dimension=0, tiled=True
    ).astype(jnp.float32)


def low_first(left_side, right_side):
    return dot_first(left_side, right_side).astype(jnp.bfloat16)


def split_columns(value_in, widths):
    pieces, start = [], 0
    for width in widths:
        pieces.append(value_in[:, start : start + width])
        start += width
    return pieces


def inverse_rms(rows_in):
    return lax.rsqrt(jnp.mean(rows_in * rows_in, axis=-1, keepdims=True) + norm_eps)


def norm_back(rows_in, gain_in, cotangent):
    inverse = inverse_rms(rows_in)
    scaled = rows_in * inverse
    weighted = cotangent * gain_in
    return inverse * (weighted - scaled * jnp.mean(weighted * scaled, axis=-1, keepdims=True))


def shards(
    x_in,
    out_grad,
    norm_one,
    w_query,
    w_key,
    w_value,
    output_gate_weight,
    mixer_input_weight,
    w_delta,
    w_bmat,
    w_cmat,
    delta_bias,
    decay_log,
    skip_gain,
    w_attn_out,
    mixer_output_weight,
    norm_two,
    w_gate,
    w_up,
    w_down,
):
    heads_count = lax.axis_size("heads")
    head_rank = lax.axis_index("heads")
    core = head_rank % 2
    block_rank = lax.axis_index("blk")
    rank = block_rank.astype(jnp.int32)[None]
    own_rows = x_in.shape[0]
    span_length = own_rows * heads_count
    half_span = span_length // 2
    span_start = block_rank * span_length
    query_width = w_query.shape[1]
    mixer_width = mixer_input_weight.shape[1]
    heads = mixer_width // MIXER_HEAD_SIZE
    state_size = w_bmat.shape[1]
    hidden_width = w_gate.shape[1]
    rows_of = w_query.shape[0]
    kv_index = head_rank * (query_width // HD) // (QH // KVH)
    kv_width = KVH * HD
    low = jnp.bfloat16
    ranks = chunk_ranks().astype(jnp.int32)

    gains = jnp.stack([norm_one, norm_two], axis=1)
    gains = jnp.pad(gains, ((0, 0), (0, LANES - 2)))
    shared = reorder(
        ranks,
        [gather_rows(jnp.concatenate([w_key, w_value, w_bmat, w_cmat, gains], axis=1))],
        inverse=True,
    )
    key_part = lax.dynamic_slice_in_dim(shared, kv_index * HD, HD, 1)
    value_part = lax.dynamic_slice_in_dim(shared, kv_width + kv_index * HD, HD, 1)
    state_part = shared[:, 2 * kv_width : 2 * kv_width + 2 * state_size]
    gain_part = shared[:, 2 * kv_width + 2 * state_size :]
    misc_part = jnp.concatenate(
        [w_delta, gain_part[:, :2], jnp.zeros((rows_of, LANES - heads - 2), low)], axis=1
    )
    in_widths = (mixer_width, mixer_width, state_size, state_size, HD, HD, query_width, LANES)
    starts = [sum(in_widths[:k]) for k in range(len(in_widths))]
    at = dict(zip(("z", "x", "b", "c", "key", "value", "query", "misc"), zip(starts, in_widths)))
    in_full = lax.all_gather(
        jnp.concatenate(
            [
                output_gate_weight,
                mixer_input_weight,
                state_part,
                key_part,
                value_part,
                w_query,
                misc_part,
            ],
            axis=1,
        ),
        ("dp", "blk"),
        axis=0,
        tiled=True,
    )
    out_widths = (query_width, mixer_width, hidden_width, hidden_width, hidden_width)
    out_full = lax.all_gather(
        jnp.concatenate([w_attn_out.T, mixer_output_weight.T, w_gate, w_up, w_down.T], axis=1),
        ("dp", "blk"),
        axis=0,
        tiled=True,
    )
    mixed_width = query_width + mixer_width
    mix_t, gate_full, up_full, down_t = split_columns(out_full, (mixed_width,) + out_widths[2:])

    x_float = x_in.astype(jnp.float32)
    x_span = gather_rows(x_in)
    ffn_grad = gather_rows(out_grad)
    in_full, x_span, ffn_grad = lax.optimization_barrier((in_full, x_span, ffn_grad))
    misc_full = in_full[:, at["misc"][0] :]
    gain_one = misc_full[:, heads].astype(jnp.float32)
    gain_two = misc_full[:, heads + 1].astype(jnp.float32)
    x_span = x_span.astype(jnp.float32)
    x_scaled = x_span * inverse_rms(x_span)
    normed_input = (x_scaled * gain_one).astype(low)

    projected = simple_product(reorder(ranks, [normed_input], inverse=True), in_full)
    positions = (span_start + jnp.arange(span_length)).astype(jnp.float32)
    freqs = rope_base ** (-2.0 * jnp.arange(HD // 2, dtype=jnp.float32) / HD)
    angles = positions[:, None] * freqs[None, :]
    cosine, sine = (jnp.cos(angles), jnp.sin(angles))
    cosine = jnp.concatenate([cosine, cosine], axis=1)
    sine = jnp.concatenate([-sine, sine], axis=1)
    queries, keys_values = rope(
        projected[:, at["key"][0] : at["misc"][0]], cosine, sine
    )
    mine = lax.dynamic_slice_in_dim(keys_values, core * half_span, half_span, 0)
    pieces = []
    for piece in from_earlier(mine):
        pieces += [piece, to_partner(piece)]

    pad_lanes = lambda vector: jnp.pad(vector, (0, LANES - heads))[None]
    bias, rate = (pad_lanes(delta_bias), pad_lanes(jnp.exp(decay_log)))
    skip = jnp.repeat(skip_gain, MIXER_HEAD_SIZE)[None]
    delta, cumulative, delta_row, cum_row, local_state, local_log = scan_first(
        projected, at, bias, rate
    )
    entry_state = chain(pack_state(local_state, local_log), 1, heads)
    attended, attn_part, log_totals = attend(rank, queries, keys_values, pieces)
    scanned, gated, states = scan(
        projected, at, delta, cumulative, delta_row, cum_row, entry_state, skip
    )
    mixers = reorder(ranks, [attn_part, gated])
    middle = x_float + scatter_rows(lambda rows: dot_last(rows, mix_t), mixers)
    middle_scaled = middle * inverse_rms(middle)
    normed_two = gather_rows((middle_scaled * gain_two).astype(low))
    ffn_gate = simple_product(normed_two, gate_full)
    ffn_up = simple_product(normed_two, up_full)
    ffn_sig = jax.nn.sigmoid(ffn_gate)
    hidden = (ffn_gate * ffn_sig * ffn_up).astype(low)

    d_hidden = simple_product(ffn_grad, down_t)
    d_ffn_gate = (d_hidden * ffn_up * (ffn_sig * (1.0 + ffn_gate * (1.0 - ffn_sig)))).astype(low)
    d_ffn_up = (d_hidden * (ffn_gate * ffn_sig)).astype(low)
    d_normed_two = scatter_rows(
        lambda rows: dot_last(rows[:, :hidden_width], gate_full)
        + dot_last(rows[:, hidden_width:], up_full),
        jnp.concatenate([d_ffn_gate, d_ffn_up], axis=1),
    )
    ffn_sums = weight_sum(
        [
            low_first(normed_two, d_ffn_gate),
            low_first(normed_two, d_ffn_up),
            low_first(ffn_grad, hidden),
        ]
    )
    grad_gate, grad_up, grad_down_t = split_columns(ffn_sums, (hidden_width,) * 3)
    grad_two_part = jnp.sum(d_normed_two * middle_scaled, axis=0)
    d_middle = out_grad.astype(jnp.float32) + norm_back(middle, gain_two, d_normed_two)
    mix_grad = gather_rows(d_middle.astype(low))
    mix_grad, hidden = lax.optimization_barrier((mix_grad, hidden))
    d_mixers = reorder(ranks, [simple_product(mix_grad, mix_t).astype(low)], inverse=True)
    d_scanned, d_gate_z, d_entry = scan_back_first(d_mixers, projected, at, scanned, cumulative)
    after_state = chain(pack_state(d_entry, local_log), -1, heads)
    d_query, d_own, d_far = attend_back(
        rank, queries, keys_values, pieces, attended, log_totals, d_mixers, cosine, sine
    )
    d_ssm_in, d_bmat, d_cmat, d_pre, sums = scan_back(
        projected,
        at,
        d_scanned,
        bias,
        rate,
        delta,
        cumulative,
        cum_row,
        states,
        after_state,
        skip,
    )
    far_half = d_far.shape[0] // 2
    d_mine = lax.dynamic_slice_in_dim(d_own, core * half_span, half_span, 0)
    d_theirs = lax.dynamic_slice_in_dim(d_own, (1 - core) * half_span, half_span, 0)
    d_mine = d_mine + to_partner(d_theirs.astype(low)).astype(jnp.float32)
    d_far = d_far[:far_half].astype(jnp.float32) + to_partner(d_far[far_half:]).astype(jnp.float32)
    d_one, d_two, d_three = (
        d_far[k * half_span : (k + 1) * half_span] for k in range(d_far.shape[0] // half_span)
    )
    d_one = d_one + on_blocks(d_two.astype(low), -1).astype(jnp.float32)
    d_mine = d_mine + on_blocks(d_one.astype(low), -1).astype(jnp.float32)
    d_mine = d_mine + on_blocks(d_three.astype(low), -3).astype(jnp.float32)
    half_cos = lax.dynamic_slice_in_dim(cosine, core * half_span, half_span, 0)
    half_sin = lax.dynamic_slice_in_dim(sine, core * half_span, half_span, 0)
    d_key = d_mine[:, :HD]
    d_key = d_key * half_cos - jnp.roll(d_key, HD // 2, axis=1) * half_sin
    d_mine = jnp.concatenate([d_key, d_mine[:, HD:]], axis=1).astype(low)
    d_keys_values = lax.dynamic_update_slice_in_dim(
        jnp.zeros((span_length, 2 * HD), low), d_mine, core * half_span, 0
    )

    d_projected = reorder(
        ranks, [d_gate_z, d_ssm_in, d_bmat, d_cmat, d_keys_values, d_query, d_pre]
    )
    d_normed_term = dot_last(d_projected, in_full)
    grad_one_part = jnp.sum(d_normed_term * x_scaled, axis=0)
    in_grads = dot_first(normed_input, d_projected)
    column = jnp.arange(LANES)[None, :]
    misc_grads = in_grads[:, at["misc"][0] :]
    for k, value in enumerate((grad_one_part, grad_two_part)):
        misc_grads = jnp.where(column == heads + k, value[:, None], misc_grads)
    in_sums = weight_sum(
        [
            low_first(mix_grad, mixers),
            in_grads[:, : at["misc"][0]].astype(low),
            misc_grads.astype(low),
        ]
    )
    grad_mix_t, in_sums = (in_sums[:, :mixed_width], in_sums[:, mixed_width:])
    (
        grad_gatez,
        grad_ssmx,
        grad_bmat_part,
        grad_cmat_part,
        grad_key_half,
        grad_value_half,
        grad_query,
        misc_sums,
    ) = split_columns(in_sums, in_widths)
    d_normed = scatter_rows(lambda rows: rows, d_normed_term)
    input_grad = d_middle + norm_back(x_float, gain_one, d_normed)
    ffn_out = scatter_rows(lambda rows: dot_last(rows, down_t), hidden)
    activations = (middle + ffn_out).astype(low)
    kv_zeros = jnp.zeros((rows_of, kv_width), jnp.float32)
    shared_sums = jnp.concatenate(
        [
            lax.dynamic_update_slice_in_dim(kv_zeros, grad_key_half, kv_index * HD, 1),
            lax.dynamic_update_slice_in_dim(kv_zeros, grad_value_half, kv_index * HD, 1),
            grad_bmat_part,
            grad_cmat_part,
            misc_sums,
        ],
        axis=1,
    )
    shared_sums = scatter_rows(
        lambda rows: rows.astype(jnp.float32), reorder(ranks, [shared_sums])
    )
    grad_key, grad_value, grad_bmat, grad_cmat, gain_sums = split_columns(
        shared_sums, (kv_width, kv_width, state_size, state_size, LANES)
    )
    small_sums = sum_blocks(sums)[:, :heads]
    grad_mix = grad_mix_t.T
    return (
        activations,
        input_grad,
        gain_sums[:, heads],
        grad_query,
        grad_key,
        grad_value,
        grad_gatez,
        grad_ssmx,
        misc_sums[:, :heads],
        grad_bmat,
        grad_cmat,
        small_sums[0],
        small_sums[1],
        small_sums[2],
        grad_mix[:query_width],
        grad_mix[query_width:],
        gain_sums[:, heads + 1],
        grad_gate,
        grad_up,
        grad_down_t.T,
    )


def solution(mesh):
    placed = (
        P(("dp", "blk", "heads"), None),
        P(("dp", "blk", "heads"), None),
        P(("dp", "blk", "heads")),
        P(("dp", "blk"), "heads"),
        P(("dp", "blk", "heads"), None),
        P(("dp", "blk", "heads"), None),
        P(("dp", "blk"), "heads"),
        P(("dp", "blk"), "heads"),
        P(("dp", "blk"), "heads"),
        P(("dp", "blk", "heads"), None),
        P(("dp", "blk", "heads"), None),
        P("heads"),
        P("heads"),
        P("heads"),
        P("heads", ("dp", "blk")),
        P("heads", ("dp", "blk")),
        P(("dp", "blk", "heads")),
        P(("dp", "blk"), "heads"),
        P(("dp", "blk"), "heads"),
        P("heads", ("dp", "blk")),
    )
    return jax.shard_map(
        shards,
        mesh=mesh,
        in_specs=placed,
        out_specs=(
            P(("dp", "blk", "heads"), None),
            P(("dp", "blk", "heads"), None),
            P(("dp", "blk", "heads")),
            P(("dp", "blk"), "heads"),
            P(("dp", "blk", "heads"), None),
            P(("dp", "blk", "heads"), None),
            P(("dp", "blk"), "heads"),
            P(("dp", "blk"), "heads"),
            P(("dp", "blk"), "heads"),
            P(("dp", "blk", "heads"), None),
            P(("dp", "blk", "heads"), None),
            P("heads"),
            P("heads"),
            P("heads"),
            P("heads", ("dp", "blk")),
            P("heads", ("dp", "blk")),
            P(("dp", "blk", "heads")),
            P(("dp", "blk"), "heads"),
            P(("dp", "blk"), "heads"),
            P("heads", ("dp", "blk")),
        ),
        check_vma=False,
    )
```

```python
import functools

import jax
import jax.numpy as jnp
from jax import lax
from jax.experimental import pallas as pl
from jax.experimental.pallas import tpu as pltpu
from jax.sharding import PartitionSpec as P

QH = 8
KVH = 2
HD = 128
MIXER_HEAD_SIZE = 64
BLOCK = 256
LANES = 128
LOG2_E = 1.4426950408889634


HIGH_PRECISION = lax.Precision.HIGHEST
norm_eps = 1e-05
rope_base = 100000000000.0


def simple_product(left_side, right_side):
    return jnp.dot(left_side, right_side, preferred_element_type=jnp.float32)


def dot_last(left_side, right_side):
    return lax.dot_general(
        left_side, right_side, (((1,), (1,)), ((), ())), preferred_element_type=jnp.float32
    )


def dot_first(left_side, right_side):
    return lax.dot_general(
        left_side, right_side, (((0,), (0,)), ((), ())), preferred_element_type=jnp.float32
    )


def compiler_params():
    return pltpu.CompilerParams(vmem_limit_bytes=50 * 1024 * 1024)


def in_vmem(count):
    return [pl.BlockSpec(memory_space=pltpu.VMEM)] * count


def mul(left_side, right_side):
    return jnp.dot(left_side, right_side, preferred_element_type=jnp.float32)


def tile_scores(key_rows, query_rows, head_size):
    return dot_last(key_rows, query_rows) * (head_size**-0.5 * LOG2_E)


def causal(scores):
    key_at = lax.broadcasted_iota(jnp.int32, scores.shape, 0)
    query_at = lax.broadcasted_iota(jnp.int32, scores.shape, 1)
    return jnp.where(key_at <= query_at, scores, -1e30)


def enter_kernel(
    ranks_ref,
    heads_ref,
    x_ref,
    misc_ref,
    key_ref,
    value_ref,
    w_query_ref,
    cos_ref,
    sin_ref,
    normed_ref,
    ordered_ref,
    query_ref,
    kv_ref,
    gains_ref,
):
    head_size = query_ref.shape[1]

    @pl.when(pl.program_id(0) == 0)
    def _():
        lane = lax.broadcasted_iota(jnp.int32, misc_ref.shape, 1)
        for k in range(2):
            column = jnp.where(lane == heads_ref[0] + k, misc_ref[...].astype(jnp.float32), 0.0)
            gains_ref[k : k + 1, :] = jnp.sum(column.T, axis=0, keepdims=True)

    cosine, sine = (cos_ref[...], sin_ref[...])

    def turn(value):
        return (value * cosine + pltpu.roll(value, head_size // 2, 1) * sine).astype(jnp.bfloat16)

    rows = x_ref[...].astype(jnp.float32)
    normed = (rows * inverse_rms(rows) * gains_ref[0:1, :]).astype(jnp.bfloat16)
    normed_ref[...] = normed
    ordered_ref[...] = normed
    kv_ref[:, :head_size] = turn(mul(normed, key_ref[...]))
    kv_ref[:, head_size:] = mul(normed, value_ref[...]).astype(jnp.bfloat16)
    query_ref[...] = turn(mul(normed, w_query_ref[...]))


def enter(ranks, heads, x_span, in_full, at, cosine, sine):
    count = ranks.shape[0]
    rows, width = x_span.shape
    head_size = cosine.shape[1]
    here = lambda columns: pl.BlockSpec((rows // count, columns), lambda k, r, h: (k, 0))
    there = lambda columns: pl.BlockSpec((rows // count, columns), lambda k, r, h: (r[k], 0))
    weight = lambda name: pl.BlockSpec(
        (width, at[name][1]), lambda k, r, h: (0, at[name][0] // at[name][1])
    )
    return pl.pallas_call(
        enter_kernel,
        grid_spec=pltpu.PrefetchScalarGridSpec(
            num_scalar_prefetch=2,
            grid=(count,),
            in_specs=[
                here(width),
                weight("misc"),
                weight("key"),
                weight("value"),
                weight("query"),
                there(head_size),
                there(head_size),
            ],
            out_specs=(
                here(width),
                there(width),
                there(head_size),
                there(2 * head_size),
                pl.BlockSpec((8, width), lambda k, r, h: (0, 0)),
            ),
        ),
        out_shape=(
            jax.ShapeDtypeStruct((rows, width), jnp.bfloat16),
            jax.ShapeDtypeStruct((rows, width), jnp.bfloat16),
            jax.ShapeDtypeStruct((rows, head_size), jnp.bfloat16),
            jax.ShapeDtypeStruct((rows, 2 * head_size), jnp.bfloat16),
            jax.ShapeDtypeStruct((8, width), jnp.float32),
        ),
        compiler_params=compiler_params(),
        cost_estimate=pl.CostEstimate(
            flops=2_000_000_000, bytes_accessed=16_000_000, transcendentals=0
        ),
        name="enter",
    )(ranks, heads, x_span, in_full, in_full, in_full, in_full, cosine, sine)


def weight_grads_kernel(counts, *refs):
    out_ref = refs[-1]
    start, used = (0, len(counts))
    for k, count in enumerate(counts):
        left = refs[k][...].T
        for ref in refs[used : used + count]:
            out_ref[:, start : start + ref.shape[1]] = mul(left, ref[...]).astype(jnp.bfloat16)
            start += ref.shape[1]
        used += count


def weight_grads(*groups):
    lefts = [left for left, _ in groups]
    rights = [right for _, group in groups for right in group]
    depth, rows = lefts[0].shape
    width = sum(right.shape[1] for right in rights)
    return pl.pallas_call(
        functools.partial(weight_grads_kernel, tuple(len(group) for _, group in groups)),
        grid=(rows // BLOCK,),
        out_shape=jax.ShapeDtypeStruct((rows, width), jnp.bfloat16),
        in_specs=[pl.BlockSpec((depth, BLOCK), lambda k: (0, k)) for _ in lefts]
        + [pl.BlockSpec(right.shape, lambda k: (0, 0)) for right in rights],
        out_specs=pl.BlockSpec((BLOCK, width), lambda k: (k, 0)),
        compiler_params=compiler_params(),
        cost_estimate=pl.CostEstimate(
            flops=2 * rows * depth * width,
            bytes_accessed=2 * (depth * (2 * rows + width) + rows * width),
            transcendentals=0,
        ),
        name="weight_grads",
    )(*lefts, *rights)


def finish_kernel(
    ranks_ref, kv_ref, sums_ref, weight_ref, extra_ref, mix_ref, gate_ref, ssm_ref, query_ref, misc_ref, shared_ref, whole_ref, *, at
):
    mixed = mix_ref.shape[0]
    mix_ref[...] = sums_ref[:, :mixed].astype(jnp.float32).T
    of = lambda name: sums_ref[:, mixed + at[name][0] : mixed + sum(at[name])].astype(jnp.float32)
    gate_ref[...] = of("z")
    ssm_ref[...] = of("x")
    query_ref[...] = of("query")
    misc = of("misc")
    misc_ref[...] = misc
    products = sums_ref[:, mixed:].astype(jnp.float32) * weight_ref[...].astype(jnp.float32)
    gain_one = extra_ref[:, 0:1]
    total = jnp.sum(products, axis=1, keepdims=True) / gain_one
    lane = lax.broadcasted_iota(jnp.int32, misc.shape, 1)
    gains = jnp.where(lane == 0, total, jnp.where(lane == 1, extra_ref[:, 1:2], 0.0))
    zero = jnp.zeros_like(misc)
    first = kv_ref[0] == 0
    key, value = (of("key"), of("value"))
    pieces = (
        jnp.where(first, key, zero),
        jnp.where(first, zero, key),
        jnp.where(first, value, zero),
        jnp.where(first, zero, value),
        of("b"),
        of("c"),
        gains,
    )
    start = 0
    for piece in pieces:
        whole_ref[:, start : start + piece.shape[1]] = piece
        start += piece.shape[1]
    count = ranks_ref.shape[0]
    size = shared_ref.shape[0] // count
    for k in range(count):
        rows = pl.ds(pl.multiple_of(ranks_ref[k] * size, size), size)
        shared_ref[k * size : (k + 1) * size, :] = whole_ref[rows, :].astype(jnp.bfloat16)


def finish(ranks, kv_index, sums, weights, extra, at, mixed):
    rows = sums.shape[0]
    shape = lambda name: jax.ShapeDtypeStruct((rows, at[name][1]), jnp.float32)
    shared = 2 * (at["key"][1] + at["value"][1]) + at["b"][1] + at["c"][1] + LANES
    return pl.pallas_call(
        functools.partial(finish_kernel, at=at),
        out_shape=(
            jax.ShapeDtypeStruct((mixed, rows), jnp.float32),
            shape("z"),
            shape("x"),
            shape("query"),
            shape("misc"),
            jax.ShapeDtypeStruct((rows, shared), jnp.bfloat16),
        ),
        in_specs=[pl.BlockSpec(memory_space=pltpu.SMEM)] * 2 + in_vmem(3),
        out_specs=tuple(in_vmem(6)),
        scratch_shapes=[pltpu.VMEM((rows, shared), jnp.float32)],
        compiler_params=compiler_params(),
        name="finish",
    )(ranks, kv_index, sums, weights, extra)


def attend_kernel(rank_ref, query_ref, own_ref, *refs):
    pieces, (out_ref, low_ref, log_ref) = (refs[:-3], refs[-3:])
    span_length, head_size = query_ref.shape
    tile = own_ref.shape[0] // 2
    for block in range(span_length // tile):
        here = slice(block * tile, (block + 1) * tile)
        query_rows = query_ref[here, :]

        def step(kv_rows, carried, masked=False):
            top, total, summed = carried
            scores = tile_scores(kv_rows[:, :head_size], query_rows, head_size)
            if masked:
                scores = causal(scores)
            new_top = jnp.maximum(top, jnp.max(scores, axis=0, keepdims=True))
            probs = jnp.exp2(scores - new_top)
            scale = jnp.exp2(top - new_top)
            total = total * scale + jnp.sum(probs, axis=0, keepdims=True)
            summed = summed * scale + dot_first(kv_rows[:, head_size:], probs.astype(jnp.bfloat16))
            return (new_top, total, summed)

        carried = (
            jnp.full((1, tile), -1e30, jnp.float32),
            jnp.zeros((1, tile), jnp.float32),
            jnp.zeros((head_size, tile), jnp.float32),
        )
        carried = step(own_ref[here, :], carried, True)
        for earlier in range(block):
            carried = step(own_ref[earlier * tile : (earlier + 1) * tile, :], carried)
        for distance in range(1, 1 + len(pieces) // 2):
            pair = pieces[2 * distance - 2 : 2 * distance]

            def both(_, carried, pair=pair):
                return step(pair[1][...], step(pair[0][...], carried))

            valid = (rank_ref[0] >= distance).astype(jnp.int32)
            carried = lax.fori_loop(0, valid, both, carried)
        top, total, summed = carried
        result = summed / total
        out_ref[:, here] = result
        low_ref[here, :] = result.T.astype(jnp.bfloat16)
        log_ref[:, here] = top + jnp.log2(total)


def attend(rank, queries, own, pieces):
    span_length, head_size = queries.shape
    return pl.pallas_call(
        attend_kernel,
        out_shape=(
            jax.ShapeDtypeStruct((head_size, span_length), jnp.float32),
            jax.ShapeDtypeStruct((span_length, head_size), jnp.bfloat16),
            jax.ShapeDtypeStruct((1, span_length), jnp.float32),
        ),
        in_specs=[pl.BlockSpec(memory_space=pltpu.SMEM)] + in_vmem(2 + len(pieces)),
        out_specs=tuple(in_vmem(3)),
        compiler_params=compiler_params(),
        cost_estimate=pl.CostEstimate(
            flops=10_000_000_000, bytes_accessed=4_000_000, transcendentals=4_000_000
        ),
        name="attend",
    )(rank, queries, own, *pieces)


def attend_back_kernel(rank_ref, query_ref, own_ref, *refs):
    pieces, refs = (refs[:-9], refs[-9:])
    out_ref, log_ref, grad_ref, cos_ref, sin_ref, d_query_ref, d_own_ref, d_far_ref, sums_ref = refs
    span_length, head_size = query_ref.shape
    tile = own_ref.shape[0] // 2
    score_scale = head_size**-0.5
    sums_ref[...] = jnp.zeros_like(sums_ref)
    for block in range(span_length // tile):
        here = slice(block * tile, (block + 1) * tile)
        query_rows = query_ref[here, :]
        grad_rows = grad_ref[here, :head_size]
        log_total = log_ref[:, here]
        delta_row = jnp.sum(
            grad_rows.astype(jnp.float32).T * out_ref[:, here], axis=0, keepdims=True
        )

        def step(kv_ref, start, at, d_query, masked=False):
            key_rows = kv_ref[start : start + tile, :head_size]
            scores = tile_scores(key_rows, query_rows, head_size)
            if masked:
                scores = causal(scores)
            probs = jnp.exp2(scores - log_total)
            d_probs = dot_last(kv_ref[start : start + tile, head_size:], grad_rows)
            d_scores = (probs * (d_probs - delta_row)).astype(jnp.bfloat16)
            rows = slice(at * tile, (at + 1) * tile)
            sums_ref[rows, head_size:] += mul(probs.astype(jnp.bfloat16), grad_rows)
            sums_ref[rows, :head_size] += mul(d_scores, query_rows)
            return d_query + dot_first(key_rows, d_scores)

        d_query = jnp.zeros((head_size, tile), jnp.float32)
        d_query = step(own_ref, block * tile, block, d_query, True)
        for earlier in range(block):
            d_query = step(own_ref, earlier * tile, earlier, d_query)
        for distance in range(1, 1 + len(pieces) // 2):

            def both(_, d_query, distance=distance):
                for k in (2 * distance - 2, 2 * distance - 1):
                    d_query = step(pieces[k], 0, 2 + k, d_query)
                return d_query

            valid = (rank_ref[0] >= distance).astype(jnp.int32)
            d_query = lax.fori_loop(0, valid, both, d_query)
        turned = d_query.T * score_scale
        d_query_ref[here, :] = (
            turned * cos_ref[here, :] - pltpu.roll(turned, head_size // 2, 1) * sin_ref[here, :]
        ).astype(jnp.bfloat16)
    lane = lax.broadcasted_iota(jnp.int32, (tile, 2 * head_size), 1)
    scale = jnp.where(lane < head_size, score_scale, 1.0)
    for at in range(2):
        rows = slice(at * tile, (at + 1) * tile)
        d_own_ref[rows, :] = sums_ref[rows, :] * scale
    for k in range(len(pieces)):
        rows = slice((2 + k) * tile, (3 + k) * tile)
        into = (k % 2) * (len(pieces) // 2) + k // 2
        d_far_ref[into * tile : (into + 1) * tile, :] = (sums_ref[rows, :] * scale).astype(
            jnp.bfloat16
        )


def attend_back(rank, queries, own, pieces, attended, log_totals, d_attn, cosine, sine):
    tile = own.shape[0] // 2
    return pl.pallas_call(
        attend_back_kernel,
        out_shape=(
            jax.ShapeDtypeStruct(queries.shape, jnp.bfloat16),
            jax.ShapeDtypeStruct(own.shape, jnp.float32),
            jax.ShapeDtypeStruct((len(pieces) * tile, own.shape[1]), jnp.bfloat16),
        ),
        in_specs=[pl.BlockSpec(memory_space=pltpu.SMEM)] + in_vmem(7 + len(pieces)),
        out_specs=tuple(in_vmem(3)),
        scratch_shapes=[pltpu.VMEM(((2 + len(pieces)) * tile, own.shape[1]), jnp.float32)],
        compiler_params=compiler_params(),
        cost_estimate=pl.CostEstimate(
            flops=25_000_000_000, bytes_accessed=8_000_000, transcendentals=4_000_000
        ),
        name="attend_back",
    )(rank, queries, own, *pieces, attended, log_totals, d_attn, cosine, sine)


def reorder_kernel(ranks_ref, *refs):
    out_ref = refs[-1]
    start = 0
    for ref in refs[:-1]:
        out_ref[:, start : start + ref.shape[1]] = ref[...].astype(out_ref.dtype)
        start += ref.shape[1]


def reorder(ranks, pieces, inverse=False):
    count = ranks.shape[0]
    rows = pieces[0].shape[0] // count
    width = sum(piece.shape[1] for piece in pieces)
    there = lambda k, ranks: (ranks[k], 0)
    here = lambda k, ranks: (k, 0)
    return pl.pallas_call(
        reorder_kernel,
        grid_spec=pltpu.PrefetchScalarGridSpec(
            num_scalar_prefetch=1,
            grid=(count,),
            in_specs=[
                pl.BlockSpec((rows, piece.shape[1]), here if inverse else there)
                for piece in pieces
            ],
            out_specs=pl.BlockSpec((rows, width), there if inverse else here),
        ),
        out_shape=jax.ShapeDtypeStruct((count * rows, width), jnp.bfloat16),
        compiler_params=compiler_params(),
        cost_estimate=pl.CostEstimate(
            flops=0, bytes_accessed=4 * count * rows * width, transcendentals=0
        ),
        name="reorder",
    )(ranks, *pieces)


def lower_ones(size, dtype=jnp.float32):
    row = lax.broadcasted_iota(jnp.int32, (size, size), 0)
    column = lax.broadcasted_iota(jnp.int32, (size, size), 1)
    return (row >= column).astype(dtype)


def precise(left_side, right_side):
    return jnp.dot(
        left_side, right_side, precision=HIGH_PRECISION, preferred_element_type=jnp.float32
    )


def spread_heads(columns, head_size, width):
    lane = lax.broadcasted_iota(jnp.int32, (columns.shape[0], 2 * head_size), 1)
    pairs = [
        jnp.where(lane < head_size, columns[:, k : k + 1], columns[:, k + 1 : k + 2])
        for k in range(0, width // head_size, 2)
    ]
    return jnp.concatenate(pairs, axis=1)


def head_ones(width, head_size, lanes, dtype):
    at = lax.broadcasted_iota(jnp.int32, (width, lanes), 0)
    lane = lax.broadcasted_iota(jnp.int32, (width, lanes), 1)
    low = lane * head_size
    return ((at >= low) & (at < low + head_size)).astype(dtype)


def scan_first_kernel(
    pre_ref, bias_ref, rate_ref, x_ref, b_ref, delta_ref, cum_ref, delta_row_ref, cum_row_ref, state_ref, log_ref
):
    @pl.when(pl.program_id(0) == 0)
    def _():
        state_ref[...] = jnp.zeros_like(state_ref)
        log_ref[...] = jnp.zeros_like(log_ref)

    delta = jax.nn.softplus(pre_ref[...] + bias_ref[...])
    log_step = -delta * rate_ref[...]
    cumulative = precise(lower_ones(log_step.shape[0]), log_step)
    delta_ref[...] = delta
    cum_ref[...] = cumulative
    delta_row_ref[...] = delta.T[:8]
    cum_row_ref[...] = cumulative.T[:8]
    ending = cumulative[-1:, :]
    weight = jnp.exp(ending - cumulative + log_ref[...]) * delta
    width = x_ref.shape[1]
    x_low = x_ref[...].astype(jnp.bfloat16).astype(jnp.float32)
    weighted = (x_low * spread_heads(weight, MIXER_HEAD_SIZE, width)).astype(jnp.bfloat16)
    state_ref[...] += dot_first(b_ref[...].astype(jnp.bfloat16), weighted)
    log_ref[...] += ending


def part(projected, start, width, order=lambda c: c):
    at = start // width
    return (projected, pl.BlockSpec((BLOCK, width), lambda c: (order(c), at)))


def run_scan(kernel, chunks, operands, out_shape, out_specs, flops, name, scratch=()):
    return pl.pallas_call(
        kernel,
        grid=(chunks,),
        out_shape=out_shape,
        in_specs=[spec for _, spec in operands],
        out_specs=out_specs,
        scratch_shapes=list(scratch),
        compiler_params=compiler_params(),
        cost_estimate=pl.CostEstimate(
            flops=flops, bytes_accessed=8_000_000, transcendentals=1_000_000
        ),
        name=name,
    )(*[array for array, _ in operands])


def whole(array):
    return (array, pl.BlockSpec(array.shape, lambda c: (0,) * array.ndim))


def scan_first(projected, at, bias, rate):
    rows, lanes = (projected.shape[0], bias.shape[1])
    chunks = rows // BLOCK
    back = lambda c: chunks - 1 - c
    width, state_size = (at["x"][1], at["b"][1])
    by_chunk = pl.BlockSpec((BLOCK, lanes), lambda c: (back(c), 0))
    across = pl.BlockSpec((8, BLOCK), lambda c: (0, back(c)))
    shape = lambda *sizes: jax.ShapeDtypeStruct(sizes, jnp.float32)
    return run_scan(
        scan_first_kernel,
        chunks,
        [
            part(projected, *at["misc"], back),
            whole(bias),
            whole(rate),
            part(projected, *at["x"], back),
            part(projected, *at["b"], back),
        ],
        (
            shape(rows, lanes),
            shape(rows, lanes),
            shape(8, rows),
            shape(8, rows),
            shape(state_size, width),
            shape(1, lanes),
        ),
        (
            by_chunk,
            by_chunk,
            across,
            across,
            pl.BlockSpec((state_size, width), lambda c: (0, 0)),
            pl.BlockSpec((1, lanes), lambda c: (0, 0)),
        ),
        1_000_000_000,
        "scan_first",
    )


def scan_kernel(
    x_ref,
    z_ref,
    b_ref,
    c_ref,
    delta_ref,
    cum_ref,
    delta_row_ref,
    cum_row_ref,
    entry_ref,
    skip_ref,
    scanned_ref,
    gated_ref,
    states_ref,
    state_ref,
):
    @pl.when(pl.program_id(0) == 0)
    def _():
        state_ref[...] = entry_ref[...]

    head_size = MIXER_HEAD_SIZE
    pair = 2 * head_size
    size, width = x_ref.shape
    state = state_ref[...]
    states_ref[0] = state
    delta, cumulative = (delta_ref[...], cum_ref[...])
    delta_row, cum_row = (delta_row_ref[...], cum_row_ref[...])
    bmat, cmat = (b_ref[...].astype(jnp.bfloat16), c_ref[...].astype(jnp.bfloat16))
    x_all = x_ref[...].astype(jnp.bfloat16)
    inner = dot_last(cmat, bmat)
    row = lax.broadcasted_iota(jnp.int32, (size, size), 0)
    column = lax.broadcasted_iota(jnp.int32, (size, size), 1)
    allowed = row >= column
    lane = lax.broadcasted_iota(jnp.int32, (size, pair), 1)
    from_state = mul(cmat, state.astype(jnp.bfloat16))
    spread = spread_heads(jnp.exp(cumulative), head_size, width)
    for first in range(0, width // head_size, 2):
        here = slice(first * head_size, first * head_size + pair)
        x_pair = x_all[:, here]
        total = from_state[:, here] * spread[:, here]
        total += skip_ref[:, here] * x_pair.astype(jnp.float32)
        for head in (first, first + 1):
            gap = cumulative[:, head : head + 1] - cum_row[head : head + 1, :]
            decay = jnp.exp(jnp.where(allowed, gap, -1e30))
            mixing = inner * decay * delta_row[head : head + 1, :]
            x_head = jnp.where((lane >= head_size) == (head > first), x_pair, 0.0)
            total += mul(mixing.astype(jnp.bfloat16), x_head.astype(jnp.bfloat16))
        scanned_ref[:, here] = total
        gate = z_ref[:, here]
        gated_ref[:, here] = (total * (gate * jax.nn.sigmoid(gate))).astype(jnp.bfloat16)
    ending = cumulative[-1:, :]
    weight = spread_heads(jnp.exp(ending - cumulative) * delta, head_size, width)
    weighted = (x_all.astype(jnp.float32) * weight).astype(jnp.bfloat16)
    state_ref[...] = state * spread[-1:, :] + dot_first(bmat, weighted)


def scan(projected, at, delta, cumulative, delta_row, cum_row, entry, skip):
    rows = projected.shape[0]
    state_size, width = entry.shape
    chunks = rows // BLOCK
    by_chunk = pl.BlockSpec((BLOCK, width), lambda c: (c, 0))
    lanes = delta.shape[1]
    across = pl.BlockSpec((8, BLOCK), lambda c: (0, c))
    return run_scan(
        scan_kernel,
        chunks,
        [
            part(projected, *at["x"]),
            part(projected, *at["z"]),
            part(projected, *at["b"]),
            part(projected, *at["c"]),
            part(delta, 0, lanes),
            part(cumulative, 0, lanes),
            (delta_row, across),
            (cum_row, across),
            whole(entry),
            whole(skip),
        ],
        (
            jax.ShapeDtypeStruct((rows, width), jnp.float32),
            jax.ShapeDtypeStruct((rows, width), jnp.bfloat16),
            jax.ShapeDtypeStruct((chunks, state_size, width), jnp.float32),
        ),
        (by_chunk, by_chunk, pl.BlockSpec((1, state_size, width), lambda c: (c, 0, 0))),
        3_000_000_000,
        "scan",
        [pltpu.VMEM((state_size, width), jnp.float32)],
    )


def scan_back_first_kernel(
    grad_ref, z_ref, scanned_ref, c_ref, cum_ref, d_scanned_ref, d_gate_ref, state_ref, log_ref
):
    @pl.when(pl.program_id(0) == 0)
    def _():
        state_ref[...] = jnp.zeros_like(state_ref)
        log_ref[...] = jnp.zeros_like(log_ref)

    gate = z_ref[...]
    chance = jax.nn.sigmoid(gate)
    grad = grad_ref[:, grad_ref.shape[1] - z_ref.shape[1] :].astype(jnp.float32)
    d_scanned = grad * (gate * chance)
    d_scanned_ref[...] = d_scanned
    d_gate_ref[...] = (
        grad * scanned_ref[...] * (chance * (1.0 + gate * (1.0 - chance)))
    ).astype(jnp.bfloat16)
    cumulative = cum_ref[...]
    decay = spread_heads(jnp.exp(cumulative + log_ref[...]), MIXER_HEAD_SIZE, z_ref.shape[1])
    state_ref[...] += dot_first(
        c_ref[...].astype(jnp.bfloat16), (d_scanned * decay).astype(jnp.bfloat16)
    )
    log_ref[...] += cumulative[-1:, :]


def scan_back_first(grads, projected, at, scanned, cumulative):
    rows, width = scanned.shape
    state_size, lanes = (at["c"][1], cumulative.shape[1])
    by_chunk = pl.BlockSpec((BLOCK, width), lambda c: (c, 0))
    return run_scan(
        scan_back_first_kernel,
        rows // BLOCK,
        [
            part(grads, 0, grads.shape[1]),
            part(projected, *at["z"]),
            part(scanned, 0, width),
            part(projected, *at["c"]),
            part(cumulative, 0, lanes),
        ],
        (
            jax.ShapeDtypeStruct((rows, width), jnp.float32),
            jax.ShapeDtypeStruct((rows, width), jnp.bfloat16),
            jax.ShapeDtypeStruct((state_size, width), jnp.float32),
        ),
        (by_chunk, by_chunk, pl.BlockSpec((state_size, width), lambda c: (0, 0))),
        1_000_000_000,
        "scan_back_first",
        [pltpu.VMEM((1, lanes), jnp.float32)],
    )


def scan_back_kernel(
    x_ref,
    grad_ref,
    b_ref,
    c_ref,
    pre_ref,
    bias_ref,
    rate_ref,
    delta_ref,
    cum_ref,
    cum_row_ref,
    states_ref,
    entry_ref,
    skip_ref,
    d_x_ref,
    d_b_ref,
    d_c_ref,
    d_pre_ref,
    sums_ref,
    state_ref,
):
    @pl.when(pl.program_id(0) == 0)
    def _():
        state_ref[...] = entry_ref[...]
        sums_ref[...] = jnp.zeros_like(sums_ref)

    head_size = MIXER_HEAD_SIZE
    pair = 2 * head_size
    size, width = x_ref.shape
    lanes = delta_ref.shape[1]
    low = jnp.bfloat16
    delta, cumulative, cum_row = (delta_ref[...], cum_ref[...], cum_row_ref[...])
    bmat, cmat = (b_ref[...].astype(low), c_ref[...].astype(low))
    x_all = x_ref[...].astype(low)
    x_single = x_all.astype(jnp.float32)
    grad = grad_ref[...]
    grad_low = grad.astype(low)
    state = states_ref[0]
    state_low = state.astype(low)
    after = state_ref[...]
    after_low = after.astype(low)
    ending = cumulative[-1:, :]
    row = lax.broadcasted_iota(jnp.int32, (size, size), 0)
    column = lax.broadcasted_iota(jnp.int32, (size, size), 1)
    later = column >= row
    before = (row > column).astype(low)
    onward = later.astype(low)
    lane = lax.broadcasted_iota(jnp.int32, (size, pair), 1)
    head_lane = lax.broadcasted_iota(jnp.int32, (size, lanes), 1)
    sum_heads = head_ones(width, head_size, lanes, low)

    inner = dot_last(bmat, cmat)
    from_after = mul(bmat, after_low)
    weight = jnp.exp(ending - cumulative)
    spread_weight = spread_heads(weight * delta, head_size, width)
    spread = spread_heads(jnp.exp(cumulative), head_size, width)
    to_end = mul((x_single * from_after).astype(low), sum_heads)
    through = jnp.exp(cumulative) * mul((grad * mul(cmat, state_low)).astype(low), sum_heads)
    carried = jnp.sum(state * after, axis=0, keepdims=True) * spread[-1:, :]
    carried = precise(carried, sum_heads.astype(jnp.float32))
    d_delta = weight * to_end
    d_log = (
        mul(onward, through.astype(low)) + mul(before, (d_delta * delta).astype(low)) + carried
    )

    d_inner = jnp.zeros((size, size), jnp.float32)
    for first in range(0, width // head_size, 2):
        here = slice(first * head_size, first * head_size + pair)
        x_pair, grad_pair = (x_all[:, here], grad_low[:, here])
        d_x = from_after[:, here] * spread_weight[:, here] + skip_ref[:, here] * grad[:, here]
        for head in (first, first + 1):
            mine = (lane >= head_size) == (head > first)
            gap = cum_row[head : head + 1, :] - cumulative[:, head : head + 1]
            decay = jnp.exp(jnp.where(later, gap, -1e30))
            delta_column = delta[:, head : head + 1]
            d_mixing = dot_last(jnp.where(mine, x_pair, 0.0).astype(low), grad_pair) * decay
            d_inner += d_mixing * delta_column
            flow = d_mixing * inner
            mixing = inner * decay * delta_column
            d_x += mul(mixing.astype(low), jnp.where(mine, grad_pair, 0.0).astype(low))
            d_delta_head = jnp.sum(flow, axis=1, keepdims=True)
            passing = mul(before, (flow * delta_column).astype(low))
            d_log_head = jnp.sum(jnp.where(later, passing, 0.0), axis=1, keepdims=True)
            d_delta += jnp.where(head_lane == head, d_delta_head, 0.0)
            d_log += jnp.where(head_lane == head, d_log_head, 0.0)
        d_x_ref[:, here] = d_x.astype(low)

    d_inner_low = d_inner.astype(low)
    scaled_grad = (grad * spread).astype(low)
    weighted = (x_single * spread_weight).astype(low)
    d_b_ref[...] = (mul(d_inner_low, cmat) + dot_last(weighted, after_low)).astype(low)
    d_c_ref[...] = (dot_first(d_inner_low, bmat) + dot_last(scaled_grad, state_low)).astype(low)
    state_ref[...] = after * spread[-1:, :] + dot_first(cmat, scaled_grad)
    rate = rate_ref[...]
    d_pre = (d_delta - d_log * rate) * jax.nn.sigmoid(pre_ref[...] + bias_ref[...])
    d_pre = jnp.where(head_lane < width // head_size, d_pre, 0.0)
    d_pre_ref[...] = d_pre.astype(low)
    skip_sum = precise(
        jnp.sum(grad * x_single, axis=0, keepdims=True), sum_heads.astype(jnp.float32)
    )
    sums_ref[0:1, :] += jnp.sum(d_pre, axis=0, keepdims=True)
    sums_ref[1:2, :] += jnp.sum(d_log * (-delta * rate), axis=0, keepdims=True)
    sums_ref[2:3, :] += skip_sum


def scan_back(
    projected, at, d_scanned, bias, rate, delta, cumulative, cum_row, states, entry, skip
):
    rows, width = d_scanned.shape
    state_size, lanes = (entry.shape[0], delta.shape[1])
    chunks = rows // BLOCK
    back = lambda c: chunks - 1 - c
    by_chunk = lambda columns: pl.BlockSpec((BLOCK, columns), lambda c: (back(c), 0))
    shape = lambda columns: jax.ShapeDtypeStruct((rows, columns), jnp.bfloat16)
    return run_scan(
        scan_back_kernel,
        chunks,
        [
            part(projected, *at["x"], back),
            part(d_scanned, 0, width, back),
            part(projected, *at["b"], back),
            part(projected, *at["c"], back),
            part(projected, *at["misc"], back),
            whole(bias),
            whole(rate),
            part(delta, 0, lanes, back),
            part(cumulative, 0, lanes, back),
            (cum_row, pl.BlockSpec((8, BLOCK), lambda c: (0, back(c)))),
            (states, pl.BlockSpec((1, state_size, width), lambda c: (back(c), 0, 0))),
            whole(entry),
            whole(skip),
        ],
        (
            shape(width),
            shape(state_size),
            shape(state_size),
            shape(lanes),
            jax.ShapeDtypeStruct((8, lanes), jnp.float32),
        ),
        (
            by_chunk(width),
            by_chunk(state_size),
            by_chunk(state_size),
            by_chunk(lanes),
            pl.BlockSpec((8, lanes), lambda c: (0, 0)),
        ),
        6_000_000_000,
        "scan_back",
        [pltpu.VMEM((state_size, width), jnp.float32)],
    )


def on_heads(value, move):
    devices = lax.axis_size("heads")
    pairs = []
    for at in range(devices):
        z, core = move(at // 2, at % 2)
        pairs.append((at, 2 * (z % (devices // 2)) + core))
    return lax.ppermute(value, "heads", pairs)


def to_partner(value):
    return on_heads(value, lambda z, core: (z, 1 - core))


def along(value):
    return on_heads(value, lambda z, core: (z + 1 - 2 * core, core))


def against(value):
    return on_heads(value, lambda z, core: (z - 1 + 2 * core, core))


def chunk_ranks():
    devices = lax.axis_size("heads")
    z, core = (lax.axis_index("heads") // 2, lax.axis_index("heads") % 2)
    step, other = (1 - 2 * core, 1 - core)
    owners = (
        (z, core),
        (z + 2, core),
        (z - step, core),
        (z - step, other),
        (z, other),
        (z + 2, other),
        (z + step, other),
        (z + step, core),
    )
    return jnp.stack([2 * ((at + devices) % (devices // 2)) + side for at, side in owners])


def gather_rows(own):
    partner = to_partner(own)
    near = along(own)
    near_other = along(partner)
    far = along(near)
    mine = (own, far, near, near_other)
    theirs = (partner, to_partner(far), to_partner(near), to_partner(near_other))
    return jnp.concatenate(mine + theirs, axis=0)


def scatter_rows(product, half):
    chunk = half // 4
    got = to_partner(product(slice(half, 2 * half)).astype(jnp.bfloat16))
    summed = product(slice(0, half)) + got.astype(jnp.float32)
    low = summed[chunk:].astype(jnp.bfloat16)
    far = against(low[:chunk])
    near_other = against(low[2 * chunk :])
    near = against((low[chunk : 2 * chunk].astype(jnp.float32) + far).astype(jnp.bfloat16))
    return summed[:chunk] + near.astype(jnp.float32) + to_partner(near_other).astype(jnp.float32)


def shift(value, step):
    devices = lax.axis_size("heads")
    return lax.ppermute(value, "heads", [(at, (at + step) % devices) for at in range(devices)])


def on_blocks(value, step):
    devices = lax.axis_size("blk")
    pairs = [(at, at + step) for at in range(devices) if 0 <= at + step < devices]
    return lax.ppermute(value, "blk", pairs)


def from_earlier(value, step=1):
    return tuple(on_blocks(value, distance * step) for distance in (1, 2, 3))


def pack_state(state, log_total):
    high = log_total.astype(jnp.bfloat16)
    rest = log_total - high.astype(jnp.float32)
    middle = rest.astype(jnp.bfloat16)
    low = (rest - middle.astype(jnp.float32)).astype(jnp.bfloat16)
    logs = jnp.concatenate([high, middle, low], axis=0)
    logs = jnp.pad(logs, ((0, 16 - logs.shape[0]), (0, state.shape[1] - logs.shape[1])))
    return jnp.concatenate([state.astype(jnp.bfloat16), logs], axis=0)


def chain(packed, step, heads):
    decays, states = [], []
    for part_in in from_earlier(packed, step):
        state, logs = (part_in[:-16].astype(jnp.float32), part_in[-16:].astype(jnp.float32))
        decays.append(jnp.repeat(jnp.exp(jnp.sum(logs[:3, :heads], axis=0)), MIXER_HEAD_SIZE)[None])
        states.append(state)
    return states[0] + decays[0] * (states[1] + decays[1] * states[2])


def sum_blocks(value):
    for axis in ("dp", "blk"):
        for bit in (1, 2):
            value = value + lax.ppermute(
                value, axis, [(at, at ^ bit) for at in range(lax.axis_size(axis))]
            )
    return value


def weight_sum(grads):
    return lax.psum_scatter(grads, ("dp", "blk"), scatter_dimension=0, tiled=True)


def split_columns(value_in, widths):
    pieces, start = [], 0
    for width in widths:
        pieces.append(value_in[:, start : start + width])
        start += width
    return pieces


def inverse_rms(rows_in):
    return lax.rsqrt(jnp.mean(rows_in * rows_in, axis=-1, keepdims=True) + norm_eps)


def norm_back(rows_in, gain_in, cotangent):
    inverse = inverse_rms(rows_in)
    scaled = rows_in * inverse
    weighted = cotangent * gain_in
    return inverse * (weighted - scaled * jnp.mean(weighted * scaled, axis=-1, keepdims=True))


def shards(
    x_in,
    out_grad,
    norm_one,
    w_query,
    w_key,
    w_value,
    output_gate_weight,
    mixer_input_weight,
    w_delta,
    w_bmat,
    w_cmat,
    delta_bias,
    decay_log,
    skip_gain,
    w_attn_out,
    mixer_output_weight,
    norm_two,
    w_gate,
    w_up,
    w_down,
):
    heads_count = lax.axis_size("heads")
    head_rank = lax.axis_index("heads")
    core = head_rank % 2
    block_rank = lax.axis_index("blk")
    rank = block_rank.astype(jnp.int32)[None]
    own_rows = x_in.shape[0]
    span_length = own_rows * heads_count
    half_span = span_length // 2
    span_start = block_rank * span_length
    query_width = w_query.shape[1]
    mixer_width = mixer_input_weight.shape[1]
    heads = mixer_width // MIXER_HEAD_SIZE
    state_size = w_bmat.shape[1]
    hidden_width = w_gate.shape[1]
    rows_of = w_query.shape[0]
    kv_index = head_rank * (query_width // HD) // (QH // KVH)
    kv_width = KVH * HD
    low = jnp.bfloat16
    ranks = chunk_ranks().astype(jnp.int32)
    turns = (head_rank + jnp.arange(heads_count)) % heads_count

    gains = jnp.stack([norm_one, norm_two], axis=1)
    gains = jnp.pad(gains, ((0, 0), (0, LANES - 2)))
    shared = jnp.concatenate([w_key, w_value, w_bmat, w_cmat, gains], axis=1)
    shared = jnp.concatenate([shared] + [shift(shared, -k) for k in range(1, heads_count)], axis=0)
    shared = reorder(turns.astype(jnp.int32), [shared], inverse=True)
    key_part = lax.dynamic_slice_in_dim(shared, kv_index * HD, HD, 1)
    value_part = lax.dynamic_slice_in_dim(shared, kv_width + kv_index * HD, HD, 1)
    state_part = shared[:, 2 * kv_width : 2 * kv_width + 2 * state_size]
    gain_part = shared[:, 2 * kv_width + 2 * state_size :][:, :2]
    misc_part = jnp.concatenate(
        [w_delta, gain_part, jnp.zeros((rows_of, LANES - heads - 2), low)], axis=1
    )
    in_names = ("z", "x", "b", "c", "misc", "key", "value", "query")
    in_widths = (mixer_width, mixer_width, state_size, state_size, LANES, HD, HD, query_width)
    starts = [sum(in_widths[:k]) for k in range(len(in_widths))]
    at = dict(zip(in_names, zip(starts, in_widths)))
    in_own = jnp.concatenate(
        [
            output_gate_weight,
            mixer_input_weight,
            state_part,
            misc_part,
            key_part,
            value_part,
            w_query,
        ],
        axis=1,
    )
    in_full = lax.all_gather(in_own, ("dp", "blk"), axis=0, tiled=True)
    out_widths = (query_width, mixer_width, hidden_width, hidden_width, hidden_width)
    out_full = lax.all_gather(
        jnp.concatenate([w_attn_out.T, mixer_output_weight.T, w_gate, w_up, w_down.T], axis=1),
        ("dp", "blk"),
        axis=0,
        tiled=True,
    )
    mixed_width = query_width + mixer_width
    mix_t, gate_full, up_full, down_t = split_columns(out_full, (mixed_width,) + out_widths[2:])

    x_float = x_in.astype(jnp.float32)
    x_span = gather_rows(x_in)
    ffn_grad = gather_rows(out_grad)
    positions = (span_start + jnp.arange(span_length)).astype(jnp.float32)
    freqs = rope_base ** (-2.0 * jnp.arange(HD // 2, dtype=jnp.float32) / HD)
    angles = positions[:, None] * freqs[None, :]
    cosine, sine = (jnp.cos(angles), jnp.sin(angles))
    cosine = jnp.concatenate([cosine, cosine], axis=1)
    sine = jnp.concatenate([-sine, sine], axis=1)
    in_full, x_span, ffn_grad, cosine, sine = lax.optimization_barrier(
        (in_full, x_span, ffn_grad, cosine, sine)
    )
    normed_input, normed_ordered, queries, keys_values, gain_rows = enter(
        ranks, jnp.full((1,), heads, jnp.int32), x_span, in_full, at, cosine, sine
    )
    gain_one, gain_two = (gain_rows[0:1], gain_rows[1:2])
    mine = lax.dynamic_slice_in_dim(keys_values, core * half_span, half_span, 0)
    pieces = []
    for piece in from_earlier(mine):
        pieces += [piece, to_partner(piece)]
    projected = simple_product(normed_ordered, in_full[:, : at["key"][0]])

    pad_lanes = lambda vector: jnp.pad(vector, (0, LANES - heads))[None]
    bias, rate = (pad_lanes(delta_bias), pad_lanes(jnp.exp(decay_log)))
    skip = jnp.repeat(skip_gain, MIXER_HEAD_SIZE)[None]
    delta, cumulative, delta_row, cum_row, local_state, local_log = scan_first(
        projected, at, bias, rate
    )
    entry_state = chain(pack_state(local_state, local_log), 1, heads)
    attended, attn_part, log_totals = attend(rank, queries, keys_values, pieces)
    scanned, gated, states = scan(
        projected, at, delta, cumulative, delta_row, cum_row, entry_state, skip
    )
    mixers = reorder(ranks, [attn_part, gated])
    middle = x_float + scatter_rows(lambda rows: dot_last(mixers[rows], mix_t), half_span)
    middle_scaled = middle * inverse_rms(middle)
    normed_two = gather_rows((middle_scaled * gain_two).astype(low))
    ffn_gate = simple_product(normed_two, gate_full)
    ffn_up = simple_product(normed_two, up_full)
    ffn_sig = jax.nn.sigmoid(ffn_gate)
    hidden = (ffn_gate * ffn_sig * ffn_up).astype(low)

    d_hidden = simple_product(ffn_grad, down_t)
    d_ffn_gate = (d_hidden * ffn_up * (ffn_sig * (1.0 + ffn_gate * (1.0 - ffn_sig)))).astype(low)
    d_ffn_up = (d_hidden * (ffn_gate * ffn_sig)).astype(low)
    d_normed_two = scatter_rows(
        lambda rows: dot_last(d_ffn_gate[rows], gate_full) + dot_last(d_ffn_up[rows], up_full),
        half_span,
    )
    ffn_sums = weight_sum(
        weight_grads((normed_two, [d_ffn_gate, d_ffn_up]), (ffn_grad, [hidden]))
    ).astype(jnp.float32)
    grad_gate, grad_up, grad_down_t = split_columns(ffn_sums, (hidden_width,) * 3)
    grad_two_part = jnp.sum(grad_gate * w_gate + grad_up * w_up, axis=1, keepdims=True)
    gain_own = gain_part.astype(jnp.float32)
    grad_two_part = grad_two_part / gain_own[:, 1:2]
    d_middle = out_grad.astype(jnp.float32) + norm_back(middle, gain_two, d_normed_two)
    mix_grad = gather_rows(d_middle.astype(low))
    mix_grad, hidden = lax.optimization_barrier((mix_grad, hidden))
    d_mixers = reorder(ranks, [simple_product(mix_grad, mix_t).astype(low)], inverse=True)
    d_scanned, d_gate_z, d_entry = scan_back_first(d_mixers, projected, at, scanned, cumulative)
    after_state = chain(pack_state(d_entry, local_log), -1, heads)
    d_query, d_own, d_far = attend_back(
        rank, queries, keys_values, pieces, attended, log_totals, d_mixers, cosine, sine
    )
    d_ssm_in, d_bmat, d_cmat, d_pre, sums = scan_back(
        projected,
        at,
        d_scanned,
        bias,
        rate,
        delta,
        cumulative,
        cum_row,
        states,
        after_state,
        skip,
    )
    far_half = d_far.shape[0] // 2
    d_mine = lax.dynamic_slice_in_dim(d_own, core * half_span, half_span, 0)
    d_theirs = lax.dynamic_slice_in_dim(d_own, (1 - core) * half_span, half_span, 0)
    d_mine = d_mine + to_partner(d_theirs.astype(low)).astype(jnp.float32)
    d_far = d_far[:far_half].astype(jnp.float32) + to_partner(d_far[far_half:]).astype(jnp.float32)
    d_one, d_two, d_three = (
        d_far[k * half_span : (k + 1) * half_span] for k in range(d_far.shape[0] // half_span)
    )
    d_one = d_one + on_blocks(d_two.astype(low), -1).astype(jnp.float32)
    d_mine = d_mine + on_blocks(d_one.astype(low), -1).astype(jnp.float32)
    d_mine = d_mine + on_blocks(d_three.astype(low), -3).astype(jnp.float32)
    half_cos = lax.dynamic_slice_in_dim(cosine, core * half_span, half_span, 0)
    half_sin = lax.dynamic_slice_in_dim(sine, core * half_span, half_span, 0)
    d_key = d_mine[:, :HD]
    d_key = d_key * half_cos - jnp.roll(d_key, HD // 2, axis=1) * half_sin
    d_mine = jnp.concatenate([d_key, d_mine[:, HD:]], axis=1).astype(low)
    d_keys_values = lax.dynamic_update_slice_in_dim(
        jnp.zeros((span_length, 2 * HD), low), d_mine, core * half_span, 0
    )

    d_projected = reorder(
        ranks, [d_gate_z, d_ssm_in, d_bmat, d_cmat, d_pre, d_keys_values, d_query]
    )
    in_sums = weight_sum(weight_grads((mix_grad, [mixers]), (normed_input, [d_projected])))
    d_normed = scatter_rows(lambda rows: dot_last(d_projected[rows], in_full), half_span)
    input_grad = d_middle + norm_back(x_float, gain_one, d_normed)
    ffn_out = scatter_rows(lambda rows: dot_last(hidden[rows], down_t), half_span)
    activations = (middle + ffn_out).astype(low)
    extra = jnp.concatenate([gain_own[:, 0:1], grad_two_part], axis=1)
    extra = jnp.pad(extra, ((0, 0), (0, LANES - 2)))
    grad_mix, grad_gatez, grad_ssmx, grad_query, misc_sums, shared_parts = finish(
        turns.astype(jnp.int32),
        kv_index.astype(jnp.int32)[None],
        in_sums,
        in_own,
        extra,
        at,
        mixed_width,
    )
    shared_sums = shared_parts[: rows_of // heads_count].astype(jnp.float32)
    for k in range(1, heads_count):
        here = slice(k * rows_of // heads_count, (k + 1) * rows_of // heads_count)
        shared_sums = shared_sums + shift(shared_parts[here], k).astype(jnp.float32)
    grad_key, grad_value, grad_bmat, grad_cmat, gain_sums = split_columns(
        shared_sums, (kv_width, kv_width, state_size, state_size, LANES)
    )
    small_sums = sum_blocks(sums)[:, :heads]
    return (
        activations,
        input_grad,
        gain_sums[:, 0],
        grad_query,
        grad_key,
        grad_value,
        grad_gatez,
        grad_ssmx,
        misc_sums[:, :heads],
        grad_bmat,
        grad_cmat,
        small_sums[0],
        small_sums[1],
        small_sums[2],
        grad_mix[:query_width],
        grad_mix[query_width:],
        gain_sums[:, 1],
        grad_gate,
        grad_up,
        grad_down_t.T,
    )


def solution(mesh):
    placed = (
        P(("dp", "blk", "heads"), None),
        P(("dp", "blk", "heads"), None),
        P(("dp", "blk", "heads")),
        P(("dp", "blk"), "heads"),
        P(("dp", "blk", "heads"), None),
        P(("dp", "blk", "heads"), None),
        P(("dp", "blk"), "heads"),
        P(("dp", "blk"), "heads"),
        P(("dp", "blk"), "heads"),
        P(("dp", "blk", "heads"), None),
        P(("dp", "blk", "heads"), None),
        P("heads"),
        P("heads"),
        P("heads"),
        P("heads", ("dp", "blk")),
        P("heads", ("dp", "blk")),
        P(("dp", "blk", "heads")),
        P(("dp", "blk"), "heads"),
        P(("dp", "blk"), "heads"),
        P("heads", ("dp", "blk")),
    )
    return jax.shard_map(
        shards,
        mesh=mesh,
        in_specs=placed,
        out_specs=(
            P(("dp", "blk", "heads"), None),
            P(("dp", "blk", "heads"), None),
            P(("dp", "blk", "heads")),
            P(("dp", "blk"), "heads"),
            P(("dp", "blk", "heads"), None),
            P(("dp", "blk", "heads"), None),
            P(("dp", "blk"), "heads"),
            P(("dp", "blk"), "heads"),
            P(("dp", "blk"), "heads"),
            P(("dp", "blk", "heads"), None),
            P(("dp", "blk", "heads"), None),
            P("heads"),
            P("heads"),
            P("heads"),
            P("heads", ("dp", "blk")),
            P("heads", ("dp", "blk")),
            P(("dp", "blk", "heads")),
            P(("dp", "blk"), "heads"),
            P(("dp", "blk"), "heads"),
            P("heads", ("dp", "blk")),
        ),
        check_vma=False,
    )
```

```python
import functools

import jax
import jax.numpy as jnp
from jax import lax
from jax.experimental import pallas as pl
from jax.experimental.pallas import tpu as pltpu
from jax.sharding import PartitionSpec as P

QH = 8
KVH = 2
HD = 128
MIXER_HEAD_SIZE = 64
BLOCK = 256
LANES = 128
LOG2_E = 1.4426950408889634


HIGH_PRECISION = lax.Precision.HIGHEST
norm_eps = 1e-05
rope_base = 100000000000.0


def simple_product(left_side, right_side):
    return jnp.dot(left_side, right_side, preferred_element_type=jnp.float32)


def dot_last(left_side, right_side):
    return lax.dot_general(
        left_side, right_side, (((1,), (1,)), ((), ())), preferred_element_type=jnp.float32
    )


def dot_first(left_side, right_side):
    return lax.dot_general(
        left_side, right_side, (((0,), (0,)), ((), ())), preferred_element_type=jnp.float32
    )


def compiler_params():
    return pltpu.CompilerParams(vmem_limit_bytes=50 * 1024 * 1024)


def in_vmem(count):
    return [pl.BlockSpec(memory_space=pltpu.VMEM)] * count


def mul(left_side, right_side):
    return jnp.dot(left_side, right_side, preferred_element_type=jnp.float32)


def tile_scores(key_rows, query_rows, head_size):
    return dot_last(key_rows, query_rows) * (head_size**-0.5 * LOG2_E)


def causal(scores):
    key_at = lax.broadcasted_iota(jnp.int32, scores.shape, 0)
    query_at = lax.broadcasted_iota(jnp.int32, scores.shape, 1)
    return jnp.where(key_at <= query_at, scores, -1e30)


def enter_kernel(
    ranks_ref,
    heads_ref,
    x_ref,
    misc_ref,
    key_ref,
    value_ref,
    w_query_ref,
    cos_ref,
    sin_ref,
    ordered_ref,
    query_ref,
    kv_ref,
    gains_ref,
):
    head_size = query_ref.shape[1]

    @pl.when(pl.program_id(0) == 0)
    def _():
        lane = lax.broadcasted_iota(jnp.int32, misc_ref.shape, 1)
        for k in range(2):
            column = jnp.where(lane == heads_ref[0] + k, misc_ref[...].astype(jnp.float32), 0.0)
            gains_ref[k : k + 1, :] = jnp.sum(column.T, axis=0, keepdims=True)

    cosine, sine = (cos_ref[...], sin_ref[...])

    def turn(value):
        return (value * cosine + pltpu.roll(value, head_size // 2, 1) * sine).astype(jnp.bfloat16)

    rows = x_ref[...].astype(jnp.float32)
    normed = (rows * inverse_rms(rows) * gains_ref[0:1, :]).astype(jnp.bfloat16)
    ordered_ref[...] = normed
    kv_ref[:, :head_size] = turn(mul(normed, key_ref[...]))
    kv_ref[:, head_size:] = mul(normed, value_ref[...]).astype(jnp.bfloat16)
    query_ref[...] = turn(mul(normed, w_query_ref[...]))


def enter(ranks, heads, x_span, in_full, at, cosine, sine):
    count = ranks.shape[0]
    rows, width = x_span.shape
    head_size = cosine.shape[1]
    here = lambda columns: pl.BlockSpec((rows // count, columns), lambda k, r, h: (k, 0))
    there = lambda columns: pl.BlockSpec((rows // count, columns), lambda k, r, h: (r[k], 0))
    weight = lambda name: pl.BlockSpec(
        (width, at[name][1]), lambda k, r, h: (0, at[name][0] // at[name][1])
    )
    return pl.pallas_call(
        enter_kernel,
        grid_spec=pltpu.PrefetchScalarGridSpec(
            num_scalar_prefetch=2,
            grid=(count,),
            in_specs=[
                here(width),
                weight("misc"),
                weight("key"),
                weight("value"),
                weight("query"),
                there(head_size),
                there(head_size),
            ],
            out_specs=(
                there(width),
                there(head_size),
                there(2 * head_size),
                pl.BlockSpec((8, width), lambda k, r, h: (0, 0)),
            ),
        ),
        out_shape=(
            jax.ShapeDtypeStruct((rows, width), jnp.bfloat16),
            jax.ShapeDtypeStruct((rows, head_size), jnp.bfloat16),
            jax.ShapeDtypeStruct((rows, 2 * head_size), jnp.bfloat16),
            jax.ShapeDtypeStruct((8, width), jnp.float32),
        ),
        compiler_params=compiler_params(),
        cost_estimate=pl.CostEstimate(
            flops=2_000_000_000, bytes_accessed=16_000_000, transcendentals=0
        ),
        name="enter",
    )(ranks, heads, x_span, in_full, in_full, in_full, in_full, cosine, sine)


def weight_part_kernel(ranks_ref, low_ref, high_ref, *refs, count):
    out_ref = refs[-1]
    left = jnp.concatenate([low_ref[...].T, high_ref[...].T], axis=0)
    start = 0
    for ref in refs[:count]:
        out_ref[:, start : start + ref.shape[1]] = mul(left, ref[...]).astype(jnp.bfloat16)
        start += ref.shape[1]


def weight_part(ranks, left, rights, place, width, buffer=None):
    depth, rows = left.shape
    columns = sum(size for _, _, size in rights)
    operands = [ranks, left, left] + [array for array, _, _ in rights]
    side = lambda offset: pl.BlockSpec((depth, LANES), lambda k, r: (0, r[2 * k + offset]))
    in_specs = [side(0), side(1)]
    for _, start, size in rights:
        in_specs.append(pl.BlockSpec((depth, size), lambda k, r, at=start // size: (0, at)))
    aliases = {}
    if buffer is not None:
        aliases = {len(operands): 0}
        operands.append(buffer)
        in_specs.append(pl.BlockSpec(memory_space=pl.ANY))
    return pl.pallas_call(
        functools.partial(weight_part_kernel, count=len(rights)),
        grid_spec=pltpu.PrefetchScalarGridSpec(
            num_scalar_prefetch=1,
            grid=(rows // (2 * LANES),),
            in_specs=in_specs,
            out_specs=pl.BlockSpec((2 * LANES, columns), lambda k, r: (k, place)),
        ),
        out_shape=jax.ShapeDtypeStruct((rows, width), jnp.bfloat16),
        input_output_aliases=aliases,
        compiler_params=compiler_params(),
        cost_estimate=pl.CostEstimate(
            flops=2 * rows * depth * columns,
            bytes_accessed=2 * (depth * (rows + columns) + rows * columns),
            transcendentals=0,
        ),
        name="weight_part",
    )(*operands)


def assemble_kernel(chunks_ref, *refs, groups):
    out_ref, sems = refs[-2:]
    copies = []
    for group, start in enumerate(groups):
        at = 0
        for ref in refs[5 * group : 5 * group + 5]:
            for k in range(ref.shape[0] // LANES):
                to = pl.ds(pl.multiple_of(chunks_ref[group, at] * LANES, LANES), LANES)
                copies.append(
                    pltpu.make_async_copy(
                        ref.at[pl.ds(k * LANES, LANES), :],
                        out_ref.at[to, pl.ds(start, ref.shape[1])],
                        sems.at[len(copies)],
                    )
                )
                at += 1
    for copy in copies:
        copy.start()
    for copy in copies:
        copy.wait()


def assemble(chunks, groups):
    widths = [pieces[0].shape[1] for pieces in groups]
    starts = tuple(sum(widths[:k]) for k in range(len(widths)))
    rows = sum(piece.shape[0] for piece in groups[0])
    pieces = [piece for group in groups for piece in group]
    return pl.pallas_call(
        functools.partial(assemble_kernel, groups=starts),
        out_shape=jax.ShapeDtypeStruct((rows, sum(widths)), jnp.bfloat16),
        in_specs=[pl.BlockSpec(memory_space=pltpu.SMEM)]
        + [pl.BlockSpec(memory_space=pl.ANY)] * len(pieces),
        out_specs=pl.BlockSpec(memory_space=pl.ANY),
        scratch_shapes=[pltpu.SemaphoreType.DMA((len(groups) * rows // LANES,))],
        compiler_params=compiler_params(),
        cost_estimate=pl.CostEstimate(
            flops=0, bytes_accessed=4 * rows * sum(widths), transcendentals=0
        ),
        name="assemble",
    )(chunks, *pieces)


def finish_kernel(
    ranks_ref,
    kv_ref,
    first_ref,
    second_ref,
    weight_ref,
    extra_ref,
    ssm_out_ref,
    attn_out_ref,
    gate_ref,
    ssm_ref,
    query_ref,
    misc_ref,
    shared_ref,
    whole_ref,
    *,
    at,
    sums_at,
):
    def of(name):
        group, start, size = sums_at[name]
        return (first_ref, second_ref)[group][:, start : start + size]

    ssm_out_ref[...] = of("ssm_out").T
    attn_out_ref[...] = of("attn_out").T
    gate_ref[...] = of("z")
    ssm_ref[...] = of("x")
    query_ref[...] = of("query")
    misc_ref[...] = of("misc")
    total = 0.0
    for name, (start, size) in at.items():
        product = of(name) * weight_ref[:, start : start + size].astype(jnp.float32)
        total += jnp.sum(product, axis=1, keepdims=True)
    total = total / extra_ref[:, 0:1]
    lane = lax.broadcasted_iota(jnp.int32, misc_ref.shape, 1)
    gains = jnp.where(lane == 0, total, jnp.where(lane == 1, extra_ref[:, 1:2], 0.0))
    zero = jnp.zeros_like(gains)
    first = kv_ref[0] == 0
    key, value = (of("key"), of("value"))
    pieces = (
        jnp.where(first, key, zero),
        jnp.where(first, zero, key),
        jnp.where(first, value, zero),
        jnp.where(first, zero, value),
        of("b"),
        of("c"),
        gains,
    )
    start = 0
    for piece in pieces:
        whole_ref[:, start : start + piece.shape[1]] = piece
        start += piece.shape[1]
    count = ranks_ref.shape[0]
    size = shared_ref.shape[0] // count
    for k in range(count):
        rows = pl.ds(pl.multiple_of(ranks_ref[k] * size, size), size)
        shared_ref[k * size : (k + 1) * size, :] = whole_ref[rows, :].astype(jnp.bfloat16)


def finish(ranks, kv_index, first, second, weights, extra, at, sums_at):
    rows = weights.shape[0]
    shape = lambda *sizes: jax.ShapeDtypeStruct(sizes, jnp.float32)
    width = lambda name: sums_at[name][2]
    shared = 2 * (width("key") + width("value")) + width("b") + width("c") + LANES
    return pl.pallas_call(
        functools.partial(finish_kernel, at=at, sums_at=sums_at),
        out_shape=(
            shape(width("ssm_out"), rows),
            shape(width("attn_out"), rows),
            shape(rows, width("z")),
            shape(rows, width("x")),
            shape(rows, width("query")),
            shape(rows, width("misc")),
            jax.ShapeDtypeStruct((rows, shared), jnp.bfloat16),
        ),
        in_specs=[pl.BlockSpec(memory_space=pltpu.SMEM)] * 2 + in_vmem(4),
        out_specs=tuple(in_vmem(7)),
        scratch_shapes=[pltpu.VMEM((rows, shared), jnp.float32)],
        compiler_params=compiler_params(),
        name="finish",
    )(ranks, kv_index, first, second, weights, extra)


def attend_kernel(rank_ref, query_ref, own_ref, *refs):
    pieces, (out_ref, low_ref, log_ref) = (refs[:-3], refs[-3:])
    span_length, head_size = query_ref.shape
    tile = own_ref.shape[0] // 2
    for block in range(span_length // tile):
        here = slice(block * tile, (block + 1) * tile)
        query_rows = query_ref[here, :]

        def step(kv_rows, carried, masked=False):
            top, total, summed = carried
            scores = tile_scores(kv_rows[:, :head_size], query_rows, head_size)
            if masked:
                scores = causal(scores)
            new_top = jnp.maximum(top, jnp.max(scores, axis=0, keepdims=True))
            probs = jnp.exp2(scores - new_top)
            scale = jnp.exp2(top - new_top)
            total = total * scale + jnp.sum(probs, axis=0, keepdims=True)
            summed = summed * scale + dot_first(kv_rows[:, head_size:], probs.astype(jnp.bfloat16))
            return (new_top, total, summed)

        carried = (
            jnp.full((1, tile), -1e30, jnp.float32),
            jnp.zeros((1, tile), jnp.float32),
            jnp.zeros((head_size, tile), jnp.float32),
        )
        carried = step(own_ref[here, :], carried, True)
        for earlier in range(block):
            carried = step(own_ref[earlier * tile : (earlier + 1) * tile, :], carried)
        for distance in range(1, 1 + len(pieces) // 2):
            pair = pieces[2 * distance - 2 : 2 * distance]

            def both(_, carried, pair=pair):
                return step(pair[1][...], step(pair[0][...], carried))

            valid = (rank_ref[0] >= distance).astype(jnp.int32)
            carried = lax.fori_loop(0, valid, both, carried)
        top, total, summed = carried
        result = summed / total
        out_ref[:, here] = result
        low_ref[here, :] = result.T.astype(jnp.bfloat16)
        log_ref[:, here] = top + jnp.log2(total)


def attend(rank, queries, own, pieces):
    span_length, head_size = queries.shape
    return pl.pallas_call(
        attend_kernel,
        out_shape=(
            jax.ShapeDtypeStruct((head_size, span_length), jnp.float32),
            jax.ShapeDtypeStruct((span_length, head_size), jnp.bfloat16),
            jax.ShapeDtypeStruct((1, span_length), jnp.float32),
        ),
        in_specs=[pl.BlockSpec(memory_space=pltpu.SMEM)] + in_vmem(2 + len(pieces)),
        out_specs=tuple(in_vmem(3)),
        compiler_params=compiler_params(),
        cost_estimate=pl.CostEstimate(
            flops=10_000_000_000, bytes_accessed=4_000_000, transcendentals=4_000_000
        ),
        name="attend",
    )(rank, queries, own, *pieces)


def attend_back_kernel(rank_ref, query_ref, own_ref, *refs):
    pieces, refs = (refs[:-9], refs[-9:])
    out_ref, log_ref, grad_ref, cos_ref, sin_ref, d_query_ref, d_own_ref, d_far_ref, sums_ref = refs
    span_length, head_size = query_ref.shape
    tile = own_ref.shape[0] // 2
    score_scale = head_size**-0.5
    sums_ref[...] = jnp.zeros_like(sums_ref)
    for block in range(span_length // tile):
        here = slice(block * tile, (block + 1) * tile)
        query_rows = query_ref[here, :]
        grad_rows = grad_ref[here, grad_ref.shape[1] - head_size :]
        log_total = log_ref[:, here]
        delta_row = jnp.sum(
            grad_rows.astype(jnp.float32).T * out_ref[:, here], axis=0, keepdims=True
        )

        def step(kv_ref, start, at, d_query, masked=False):
            key_rows = kv_ref[start : start + tile, :head_size]
            scores = tile_scores(key_rows, query_rows, head_size)
            if masked:
                scores = causal(scores)
            probs = jnp.exp2(scores - log_total)
            d_probs = dot_last(kv_ref[start : start + tile, head_size:], grad_rows)
            d_scores = (probs * (d_probs - delta_row)).astype(jnp.bfloat16)
            rows = slice(at * tile, (at + 1) * tile)
            sums_ref[rows, head_size:] += mul(probs.astype(jnp.bfloat16), grad_rows)
            sums_ref[rows, :head_size] += mul(d_scores, query_rows)
            return d_query + dot_first(key_rows, d_scores)

        d_query = jnp.zeros((head_size, tile), jnp.float32)
        d_query = step(own_ref, block * tile, block, d_query, True)
        for earlier in range(block):
            d_query = step(own_ref, earlier * tile, earlier, d_query)
        for distance in range(1, 1 + len(pieces) // 2):

            def both(_, d_query, distance=distance):
                for k in (2 * distance - 2, 2 * distance - 1):
                    d_query = step(pieces[k], 0, 2 + k, d_query)
                return d_query

            valid = (rank_ref[0] >= distance).astype(jnp.int32)
            d_query = lax.fori_loop(0, valid, both, d_query)
        turned = d_query.T * score_scale
        d_query_ref[here, :] = (
            turned * cos_ref[here, :] - pltpu.roll(turned, head_size // 2, 1) * sin_ref[here, :]
        ).astype(jnp.bfloat16)
    lane = lax.broadcasted_iota(jnp.int32, (tile, 2 * head_size), 1)
    scale = jnp.where(lane < head_size, score_scale, 1.0)
    for at in range(2):
        rows = slice(at * tile, (at + 1) * tile)
        d_own_ref[rows, :] = sums_ref[rows, :] * scale
    for k in range(len(pieces)):
        rows = slice((2 + k) * tile, (3 + k) * tile)
        into = (k % 2) * (len(pieces) // 2) + k // 2
        d_far_ref[into * tile : (into + 1) * tile, :] = (sums_ref[rows, :] * scale).astype(
            jnp.bfloat16
        )


def attend_back(rank, queries, own, pieces, attended, log_totals, d_attn, cosine, sine):
    tile = own.shape[0] // 2
    return pl.pallas_call(
        attend_back_kernel,
        out_shape=(
            jax.ShapeDtypeStruct(queries.shape, jnp.bfloat16),
            jax.ShapeDtypeStruct(own.shape, jnp.float32),
            jax.ShapeDtypeStruct((len(pieces) * tile, own.shape[1]), jnp.bfloat16),
        ),
        in_specs=[pl.BlockSpec(memory_space=pltpu.SMEM)] + in_vmem(7 + len(pieces)),
        out_specs=tuple(in_vmem(3)),
        scratch_shapes=[pltpu.VMEM(((2 + len(pieces)) * tile, own.shape[1]), jnp.float32)],
        compiler_params=compiler_params(),
        cost_estimate=pl.CostEstimate(
            flops=25_000_000_000, bytes_accessed=8_000_000, transcendentals=4_000_000
        ),
        name="attend_back",
    )(rank, queries, own, *pieces, attended, log_totals, d_attn, cosine, sine)


def reorder_kernel(ranks_ref, *refs):
    out_ref = refs[-1]
    start = 0
    for ref in refs[:-1]:
        out_ref[:, start : start + ref.shape[1]] = ref[...].astype(out_ref.dtype)
        start += ref.shape[1]


def reorder(ranks, pieces, inverse=False):
    count = ranks.shape[0]
    rows = pieces[0].shape[0] // count
    width = sum(piece.shape[1] for piece in pieces)
    there = lambda k, ranks: (ranks[k], 0)
    here = lambda k, ranks: (k, 0)
    return pl.pallas_call(
        reorder_kernel,
        grid_spec=pltpu.PrefetchScalarGridSpec(
            num_scalar_prefetch=1,
            grid=(count,),
            in_specs=[
                pl.BlockSpec((rows, piece.shape[1]), here if inverse else there)
                for piece in pieces
            ],
            out_specs=pl.BlockSpec((rows, width), there if inverse else here),
        ),
        out_shape=jax.ShapeDtypeStruct((count * rows, width), jnp.bfloat16),
        compiler_params=compiler_params(),
        cost_estimate=pl.CostEstimate(
            flops=0, bytes_accessed=4 * count * rows * width, transcendentals=0
        ),
        name="reorder",
    )(ranks, *pieces)


def lower_ones(size, dtype=jnp.float32):
    row = lax.broadcasted_iota(jnp.int32, (size, size), 0)
    column = lax.broadcasted_iota(jnp.int32, (size, size), 1)
    return (row >= column).astype(dtype)


def precise(left_side, right_side):
    return jnp.dot(
        left_side, right_side, precision=HIGH_PRECISION, preferred_element_type=jnp.float32
    )


def spread_heads(columns, head_size, width):
    lane = lax.broadcasted_iota(jnp.int32, (columns.shape[0], 2 * head_size), 1)
    pairs = [
        jnp.where(lane < head_size, columns[:, k : k + 1], columns[:, k + 1 : k + 2])
        for k in range(0, width // head_size, 2)
    ]
    return jnp.concatenate(pairs, axis=1)


def head_ones(width, head_size, lanes, dtype):
    at = lax.broadcasted_iota(jnp.int32, (width, lanes), 0)
    lane = lax.broadcasted_iota(jnp.int32, (width, lanes), 1)
    low = lane * head_size
    return ((at >= low) & (at < low + head_size)).astype(dtype)


def scan_first_kernel(
    pre_ref, bias_ref, rate_ref, x_ref, b_ref, delta_ref, cum_ref, delta_row_ref, cum_row_ref, state_ref, log_ref
):
    @pl.when(pl.program_id(0) == 0)
    def _():
        state_ref[...] = jnp.zeros_like(state_ref)
        log_ref[...] = jnp.zeros_like(log_ref)

    delta = jax.nn.softplus(pre_ref[...] + bias_ref[...])
    log_step = -delta * rate_ref[...]
    cumulative = precise(lower_ones(log_step.shape[0]), log_step)
    delta_ref[...] = delta
    cum_ref[...] = cumulative
    delta_row_ref[...] = delta.T[:8]
    cum_row_ref[...] = cumulative.T[:8]
    ending = cumulative[-1:, :]
    weight = jnp.exp(ending - cumulative + log_ref[...]) * delta
    width = x_ref.shape[1]
    x_low = x_ref[...].astype(jnp.bfloat16).astype(jnp.float32)
    weighted = (x_low * spread_heads(weight, MIXER_HEAD_SIZE, width)).astype(jnp.bfloat16)
    state_ref[...] += dot_first(b_ref[...].astype(jnp.bfloat16), weighted)
    log_ref[...] += ending


def part(projected, start, width, order=lambda c: c):
    at = start // width
    return (projected, pl.BlockSpec((BLOCK, width), lambda c: (order(c), at)))


def run_scan(kernel, chunks, operands, out_shape, out_specs, flops, name, scratch=()):
    return pl.pallas_call(
        kernel,
        grid=(chunks,),
        out_shape=out_shape,
        in_specs=[spec for _, spec in operands],
        out_specs=out_specs,
        scratch_shapes=list(scratch),
        compiler_params=compiler_params(),
        cost_estimate=pl.CostEstimate(
            flops=flops, bytes_accessed=8_000_000, transcendentals=1_000_000
        ),
        name=name,
    )(*[array for array, _ in operands])


def whole(array):
    return (array, pl.BlockSpec(array.shape, lambda c: (0,) * array.ndim))


def scan_first(at, bias, rate):
    rows, lanes = (at["x"][0].shape[0], bias.shape[1])
    chunks = rows // BLOCK
    back = lambda c: chunks - 1 - c
    width, state_size = (at["x"][2], at["b"][2])
    by_chunk = pl.BlockSpec((BLOCK, lanes), lambda c: (back(c), 0))
    across = pl.BlockSpec((8, BLOCK), lambda c: (0, back(c)))
    shape = lambda *sizes: jax.ShapeDtypeStruct(sizes, jnp.float32)
    return run_scan(
        scan_first_kernel,
        chunks,
        [
            part(*at["misc"], back),
            whole(bias),
            whole(rate),
            part(*at["x"], back),
            part(*at["b"], back),
        ],
        (
            shape(rows, lanes),
            shape(rows, lanes),
            shape(8, rows),
            shape(8, rows),
            shape(state_size, width),
            shape(1, lanes),
        ),
        (
            by_chunk,
            by_chunk,
            across,
            across,
            pl.BlockSpec((state_size, width), lambda c: (0, 0)),
            pl.BlockSpec((1, lanes), lambda c: (0, 0)),
        ),
        1_000_000_000,
        "scan_first",
    )


def scan_kernel(
    x_ref,
    z_ref,
    b_ref,
    c_ref,
    delta_ref,
    cum_ref,
    delta_row_ref,
    cum_row_ref,
    entry_ref,
    skip_ref,
    scanned_ref,
    gated_ref,
    states_ref,
    state_ref,
):
    @pl.when(pl.program_id(0) == 0)
    def _():
        state_ref[...] = entry_ref[...]

    head_size = MIXER_HEAD_SIZE
    pair = 2 * head_size
    size, width = x_ref.shape
    state = state_ref[...]
    states_ref[0] = state
    delta, cumulative = (delta_ref[...], cum_ref[...])
    delta_row, cum_row = (delta_row_ref[...], cum_row_ref[...])
    bmat, cmat = (b_ref[...].astype(jnp.bfloat16), c_ref[...].astype(jnp.bfloat16))
    x_all = x_ref[...].astype(jnp.bfloat16)
    inner = dot_last(cmat, bmat)
    row = lax.broadcasted_iota(jnp.int32, (size, size), 0)
    column = lax.broadcasted_iota(jnp.int32, (size, size), 1)
    allowed = row >= column
    lane = lax.broadcasted_iota(jnp.int32, (size, pair), 1)
    from_state = mul(cmat, state.astype(jnp.bfloat16))
    spread = spread_heads(jnp.exp(cumulative), head_size, width)
    for first in range(0, width // head_size, 2):
        here = slice(first * head_size, first * head_size + pair)
        x_pair = x_all[:, here]
        total = from_state[:, here] * spread[:, here]
        total += skip_ref[:, here] * x_pair.astype(jnp.float32)
        for head in (first, first + 1):
            gap = cumulative[:, head : head + 1] - cum_row[head : head + 1, :]
            decay = jnp.exp(jnp.where(allowed, gap, -1e30))
            mixing = inner * decay * delta_row[head : head + 1, :]
            x_head = jnp.where((lane >= head_size) == (head > first), x_pair, 0.0)
            total += mul(mixing.astype(jnp.bfloat16), x_head.astype(jnp.bfloat16))
        scanned_ref[:, here] = total
        gate = z_ref[:, here]
        gated_ref[:, here] = (total * (gate * jax.nn.sigmoid(gate))).astype(jnp.bfloat16)
    ending = cumulative[-1:, :]
    weight = spread_heads(jnp.exp(ending - cumulative) * delta, head_size, width)
    weighted = (x_all.astype(jnp.float32) * weight).astype(jnp.bfloat16)
    state_ref[...] = state * spread[-1:, :] + dot_first(bmat, weighted)


def scan(at, delta, cumulative, delta_row, cum_row, entry, skip):
    rows = delta.shape[0]
    state_size, width = entry.shape
    chunks = rows // BLOCK
    by_chunk = pl.BlockSpec((BLOCK, width), lambda c: (c, 0))
    lanes = delta.shape[1]
    across = pl.BlockSpec((8, BLOCK), lambda c: (0, c))
    return run_scan(
        scan_kernel,
        chunks,
        [
            part(*at["x"]),
            part(*at["z"]),
            part(*at["b"]),
            part(*at["c"]),
            part(delta, 0, lanes),
            part(cumulative, 0, lanes),
            (delta_row, across),
            (cum_row, across),
            whole(entry),
            whole(skip),
        ],
        (
            jax.ShapeDtypeStruct((rows, width), jnp.float32),
            jax.ShapeDtypeStruct((rows, width), jnp.bfloat16),
            jax.ShapeDtypeStruct((chunks, state_size, width), jnp.float32),
        ),
        (by_chunk, by_chunk, pl.BlockSpec((1, state_size, width), lambda c: (c, 0, 0))),
        3_000_000_000,
        "scan",
        [pltpu.VMEM((state_size, width), jnp.float32)],
    )


def scan_back_first_kernel(
    grad_ref, z_ref, scanned_ref, c_ref, cum_ref, d_scanned_ref, d_gate_ref, state_ref, log_ref
):
    @pl.when(pl.program_id(0) == 0)
    def _():
        state_ref[...] = jnp.zeros_like(state_ref)
        log_ref[...] = jnp.zeros_like(log_ref)

    gate = z_ref[...]
    chance = jax.nn.sigmoid(gate)
    grad = grad_ref[:, : z_ref.shape[1]].astype(jnp.float32)
    d_scanned = grad * (gate * chance)
    d_scanned_ref[...] = d_scanned
    d_gate_ref[...] = (
        grad * scanned_ref[...] * (chance * (1.0 + gate * (1.0 - chance)))
    ).astype(jnp.bfloat16)
    cumulative = cum_ref[...]
    decay = spread_heads(jnp.exp(cumulative + log_ref[...]), MIXER_HEAD_SIZE, z_ref.shape[1])
    state_ref[...] += dot_first(
        c_ref[...].astype(jnp.bfloat16), (d_scanned * decay).astype(jnp.bfloat16)
    )
    log_ref[...] += cumulative[-1:, :]


def scan_back_first(grads, at, scanned, cumulative):
    rows, width = scanned.shape
    state_size, lanes = (at["c"][2], cumulative.shape[1])
    by_chunk = pl.BlockSpec((BLOCK, width), lambda c: (c, 0))
    return run_scan(
        scan_back_first_kernel,
        rows // BLOCK,
        [
            part(grads, 0, grads.shape[1]),
            part(*at["z"]),
            part(scanned, 0, width),
            part(*at["c"]),
            part(cumulative, 0, lanes),
        ],
        (
            jax.ShapeDtypeStruct((rows, width), jnp.float32),
            jax.ShapeDtypeStruct((rows, width), jnp.bfloat16),
            jax.ShapeDtypeStruct((state_size, width), jnp.float32),
        ),
        (by_chunk, by_chunk, pl.BlockSpec((state_size, width), lambda c: (0, 0))),
        1_000_000_000,
        "scan_back_first",
        [pltpu.VMEM((1, lanes), jnp.float32)],
    )


def scan_back_kernel(
    x_ref,
    grad_ref,
    b_ref,
    c_ref,
    pre_ref,
    bias_ref,
    rate_ref,
    delta_ref,
    cum_ref,
    cum_row_ref,
    states_ref,
    entry_ref,
    skip_ref,
    d_x_ref,
    d_b_ref,
    d_c_ref,
    d_pre_ref,
    sums_ref,
    state_ref,
):
    @pl.when(pl.program_id(0) == 0)
    def _():
        state_ref[...] = entry_ref[...]
        sums_ref[...] = jnp.zeros_like(sums_ref)

    head_size = MIXER_HEAD_SIZE
    pair = 2 * head_size
    size, width = x_ref.shape
    lanes = delta_ref.shape[1]
    low = jnp.bfloat16
    delta, cumulative, cum_row = (delta_ref[...], cum_ref[...], cum_row_ref[...])
    bmat, cmat = (b_ref[...].astype(low), c_ref[...].astype(low))
    x_all = x_ref[...].astype(low)
    x_single = x_all.astype(jnp.float32)
    grad = grad_ref[...]
    grad_low = grad.astype(low)
    state = states_ref[0]
    state_low = state.astype(low)
    after = state_ref[...]
    after_low = after.astype(low)
    ending = cumulative[-1:, :]
    row = lax.broadcasted_iota(jnp.int32, (size, size), 0)
    column = lax.broadcasted_iota(jnp.int32, (size, size), 1)
    later = column >= row
    before = (row > column).astype(low)
    onward = later.astype(low)
    lane = lax.broadcasted_iota(jnp.int32, (size, pair), 1)
    head_lane = lax.broadcasted_iota(jnp.int32, (size, lanes), 1)
    sum_heads = head_ones(width, head_size, lanes, low)

    inner = dot_last(bmat, cmat)
    from_after = mul(bmat, after_low)
    weight = jnp.exp(ending - cumulative)
    spread_weight = spread_heads(weight * delta, head_size, width)
    spread = spread_heads(jnp.exp(cumulative), head_size, width)
    to_end = mul((x_single * from_after).astype(low), sum_heads)
    through = jnp.exp(cumulative) * mul((grad * mul(cmat, state_low)).astype(low), sum_heads)
    carried = jnp.sum(state * after, axis=0, keepdims=True) * spread[-1:, :]
    carried = precise(carried, sum_heads.astype(jnp.float32))
    d_delta = weight * to_end
    d_log = (
        mul(onward, through.astype(low)) + mul(before, (d_delta * delta).astype(low)) + carried
    )

    d_inner = jnp.zeros((size, size), jnp.float32)
    for first in range(0, width // head_size, 2):
        here = slice(first * head_size, first * head_size + pair)
        x_pair, grad_pair = (x_all[:, here], grad_low[:, here])
        d_x = from_after[:, here] * spread_weight[:, here] + skip_ref[:, here] * grad[:, here]
        for head in (first, first + 1):
            mine = (lane >= head_size) == (head > first)
            gap = cum_row[head : head + 1, :] - cumulative[:, head : head + 1]
            decay = jnp.exp(jnp.where(later, gap, -1e30))
            delta_column = delta[:, head : head + 1]
            d_mixing = dot_last(jnp.where(mine, x_pair, 0.0).astype(low), grad_pair) * decay
            d_inner += d_mixing * delta_column
            flow = d_mixing * inner
            mixing = inner * decay * delta_column
            d_x += mul(mixing.astype(low), jnp.where(mine, grad_pair, 0.0).astype(low))
            d_delta_head = jnp.sum(flow, axis=1, keepdims=True)
            passing = mul(before, (flow * delta_column).astype(low))
            d_log_head = jnp.sum(jnp.where(later, passing, 0.0), axis=1, keepdims=True)
            d_delta += jnp.where(head_lane == head, d_delta_head, 0.0)
            d_log += jnp.where(head_lane == head, d_log_head, 0.0)
        d_x_ref[:, here] = d_x.astype(low)

    d_inner_low = d_inner.astype(low)
    scaled_grad = (grad * spread).astype(low)
    weighted = (x_single * spread_weight).astype(low)
    d_b_ref[...] = (mul(d_inner_low, cmat) + dot_last(weighted, after_low)).astype(low)
    d_c_ref[...] = (dot_first(d_inner_low, bmat) + dot_last(scaled_grad, state_low)).astype(low)
    state_ref[...] = after * spread[-1:, :] + dot_first(cmat, scaled_grad)
    rate = rate_ref[...]
    d_pre = (d_delta - d_log * rate) * jax.nn.sigmoid(pre_ref[...] + bias_ref[...])
    d_pre = jnp.where(head_lane < width // head_size, d_pre, 0.0)
    d_pre_ref[...] = d_pre.astype(low)
    skip_sum = precise(
        jnp.sum(grad * x_single, axis=0, keepdims=True), sum_heads.astype(jnp.float32)
    )
    sums_ref[0:1, :] += jnp.sum(d_pre, axis=0, keepdims=True)
    sums_ref[1:2, :] += jnp.sum(d_log * (-delta * rate), axis=0, keepdims=True)
    sums_ref[2:3, :] += skip_sum


def scan_back(
    at, d_scanned, bias, rate, delta, cumulative, cum_row, states, entry, skip
):
    rows, width = d_scanned.shape
    state_size, lanes = (entry.shape[0], delta.shape[1])
    chunks = rows // BLOCK
    back = lambda c: chunks - 1 - c
    by_chunk = lambda columns: pl.BlockSpec((BLOCK, columns), lambda c: (back(c), 0))
    shape = lambda columns: jax.ShapeDtypeStruct((rows, columns), jnp.bfloat16)
    return run_scan(
        scan_back_kernel,
        chunks,
        [
            part(*at["x"], back),
            part(d_scanned, 0, width, back),
            part(*at["b"], back),
            part(*at["c"], back),
            part(*at["misc"], back),
            whole(bias),
            whole(rate),
            part(delta, 0, lanes, back),
            part(cumulative, 0, lanes, back),
            (cum_row, pl.BlockSpec((8, BLOCK), lambda c: (0, back(c)))),
            (states, pl.BlockSpec((1, state_size, width), lambda c: (back(c), 0, 0))),
            whole(entry),
            whole(skip),
        ],
        (
            shape(width),
            shape(state_size),
            shape(state_size),
            shape(lanes),
            jax.ShapeDtypeStruct((8, lanes), jnp.float32),
        ),
        (
            by_chunk(width),
            by_chunk(state_size),
            by_chunk(state_size),
            by_chunk(lanes),
            pl.BlockSpec((8, lanes), lambda c: (0, 0)),
        ),
        6_000_000_000,
        "scan_back",
        [pltpu.VMEM((state_size, width), jnp.float32)],
    )


def on_heads(value, move):
    devices = lax.axis_size("heads")
    pairs = []
    for at in range(devices):
        z, core = move(at // 2, at % 2)
        pairs.append((at, 2 * (z % (devices // 2)) + core))
    return lax.ppermute(value, "heads", pairs)


def to_partner(value):
    return on_heads(value, lambda z, core: (z, 1 - core))


def along(value):
    return on_heads(value, lambda z, core: (z + 1 - 2 * core, core))


def against(value):
    return on_heads(value, lambda z, core: (z - 1 + 2 * core, core))


def chunk_ranks():
    devices = lax.axis_size("heads")
    z, core = (lax.axis_index("heads") // 2, lax.axis_index("heads") % 2)
    step, other = (1 - 2 * core, 1 - core)
    owners = (
        (z, core),
        (z + 2, core),
        (z - step, core),
        (z - step, other),
        (z, other),
        (z + 2, other),
        (z + step, other),
        (z + step, core),
    )
    return jnp.stack([2 * ((at + devices) % (devices // 2)) + side for at, side in owners])


def gather_rows(own):
    partner = to_partner(own)
    near = along(own)
    near_other = along(partner)
    far = along(near)
    mine = (own, far, near, near_other)
    theirs = (partner, to_partner(far), to_partner(near), to_partner(near_other))
    return jnp.concatenate(mine + theirs, axis=0)


def scatter_rows(product, half):
    chunk = half // 4
    got = to_partner(product(slice(half, 2 * half)).astype(jnp.bfloat16))
    summed = product(slice(0, half)) + got.astype(jnp.float32)
    low = summed[chunk:].astype(jnp.bfloat16)
    far = against(low[:chunk])
    near_other = against(low[2 * chunk :])
    near = against((low[chunk : 2 * chunk].astype(jnp.float32) + far).astype(jnp.bfloat16))
    return summed[:chunk] + near.astype(jnp.float32) + to_partner(near_other).astype(jnp.float32)


def shift(value, step):
    devices = lax.axis_size("heads")
    return lax.ppermute(value, "heads", [(at, (at + step) % devices) for at in range(devices)])


def on_blocks(value, step):
    devices = lax.axis_size("blk")
    pairs = [(at, at + step) for at in range(devices) if 0 <= at + step < devices]
    return lax.ppermute(value, "blk", pairs)


def from_earlier(value, step=1):
    return tuple(on_blocks(value, distance * step) for distance in (1, 2, 3))


def pack_state(state, log_total):
    high = log_total.astype(jnp.bfloat16)
    rest = log_total - high.astype(jnp.float32)
    middle = rest.astype(jnp.bfloat16)
    low = (rest - middle.astype(jnp.float32)).astype(jnp.bfloat16)
    logs = jnp.concatenate([high, middle, low], axis=0)
    logs = jnp.pad(logs, ((0, 16 - logs.shape[0]), (0, state.shape[1] - logs.shape[1])))
    return jnp.concatenate([state.astype(jnp.bfloat16), logs], axis=0)


def chain(packed, step, heads):
    decays, states = [], []
    for part_in in from_earlier(packed, step):
        state, logs = (part_in[:-16].astype(jnp.float32), part_in[-16:].astype(jnp.float32))
        decays.append(jnp.repeat(jnp.exp(jnp.sum(logs[:3, :heads], axis=0)), MIXER_HEAD_SIZE)[None])
        states.append(state)
    return states[0] + decays[0] * (states[1] + decays[1] * states[2])


def sum_blocks(value):
    for axis in ("dp", "blk"):
        for bit in (1, 2):
            value = value + lax.ppermute(
                value, axis, [(at, at ^ bit) for at in range(lax.axis_size(axis))]
            )
    return value


def on_ring(value, axis, step):
    devices = lax.axis_size(axis)
    return lax.ppermute(value, axis, [(at, (at + step) % devices) for at in range(devices)])


def ring_gather(own, axis):
    half = own.shape[0] // 2
    before = on_ring(own, axis, 1)
    behind = on_ring(own, axis, -1)
    top = on_ring(before[:half], axis, 1)
    bottom = on_ring(behind[half:], axis, -1)
    return [own, before, behind, top, bottom]


def grid_gather(own, first, second):
    return ring_gather(jnp.concatenate(ring_gather(own, first), axis=0), second)


def grid_chunks(first, second):
    turns = jnp.array([0, 3, 1, 2])
    outer = (lax.axis_index(second) + turns)[:, None] % lax.axis_size(second)
    inner = (lax.axis_index(first) + turns)[None, :] % lax.axis_size(first)
    dp, blk = (inner, outer) if first == "dp" else (outer, inner)
    return (dp * lax.axis_size("blk") + blk).reshape(-1).astype(jnp.int32)


def ring_sum(value, axis):
    chunk = value.shape[0] // 4
    half = chunk // 2
    top = lambda k: value[k * chunk : k * chunk + half]
    bottom = lambda k: value[k * chunk + half : (k + 1) * chunk]
    single = lambda part_in: part_in.astype(jnp.float32)
    from_before = on_ring(top(2), axis, 1)
    from_behind = on_ring(bottom(2), axis, -1)
    before_bottom = on_ring(bottom(1), axis, 1)
    behind_top = on_ring(top(3), axis, -1)
    before_top = on_ring((single(top(1)) + single(from_before)).astype(value.dtype), axis, 1)
    behind_bottom = on_ring((single(bottom(3)) + single(from_behind)).astype(value.dtype), axis, -1)
    return jnp.concatenate(
        [
            single(top(0)) + single(before_top) + single(behind_top),
            single(bottom(0)) + single(before_bottom) + single(behind_bottom),
        ],
        axis=0,
    )


def grid_sum(value, first, second):
    return ring_sum(ring_sum(value, first).astype(value.dtype), second)


def grid_turns(first, second):
    turns = jnp.arange(4)
    outer = (lax.axis_index(first) + turns)[:, None] % lax.axis_size(first)
    inner = (lax.axis_index(second) + turns)[None, :] % lax.axis_size(second)
    dp, blk = (outer, inner) if first == "dp" else (inner, outer)
    return (dp * lax.axis_size("blk") + blk).reshape(-1).astype(jnp.int32)


def weight_sum(grads):
    return lax.psum_scatter(grads, ("dp", "blk"), scatter_dimension=0, tiled=True)


def split_columns(value_in, widths):
    pieces, start = [], 0
    for width in widths:
        pieces.append(value_in[:, start : start + width])
        start += width
    return pieces


def inverse_rms(rows_in):
    return lax.rsqrt(jnp.mean(rows_in * rows_in, axis=-1, keepdims=True) + norm_eps)


def norm_back(rows_in, gain_in, cotangent):
    inverse = inverse_rms(rows_in)
    scaled = rows_in * inverse
    weighted = cotangent * gain_in
    return inverse * (weighted - scaled * jnp.mean(weighted * scaled, axis=-1, keepdims=True))


def shards(
    x_in,
    out_grad,
    norm_one,
    w_query,
    w_key,
    w_value,
    output_gate_weight,
    mixer_input_weight,
    w_delta,
    w_bmat,
    w_cmat,
    delta_bias,
    decay_log,
    skip_gain,
    w_attn_out,
    mixer_output_weight,
    norm_two,
    w_gate,
    w_up,
    w_down,
):
    heads_count = lax.axis_size("heads")
    head_rank = lax.axis_index("heads")
    core = head_rank % 2
    block_rank = lax.axis_index("blk")
    rank = block_rank.astype(jnp.int32)[None]
    own_rows = x_in.shape[0]
    span_length = own_rows * heads_count
    half_span = span_length // 2
    span_start = block_rank * span_length
    query_width = w_query.shape[1]
    mixer_width = mixer_input_weight.shape[1]
    heads = mixer_width // MIXER_HEAD_SIZE
    state_size = w_bmat.shape[1]
    hidden_width = w_gate.shape[1]
    rows_of = w_query.shape[0]
    kv_index = head_rank * (query_width // HD) // (QH // KVH)
    kv_width = KVH * HD
    low = jnp.bfloat16
    ranks = chunk_ranks().astype(jnp.int32)
    turns = (head_rank + jnp.arange(heads_count)) % heads_count

    gains = jnp.stack([norm_one, norm_two], axis=1)
    gains = jnp.pad(gains, ((0, 0), (0, LANES - 2)))
    shared = jnp.concatenate([w_key, w_value, w_bmat, w_cmat, gains], axis=1)
    shared = jnp.concatenate([shared] + [shift(shared, -k) for k in range(1, heads_count)], axis=0)
    shared = reorder(turns.astype(jnp.int32), [shared], inverse=True)
    key_part = lax.dynamic_slice_in_dim(shared, kv_index * HD, HD, 1)
    value_part = lax.dynamic_slice_in_dim(shared, kv_width + kv_index * HD, HD, 1)
    state_part = shared[:, 2 * kv_width : 2 * kv_width + 2 * state_size]
    gain_part = shared[:, 2 * kv_width + 2 * state_size :][:, :2]
    misc_part = jnp.concatenate(
        [w_delta, gain_part, jnp.zeros((rows_of, LANES - heads - 2), low)], axis=1
    )
    in_names = ("z", "x", "query", "b", "c", "misc", "key", "value")
    in_widths = (mixer_width, mixer_width, query_width, state_size, state_size, LANES, HD, HD)
    starts = [sum(in_widths[:k]) for k in range(len(in_widths))]
    at = dict(zip(in_names, zip(starts, in_widths)))
    in_first = jnp.concatenate([output_gate_weight, mixer_input_weight, w_query], axis=1)
    in_second = jnp.concatenate([state_part, misc_part, key_part, value_part], axis=1)
    in_own = jnp.concatenate([in_first, in_second], axis=1)
    first_pieces = grid_gather(in_first, "dp", "blk")
    second_pieces = grid_gather(in_second, "blk", "dp")
    out_own = jnp.concatenate(
        [mixer_output_weight.T, w_attn_out.T, w_gate, w_up, w_down.T], axis=1
    )
    out_own, _ = lax.optimization_barrier((out_own, misc_part))
    out_full = lax.all_gather(out_own, ("dp", "blk"), axis=0, tiled=True)
    mixed_width = query_width + mixer_width
    mix_t, gate_full, up_full, down_t = split_columns(out_full, (mixed_width,) + (hidden_width,) * 3)

    x_float = x_in.astype(jnp.float32)
    x_span = gather_rows(x_in)
    positions = (span_start + jnp.arange(span_length)).astype(jnp.float32)
    freqs = rope_base ** (-2.0 * jnp.arange(HD // 2, dtype=jnp.float32) / HD)
    angles = positions[:, None] * freqs[None, :]
    cosine, sine = (jnp.cos(angles), jnp.sin(angles))
    cosine = jnp.concatenate([cosine, cosine], axis=1)
    sine = jnp.concatenate([-sine, sine], axis=1)
    in_full = assemble(
        jnp.stack([grid_chunks("dp", "blk"), grid_chunks("blk", "dp")]),
        [first_pieces, second_pieces],
    )
    in_full, x_span, cosine, sine = lax.optimization_barrier((in_full, x_span, cosine, sine))
    normed_ordered, queries, keys_values, gain_rows = enter(
        ranks, jnp.full((1,), heads, jnp.int32), x_span, in_full, at, cosine, sine
    )
    gain_one, gain_two = (gain_rows[0:1], gain_rows[1:2])
    out_later, keys_values = lax.optimization_barrier((out_grad, keys_values))
    ffn_grad = gather_rows(out_later)
    mine = lax.dynamic_slice_in_dim(keys_values, core * half_span, half_span, 0)
    pieces = []
    for piece in from_earlier(mine):
        pieces += [piece, to_partner(piece)]
    gate_raw = simple_product(normed_ordered, in_full[:, :mixer_width])
    normed_later, pieces[0] = lax.optimization_barrier((normed_ordered, pieces[0]))
    x_raw = simple_product(normed_later, in_full[:, mixer_width : 2 * mixer_width])
    state_raw = simple_product(normed_later, in_full[:, at["b"][0] : at["key"][0]])
    raw = {
        "z": (gate_raw, 0, mixer_width),
        "x": (x_raw, 0, mixer_width),
        "b": (state_raw, 0, state_size),
        "c": (state_raw, state_size, state_size),
        "misc": (state_raw, 2 * state_size, LANES),
    }

    pad_lanes = lambda vector: jnp.pad(vector, (0, LANES - heads))[None]
    bias, rate = (pad_lanes(delta_bias), pad_lanes(jnp.exp(decay_log)))
    skip = jnp.repeat(skip_gain, MIXER_HEAD_SIZE)[None]
    delta, cumulative, delta_row, cum_row, local_state, local_log = scan_first(raw, bias, rate)
    entry_state = chain(pack_state(local_state, local_log), 1, heads)
    attended, attn_part, log_totals = attend(rank, queries, keys_values, pieces)
    entry_state, attn_part = lax.optimization_barrier((entry_state, attn_part))
    scanned, gated, states = scan(raw, delta, cumulative, delta_row, cum_row, entry_state, skip)
    mixers = reorder(ranks, [gated, attn_part])
    mixers, ffn_grad = lax.optimization_barrier((mixers, ffn_grad))
    middle = x_float + scatter_rows(lambda rows: dot_last(mixers[rows], mix_t), half_span)
    middle_scaled = middle * inverse_rms(middle)
    normed_two = gather_rows((middle_scaled * gain_two).astype(low))
    ffn_gate = simple_product(normed_two, gate_full)
    ffn_up = simple_product(normed_two, up_full)
    ffn_sig = jax.nn.sigmoid(ffn_gate)
    hidden = (ffn_gate * ffn_sig * ffn_up).astype(low)

    d_hidden = simple_product(ffn_grad, down_t)
    d_ffn_gate = (d_hidden * ffn_up * (ffn_sig * (1.0 + ffn_gate * (1.0 - ffn_sig)))).astype(low)
    d_ffn_up = (d_hidden * (ffn_gate * ffn_sig)).astype(low)
    d_normed_two = scatter_rows(
        lambda rows: dot_last(d_ffn_gate[rows], gate_full) + dot_last(d_ffn_up[rows], up_full),
        half_span,
    )
    plain = jnp.arange(normed_two.shape[1] // LANES, dtype=jnp.int32)
    ffn_grads = None
    for place, (left, right) in enumerate(
        ((normed_two, d_ffn_gate), (normed_two, d_ffn_up), (ffn_grad, hidden))
    ):
        ffn_grads = weight_part(
            plain, left, [(right, 0, hidden_width)], place, 3 * hidden_width, ffn_grads
        )
    ffn_sums = weight_sum(ffn_grads).astype(jnp.float32)
    grad_gate, grad_up, grad_down_t = split_columns(ffn_sums, (hidden_width,) * 3)
    grad_two_part = jnp.sum(grad_gate * w_gate + grad_up * w_up, axis=1, keepdims=True)
    gain_own = gain_part.astype(jnp.float32)
    grad_two_part = grad_two_part / gain_own[:, 1:2]
    d_middle = out_grad.astype(jnp.float32) + norm_back(middle, gain_two, d_normed_two)
    mix_grad = gather_rows(d_middle.astype(low))
    mix_grad, hidden = lax.optimization_barrier((mix_grad, hidden))
    d_mixers = reorder(ranks, [simple_product(mix_grad, mix_t).astype(low)], inverse=True)
    d_scanned, d_gate_z, d_entry = scan_back_first(d_mixers, raw, scanned, cumulative)
    d_entry, d_mixers = lax.optimization_barrier((pack_state(d_entry, local_log), d_mixers))
    after_state = chain(d_entry, -1, heads)
    d_query, d_own, d_far = attend_back(
        rank, queries, keys_values, pieces, attended, log_totals, d_mixers, cosine, sine
    )
    after_state, d_query = lax.optimization_barrier((after_state, d_query))
    d_ssm_in, d_bmat, d_cmat, d_pre, sums = scan_back(
        raw, d_scanned, bias, rate, delta, cumulative, cum_row, states, after_state, skip
    )
    first_turns, second_turns = (grid_turns("dp", "blk"), grid_turns("blk", "dp"))
    first_width = 3 * mixer_width
    first_grads = weight_part(
        first_turns, mix_grad, [(mixers, 0, mixer_width)], 0, first_width
    )
    first_grads = weight_part(
        first_turns, normed_ordered, [(d_gate_z, 0, mixer_width)], 1, first_width, first_grads
    )
    first_grads = weight_part(
        first_turns, normed_ordered, [(d_ssm_in, 0, mixer_width)], 2, first_width, first_grads
    )
    first_sums = grid_sum(first_grads, "dp", "blk")
    far_half = d_far.shape[0] // 2
    d_mine = lax.dynamic_slice_in_dim(d_own, core * half_span, half_span, 0)
    d_theirs = lax.dynamic_slice_in_dim(d_own, (1 - core) * half_span, half_span, 0)
    d_mine = d_mine + to_partner(d_theirs.astype(low)).astype(jnp.float32)
    d_far = d_far[:far_half].astype(jnp.float32) + to_partner(d_far[far_half:]).astype(jnp.float32)
    d_one, d_two, d_three = (
        d_far[k * half_span : (k + 1) * half_span] for k in range(d_far.shape[0] // half_span)
    )
    d_one = d_one + on_blocks(d_two.astype(low), -1).astype(jnp.float32)
    d_mine = d_mine + on_blocks(d_one.astype(low), -1).astype(jnp.float32)
    d_mine = d_mine + on_blocks(d_three.astype(low), -3).astype(jnp.float32)
    half_cos = lax.dynamic_slice_in_dim(cosine, core * half_span, half_span, 0)
    half_sin = lax.dynamic_slice_in_dim(sine, core * half_span, half_span, 0)
    d_key = d_mine[:, :HD]
    d_key = d_key * half_cos - jnp.roll(d_key, HD // 2, axis=1) * half_sin
    d_mine = jnp.concatenate([d_key, d_mine[:, HD:]], axis=1).astype(low)
    d_keys_values = lax.dynamic_update_slice_in_dim(
        jnp.zeros((span_length, 2 * HD), low), d_mine, core * half_span, 0
    )

    rest_width = 2 * state_size + LANES + 2 * HD + query_width
    second_width = rest_width + query_width
    second_grads = weight_part(
        second_turns,
        mix_grad,
        [(mixers, mixer_width, query_width)],
        rest_width // query_width,
        second_width,
    )
    second_grads = weight_part(
        second_turns,
        normed_ordered,
        [
            (d_bmat, 0, state_size),
            (d_cmat, 0, state_size),
            (d_pre, 0, LANES),
            (d_keys_values, 0, 2 * HD),
            (d_query, 0, query_width),
        ],
        0,
        second_width,
        second_grads,
    )
    second_sums = grid_sum(second_grads, "blk", "dp")
    ffn_out = scatter_rows(lambda rows: dot_last(hidden[rows], down_t), half_span)
    activations = (middle + ffn_out).astype(low)
    d_pre, activations = lax.optimization_barrier((d_pre, activations))
    d_projected = reorder(
        ranks, [d_gate_z, d_ssm_in, d_query, d_bmat, d_cmat, d_pre, d_keys_values]
    )
    d_normed = scatter_rows(lambda rows: dot_last(d_projected[rows], in_full), half_span)
    input_grad = d_middle + norm_back(x_float, gain_one, d_normed)
    sums_at = {
        "ssm_out": (0, 0, mixer_width),
        "z": (0, mixer_width, mixer_width),
        "x": (0, 2 * mixer_width, mixer_width),
        "b": (1, 0, state_size),
        "c": (1, state_size, state_size),
        "misc": (1, 2 * state_size, LANES),
        "key": (1, 2 * state_size + LANES, HD),
        "value": (1, 2 * state_size + LANES + HD, HD),
        "query": (1, 2 * state_size + LANES + 2 * HD, query_width),
        "attn_out": (1, rest_width, query_width),
    }
    extra = jnp.concatenate([gain_own[:, 0:1], grad_two_part], axis=1)
    extra = jnp.pad(extra, ((0, 0), (0, LANES - 2)))
    grad_ssm_out, grad_attn_out, grad_gatez, grad_ssmx, grad_query, misc_sums, shared_parts = finish(
        turns.astype(jnp.int32),
        kv_index.astype(jnp.int32)[None],
        first_sums,
        second_sums,
        in_own,
        extra,
        at,
        sums_at,
    )
    shared_sums = shared_parts[: rows_of // heads_count].astype(jnp.float32)
    for k in range(1, heads_count):
        here = slice(k * rows_of // heads_count, (k + 1) * rows_of // heads_count)
        shared_sums = shared_sums + shift(shared_parts[here], k).astype(jnp.float32)
    grad_key, grad_value, grad_bmat, grad_cmat, gain_sums = split_columns(
        shared_sums, (kv_width, kv_width, state_size, state_size, LANES)
    )
    small_sums = sum_blocks(sums)[:, :heads]
    return (
        activations,
        input_grad,
        gain_sums[:, 0],
        grad_query,
        grad_key,
        grad_value,
        grad_gatez,
        grad_ssmx,
        misc_sums[:, :heads],
        grad_bmat,
        grad_cmat,
        small_sums[0],
        small_sums[1],
        small_sums[2],
        grad_attn_out,
        grad_ssm_out,
        gain_sums[:, 1],
        grad_gate,
        grad_up,
        grad_down_t.T,
    )


def solution(mesh):
    placed = (
        P(("dp", "blk", "heads"), None),
        P(("dp", "blk", "heads"), None),
        P(("dp", "blk", "heads")),
        P(("dp", "blk"), "heads"),
        P(("dp", "blk", "heads"), None),
        P(("dp", "blk", "heads"), None),
        P(("dp", "blk"), "heads"),
        P(("dp", "blk"), "heads"),
        P(("dp", "blk"), "heads"),
        P(("dp", "blk", "heads"), None),
        P(("dp", "blk", "heads"), None),
        P("heads"),
        P("heads"),
        P("heads"),
        P("heads", ("dp", "blk")),
        P("heads", ("dp", "blk")),
        P(("dp", "blk", "heads")),
        P(("dp", "blk"), "heads"),
        P(("dp", "blk"), "heads"),
        P("heads", ("dp", "blk")),
    )
    return jax.shard_map(
        shards,
        mesh=mesh,
        in_specs=placed,
        out_specs=(
            P(("dp", "blk", "heads"), None),
            P(("dp", "blk", "heads"), None),
            P(("dp", "blk", "heads")),
            P(("dp", "blk"), "heads"),
            P(("dp", "blk", "heads"), None),
            P(("dp", "blk", "heads"), None),
            P(("dp", "blk"), "heads"),
            P(("dp", "blk"), "heads"),
            P(("dp", "blk"), "heads"),
            P(("dp", "blk", "heads"), None),
            P(("dp", "blk", "heads"), None),
            P("heads"),
            P("heads"),
            P("heads"),
            P("heads", ("dp", "blk")),
            P("heads", ("dp", "blk")),
            P(("dp", "blk", "heads")),
            P(("dp", "blk"), "heads"),
            P(("dp", "blk"), "heads"),
            P("heads", ("dp", "blk")),
        ),
        check_vma=False,
    )
```

```python
import functools

import jax
import jax.numpy as jnp
from jax import lax
from jax.experimental import pallas as pl
from jax.experimental.pallas import tpu as pltpu
from jax.sharding import PartitionSpec as P

QH = 8
KVH = 2
HD = 128
MIXER_HEAD_SIZE = 64
BLOCK = 256
LANES = 128
LOG2_E = 1.4426950408889634


HIGH_PRECISION = lax.Precision.HIGHEST
norm_eps = 1e-05
rope_base = 100000000000.0


def simple_product(left_side, right_side):
    return jnp.dot(left_side, right_side, preferred_element_type=jnp.float32)


def dot_last(left_side, right_side):
    return lax.dot_general(
        left_side, right_side, (((1,), (1,)), ((), ())), preferred_element_type=jnp.float32
    )


def dot_first(left_side, right_side):
    return lax.dot_general(
        left_side, right_side, (((0,), (0,)), ((), ())), preferred_element_type=jnp.float32
    )


def compiler_params():
    return pltpu.CompilerParams(vmem_limit_bytes=50 * 1024 * 1024)


def in_vmem(count):
    return [pl.BlockSpec(memory_space=pltpu.VMEM)] * count


def mul(left_side, right_side):
    return jnp.dot(left_side, right_side, preferred_element_type=jnp.float32)


def tile_scores(key_rows, query_rows, head_size):
    return dot_last(key_rows, query_rows) * (head_size**-0.5 * LOG2_E)


def causal(scores):
    key_at = lax.broadcasted_iota(jnp.int32, scores.shape, 0)
    query_at = lax.broadcasted_iota(jnp.int32, scores.shape, 1)
    return jnp.where(key_at <= query_at, scores, -1e30)


def enter_kernel(
    ranks_ref,
    heads_ref,
    x_ref,
    misc_ref,
    key_ref,
    value_ref,
    w_query_ref,
    cos_ref,
    sin_ref,
    ordered_ref,
    query_ref,
    kv_ref,
    gains_ref,
):
    head_size = query_ref.shape[1]

    @pl.when(pl.program_id(0) == 0)
    def _():
        lane = lax.broadcasted_iota(jnp.int32, misc_ref.shape, 1)
        for k in range(2):
            column = jnp.where(lane == heads_ref[0] + k, misc_ref[...].astype(jnp.float32), 0.0)
            gains_ref[k : k + 1, :] = jnp.sum(column.T, axis=0, keepdims=True)

    cosine, sine = (cos_ref[...], sin_ref[...])

    def turn(value):
        return (value * cosine + pltpu.roll(value, head_size // 2, 1) * sine).astype(jnp.bfloat16)

    rows = x_ref[...].astype(jnp.float32)
    normed = (rows * inverse_rms(rows) * gains_ref[0:1, :]).astype(jnp.bfloat16)
    ordered_ref[...] = normed
    kv_ref[:, :head_size] = turn(mul(normed, key_ref[...]))
    kv_ref[:, head_size:] = mul(normed, value_ref[...]).astype(jnp.bfloat16)
    query_ref[...] = turn(mul(normed, w_query_ref[...]))


def enter(ranks, heads, x_span, in_full, at, cosine, sine):
    count = ranks.shape[0]
    rows, width = x_span.shape
    head_size = cosine.shape[1]
    here = lambda columns: pl.BlockSpec((rows // count, columns), lambda k, r, h: (k, 0))
    there = lambda columns: pl.BlockSpec((rows // count, columns), lambda k, r, h: (r[k], 0))
    weight = lambda name: pl.BlockSpec(
        (width, at[name][1]), lambda k, r, h: (0, at[name][0] // at[name][1])
    )
    return pl.pallas_call(
        enter_kernel,
        grid_spec=pltpu.PrefetchScalarGridSpec(
            num_scalar_prefetch=2,
            grid=(count,),
            in_specs=[
                here(width),
                weight("misc"),
                weight("key"),
                weight("value"),
                weight("query"),
                there(head_size),
                there(head_size),
            ],
            out_specs=(
                there(width),
                there(head_size),
                there(2 * head_size),
                pl.BlockSpec((8, width), lambda k, r, h: (0, 0)),
            ),
        ),
        out_shape=(
            jax.ShapeDtypeStruct((rows, width), jnp.bfloat16),
            jax.ShapeDtypeStruct((rows, head_size), jnp.bfloat16),
            jax.ShapeDtypeStruct((rows, 2 * head_size), jnp.bfloat16),
            jax.ShapeDtypeStruct((8, width), jnp.float32),
        ),
        compiler_params=compiler_params(),
        cost_estimate=pl.CostEstimate(
            flops=2_000_000_000, bytes_accessed=16_000_000, transcendentals=0
        ),
        name="enter",
    )(ranks, heads, x_span, in_full, in_full, in_full, in_full, cosine, sine)


def weight_grads_kernel(ranks_ref, *refs, counts, split, after):
    outs = refs[-len(split) :]
    used = 2 * len(counts)
    products = []
    for k, count in enumerate(counts):
        left = jnp.concatenate([refs[2 * k][...].T, refs[2 * k + 1][...].T], axis=0)
        products += [mul(left, ref[...]).astype(jnp.bfloat16) for ref in refs[used : used + count]]
        used += count
    start = 0
    for out_ref, count in zip(outs, split):
        at = 0
        for product in products[start : start + count]:
            out_ref[:, at : at + product.shape[1]] = product
            at += product.shape[1]
        start += count


def weight_grads(ranks, groups, split, after=()):
    lefts = [left for left, _ in groups]
    rights = [right for _, group in groups for right in group]
    depth, rows = lefts[0].shape
    widths, start = [], 0
    for count in split:
        widths.append(sum(right.shape[1] for right in rights[start : start + count]))
        start += count
    side = lambda offset: pl.BlockSpec((depth, LANES), lambda k, r: (0, r[2 * k + offset]))
    return pl.pallas_call(
        functools.partial(
            weight_grads_kernel,
            counts=tuple(len(group) for _, group in groups),
            split=tuple(split),
            after=len(after),
        ),
        grid_spec=pltpu.PrefetchScalarGridSpec(
            num_scalar_prefetch=1,
            grid=(rows // (2 * LANES),),
            in_specs=[side(offset) for _ in lefts for offset in range(2)]
            + [pl.BlockSpec(right.shape, lambda k, r: (0, 0)) for right in rights]
            + [pl.BlockSpec(memory_space=pl.ANY)] * len(after),
            out_specs=[pl.BlockSpec((2 * LANES, width), lambda k, r: (k, 0)) for width in widths],
        ),
        out_shape=[jax.ShapeDtypeStruct((rows, width), jnp.bfloat16) for width in widths],
        compiler_params=compiler_params(),
        cost_estimate=pl.CostEstimate(
            flops=2 * rows * depth * sum(widths),
            bytes_accessed=2 * (depth * (2 * rows + sum(widths)) + rows * sum(widths)),
            transcendentals=0,
        ),
        name="weight_grads",
    )(ranks, *[left for left in lefts for _ in range(2)], *rights, *after)


def pack_kernel(ssm_ref, attn_ref, gate_ref, up_ref, down_ref, after_ref, out_ref):
    start = 0
    pieces = (ssm_ref[...].T, attn_ref[...].T, gate_ref[...], up_ref[...], down_ref[...].T)
    for piece in pieces:
        out_ref[:, start : start + piece.shape[1]] = piece
        start += piece.shape[1]


def pack(ssm_out, attn_out, gate, up, down, after):
    width = ssm_out.shape[0] + attn_out.shape[0] + gate.shape[1] + up.shape[1] + down.shape[0]
    return pl.pallas_call(
        pack_kernel,
        out_shape=jax.ShapeDtypeStruct((gate.shape[0], width), jnp.bfloat16),
        in_specs=in_vmem(5) + [pl.BlockSpec(memory_space=pl.ANY)],
        out_specs=pl.BlockSpec(memory_space=pltpu.VMEM),
        compiler_params=compiler_params(),
        name="pack",
    )(ssm_out, attn_out, gate, up, down, after)


def assemble_kernel(chunks_ref, *refs, groups):
    out_ref = refs[-1]
    for group, start in enumerate(groups):
        at = 0
        for ref in refs[5 * group : 5 * group + 5]:
            for k in range(ref.shape[0] // LANES):
                to = pl.ds(pl.multiple_of(chunks_ref[group, at] * LANES, LANES), LANES)
                out_ref[to, start : start + ref.shape[1]] = ref[k * LANES : (k + 1) * LANES, :]
                at += 1


def assemble(chunks, groups):
    widths = [pieces[0].shape[1] for pieces in groups]
    starts = tuple(sum(widths[:k]) for k in range(len(widths)))
    rows = sum(piece.shape[0] for piece in groups[0])
    pieces = [piece for group in groups for piece in group]
    return pl.pallas_call(
        functools.partial(assemble_kernel, groups=starts),
        out_shape=jax.ShapeDtypeStruct((rows, sum(widths)), jnp.bfloat16),
        in_specs=[pl.BlockSpec(memory_space=pltpu.SMEM)] + in_vmem(len(pieces)),
        out_specs=pl.BlockSpec(memory_space=pltpu.VMEM),
        compiler_params=compiler_params(),
        cost_estimate=pl.CostEstimate(
            flops=0, bytes_accessed=4 * rows * sum(widths), transcendentals=0
        ),
        name="assemble",
    )(chunks, *pieces)


def finish_kernel(
    ranks_ref,
    kv_ref,
    first_ref,
    second_ref,
    third_ref,
    weight_ref,
    extra_ref,
    ssm_out_ref,
    attn_out_ref,
    gate_ref,
    ssm_ref,
    query_ref,
    misc_ref,
    shared_ref,
    whole_ref,
    *,
    at,
    sums_at,
):
    def of(name):
        group, start, size = sums_at[name]
        return (first_ref, second_ref, third_ref)[group][:, start : start + size].astype(jnp.float32)

    ssm_out_ref[...] = of("ssm_out").T
    attn_out_ref[...] = of("attn_out").T
    gate_ref[...] = of("z")
    ssm_ref[...] = of("x")
    query_ref[...] = of("query")
    misc_ref[...] = of("misc")
    total = 0.0
    for name, (start, size) in at.items():
        product = of(name) * weight_ref[:, start : start + size].astype(jnp.float32)
        total += jnp.sum(product, axis=1, keepdims=True)
    total = total / extra_ref[:, 0:1]
    lane = lax.broadcasted_iota(jnp.int32, misc_ref.shape, 1)
    gains = jnp.where(lane == 0, total, jnp.where(lane == 1, extra_ref[:, 1:2], 0.0))
    zero = jnp.zeros_like(gains)
    first = kv_ref[0] == 0
    key, value = (of("key"), of("value"))
    pieces = (
        jnp.where(first, key, zero),
        jnp.where(first, zero, key),
        jnp.where(first, value, zero),
        jnp.where(first, zero, value),
        of("b"),
        of("c"),
        gains,
    )
    start = 0
    for piece in pieces:
        whole_ref[:, start : start + piece.shape[1]] = piece
        start += piece.shape[1]
    count = ranks_ref.shape[0]
    size = shared_ref.shape[0] // count
    for k in range(count):
        rows = pl.ds(pl.multiple_of(ranks_ref[k] * size, size), size)
        shared_ref[k * size : (k + 1) * size, :] = whole_ref[rows, :].astype(jnp.bfloat16)


def finish(ranks, kv_index, sums, weights, extra, at, sums_at):
    rows = weights.shape[0]
    shape = lambda *sizes: jax.ShapeDtypeStruct(sizes, jnp.float32)
    width = lambda name: sums_at[name][2]
    shared = 2 * (width("key") + width("value")) + width("b") + width("c") + LANES
    return pl.pallas_call(
        functools.partial(finish_kernel, at=at, sums_at=sums_at),
        out_shape=(
            shape(width("ssm_out"), rows),
            shape(width("attn_out"), rows),
            shape(rows, width("z")),
            shape(rows, width("x")),
            shape(rows, width("query")),
            shape(rows, width("misc")),
            jax.ShapeDtypeStruct((rows, shared), jnp.bfloat16),
        ),
        in_specs=[pl.BlockSpec(memory_space=pltpu.SMEM)] * 2 + in_vmem(5),
        out_specs=tuple(in_vmem(7)),
        scratch_shapes=[pltpu.VMEM((rows, shared), jnp.float32)],
        compiler_params=compiler_params(),
        name="finish",
    )(ranks, kv_index, *sums, weights, extra)


def attend_kernel(rank_ref, query_ref, own_ref, *refs):
    pieces, (out_ref, low_ref, log_ref) = (refs[:-3], refs[-3:])
    span_length, head_size = query_ref.shape
    tile = own_ref.shape[0] // 2
    for block in range(span_length // tile):
        here = slice(block * tile, (block + 1) * tile)
        query_rows = query_ref[here, :]

        def step(kv_rows, carried, masked=False):
            top, total, summed = carried
            scores = tile_scores(kv_rows[:, :head_size], query_rows, head_size)
            if masked:
                scores = causal(scores)
            new_top = jnp.maximum(top, jnp.max(scores, axis=0, keepdims=True))
            probs = jnp.exp2(scores - new_top)
            scale = jnp.exp2(top - new_top)
            total = total * scale + jnp.sum(probs, axis=0, keepdims=True)
            summed = summed * scale + dot_first(kv_rows[:, head_size:], probs.astype(jnp.bfloat16))
            return (new_top, total, summed)

        carried = (
            jnp.full((1, tile), -1e30, jnp.float32),
            jnp.zeros((1, tile), jnp.float32),
            jnp.zeros((head_size, tile), jnp.float32),
        )
        carried = step(own_ref[here, :], carried, True)
        for earlier in range(block):
            carried = step(own_ref[earlier * tile : (earlier + 1) * tile, :], carried)
        for distance in range(1, 1 + len(pieces) // 2):
            pair = pieces[2 * distance - 2 : 2 * distance]

            def both(_, carried, pair=pair):
                return step(pair[1][...], step(pair[0][...], carried))

            valid = (rank_ref[0] >= distance).astype(jnp.int32)
            carried = lax.fori_loop(0, valid, both, carried)
        top, total, summed = carried
        result = summed / total
        out_ref[:, here] = result
        low_ref[here, :] = result.T.astype(jnp.bfloat16)
        log_ref[:, here] = top + jnp.log2(total)


def attend(rank, queries, own, pieces):
    span_length, head_size = queries.shape
    return pl.pallas_call(
        attend_kernel,
        out_shape=(
            jax.ShapeDtypeStruct((head_size, span_length), jnp.float32),
            jax.ShapeDtypeStruct((span_length, head_size), jnp.bfloat16),
            jax.ShapeDtypeStruct((1, span_length), jnp.float32),
        ),
        in_specs=[pl.BlockSpec(memory_space=pltpu.SMEM)] + in_vmem(2 + len(pieces)),
        out_specs=tuple(in_vmem(3)),
        compiler_params=compiler_params(),
        cost_estimate=pl.CostEstimate(
            flops=10_000_000_000, bytes_accessed=4_000_000, transcendentals=4_000_000
        ),
        name="attend",
    )(rank, queries, own, *pieces)


def attend_back_kernel(rank_ref, query_ref, own_ref, *refs):
    pieces, refs = (refs[:-10], refs[-10:])
    out_ref, log_ref, grad_ref, cos_ref, sin_ref, _, d_query_ref, d_own_ref, d_far_ref, sums_ref = refs
    span_length, head_size = query_ref.shape
    tile = own_ref.shape[0] // 2
    score_scale = head_size**-0.5
    sums_ref[...] = jnp.zeros_like(sums_ref)
    for block in range(span_length // tile):
        here = slice(block * tile, (block + 1) * tile)
        query_rows = query_ref[here, :]
        grad_rows = grad_ref[here, grad_ref.shape[1] - head_size :]
        log_total = log_ref[:, here]
        delta_row = jnp.sum(
            grad_rows.astype(jnp.float32).T * out_ref[:, here], axis=0, keepdims=True
        )

        def step(kv_ref, start, at, d_query, masked=False):
            key_rows = kv_ref[start : start + tile, :head_size]
            scores = tile_scores(key_rows, query_rows, head_size)
            if masked:
                scores = causal(scores)
            probs = jnp.exp2(scores - log_total)
            d_probs = dot_last(kv_ref[start : start + tile, head_size:], grad_rows)
            d_scores = (probs * (d_probs - delta_row)).astype(jnp.bfloat16)
            rows = slice(at * tile, (at + 1) * tile)
            sums_ref[rows, head_size:] += mul(probs.astype(jnp.bfloat16), grad_rows)
            sums_ref[rows, :head_size] += mul(d_scores, query_rows)
            return d_query + dot_first(key_rows, d_scores)

        d_query = jnp.zeros((head_size, tile), jnp.float32)
        d_query = step(own_ref, block * tile, block, d_query, True)
        for earlier in range(block):
            d_query = step(own_ref, earlier * tile, earlier, d_query)
        for distance in range(1, 1 + len(pieces) // 2):

            def both(_, d_query, distance=distance):
                for k in (2 * distance - 2, 2 * distance - 1):
                    d_query = step(pieces[k], 0, 2 + k, d_query)
                return d_query

            valid = (rank_ref[0] >= distance).astype(jnp.int32)
            d_query = lax.fori_loop(0, valid, both, d_query)
        turned = d_query.T * score_scale
        d_query_ref[here, :] = (
            turned * cos_ref[here, :] - pltpu.roll(turned, head_size // 2, 1) * sin_ref[here, :]
        ).astype(jnp.bfloat16)
    lane = lax.broadcasted_iota(jnp.int32, (tile, 2 * head_size), 1)
    scale = jnp.where(lane < head_size, score_scale, 1.0)
    for at in range(2):
        rows = slice(at * tile, (at + 1) * tile)
        d_own_ref[rows, :] = sums_ref[rows, :] * scale
    for k in range(len(pieces)):
        rows = slice((2 + k) * tile, (3 + k) * tile)
        into = (k % 2) * (len(pieces) // 2) + k // 2
        d_far_ref[into * tile : (into + 1) * tile, :] = (sums_ref[rows, :] * scale).astype(
            jnp.bfloat16
        )


def attend_back(rank, queries, own, pieces, attended, log_totals, d_attn, cosine, sine, after):
    tile = own.shape[0] // 2
    return pl.pallas_call(
        attend_back_kernel,
        out_shape=(
            jax.ShapeDtypeStruct(queries.shape, jnp.bfloat16),
            jax.ShapeDtypeStruct(own.shape, jnp.float32),
            jax.ShapeDtypeStruct((len(pieces) * tile, own.shape[1]), jnp.bfloat16),
        ),
        in_specs=[pl.BlockSpec(memory_space=pltpu.SMEM)]
        + in_vmem(7 + len(pieces))
        + [pl.BlockSpec(memory_space=pl.ANY)],
        out_specs=tuple(in_vmem(3)),
        scratch_shapes=[pltpu.VMEM(((2 + len(pieces)) * tile, own.shape[1]), jnp.float32)],
        compiler_params=compiler_params(),
        cost_estimate=pl.CostEstimate(
            flops=25_000_000_000, bytes_accessed=8_000_000, transcendentals=4_000_000
        ),
        name="attend_back",
    )(rank, queries, own, *pieces, attended, log_totals, d_attn, cosine, sine, after)


def reorder_kernel(ranks_ref, *refs, count):
    out_ref = refs[-1]
    start = 0
    for ref in refs[:count]:
        out_ref[:, start : start + ref.shape[1]] = ref[...].astype(out_ref.dtype)
        start += ref.shape[1]


def reorder(ranks, pieces, inverse=False, after=()):
    count = ranks.shape[0]
    rows = pieces[0].shape[0] // count
    width = sum(piece.shape[1] for piece in pieces)
    there = lambda k, ranks: (ranks[k], 0)
    here = lambda k, ranks: (k, 0)
    return pl.pallas_call(
        functools.partial(reorder_kernel, count=len(pieces)),
        grid_spec=pltpu.PrefetchScalarGridSpec(
            num_scalar_prefetch=1,
            grid=(count,),
            in_specs=[
                pl.BlockSpec((rows, piece.shape[1]), here if inverse else there)
                for piece in pieces
            ]
            + [pl.BlockSpec(memory_space=pl.ANY)] * len(after),
            out_specs=pl.BlockSpec((rows, width), there if inverse else here),
        ),
        out_shape=jax.ShapeDtypeStruct((count * rows, width), jnp.bfloat16),
        compiler_params=compiler_params(),
        cost_estimate=pl.CostEstimate(
            flops=0, bytes_accessed=4 * count * rows * width, transcendentals=0
        ),
        name="reorder",
    )(ranks, *pieces, *after)


def lower_ones(size, dtype=jnp.float32):
    row = lax.broadcasted_iota(jnp.int32, (size, size), 0)
    column = lax.broadcasted_iota(jnp.int32, (size, size), 1)
    return (row >= column).astype(dtype)


def precise(left_side, right_side):
    return jnp.dot(
        left_side, right_side, precision=HIGH_PRECISION, preferred_element_type=jnp.float32
    )


def spread_heads(columns, head_size, width):
    lane = lax.broadcasted_iota(jnp.int32, (columns.shape[0], 2 * head_size), 1)
    pairs = [
        jnp.where(lane < head_size, columns[:, k : k + 1], columns[:, k + 1 : k + 2])
        for k in range(0, width // head_size, 2)
    ]
    return jnp.concatenate(pairs, axis=1)


def head_ones(width, head_size, lanes, dtype):
    at = lax.broadcasted_iota(jnp.int32, (width, lanes), 0)
    lane = lax.broadcasted_iota(jnp.int32, (width, lanes), 1)
    low = lane * head_size
    return ((at >= low) & (at < low + head_size)).astype(dtype)


def scan_first_kernel(
    pre_ref, bias_ref, rate_ref, x_ref, b_ref, delta_ref, cum_ref, delta_row_ref, cum_row_ref, state_ref, log_ref
):
    @pl.when(pl.program_id(0) == 0)
    def _():
        state_ref[...] = jnp.zeros_like(state_ref)
        log_ref[...] = jnp.zeros_like(log_ref)

    delta = jax.nn.softplus(pre_ref[...] + bias_ref[...])
    log_step = -delta * rate_ref[...]
    cumulative = precise(lower_ones(log_step.shape[0]), log_step)
    delta_ref[...] = delta
    cum_ref[...] = cumulative
    delta_row_ref[...] = delta.T[:8]
    cum_row_ref[...] = cumulative.T[:8]
    ending = cumulative[-1:, :]
    weight = jnp.exp(ending - cumulative + log_ref[...]) * delta
    width = x_ref.shape[1]
    x_low = x_ref[...].astype(jnp.bfloat16).astype(jnp.float32)
    weighted = (x_low * spread_heads(weight, MIXER_HEAD_SIZE, width)).astype(jnp.bfloat16)
    state_ref[...] += dot_first(b_ref[...].astype(jnp.bfloat16), weighted)
    log_ref[...] += ending


def part(projected, start, width, order=lambda c: c):
    at = start // width
    return (projected, pl.BlockSpec((BLOCK, width), lambda c: (order(c), at)))


def run_scan(kernel, chunks, operands, out_shape, out_specs, flops, name, scratch=(), after=()):
    count = len(operands)
    operands = operands + [(array, pl.BlockSpec(memory_space=pl.ANY)) for array in after]

    def call(*refs):
        kernel(*refs[:count], *refs[count + len(after) :])

    return pl.pallas_call(
        call,
        grid=(chunks,),
        out_shape=out_shape,
        in_specs=[spec for _, spec in operands],
        out_specs=out_specs,
        scratch_shapes=list(scratch),
        compiler_params=compiler_params(),
        cost_estimate=pl.CostEstimate(
            flops=flops, bytes_accessed=8_000_000, transcendentals=1_000_000
        ),
        name=name,
    )(*[array for array, _ in operands])


def whole(array):
    return (array, pl.BlockSpec(array.shape, lambda c: (0,) * array.ndim))


def scan_first(at, bias, rate):
    rows, lanes = (at["x"][0].shape[0], bias.shape[1])
    chunks = rows // BLOCK
    back = lambda c: chunks - 1 - c
    width, state_size = (at["x"][2], at["b"][2])
    by_chunk = pl.BlockSpec((BLOCK, lanes), lambda c: (back(c), 0))
    across = pl.BlockSpec((8, BLOCK), lambda c: (0, back(c)))
    shape = lambda *sizes: jax.ShapeDtypeStruct(sizes, jnp.float32)
    return run_scan(
        scan_first_kernel,
        chunks,
        [
            part(*at["misc"], back),
            whole(bias),
            whole(rate),
            part(*at["x"], back),
            part(*at["b"], back),
        ],
        (
            shape(rows, lanes),
            shape(rows, lanes),
            shape(8, rows),
            shape(8, rows),
            shape(state_size, width),
            shape(1, lanes),
        ),
        (
            by_chunk,
            by_chunk,
            across,
            across,
            pl.BlockSpec((state_size, width), lambda c: (0, 0)),
            pl.BlockSpec((1, lanes), lambda c: (0, 0)),
        ),
        1_000_000_000,
        "scan_first",
    )


def scan_kernel(
    x_ref,
    z_ref,
    b_ref,
    c_ref,
    delta_ref,
    cum_ref,
    delta_row_ref,
    cum_row_ref,
    entry_ref,
    skip_ref,
    scanned_ref,
    gated_ref,
    states_ref,
    state_ref,
):
    @pl.when(pl.program_id(0) == 0)
    def _():
        state_ref[...] = entry_ref[...]

    head_size = MIXER_HEAD_SIZE
    pair = 2 * head_size
    size, width = x_ref.shape
    state = state_ref[...]
    states_ref[0] = state
    delta, cumulative = (delta_ref[...], cum_ref[...])
    delta_row, cum_row = (delta_row_ref[...], cum_row_ref[...])
    bmat, cmat = (b_ref[...].astype(jnp.bfloat16), c_ref[...].astype(jnp.bfloat16))
    x_all = x_ref[...].astype(jnp.bfloat16)
    inner = dot_last(cmat, bmat)
    row = lax.broadcasted_iota(jnp.int32, (size, size), 0)
    column = lax.broadcasted_iota(jnp.int32, (size, size), 1)
    allowed = row >= column
    lane = lax.broadcasted_iota(jnp.int32, (size, pair), 1)
    from_state = mul(cmat, state.astype(jnp.bfloat16))
    spread = spread_heads(jnp.exp(cumulative), head_size, width)
    for first in range(0, width // head_size, 2):
        here = slice(first * head_size, first * head_size + pair)
        x_pair = x_all[:, here]
        total = from_state[:, here] * spread[:, here]
        total += skip_ref[:, here] * x_pair.astype(jnp.float32)
        for head in (first, first + 1):
            gap = cumulative[:, head : head + 1] - cum_row[head : head + 1, :]
            decay = jnp.exp(jnp.where(allowed, gap, -1e30))
            mixing = inner * decay * delta_row[head : head + 1, :]
            x_head = jnp.where((lane >= head_size) == (head > first), x_pair, 0.0)
            total += mul(mixing.astype(jnp.bfloat16), x_head.astype(jnp.bfloat16))
        scanned_ref[:, here] = total
        gate = z_ref[:, here]
        gated_ref[:, here] = (total * (gate * jax.nn.sigmoid(gate))).astype(jnp.bfloat16)
    ending = cumulative[-1:, :]
    weight = spread_heads(jnp.exp(ending - cumulative) * delta, head_size, width)
    weighted = (x_all.astype(jnp.float32) * weight).astype(jnp.bfloat16)
    state_ref[...] = state * spread[-1:, :] + dot_first(bmat, weighted)


def scan(at, delta, cumulative, delta_row, cum_row, entry, skip, after):
    rows = delta.shape[0]
    state_size, width = entry.shape
    chunks = rows // BLOCK
    by_chunk = pl.BlockSpec((BLOCK, width), lambda c: (c, 0))
    lanes = delta.shape[1]
    across = pl.BlockSpec((8, BLOCK), lambda c: (0, c))
    return run_scan(
        scan_kernel,
        chunks,
        [
            part(*at["x"]),
            part(*at["z"]),
            part(*at["b"]),
            part(*at["c"]),
            part(delta, 0, lanes),
            part(cumulative, 0, lanes),
            (delta_row, across),
            (cum_row, across),
            whole(entry),
            whole(skip),
        ],
        (
            jax.ShapeDtypeStruct((rows, width), jnp.float32),
            jax.ShapeDtypeStruct((rows, width), jnp.bfloat16),
            jax.ShapeDtypeStruct((chunks, state_size, width), jnp.float32),
        ),
        (by_chunk, by_chunk, pl.BlockSpec((1, state_size, width), lambda c: (c, 0, 0))),
        3_000_000_000,
        "scan",
        [pltpu.VMEM((state_size, width), jnp.float32)],
        after,
    )


def scan_back_first_kernel(
    grad_ref, z_ref, scanned_ref, c_ref, cum_ref, d_scanned_ref, d_gate_ref, state_ref, log_ref
):
    @pl.when(pl.program_id(0) == 0)
    def _():
        state_ref[...] = jnp.zeros_like(state_ref)
        log_ref[...] = jnp.zeros_like(log_ref)

    gate = z_ref[...]
    chance = jax.nn.sigmoid(gate)
    grad = grad_ref[:, : z_ref.shape[1]].astype(jnp.float32)
    d_scanned = grad * (gate * chance)
    d_scanned_ref[...] = d_scanned
    d_gate_ref[...] = (
        grad * scanned_ref[...] * (chance * (1.0 + gate * (1.0 - chance)))
    ).astype(jnp.bfloat16)
    cumulative = cum_ref[...]
    decay = spread_heads(jnp.exp(cumulative + log_ref[...]), MIXER_HEAD_SIZE, z_ref.shape[1])
    state_ref[...] += dot_first(
        c_ref[...].astype(jnp.bfloat16), (d_scanned * decay).astype(jnp.bfloat16)
    )
    log_ref[...] += cumulative[-1:, :]


def scan_back_first(grads, at, scanned, cumulative):
    rows, width = scanned.shape
    state_size, lanes = (at["c"][2], cumulative.shape[1])
    by_chunk = pl.BlockSpec((BLOCK, width), lambda c: (c, 0))
    return run_scan(
        scan_back_first_kernel,
        rows // BLOCK,
        [
            part(grads, 0, grads.shape[1]),
            part(*at["z"]),
            part(scanned, 0, width),
            part(*at["c"]),
            part(cumulative, 0, lanes),
        ],
        (
            jax.ShapeDtypeStruct((rows, width), jnp.float32),
            jax.ShapeDtypeStruct((rows, width), jnp.bfloat16),
            jax.ShapeDtypeStruct((state_size, width), jnp.float32),
        ),
        (by_chunk, by_chunk, pl.BlockSpec((state_size, width), lambda c: (0, 0))),
        1_000_000_000,
        "scan_back_first",
        [pltpu.VMEM((1, lanes), jnp.float32)],
    )


def scan_back_kernel(
    x_ref,
    grad_ref,
    b_ref,
    c_ref,
    pre_ref,
    bias_ref,
    rate_ref,
    delta_ref,
    cum_ref,
    cum_row_ref,
    states_ref,
    entry_ref,
    skip_ref,
    d_x_ref,
    d_b_ref,
    d_c_ref,
    d_pre_ref,
    sums_ref,
    state_ref,
):
    @pl.when(pl.program_id(0) == 0)
    def _():
        state_ref[...] = entry_ref[...]
        sums_ref[...] = jnp.zeros_like(sums_ref)

    head_size = MIXER_HEAD_SIZE
    pair = 2 * head_size
    size, width = x_ref.shape
    lanes = delta_ref.shape[1]
    low = jnp.bfloat16
    delta, cumulative, cum_row = (delta_ref[...], cum_ref[...], cum_row_ref[...])
    bmat, cmat = (b_ref[...].astype(low), c_ref[...].astype(low))
    x_all = x_ref[...].astype(low)
    x_single = x_all.astype(jnp.float32)
    grad = grad_ref[...]
    grad_low = grad.astype(low)
    state = states_ref[0]
    state_low = state.astype(low)
    after = state_ref[...]
    after_low = after.astype(low)
    ending = cumulative[-1:, :]
    row = lax.broadcasted_iota(jnp.int32, (size, size), 0)
    column = lax.broadcasted_iota(jnp.int32, (size, size), 1)
    later = column >= row
    before = (row > column).astype(low)
    onward = later.astype(low)
    lane = lax.broadcasted_iota(jnp.int32, (size, pair), 1)
    head_lane = lax.broadcasted_iota(jnp.int32, (size, lanes), 1)
    sum_heads = head_ones(width, head_size, lanes, low)

    inner = dot_last(bmat, cmat)
    from_after = mul(bmat, after_low)
    weight = jnp.exp(ending - cumulative)
    spread_weight = spread_heads(weight * delta, head_size, width)
    spread = spread_heads(jnp.exp(cumulative), head_size, width)
    to_end = mul((x_single * from_after).astype(low), sum_heads)
    through = jnp.exp(cumulative) * mul((grad * mul(cmat, state_low)).astype(low), sum_heads)
    carried = jnp.sum(state * after, axis=0, keepdims=True) * spread[-1:, :]
    carried = precise(carried, sum_heads.astype(jnp.float32))
    d_delta = weight * to_end
    d_log = (
        mul(onward, through.astype(low)) + mul(before, (d_delta * delta).astype(low)) + carried
    )

    d_inner = jnp.zeros((size, size), jnp.float32)
    for first in range(0, width // head_size, 2):
        here = slice(first * head_size, first * head_size + pair)
        x_pair, grad_pair = (x_all[:, here], grad_low[:, here])
        d_x = from_after[:, here] * spread_weight[:, here] + skip_ref[:, here] * grad[:, here]
        for head in (first, first + 1):
            mine = (lane >= head_size) == (head > first)
            gap = cum_row[head : head + 1, :] - cumulative[:, head : head + 1]
            decay = jnp.exp(jnp.where(later, gap, -1e30))
            delta_column = delta[:, head : head + 1]
            d_mixing = dot_last(jnp.where(mine, x_pair, 0.0).astype(low), grad_pair) * decay
            d_inner += d_mixing * delta_column
            flow = d_mixing * inner
            mixing = inner * decay * delta_column
            d_x += mul(mixing.astype(low), jnp.where(mine, grad_pair, 0.0).astype(low))
            d_delta_head = jnp.sum(flow, axis=1, keepdims=True)
            passing = mul(before, (flow * delta_column).astype(low))
            d_log_head = jnp.sum(jnp.where(later, passing, 0.0), axis=1, keepdims=True)
            d_delta += jnp.where(head_lane == head, d_delta_head, 0.0)
            d_log += jnp.where(head_lane == head, d_log_head, 0.0)
        d_x_ref[:, here] = d_x.astype(low)

    d_inner_low = d_inner.astype(low)
    scaled_grad = (grad * spread).astype(low)
    weighted = (x_single * spread_weight).astype(low)
    d_b_ref[...] = (mul(d_inner_low, cmat) + dot_last(weighted, after_low)).astype(low)
    d_c_ref[...] = (dot_first(d_inner_low, bmat) + dot_last(scaled_grad, state_low)).astype(low)
    state_ref[...] = after * spread[-1:, :] + dot_first(cmat, scaled_grad)
    rate = rate_ref[...]
    d_pre = (d_delta - d_log * rate) * jax.nn.sigmoid(pre_ref[...] + bias_ref[...])
    d_pre = jnp.where(head_lane < width // head_size, d_pre, 0.0)
    d_pre_ref[...] = d_pre.astype(low)
    skip_sum = precise(
        jnp.sum(grad * x_single, axis=0, keepdims=True), sum_heads.astype(jnp.float32)
    )
    sums_ref[0:1, :] += jnp.sum(d_pre, axis=0, keepdims=True)
    sums_ref[1:2, :] += jnp.sum(d_log * (-delta * rate), axis=0, keepdims=True)
    sums_ref[2:3, :] += skip_sum


def scan_back(
    at, d_scanned, bias, rate, delta, cumulative, cum_row, states, entry, skip, after
):
    rows, width = d_scanned.shape
    state_size, lanes = (entry.shape[0], delta.shape[1])
    chunks = rows // BLOCK
    back = lambda c: chunks - 1 - c
    by_chunk = lambda columns: pl.BlockSpec((BLOCK, columns), lambda c: (back(c), 0))
    shape = lambda columns: jax.ShapeDtypeStruct((rows, columns), jnp.bfloat16)
    return run_scan(
        scan_back_kernel,
        chunks,
        [
            part(*at["x"], back),
            part(d_scanned, 0, width, back),
            part(*at["b"], back),
            part(*at["c"], back),
            part(*at["misc"], back),
            whole(bias),
            whole(rate),
            part(delta, 0, lanes, back),
            part(cumulative, 0, lanes, back),
            (cum_row, pl.BlockSpec((8, BLOCK), lambda c: (0, back(c)))),
            (states, pl.BlockSpec((1, state_size, width), lambda c: (back(c), 0, 0))),
            whole(entry),
            whole(skip),
        ],
        (
            shape(width),
            shape(state_size),
            shape(state_size),
            shape(lanes),
            jax.ShapeDtypeStruct((8, lanes), jnp.float32),
        ),
        (
            by_chunk(width),
            by_chunk(state_size),
            by_chunk(state_size),
            by_chunk(lanes),
            pl.BlockSpec((8, lanes), lambda c: (0, 0)),
        ),
        6_000_000_000,
        "scan_back",
        [pltpu.VMEM((state_size, width), jnp.float32)],
        after,
    )


def on_heads(value, move):
    devices = lax.axis_size("heads")
    pairs = []
    for at in range(devices):
        z, core = move(at // 2, at % 2)
        pairs.append((at, 2 * (z % (devices // 2)) + core))
    return lax.ppermute(value, "heads", pairs)


def to_partner(value):
    return on_heads(value, lambda z, core: (z, 1 - core))


def along(value):
    return on_heads(value, lambda z, core: (z + 1 - 2 * core, core))


def against(value):
    return on_heads(value, lambda z, core: (z - 1 + 2 * core, core))


def chunk_ranks():
    devices = lax.axis_size("heads")
    z, core = (lax.axis_index("heads") // 2, lax.axis_index("heads") % 2)
    step, other = (1 - 2 * core, 1 - core)
    owners = (
        (z, core),
        (z + 2, core),
        (z - step, core),
        (z - step, other),
        (z, other),
        (z + 2, other),
        (z + step, other),
        (z + step, core),
    )
    return jnp.stack([2 * ((at + devices) % (devices // 2)) + side for at, side in owners])


def gather_rows(own):
    partner = to_partner(own)
    near = along(own)
    near_other = along(partner)
    far = along(near)
    mine = (own, far, near, near_other)
    theirs = (partner, to_partner(far), to_partner(near), to_partner(near_other))
    return jnp.concatenate(mine + theirs, axis=0)


def scatter_rows(product, half):
    chunk = half // 4
    got = to_partner(product(slice(half, 2 * half)).astype(jnp.bfloat16))
    summed = product(slice(0, half)) + got.astype(jnp.float32)
    low = summed[chunk:].astype(jnp.bfloat16)
    far = against(low[:chunk])
    near_other = against(low[2 * chunk :])
    near = against((low[chunk : 2 * chunk].astype(jnp.float32) + far).astype(jnp.bfloat16))
    return summed[:chunk] + near.astype(jnp.float32) + to_partner(near_other).astype(jnp.float32)


def across(value, bit):
    devices = lax.axis_size("heads")
    return lax.ppermute(value, "heads", [(at, at ^ bit) for at in range(devices)])


def gather_small(value):
    for bit in (1, 2, 4):
        value = jnp.concatenate([value, across(value, bit)], axis=0)
    return value


def scatter_small(value):
    for bit in (4, 2, 1):
        half = value.shape[0] // 2
        got = across(value[half:].astype(jnp.bfloat16), bit)
        value = value[:half].astype(jnp.float32) + got.astype(jnp.float32)
    return value


def on_blocks(value, step):
    devices = lax.axis_size("blk")
    pairs = [(at, at + step) for at in range(devices) if 0 <= at + step < devices]
    return lax.ppermute(value, "blk", pairs)


def from_earlier(value, step=1):
    return tuple(on_blocks(value, distance * step) for distance in (1, 2, 3))


def pack_state(state, log_total):
    high = log_total.astype(jnp.bfloat16)
    rest = log_total - high.astype(jnp.float32)
    middle = rest.astype(jnp.bfloat16)
    low = (rest - middle.astype(jnp.float32)).astype(jnp.bfloat16)
    logs = jnp.concatenate([high, middle, low], axis=0)
    logs = jnp.pad(logs, ((0, 16 - logs.shape[0]), (0, state.shape[1] - logs.shape[1])))
    return jnp.concatenate([state.astype(jnp.bfloat16), logs], axis=0)


def chain(packed, step, heads):
    decays, states = [], []
    for part_in in from_earlier(packed, step):
        state, logs = (part_in[:-16].astype(jnp.float32), part_in[-16:].astype(jnp.float32))
        decays.append(jnp.repeat(jnp.exp(jnp.sum(logs[:3, :heads], axis=0)), MIXER_HEAD_SIZE)[None])
        states.append(state)
    return states[0] + decays[0] * (states[1] + decays[1] * states[2])


def sum_blocks(value):
    for axis in ("dp", "blk"):
        for bit in (1, 2):
            value = value + lax.ppermute(
                value, axis, [(at, at ^ bit) for at in range(lax.axis_size(axis))]
            )
    return value


def on_ring(value, axis, step):
    devices = lax.axis_size(axis)
    return lax.ppermute(value, axis, [(at, (at + step) % devices) for at in range(devices)])


def ring_gather(own, axis):
    half = own.shape[0] // 2
    before = on_ring(own, axis, 1)
    behind = on_ring(own, axis, -1)
    top = on_ring(before[:half], axis, 1)
    bottom = on_ring(behind[half:], axis, -1)
    return [own, before, behind, top, bottom]


def grid_gather(own, first, second):
    return ring_gather(jnp.concatenate(ring_gather(own, first), axis=0), second)


def grid_chunks(first, second):
    turns = jnp.array([0, 3, 1, 2])
    outer = (lax.axis_index(second) + turns)[:, None] % lax.axis_size(second)
    inner = (lax.axis_index(first) + turns)[None, :] % lax.axis_size(first)
    dp, blk = (inner, outer) if first == "dp" else (outer, inner)
    return (dp * lax.axis_size("blk") + blk).reshape(-1).astype(jnp.int32)


def weight_sum(grads):
    return lax.psum_scatter(grads, ("dp", "blk"), scatter_dimension=0, tiled=True)


def ring_sum(chunk, axis):
    half = chunk(0).shape[0] // 2
    single = lambda part_in: part_in.astype(jnp.float32)
    from_before = on_ring(chunk(2)[:half], axis, 1)
    from_behind = on_ring(chunk(2)[half:], axis, -1)
    ahead, back = (chunk(1), chunk(3))
    top = (single(ahead[:half]) + single(from_before)).astype(ahead.dtype)
    bottom = (single(back[half:]) + single(from_behind)).astype(back.dtype)
    ahead = on_ring(jnp.concatenate([top, ahead[half:]], axis=0), axis, 1)
    back = on_ring(jnp.concatenate([back[:half], bottom], axis=0), axis, -1)
    return single(chunk(0)) + single(ahead) + single(back)


def grid_sum(value, first):
    value = value.reshape((4, 4, -1, value.shape[1]))
    if first == "dp":
        part_sum = ring_sum(lambda k: value[k], "dp").astype(value.dtype)
        return ring_sum(lambda k: part_sum[k], "blk")
    part_sum = ring_sum(lambda k: value[:, k], "blk").astype(value.dtype)
    return ring_sum(lambda k: part_sum[k], "dp")


def grid_turns():
    turns = jnp.arange(4)
    dp = (lax.axis_index("dp") + turns)[:, None] % lax.axis_size("dp")
    blk = (lax.axis_index("blk") + turns)[None, :] % lax.axis_size("blk")
    return (dp * lax.axis_size("blk") + blk).reshape(-1).astype(jnp.int32)


def split_columns(value_in, widths):
    pieces, start = [], 0
    for width in widths:
        pieces.append(value_in[:, start : start + width])
        start += width
    return pieces


def inverse_rms(rows_in):
    return lax.rsqrt(jnp.mean(rows_in * rows_in, axis=-1, keepdims=True) + norm_eps)


def norm_back(rows_in, gain_in, cotangent):
    inverse = inverse_rms(rows_in)
    scaled = rows_in * inverse
    weighted = cotangent * gain_in
    return inverse * (weighted - scaled * jnp.mean(weighted * scaled, axis=-1, keepdims=True))


def shards(
    x_in,
    out_grad,
    norm_one,
    w_query,
    w_key,
    w_value,
    output_gate_weight,
    mixer_input_weight,
    w_delta,
    w_bmat,
    w_cmat,
    delta_bias,
    decay_log,
    skip_gain,
    w_attn_out,
    mixer_output_weight,
    norm_two,
    w_gate,
    w_up,
    w_down,
):
    heads_count = lax.axis_size("heads")
    head_rank = lax.axis_index("heads")
    core = head_rank % 2
    block_rank = lax.axis_index("blk")
    rank = block_rank.astype(jnp.int32)[None]
    own_rows = x_in.shape[0]
    span_length = own_rows * heads_count
    half_span = span_length // 2
    span_start = block_rank * span_length
    query_width = w_query.shape[1]
    mixer_width = mixer_input_weight.shape[1]
    heads = mixer_width // MIXER_HEAD_SIZE
    state_size = w_bmat.shape[1]
    hidden_width = w_gate.shape[1]
    rows_of = w_query.shape[0]
    kv_index = head_rank * (query_width // HD) // (QH // KVH)
    kv_width = KVH * HD
    low = jnp.bfloat16
    ranks = chunk_ranks().astype(jnp.int32)
    turns = (head_rank ^ jnp.arange(heads_count)).astype(jnp.int32)

    gains = jnp.stack([norm_one, norm_two], axis=1)
    gains = jnp.pad(gains, ((0, 0), (0, LANES - 2)))
    shared = jnp.concatenate([w_key, w_value, w_bmat, w_cmat, gains], axis=1)
    shared = reorder(turns, [gather_small(shared)], inverse=True)
    key_part = lax.dynamic_slice_in_dim(shared, kv_index * HD, HD, 1)
    value_part = lax.dynamic_slice_in_dim(shared, kv_width + kv_index * HD, HD, 1)
    state_part = shared[:, 2 * kv_width : 2 * kv_width + 2 * state_size]
    gain_part = shared[:, 2 * kv_width + 2 * state_size :][:, :2]
    misc_part = jnp.concatenate(
        [w_delta, gain_part, jnp.zeros((rows_of, LANES - heads - 2), low)], axis=1
    )
    in_names = ("z", "x", "query", "b", "c", "misc", "key", "value")
    in_widths = (mixer_width, mixer_width, query_width, state_size, state_size, LANES, HD, HD)
    starts = [sum(in_widths[:k]) for k in range(len(in_widths))]
    at = dict(zip(in_names, zip(starts, in_widths)))
    in_first = jnp.concatenate([output_gate_weight, mixer_input_weight, w_query], axis=1)
    in_second = jnp.concatenate([state_part, misc_part, key_part, value_part], axis=1)
    in_own = jnp.concatenate([in_first, in_second], axis=1)
    first_shards = jnp.concatenate(ring_gather(in_first, "dp"), axis=0)
    first_pieces = ring_gather(first_shards, "blk")
    second_pieces = grid_gather(in_second, "blk", "dp")
    out_own = pack(mixer_output_weight, w_attn_out, w_gate, w_up, w_down, first_shards)
    out_full = lax.all_gather(out_own, ("dp", "blk"), axis=0, tiled=True)
    mixed_width = query_width + mixer_width
    mix_t, gate_full, up_full, down_t = split_columns(out_full, (mixed_width,) + (hidden_width,) * 3)

    x_float = x_in.astype(jnp.float32)
    x_span = gather_rows(x_in)
    positions = (span_start + jnp.arange(span_length)).astype(jnp.float32)
    freqs = rope_base ** (-2.0 * jnp.arange(HD // 2, dtype=jnp.float32) / HD)
    angles = positions[:, None] * freqs[None, :]
    cosine, sine = (jnp.cos(angles), jnp.sin(angles))
    cosine = jnp.concatenate([cosine, cosine], axis=1)
    sine = jnp.concatenate([-sine, sine], axis=1)
    in_full = assemble(
        jnp.stack([grid_chunks("dp", "blk"), grid_chunks("blk", "dp")]),
        [first_pieces, second_pieces],
    )
    normed_ordered, queries, keys_values, gain_rows = enter(
        ranks, jnp.full((1,), heads, jnp.int32), x_span, in_full, at, cosine, sine
    )
    gain_one, gain_two = (gain_rows[0:1], gain_rows[1:2])
    ffn_grad = gather_rows(out_grad + (0.0 * keys_values[0, 0]).astype(low))
    mine = lax.dynamic_slice_in_dim(keys_values, core * half_span, half_span, 0)
    pieces = []
    for piece in from_earlier(mine):
        pieces += [piece, to_partner(piece)]
    gate_raw = simple_product(normed_ordered, in_full[:, :mixer_width])
    x_raw = simple_product(normed_ordered, in_full[:, mixer_width : 2 * mixer_width])
    state_raw = simple_product(normed_ordered, in_full[:, at["b"][0] : at["key"][0]])
    raw = {
        "z": (gate_raw, 0, mixer_width),
        "x": (x_raw, 0, mixer_width),
        "b": (state_raw, 0, state_size),
        "c": (state_raw, state_size, state_size),
        "misc": (state_raw, 2 * state_size, LANES),
    }

    pad_lanes = lambda vector: jnp.pad(vector, (0, LANES - heads))[None]
    bias, rate = (pad_lanes(delta_bias), pad_lanes(jnp.exp(decay_log)))
    skip = jnp.repeat(skip_gain, MIXER_HEAD_SIZE)[None]
    delta, cumulative, delta_row, cum_row, local_state, local_log = scan_first(raw, bias, rate)
    entry_state = chain(pack_state(local_state, local_log), 1, heads)
    attended, attn_part, log_totals = attend(rank, queries, keys_values, pieces)
    scanned, gated, states = scan(
        raw, delta, cumulative, delta_row, cum_row, entry_state, skip, [attn_part]
    )
    mixers = reorder(ranks, [gated, attn_part], after=[ffn_grad])
    middle = x_float + scatter_rows(lambda rows: dot_last(mixers[rows], mix_t), half_span)
    middle_scaled = middle * inverse_rms(middle)
    normed_two = gather_rows((middle_scaled * gain_two).astype(low))
    ffn_gate = simple_product(normed_two, gate_full)
    ffn_up = simple_product(normed_two, up_full)
    ffn_sig = jax.nn.sigmoid(ffn_gate)
    hidden = (ffn_gate * ffn_sig * ffn_up).astype(low)

    d_hidden = simple_product(ffn_grad, down_t)
    d_ffn_gate = (d_hidden * ffn_up * (ffn_sig * (1.0 + ffn_gate * (1.0 - ffn_sig)))).astype(low)
    d_ffn_up = (d_hidden * (ffn_gate * ffn_sig)).astype(low)
    d_normed_two = scatter_rows(
        lambda rows: dot_last(d_ffn_gate[rows], gate_full) + dot_last(d_ffn_up[rows], up_full),
        half_span,
    )
    plain = jnp.arange(normed_two.shape[1] // LANES, dtype=jnp.int32)
    (ffn_grads,) = weight_grads(
        plain, [(normed_two, [d_ffn_gate, d_ffn_up]), (ffn_grad, [hidden])], (3,)
    )
    ffn_sums = weight_sum(ffn_grads).astype(jnp.float32)
    grad_gate, grad_up, grad_down_t = split_columns(ffn_sums, (hidden_width,) * 3)
    grad_two_part = jnp.sum(grad_gate * w_gate + grad_up * w_up, axis=1, keepdims=True)
    gain_own = gain_part.astype(jnp.float32)
    grad_two_part = grad_two_part / gain_own[:, 1:2]
    d_middle = out_grad.astype(jnp.float32) + norm_back(middle, gain_two, d_normed_two)
    mix_grad = gather_rows(d_middle.astype(low))
    d_mixers = reorder(
        ranks, [simple_product(mix_grad, mix_t).astype(low)], inverse=True, after=[ffn_grads]
    )
    d_scanned, d_gate_z, d_entry = scan_back_first(d_mixers, raw, scanned, cumulative)
    d_entry = pack_state(d_entry, local_log)
    after_state = chain(d_entry, -1, heads)
    d_query, d_own, d_far = attend_back(
        rank, queries, keys_values, pieces, attended, log_totals, d_mixers, cosine, sine, d_entry
    )
    (mix_grads,) = weight_grads(
        plain, [(mix_grad, [mixers]), (normed_ordered, [d_gate_z])], (2,), [d_query]
    )
    mix_sums = weight_sum(mix_grads)
    d_ssm_in, d_bmat, d_cmat, d_pre, sums = scan_back(
        raw,
        d_scanned,
        bias,
        rate,
        delta,
        cumulative,
        cum_row,
        states,
        after_state,
        skip,
        [mix_grads],
    )
    hidden_later = hidden + (0.0 * d_query[0, 0]).astype(low)
    ffn_out = scatter_rows(lambda rows: dot_last(hidden_later[rows], down_t), half_span)
    activations = (middle + ffn_out).astype(low)
    far_half = d_far.shape[0] // 2
    d_mine = lax.dynamic_slice_in_dim(d_own, core * half_span, half_span, 0)
    d_theirs = lax.dynamic_slice_in_dim(d_own, (1 - core) * half_span, half_span, 0)
    d_mine = d_mine + to_partner(d_theirs.astype(low)).astype(jnp.float32)
    d_far = d_far[:far_half].astype(jnp.float32) + to_partner(d_far[far_half:]).astype(jnp.float32)
    d_one, d_two, d_three = (
        d_far[k * half_span : (k + 1) * half_span] for k in range(d_far.shape[0] // half_span)
    )
    d_one = d_one + on_blocks(d_two.astype(low), -1).astype(jnp.float32)
    d_mine = d_mine + on_blocks(d_one.astype(low), -1).astype(jnp.float32)
    d_mine = d_mine + on_blocks(d_three.astype(low), -3).astype(jnp.float32)
    half_cos = lax.dynamic_slice_in_dim(cosine, core * half_span, half_span, 0)
    half_sin = lax.dynamic_slice_in_dim(sine, core * half_span, half_span, 0)
    d_key = d_mine[:, :HD]
    d_key = d_key * half_cos - jnp.roll(d_key, HD // 2, axis=1) * half_sin
    d_mine = jnp.concatenate([d_key, d_mine[:, HD:]], axis=1).astype(low)
    d_keys_values = lax.dynamic_update_slice_in_dim(
        jnp.zeros((span_length, 2 * HD), low), d_mine, core * half_span, 0
    )

    first_grads, second_grads = weight_grads(
        grid_turns(),
        [(normed_ordered, [d_ssm_in, d_query, d_pre, d_bmat, d_cmat, d_keys_values])],
        (3, 3),
        [activations],
    )
    first_sums, second_sums = (grid_sum(first_grads, "dp"), grid_sum(second_grads, "blk"))
    d_projected = reorder(
        ranks,
        [d_gate_z, d_ssm_in, d_query, d_bmat, d_cmat, d_pre, d_keys_values],
        after=[first_grads],
    )
    d_normed = scatter_rows(lambda rows: dot_last(d_projected[rows], in_full), half_span)
    input_grad = d_middle + norm_back(x_float, gain_one, d_normed)
    sums_at = {
        "ssm_out": (2, 0, mixer_width),
        "attn_out": (2, mixer_width, query_width),
        "z": (2, mixed_width, mixer_width),
        "x": (0, 0, mixer_width),
        "query": (0, mixer_width, query_width),
        "misc": (0, mixer_width + query_width, LANES),
        "b": (1, 0, state_size),
        "c": (1, state_size, state_size),
        "key": (1, 2 * state_size, HD),
        "value": (1, 2 * state_size + HD, HD),
    }
    extra = jnp.concatenate([gain_own[:, 0:1], grad_two_part], axis=1)
    extra = jnp.pad(extra, ((0, 0), (0, LANES - 2)))
    grad_ssm_out, grad_attn_out, grad_gatez, grad_ssmx, grad_query, misc_sums, shared_parts = finish(
        turns,
        kv_index.astype(jnp.int32)[None],
        (first_sums, second_sums, mix_sums),
        in_own,
        extra,
        at,
        sums_at,
    )
    shared_sums = scatter_small(shared_parts)
    grad_key, grad_value, grad_bmat, grad_cmat, gain_sums = split_columns(
        shared_sums, (kv_width, kv_width, state_size, state_size, LANES)
    )
    small_sums = sum_blocks(sums)[:, :heads]
    return (
        activations,
        input_grad,
        gain_sums[:, 0],
        grad_query,
        grad_key,
        grad_value,
        grad_gatez,
        grad_ssmx,
        misc_sums[:, :heads],
        grad_bmat,
        grad_cmat,
        small_sums[0],
        small_sums[1],
        small_sums[2],
        grad_attn_out,
        grad_ssm_out,
        gain_sums[:, 1],
        grad_gate,
        grad_up,
        grad_down_t.T,
    )


def solution(mesh):
    placed = (
        P(("dp", "blk", "heads"), None),
        P(("dp", "blk", "heads"), None),
        P(("dp", "blk", "heads")),
        P(("dp", "blk"), "heads"),
        P(("dp", "blk", "heads"), None),
        P(("dp", "blk", "heads"), None),
        P(("dp", "blk"), "heads"),
        P(("dp", "blk"), "heads"),
        P(("dp", "blk"), "heads"),
        P(("dp", "blk", "heads"), None),
        P(("dp", "blk", "heads"), None),
        P("heads"),
        P("heads"),
        P("heads"),
        P("heads", ("dp", "blk")),
        P("heads", ("dp", "blk")),
        P(("dp", "blk", "heads")),
        P(("dp", "blk"), "heads"),
        P(("dp", "blk"), "heads"),
        P("heads", ("dp", "blk")),
    )
    return jax.shard_map(
        shards,
        mesh=mesh,
        in_specs=placed,
        out_specs=(
            P(("dp", "blk", "heads"), None),
            P(("dp", "blk", "heads"), None),
            P(("dp", "blk", "heads")),
            P(("dp", "blk"), "heads"),
            P(("dp", "blk", "heads"), None),
            P(("dp", "blk", "heads"), None),
            P(("dp", "blk"), "heads"),
            P(("dp", "blk"), "heads"),
            P(("dp", "blk"), "heads"),
            P(("dp", "blk", "heads"), None),
            P(("dp", "blk", "heads"), None),
            P("heads"),
            P("heads"),
            P("heads"),
            P("heads", ("dp", "blk")),
            P("heads", ("dp", "blk")),
            P(("dp", "blk", "heads")),
            P(("dp", "blk"), "heads"),
            P(("dp", "blk"), "heads"),
            P("heads", ("dp", "blk")),
        ),
        check_vma=False,
    )
```

```python
import functools

import jax
import jax.numpy as jnp
from jax import lax
from jax.experimental import pallas as pl
from jax.experimental.pallas import tpu as pltpu
from jax.sharding import PartitionSpec as P

QH = 8
KVH = 2
HD = 128
MIXER_HEAD_SIZE = 64
BLOCK = 256
LANES = 128
LOG2_E = 1.4426950408889634


HIGH_PRECISION = lax.Precision.HIGHEST
norm_eps = 1e-05
rope_base = 100000000000.0


def simple_product(left_side, right_side):
    return jnp.dot(left_side, right_side, preferred_element_type=jnp.float32)


def dot_last(left_side, right_side):
    return lax.dot_general(
        left_side, right_side, (((1,), (1,)), ((), ())), preferred_element_type=jnp.float32
    )


def dot_first(left_side, right_side):
    return lax.dot_general(
        left_side, right_side, (((0,), (0,)), ((), ())), preferred_element_type=jnp.float32
    )


def compiler_params():
    return pltpu.CompilerParams(vmem_limit_bytes=50 * 1024 * 1024)


def in_vmem(count):
    return [pl.BlockSpec(memory_space=pltpu.VMEM)] * count


def mul(left_side, right_side):
    return jnp.dot(left_side, right_side, preferred_element_type=jnp.float32)


def tile_scores(key_rows, query_rows, head_size):
    return dot_last(key_rows, query_rows) * (head_size**-0.5 * LOG2_E)


def causal(scores):
    key_at = lax.broadcasted_iota(jnp.int32, scores.shape, 0)
    query_at = lax.broadcasted_iota(jnp.int32, scores.shape, 1)
    return jnp.where(key_at <= query_at, scores, -1e30)


def enter_kernel(
    ranks_ref,
    heads_ref,
    x_ref,
    misc_ref,
    key_ref,
    value_ref,
    w_query_ref,
    cos_ref,
    sin_ref,
    _,
    __,
    ordered_ref,
    query_ref,
    kv_ref,
    gains_ref,
):
    head_size = query_ref.shape[1]

    @pl.when(pl.program_id(0) == 0)
    def _():
        lane = lax.broadcasted_iota(jnp.int32, misc_ref.shape, 1)
        for k in range(2):
            column = jnp.where(lane == heads_ref[0] + k, misc_ref[...].astype(jnp.float32), 0.0)
            gains_ref[k : k + 1, :] = jnp.sum(column.T, axis=0, keepdims=True)

    cosine, sine = (cos_ref[...], sin_ref[...])

    def turn(value):
        return (value * cosine + pltpu.roll(value, head_size // 2, 1) * sine).astype(jnp.bfloat16)

    rows = x_ref[...].astype(jnp.float32)
    normed = (rows * inverse_rms(rows) * gains_ref[0:1, :]).astype(jnp.bfloat16)
    ordered_ref[...] = normed
    kv_ref[:, :head_size] = turn(mul(normed, key_ref[...]))
    kv_ref[:, head_size:] = mul(normed, value_ref[...]).astype(jnp.bfloat16)
    query_ref[...] = turn(mul(normed, w_query_ref[...]))


def enter(ranks, heads, x_span, in_full, at, cosine, sine, after):
    count = ranks.shape[0]
    rows, width = x_span.shape
    head_size = cosine.shape[1]
    here = lambda columns: pl.BlockSpec((rows // count, columns), lambda k, r, h: (k, 0))
    there = lambda columns: pl.BlockSpec((rows // count, columns), lambda k, r, h: (r[k], 0))
    weight = lambda name: pl.BlockSpec(
        (width, at[name][1]), lambda k, r, h: (0, at[name][0] // at[name][1])
    )
    return pl.pallas_call(
        enter_kernel,
        grid_spec=pltpu.PrefetchScalarGridSpec(
            num_scalar_prefetch=2,
            grid=(count,),
            in_specs=[
                here(width),
                weight("misc"),
                weight("key"),
                weight("value"),
                weight("query"),
                there(head_size),
                there(head_size),
            ]
            + [pl.BlockSpec(memory_space=pl.ANY)] * 2,
            out_specs=(
                there(width),
                there(head_size),
                there(2 * head_size),
                pl.BlockSpec((8, width), lambda k, r, h: (0, 0)),
            ),
        ),
        out_shape=(
            jax.ShapeDtypeStruct((rows, width), jnp.bfloat16),
            jax.ShapeDtypeStruct((rows, head_size), jnp.bfloat16),
            jax.ShapeDtypeStruct((rows, 2 * head_size), jnp.bfloat16),
            jax.ShapeDtypeStruct((8, width), jnp.float32),
        ),
        compiler_params=compiler_params(),
        cost_estimate=pl.CostEstimate(
            flops=2_000_000_000, bytes_accessed=16_000_000, transcendentals=0
        ),
        name="enter",
    )(ranks, heads, x_span, in_full, in_full, in_full, in_full, cosine, sine, *after)


def weight_grads_kernel(*refs, counts, turned):
    out_ref = refs[-1]
    start, used = (0, len(counts))
    for k, count in enumerate(counts):
        left = refs[k][...] if turned[k] else refs[k][...].T
        for ref in refs[used : used + count]:
            out_ref[:, start : start + ref.shape[1]] = mul(left, ref[...]).astype(jnp.bfloat16)
            start += ref.shape[1]
        used += count


def weight_grads(groups, width, start=0, buffer=None, after=()):
    turned = tuple(turn for _, _, turn in groups)
    rights = [right for _, group, _ in groups for right in group]
    columns = sum(right.shape[1] for right in rights)
    depth = rights[0].shape[0]
    rows = groups[0][0].shape[0 if turned[0] else 1]
    tall = pl.BlockSpec((BLOCK, depth), lambda k: (k, 0))
    wide = pl.BlockSpec((depth, BLOCK), lambda k: (0, k))
    operands = [left for left, _, _ in groups] + rights
    count = len(operands)
    extra = list(after) if buffer is None else [buffer] + list(after)

    def call(*refs):
        weight_grads_kernel(
            *refs[:count],
            refs[-1],
            counts=tuple(len(group) for _, group, _ in groups),
            turned=turned,
        )

    return pl.pallas_call(
        call,
        grid=(rows // BLOCK,),
        out_shape=jax.ShapeDtypeStruct((rows, width), jnp.bfloat16),
        in_specs=[tall if turn else wide for turn in turned]
        + [pl.BlockSpec(right.shape, lambda k: (0, 0)) for right in rights]
        + [pl.BlockSpec(memory_space=pl.ANY)] * len(extra),
        out_specs=pl.BlockSpec(
            (pl.Element(BLOCK), pl.Element(columns)), lambda k: (k * BLOCK, start)
        ),
        input_output_aliases={} if buffer is None else {count: 0},
        compiler_params=compiler_params(),
        cost_estimate=pl.CostEstimate(
            flops=2 * rows * depth * columns,
            bytes_accessed=2 * (depth * (2 * rows + columns) + rows * columns),
            transcendentals=0,
        ),
        name="weight_grads",
    )(*operands, *extra)


def pack_kernel(*refs, turned):
    out_ref = refs[-1]
    start = 0
    for ref, turn in zip(refs, turned):
        piece = ref[...].T if turn else ref[...]
        out_ref[:, start : start + piece.shape[1]] = piece
        start += piece.shape[1]


def pack(pieces, turned, after):
    sizes = [piece.shape[::-1] if turn else piece.shape for piece, turn in zip(pieces, turned)]
    return pl.pallas_call(
        functools.partial(pack_kernel, turned=turned),
        out_shape=jax.ShapeDtypeStruct(
            (sizes[0][0], sum(size[1] for size in sizes)), jnp.bfloat16
        ),
        in_specs=in_vmem(len(pieces)) + [pl.BlockSpec(memory_space=pl.ANY)],
        out_specs=pl.BlockSpec(memory_space=pltpu.VMEM),
        compiler_params=compiler_params(),
        name="pack",
    )(*pieces, after)


def finish_kernel(
    ranks_ref,
    kv_ref,
    sums_ref,
    weight_ref,
    extra_ref,
    ssm_out_ref,
    attn_out_ref,
    gate_ref,
    ssm_ref,
    query_ref,
    misc_ref,
    shared_ref,
    whole_ref,
    *,
    at,
    sums_at,
):
    def of(name):
        start, size = sums_at[name]
        return sums_ref[:, start : start + size].astype(jnp.float32)

    ssm_out_ref[...] = of("ssm_out").T
    attn_out_ref[...] = of("attn_out").T
    gate_ref[...] = of("z")
    ssm_ref[...] = of("x")
    query_ref[...] = of("query")
    misc_ref[...] = of("misc")
    total = 0.0
    for name, (start, size) in at.items():
        product = of(name) * weight_ref[:, start : start + size].astype(jnp.float32)
        total += jnp.sum(product, axis=1, keepdims=True)
    total = total / extra_ref[:, 0:1]
    lane = lax.broadcasted_iota(jnp.int32, misc_ref.shape, 1)
    gains = jnp.where(lane == 0, total, jnp.where(lane == 1, extra_ref[:, 1:2], 0.0))
    zero = jnp.zeros_like(gains)
    first = kv_ref[0] == 0
    key, value = (of("key"), of("value"))
    pieces = (
        jnp.where(first, key, zero),
        jnp.where(first, zero, key),
        jnp.where(first, value, zero),
        jnp.where(first, zero, value),
        of("b"),
        of("c"),
        gains,
    )
    start = 0
    for piece in pieces:
        whole_ref[:, start : start + piece.shape[1]] = piece
        start += piece.shape[1]
    count = ranks_ref.shape[0]
    size = shared_ref.shape[0] // count
    for k in range(count):
        rows = pl.ds(pl.multiple_of(ranks_ref[k] * size, size), size)
        shared_ref[k * size : (k + 1) * size, :] = whole_ref[rows, :].astype(jnp.bfloat16)


def finish(ranks, kv_index, sums, weights, extra, at, sums_at):
    rows = weights.shape[0]
    shape = lambda *sizes: jax.ShapeDtypeStruct(sizes, jnp.float32)
    width = lambda name: sums_at[name][1]
    shared = 2 * (width("key") + width("value")) + width("b") + width("c") + LANES
    return pl.pallas_call(
        functools.partial(finish_kernel, at=at, sums_at=sums_at),
        out_shape=(
            shape(width("ssm_out"), rows),
            shape(width("attn_out"), rows),
            shape(rows, width("z")),
            shape(rows, width("x")),
            shape(rows, width("query")),
            shape(rows, width("misc")),
            jax.ShapeDtypeStruct((rows, shared), jnp.bfloat16),
        ),
        in_specs=[pl.BlockSpec(memory_space=pltpu.SMEM)] * 2 + in_vmem(3),
        out_specs=tuple(in_vmem(7)),
        scratch_shapes=[pltpu.VMEM((rows, shared), jnp.float32)],
        compiler_params=compiler_params(),
        name="finish",
    )(ranks, kv_index, sums, weights, extra)


def attend_kernel(rank_ref, query_ref, own_ref, *refs):
    pieces, (out_ref, low_ref, log_ref) = (refs[:-3], refs[-3:])
    span_length, head_size = query_ref.shape
    tile = own_ref.shape[0] // 2
    for block in range(span_length // tile):
        here = slice(block * tile, (block + 1) * tile)
        query_rows = query_ref[here, :]

        def step(kv_rows, carried, masked=False):
            top, total, summed = carried
            scores = tile_scores(kv_rows[:, :head_size], query_rows, head_size)
            if masked:
                scores = causal(scores)
            new_top = jnp.maximum(top, jnp.max(scores, axis=0, keepdims=True))
            probs = jnp.exp2(scores - new_top)
            scale = jnp.exp2(top - new_top)
            total = total * scale + jnp.sum(probs, axis=0, keepdims=True)
            summed = summed * scale + dot_first(kv_rows[:, head_size:], probs.astype(jnp.bfloat16))
            return (new_top, total, summed)

        carried = (
            jnp.full((1, tile), -1e30, jnp.float32),
            jnp.zeros((1, tile), jnp.float32),
            jnp.zeros((head_size, tile), jnp.float32),
        )
        carried = step(own_ref[here, :], carried, True)
        for earlier in range(block):
            carried = step(own_ref[earlier * tile : (earlier + 1) * tile, :], carried)
        for distance in range(1, 1 + len(pieces) // 2):
            pair = pieces[2 * distance - 2 : 2 * distance]

            def both(_, carried, pair=pair):
                return step(pair[1][...], step(pair[0][...], carried))

            valid = (rank_ref[0] >= distance).astype(jnp.int32)
            carried = lax.fori_loop(0, valid, both, carried)
        top, total, summed = carried
        result = summed / total
        out_ref[:, here] = result
        low_ref[here, :] = result.T.astype(jnp.bfloat16)
        log_ref[:, here] = top + jnp.log2(total)


def attend(rank, queries, own, pieces):
    span_length, head_size = queries.shape
    return pl.pallas_call(
        attend_kernel,
        out_shape=(
            jax.ShapeDtypeStruct((head_size, span_length), jnp.float32),
            jax.ShapeDtypeStruct((span_length, head_size), jnp.bfloat16),
            jax.ShapeDtypeStruct((1, span_length), jnp.float32),
        ),
        in_specs=[pl.BlockSpec(memory_space=pltpu.SMEM)] + in_vmem(2 + len(pieces)),
        out_specs=tuple(in_vmem(3)),
        compiler_params=compiler_params(),
        cost_estimate=pl.CostEstimate(
            flops=10_000_000_000, bytes_accessed=4_000_000, transcendentals=4_000_000
        ),
        name="attend",
    )(rank, queries, own, *pieces)


def attend_back_kernel(rank_ref, query_ref, own_ref, *refs):
    pieces, refs = (refs[:-13], refs[-13:])
    out_ref, log_ref, grad_ref, cos_ref, sin_ref, *_, d_query_ref, d_own_ref, d_far_ref, sums_ref = refs
    span_length, head_size = query_ref.shape
    tile = own_ref.shape[0] // 2
    score_scale = head_size**-0.5
    sums_ref[...] = jnp.zeros_like(sums_ref)
    for block in range(span_length // tile):
        here = slice(block * tile, (block + 1) * tile)
        query_rows = query_ref[here, :]
        grad_rows = grad_ref[here, grad_ref.shape[1] - head_size :]
        log_total = log_ref[:, here]
        delta_row = jnp.sum(
            grad_rows.astype(jnp.float32).T * out_ref[:, here], axis=0, keepdims=True
        )

        def step(kv_ref, start, at, d_query, masked=False):
            key_rows = kv_ref[start : start + tile, :head_size]
            scores = tile_scores(key_rows, query_rows, head_size)
            if masked:
                scores = causal(scores)
            probs = jnp.exp2(scores - log_total)
            d_probs = dot_last(kv_ref[start : start + tile, head_size:], grad_rows)
            d_scores = (probs * (d_probs - delta_row)).astype(jnp.bfloat16)
            rows = slice(at * tile, (at + 1) * tile)
            sums_ref[rows, head_size:] += mul(probs.astype(jnp.bfloat16), grad_rows)
            sums_ref[rows, :head_size] += mul(d_scores, query_rows)
            return d_query + dot_first(key_rows, d_scores)

        d_query = jnp.zeros((head_size, tile), jnp.float32)
        d_query = step(own_ref, block * tile, block, d_query, True)
        for earlier in range(block):
            d_query = step(own_ref, earlier * tile, earlier, d_query)
        for distance in range(1, 1 + len(pieces) // 2):

            def both(_, d_query, distance=distance):
                for k in (2 * distance - 2, 2 * distance - 1):
                    d_query = step(pieces[k], 0, 2 + k, d_query)
                return d_query

            valid = (rank_ref[0] >= distance).astype(jnp.int32)
            d_query = lax.fori_loop(0, valid, both, d_query)
        turned = d_query.T * score_scale
        d_query_ref[here, :] = (
            turned * cos_ref[here, :] - pltpu.roll(turned, head_size // 2, 1) * sin_ref[here, :]
        ).astype(jnp.bfloat16)
    lane = lax.broadcasted_iota(jnp.int32, (tile, 2 * head_size), 1)
    scale = jnp.where(lane < head_size, score_scale, 1.0)
    for at in range(2):
        rows = slice(at * tile, (at + 1) * tile)
        d_own_ref[rows, :] = sums_ref[rows, :] * scale
    for k in range(len(pieces)):
        rows = slice((2 + k) * tile, (3 + k) * tile)
        into = (k % 2) * (len(pieces) // 2) + k // 2
        d_far_ref[into * tile : (into + 1) * tile, :] = (sums_ref[rows, :] * scale).astype(
            jnp.bfloat16
        )


def attend_back(rank, queries, own, pieces, attended, log_totals, d_attn, cosine, sine, after):
    tile = own.shape[0] // 2
    return pl.pallas_call(
        attend_back_kernel,
        out_shape=(
            jax.ShapeDtypeStruct(queries.shape, jnp.bfloat16),
            jax.ShapeDtypeStruct(own.shape, jnp.float32),
            jax.ShapeDtypeStruct((len(pieces) * tile, own.shape[1]), jnp.bfloat16),
        ),
        in_specs=[pl.BlockSpec(memory_space=pltpu.SMEM)]
        + in_vmem(7 + len(pieces))
        + [pl.BlockSpec(memory_space=pl.ANY)] * len(after),
        out_specs=tuple(in_vmem(3)),
        scratch_shapes=[pltpu.VMEM(((2 + len(pieces)) * tile, own.shape[1]), jnp.float32)],
        compiler_params=compiler_params(),
        cost_estimate=pl.CostEstimate(
            flops=25_000_000_000, bytes_accessed=8_000_000, transcendentals=4_000_000
        ),
        name="attend_back",
    )(rank, queries, own, *pieces, attended, log_totals, d_attn, cosine, sine, *after)


def reorder_kernel(ranks_ref, *refs, count):
    out_ref = refs[-1]
    start = 0
    for ref in refs[:count]:
        out_ref[:, start : start + ref.shape[1]] = ref[...].astype(out_ref.dtype)
        start += ref.shape[1]


def reorder(ranks, pieces, inverse=False, after=()):
    count = ranks.shape[0]
    rows = pieces[0].shape[0] // count
    width = sum(piece.shape[1] for piece in pieces)
    there = lambda k, ranks: (ranks[k], 0)
    here = lambda k, ranks: (k, 0)
    return pl.pallas_call(
        functools.partial(reorder_kernel, count=len(pieces)),
        grid_spec=pltpu.PrefetchScalarGridSpec(
            num_scalar_prefetch=1,
            grid=(count,),
            in_specs=[
                pl.BlockSpec((rows, piece.shape[1]), here if inverse else there)
                for piece in pieces
            ]
            + [pl.BlockSpec(memory_space=pl.ANY)] * len(after),
            out_specs=pl.BlockSpec((rows, width), there if inverse else here),
        ),
        out_shape=jax.ShapeDtypeStruct((count * rows, width), jnp.bfloat16),
        compiler_params=compiler_params(),
        cost_estimate=pl.CostEstimate(
            flops=0, bytes_accessed=4 * count * rows * width, transcendentals=0
        ),
        name="reorder",
    )(ranks, *pieces, *after)


def lower_ones(size, dtype=jnp.float32):
    row = lax.broadcasted_iota(jnp.int32, (size, size), 0)
    column = lax.broadcasted_iota(jnp.int32, (size, size), 1)
    return (row >= column).astype(dtype)


def precise(left_side, right_side):
    return jnp.dot(
        left_side, right_side, precision=HIGH_PRECISION, preferred_element_type=jnp.float32
    )


def spread_heads(columns, head_size, width):
    lane = lax.broadcasted_iota(jnp.int32, (columns.shape[0], 2 * head_size), 1)
    pairs = [
        jnp.where(lane < head_size, columns[:, k : k + 1], columns[:, k + 1 : k + 2])
        for k in range(0, width // head_size, 2)
    ]
    return jnp.concatenate(pairs, axis=1)


def head_ones(width, head_size, lanes, dtype):
    at = lax.broadcasted_iota(jnp.int32, (width, lanes), 0)
    lane = lax.broadcasted_iota(jnp.int32, (width, lanes), 1)
    low = lane * head_size
    return ((at >= low) & (at < low + head_size)).astype(dtype)


def scan_first_kernel(
    pre_ref, bias_ref, rate_ref, x_ref, b_ref, delta_ref, cum_ref, delta_row_ref, cum_row_ref, state_ref, log_ref
):
    @pl.when(pl.program_id(0) == 0)
    def _():
        state_ref[...] = jnp.zeros_like(state_ref)
        log_ref[...] = jnp.zeros_like(log_ref)

    delta = jax.nn.softplus(pre_ref[...] + bias_ref[...])
    log_step = -delta * rate_ref[...]
    cumulative = precise(lower_ones(log_step.shape[0]), log_step)
    delta_ref[...] = delta
    cum_ref[...] = cumulative
    delta_row_ref[...] = delta.T[:8]
    cum_row_ref[...] = cumulative.T[:8]
    ending = cumulative[-1:, :]
    weight = jnp.exp(ending - cumulative + log_ref[...]) * delta
    width = x_ref.shape[1]
    x_low = x_ref[...].astype(jnp.bfloat16).astype(jnp.float32)
    weighted = (x_low * spread_heads(weight, MIXER_HEAD_SIZE, width)).astype(jnp.bfloat16)
    state_ref[...] += dot_first(b_ref[...].astype(jnp.bfloat16), weighted)
    log_ref[...] += ending


def part(projected, start, width, order=lambda c: c):
    at = start // width
    return (projected, pl.BlockSpec((BLOCK, width), lambda c: (order(c), at)))


def run_scan(kernel, chunks, operands, out_shape, out_specs, flops, name, scratch=(), after=()):
    count = len(operands)
    operands = operands + [(array, pl.BlockSpec(memory_space=pl.ANY)) for array in after]

    def call(*refs):
        kernel(*refs[:count], *refs[count + len(after) :])

    return pl.pallas_call(
        call,
        grid=(chunks,),
        out_shape=out_shape,
        in_specs=[spec for _, spec in operands],
        out_specs=out_specs,
        scratch_shapes=list(scratch),
        compiler_params=compiler_params(),
        cost_estimate=pl.CostEstimate(
            flops=flops, bytes_accessed=8_000_000, transcendentals=1_000_000
        ),
        name=name,
    )(*[array for array, _ in operands])


def whole(array):
    return (array, pl.BlockSpec(array.shape, lambda c: (0,) * array.ndim))


def scan_first(at, bias, rate):
    rows, lanes = (at["x"][0].shape[0], bias.shape[1])
    chunks = rows // BLOCK
    back = lambda c: chunks - 1 - c
    width, state_size = (at["x"][2], at["b"][2])
    by_chunk = pl.BlockSpec((BLOCK, lanes), lambda c: (back(c), 0))
    across = pl.BlockSpec((8, BLOCK), lambda c: (0, back(c)))
    shape = lambda *sizes: jax.ShapeDtypeStruct(sizes, jnp.float32)
    return run_scan(
        scan_first_kernel,
        chunks,
        [
            part(*at["misc"], back),
            whole(bias),
            whole(rate),
            part(*at["x"], back),
            part(*at["b"], back),
        ],
        (
            shape(rows, lanes),
            shape(rows, lanes),
            shape(8, rows),
            shape(8, rows),
            shape(state_size, width),
            shape(1, lanes),
        ),
        (
            by_chunk,
            by_chunk,
            across,
            across,
            pl.BlockSpec((state_size, width), lambda c: (0, 0)),
            pl.BlockSpec((1, lanes), lambda c: (0, 0)),
        ),
        1_000_000_000,
        "scan_first",
    )


def chained(refs, width):
    state = jnp.zeros((refs[0].shape[0] - 16, width), jnp.float32)
    for ref in reversed(refs):
        logs = ref[-16:, :LANES].astype(jnp.float32)
        decay = jnp.exp(jnp.sum(logs[:3], axis=0, keepdims=True))
        state = ref[:-16].astype(jnp.float32) + spread_heads(decay, MIXER_HEAD_SIZE, width) * state
    return state


def scan_kernel(
    x_ref,
    z_ref,
    b_ref,
    c_ref,
    delta_ref,
    cum_ref,
    delta_row_ref,
    cum_row_ref,
    near_ref,
    next_ref,
    far_ref,
    skip_ref,
    scanned_ref,
    gated_ref,
    states_ref,
    state_ref,
):
    @pl.when(pl.program_id(0) == 0)
    def _():
        state_ref[...] = chained((near_ref, next_ref, far_ref), x_ref.shape[1])

    head_size = MIXER_HEAD_SIZE
    pair = 2 * head_size
    size, width = x_ref.shape
    state = state_ref[...]
    states_ref[0] = state
    delta, cumulative = (delta_ref[...], cum_ref[...])
    delta_row, cum_row = (delta_row_ref[...], cum_row_ref[...])
    bmat, cmat = (b_ref[...].astype(jnp.bfloat16), c_ref[...].astype(jnp.bfloat16))
    x_all = x_ref[...].astype(jnp.bfloat16)
    inner = dot_last(cmat, bmat)
    row = lax.broadcasted_iota(jnp.int32, (size, size), 0)
    column = lax.broadcasted_iota(jnp.int32, (size, size), 1)
    allowed = row >= column
    lane = lax.broadcasted_iota(jnp.int32, (size, pair), 1)
    from_state = mul(cmat, state.astype(jnp.bfloat16))
    spread = spread_heads(jnp.exp(cumulative), head_size, width)
    for first in range(0, width // head_size, 2):
        here = slice(first * head_size, first * head_size + pair)
        x_pair = x_all[:, here]
        total = from_state[:, here] * spread[:, here]
        total += skip_ref[:, here] * x_pair.astype(jnp.float32)
        for head in (first, first + 1):
            gap = cumulative[:, head : head + 1] - cum_row[head : head + 1, :]
            decay = jnp.exp(jnp.where(allowed, gap, -1e30))
            mixing = inner * decay * delta_row[head : head + 1, :]
            x_head = jnp.where((lane >= head_size) == (head > first), x_pair, 0.0)
            total += mul(mixing.astype(jnp.bfloat16), x_head.astype(jnp.bfloat16))
        scanned_ref[:, here] = total
        gate = z_ref[:, here]
        gated_ref[:, here] = (total * (gate * jax.nn.sigmoid(gate))).astype(jnp.bfloat16)
    ending = cumulative[-1:, :]
    weight = spread_heads(jnp.exp(ending - cumulative) * delta, head_size, width)
    weighted = (x_all.astype(jnp.float32) * weight).astype(jnp.bfloat16)
    state_ref[...] = state * spread[-1:, :] + dot_first(bmat, weighted)


def scan(at, delta, cumulative, delta_row, cum_row, entry, skip, after):
    rows = delta.shape[0]
    state_size, width = (at["b"][2], at["x"][2])
    chunks = rows // BLOCK
    by_chunk = pl.BlockSpec((BLOCK, width), lambda c: (c, 0))
    lanes = delta.shape[1]
    across = pl.BlockSpec((8, BLOCK), lambda c: (0, c))
    return run_scan(
        scan_kernel,
        chunks,
        [
            part(*at["x"]),
            part(*at["z"]),
            part(*at["b"]),
            part(*at["c"]),
            part(delta, 0, lanes),
            part(cumulative, 0, lanes),
            (delta_row, across),
            (cum_row, across),
            *[whole(packed) for packed in entry],
            whole(skip),
        ],
        (
            jax.ShapeDtypeStruct((rows, width), jnp.float32),
            jax.ShapeDtypeStruct((rows, width), jnp.bfloat16),
            jax.ShapeDtypeStruct((chunks, state_size, width), jnp.float32),
        ),
        (by_chunk, by_chunk, pl.BlockSpec((1, state_size, width), lambda c: (c, 0, 0))),
        3_000_000_000,
        "scan",
        [pltpu.VMEM((state_size, width), jnp.float32)],
        after,
    )


def scan_back_first_kernel(
    grad_ref, z_ref, scanned_ref, c_ref, cum_ref, d_scanned_ref, d_gate_ref, state_ref, log_ref
):
    @pl.when(pl.program_id(0) == 0)
    def _():
        state_ref[...] = jnp.zeros_like(state_ref)
        log_ref[...] = jnp.zeros_like(log_ref)

    gate = z_ref[...]
    chance = jax.nn.sigmoid(gate)
    grad = grad_ref[:, : z_ref.shape[1]].astype(jnp.float32)
    d_scanned = grad * (gate * chance)
    d_scanned_ref[...] = d_scanned
    d_gate_ref[...] = (
        grad * scanned_ref[...] * (chance * (1.0 + gate * (1.0 - chance)))
    ).astype(jnp.bfloat16)
    cumulative = cum_ref[...]
    decay = spread_heads(jnp.exp(cumulative + log_ref[...]), MIXER_HEAD_SIZE, z_ref.shape[1])
    state_ref[...] += dot_first(
        c_ref[...].astype(jnp.bfloat16), (d_scanned * decay).astype(jnp.bfloat16)
    )
    log_ref[...] += cumulative[-1:, :]


def scan_back_first(grads, at, scanned, cumulative):
    rows, width = scanned.shape
    state_size, lanes = (at["c"][2], cumulative.shape[1])
    by_chunk = pl.BlockSpec((BLOCK, width), lambda c: (c, 0))
    return run_scan(
        scan_back_first_kernel,
        rows // BLOCK,
        [
            part(grads, 0, grads.shape[1]),
            part(*at["z"]),
            part(scanned, 0, width),
            part(*at["c"]),
            part(cumulative, 0, lanes),
        ],
        (
            jax.ShapeDtypeStruct((rows, width), jnp.float32),
            jax.ShapeDtypeStruct((rows, width), jnp.bfloat16),
            jax.ShapeDtypeStruct((state_size, width), jnp.float32),
        ),
        (by_chunk, by_chunk, pl.BlockSpec((state_size, width), lambda c: (0, 0))),
        1_000_000_000,
        "scan_back_first",
        [pltpu.VMEM((1, lanes), jnp.float32)],
    )


def scan_back_kernel(
    x_ref,
    grad_ref,
    b_ref,
    c_ref,
    pre_ref,
    bias_ref,
    rate_ref,
    delta_ref,
    cum_ref,
    cum_row_ref,
    states_ref,
    near_ref,
    next_ref,
    far_ref,
    skip_ref,
    d_x_ref,
    d_b_ref,
    d_c_ref,
    d_pre_ref,
    sums_ref,
    state_ref,
):
    @pl.when(pl.program_id(0) == 0)
    def _():
        state_ref[...] = chained((near_ref, next_ref, far_ref), x_ref.shape[1])
        sums_ref[...] = jnp.zeros_like(sums_ref)

    head_size = MIXER_HEAD_SIZE
    pair = 2 * head_size
    size, width = x_ref.shape
    lanes = delta_ref.shape[1]
    low = jnp.bfloat16
    delta, cumulative, cum_row = (delta_ref[...], cum_ref[...], cum_row_ref[...])
    bmat, cmat = (b_ref[...].astype(low), c_ref[...].astype(low))
    x_all = x_ref[...].astype(low)
    x_single = x_all.astype(jnp.float32)
    grad = grad_ref[...]
    grad_low = grad.astype(low)
    state = states_ref[0]
    state_low = state.astype(low)
    after = state_ref[...]
    after_low = after.astype(low)
    ending = cumulative[-1:, :]
    row = lax.broadcasted_iota(jnp.int32, (size, size), 0)
    column = lax.broadcasted_iota(jnp.int32, (size, size), 1)
    later = column >= row
    before = (row > column).astype(low)
    onward = later.astype(low)
    lane = lax.broadcasted_iota(jnp.int32, (size, pair), 1)
    head_lane = lax.broadcasted_iota(jnp.int32, (size, lanes), 1)
    sum_heads = head_ones(width, head_size, lanes, low)

    inner = dot_last(bmat, cmat)
    from_after = mul(bmat, after_low)
    weight = jnp.exp(ending - cumulative)
    spread_weight = spread_heads(weight * delta, head_size, width)
    spread = spread_heads(jnp.exp(cumulative), head_size, width)
    to_end = mul((x_single * from_after).astype(low), sum_heads)
    through = jnp.exp(cumulative) * mul((grad * mul(cmat, state_low)).astype(low), sum_heads)
    carried = jnp.sum(state * after, axis=0, keepdims=True) * spread[-1:, :]
    carried = precise(carried, sum_heads.astype(jnp.float32))
    d_delta = weight * to_end
    d_log = (
        mul(onward, through.astype(low)) + mul(before, (d_delta * delta).astype(low)) + carried
    )

    d_inner = jnp.zeros((size, size), jnp.float32)
    for first in range(0, width // head_size, 2):
        here = slice(first * head_size, first * head_size + pair)
        x_pair, grad_pair = (x_all[:, here], grad_low[:, here])
        d_x = from_after[:, here] * spread_weight[:, here] + skip_ref[:, here] * grad[:, here]
        for head in (first, first + 1):
            mine = (lane >= head_size) == (head > first)
            gap = cum_row[head : head + 1, :] - cumulative[:, head : head + 1]
            decay = jnp.exp(jnp.where(later, gap, -1e30))
            delta_column = delta[:, head : head + 1]
            d_mixing = dot_last(jnp.where(mine, x_pair, 0.0).astype(low), grad_pair) * decay
            d_inner += d_mixing * delta_column
            flow = d_mixing * inner
            mixing = inner * decay * delta_column
            d_x += mul(mixing.astype(low), jnp.where(mine, grad_pair, 0.0).astype(low))
            d_delta_head = jnp.sum(flow, axis=1, keepdims=True)
            passing = mul(before, (flow * delta_column).astype(low))
            d_log_head = jnp.sum(jnp.where(later, passing, 0.0), axis=1, keepdims=True)
            d_delta += jnp.where(head_lane == head, d_delta_head, 0.0)
            d_log += jnp.where(head_lane == head, d_log_head, 0.0)
        d_x_ref[:, here] = d_x.astype(low)

    d_inner_low = d_inner.astype(low)
    scaled_grad = (grad * spread).astype(low)
    weighted = (x_single * spread_weight).astype(low)
    d_b_ref[...] = (mul(d_inner_low, cmat) + dot_last(weighted, after_low)).astype(low)
    d_c_ref[...] = (dot_first(d_inner_low, bmat) + dot_last(scaled_grad, state_low)).astype(low)
    state_ref[...] = after * spread[-1:, :] + dot_first(cmat, scaled_grad)
    rate = rate_ref[...]
    d_pre = (d_delta - d_log * rate) * jax.nn.sigmoid(pre_ref[...] + bias_ref[...])
    d_pre = jnp.where(head_lane < width // head_size, d_pre, 0.0)
    d_pre_ref[...] = d_pre.astype(low)
    skip_sum = precise(
        jnp.sum(grad * x_single, axis=0, keepdims=True), sum_heads.astype(jnp.float32)
    )
    sums_ref[0:1, :] += jnp.sum(d_pre, axis=0, keepdims=True)
    sums_ref[1:2, :] += jnp.sum(d_log * (-delta * rate), axis=0, keepdims=True)
    sums_ref[2:3, :] += skip_sum


def scan_back(
    at, d_scanned, bias, rate, delta, cumulative, cum_row, states, entry, skip, after
):
    rows, width = d_scanned.shape
    state_size, lanes = (at["b"][2], delta.shape[1])
    chunks = rows // BLOCK
    back = lambda c: chunks - 1 - c
    by_chunk = lambda columns: pl.BlockSpec((BLOCK, columns), lambda c: (back(c), 0))
    shape = lambda columns: jax.ShapeDtypeStruct((rows, columns), jnp.bfloat16)
    return run_scan(
        scan_back_kernel,
        chunks,
        [
            part(*at["x"], back),
            part(d_scanned, 0, width, back),
            part(*at["b"], back),
            part(*at["c"], back),
            part(*at["misc"], back),
            whole(bias),
            whole(rate),
            part(delta, 0, lanes, back),
            part(cumulative, 0, lanes, back),
            (cum_row, pl.BlockSpec((8, BLOCK), lambda c: (0, back(c)))),
            (states, pl.BlockSpec((1, state_size, width), lambda c: (back(c), 0, 0))),
            *[whole(packed) for packed in entry],
            whole(skip),
        ],
        (
            shape(width),
            shape(state_size),
            shape(state_size),
            shape(lanes),
            jax.ShapeDtypeStruct((8, lanes), jnp.float32),
        ),
        (
            by_chunk(width),
            by_chunk(state_size),
            by_chunk(state_size),
            by_chunk(lanes),
            pl.BlockSpec((8, lanes), lambda c: (0, 0)),
        ),
        6_000_000_000,
        "scan_back",
        [pltpu.VMEM((state_size, width), jnp.float32)],
        after,
    )


def on_heads(value, move):
    devices = lax.axis_size("heads")
    pairs = []
    for at in range(devices):
        z, core = move(at // 2, at % 2)
        pairs.append((at, 2 * (z % (devices // 2)) + core))
    return lax.ppermute(value, "heads", pairs)


def to_partner(value):
    return on_heads(value, lambda z, core: (z, 1 - core))


def along(value):
    return on_heads(value, lambda z, core: (z + 1 - 2 * core, core))


def against(value):
    return on_heads(value, lambda z, core: (z - 1 + 2 * core, core))


def chunk_ranks():
    devices = lax.axis_size("heads")
    z, core = (lax.axis_index("heads") // 2, lax.axis_index("heads") % 2)
    step, other = (1 - 2 * core, 1 - core)
    owners = (
        (z, core),
        (z + 2, core),
        (z - step, core),
        (z - step, other),
        (z, other),
        (z + 2, other),
        (z + step, other),
        (z + step, core),
    )
    return jnp.stack([2 * ((at + devices) % (devices // 2)) + side for at, side in owners])


def gather_rows(own):
    partner = to_partner(own)
    near = along(own)
    near_other = along(partner)
    far = along(near)
    mine = (own, far, near, near_other)
    theirs = (partner, to_partner(far), to_partner(near), to_partner(near_other))
    return jnp.concatenate(mine + theirs, axis=0)


def scatter_rows(product, half):
    chunk = half // 4
    got = to_partner(product(slice(half, 2 * half)).astype(jnp.bfloat16))
    summed = product(slice(0, half)) + got.astype(jnp.float32)
    low = summed[chunk:].astype(jnp.bfloat16)
    far = against(low[:chunk])
    near_other = against(low[2 * chunk :])
    near = against((low[chunk : 2 * chunk].astype(jnp.float32) + far).astype(jnp.bfloat16))
    return summed[:chunk] + near.astype(jnp.float32) + to_partner(near_other).astype(jnp.float32)


def across(value, bit):
    devices = lax.axis_size("heads")
    return lax.ppermute(value, "heads", [(at, at ^ bit) for at in range(devices)])


def gather_small(value):
    for bit in (1, 2, 4):
        value = jnp.concatenate([value, across(value, bit)], axis=0)
    return value


def scatter_small(value):
    for bit in (4, 2, 1):
        half = value.shape[0] // 2
        got = across(value[half:].astype(jnp.bfloat16), bit)
        value = value[:half].astype(jnp.float32) + got.astype(jnp.float32)
    return value


def on_blocks(value, step):
    devices = lax.axis_size("blk")
    pairs = [(at, at + step) for at in range(devices) if 0 <= at + step < devices]
    return lax.ppermute(value, "blk", pairs)


def from_earlier(value, step=1):
    return tuple(on_blocks(value, distance * step) for distance in (1, 2, 3))


def pack_state(state, log_total):
    high = log_total.astype(jnp.bfloat16)
    rest = log_total - high.astype(jnp.float32)
    middle = rest.astype(jnp.bfloat16)
    low = (rest - middle.astype(jnp.float32)).astype(jnp.bfloat16)
    logs = jnp.concatenate([high, middle, low], axis=0)
    logs = jnp.pad(logs, ((0, 16 - logs.shape[0]), (0, state.shape[1] - logs.shape[1])))
    return jnp.concatenate([state.astype(jnp.bfloat16), logs], axis=0)


def sum_blocks(value):
    for axis in ("dp", "blk"):
        for bit in (1, 2):
            value = value + lax.ppermute(
                value, axis, [(at, at ^ bit) for at in range(lax.axis_size(axis))]
            )
    return value


def weight_sum(grads):
    return lax.psum_scatter(grads, ("dp", "blk"), scatter_dimension=0, tiled=True)


def split_columns(value_in, widths):
    pieces, start = [], 0
    for width in widths:
        pieces.append(value_in[:, start : start + width])
        start += width
    return pieces


def inverse_rms(rows_in):
    return lax.rsqrt(jnp.mean(rows_in * rows_in, axis=-1, keepdims=True) + norm_eps)


def norm_back(rows_in, gain_in, cotangent):
    inverse = inverse_rms(rows_in)
    scaled = rows_in * inverse
    weighted = cotangent * gain_in
    return inverse * (weighted - scaled * jnp.mean(weighted * scaled, axis=-1, keepdims=True))


def shards(
    x_in,
    out_grad,
    norm_one,
    w_query,
    w_key,
    w_value,
    output_gate_weight,
    mixer_input_weight,
    w_delta,
    w_bmat,
    w_cmat,
    delta_bias,
    decay_log,
    skip_gain,
    w_attn_out,
    mixer_output_weight,
    norm_two,
    w_gate,
    w_up,
    w_down,
):
    heads_count = lax.axis_size("heads")
    head_rank = lax.axis_index("heads")
    core = head_rank % 2
    block_rank = lax.axis_index("blk")
    rank = block_rank.astype(jnp.int32)[None]
    own_rows = x_in.shape[0]
    span_length = own_rows * heads_count
    half_span = span_length // 2
    span_start = block_rank * span_length
    query_width = w_query.shape[1]
    mixer_width = mixer_input_weight.shape[1]
    heads = mixer_width // MIXER_HEAD_SIZE
    state_size = w_bmat.shape[1]
    hidden_width = w_gate.shape[1]
    rows_of = w_query.shape[0]
    kv_index = head_rank * (query_width // HD) // (QH // KVH)
    kv_width = KVH * HD
    low = jnp.bfloat16
    ranks = chunk_ranks().astype(jnp.int32)
    turns = (head_rank ^ jnp.arange(heads_count)).astype(jnp.int32)

    gains = jnp.stack([norm_one, norm_two], axis=1)
    gains = jnp.pad(gains, ((0, 0), (0, LANES - 2)))
    shared = jnp.concatenate([w_key, w_value, w_bmat, w_cmat, gains], axis=1)
    shared = reorder(turns, [gather_small(shared)], inverse=True)
    key_part = lax.dynamic_slice_in_dim(shared, kv_index * HD, HD, 1)
    value_part = lax.dynamic_slice_in_dim(shared, kv_width + kv_index * HD, HD, 1)
    state_part = shared[:, 2 * kv_width : 2 * kv_width + 2 * state_size]
    gain_part = shared[:, 2 * kv_width + 2 * state_size :][:, :2]
    misc_part = jnp.concatenate(
        [w_delta, gain_part, jnp.zeros((rows_of, LANES - heads - 2), low)], axis=1
    )
    in_names = ("z", "x", "query", "b", "c", "misc", "key", "value")
    in_widths = (mixer_width, mixer_width, query_width, state_size, state_size, LANES, HD, HD)
    starts = [sum(in_widths[:k]) for k in range(len(in_widths))]
    at = dict(zip(in_names, zip(starts, in_widths)))
    in_first = jnp.concatenate([output_gate_weight, mixer_input_weight, w_query], axis=1)
    in_second = jnp.concatenate([state_part, misc_part, key_part, value_part], axis=1)
    in_own = jnp.concatenate([in_first, in_second], axis=1)
    in_full = lax.all_gather(in_own, ("dp", "blk"), axis=0, tiled=True)
    x_float = x_in.astype(jnp.float32)
    zero = 0.0 * in_own[0, 0]
    x_span = gather_rows(x_in + zero)
    ffn_grad = gather_rows(out_grad + 0.0 * x_span[0, 0])
    mix_own = pack((mixer_output_weight, w_attn_out), (True, True), x_span)
    ffn_own = pack((w_gate, w_up, w_down), (False, False, True), mix_own)
    mix_t = lax.all_gather(mix_own, ("dp", "blk"), axis=0, tiled=True)
    ffn_full = lax.all_gather(ffn_own, ("dp", "blk"), axis=0, tiled=True)
    mixed_width = query_width + mixer_width
    gate_full, up_full, down_t = split_columns(ffn_full, (hidden_width,) * 3)
    positions = (span_start + jnp.arange(span_length)).astype(jnp.float32)
    freqs = rope_base ** (-2.0 * jnp.arange(HD // 2, dtype=jnp.float32) / HD)
    angles = positions[:, None] * freqs[None, :]
    cosine, sine = (jnp.cos(angles), jnp.sin(angles))
    cosine = jnp.concatenate([cosine, cosine], axis=1)
    sine = jnp.concatenate([-sine, sine], axis=1)
    normed_ordered, queries, keys_values, gain_rows = enter(
        ranks, jnp.full((1,), heads, jnp.int32), x_span, in_full, at, cosine, sine, [ffn_grad, ffn_own]
    )
    gain_one, gain_two = (gain_rows[0:1], gain_rows[1:2])
    mine = lax.dynamic_slice_in_dim(keys_values, core * half_span, half_span, 0)
    pieces = []
    for piece in from_earlier(mine):
        pieces += [piece, to_partner(piece)]
    gate_raw = simple_product(normed_ordered, in_full[:, :mixer_width])
    x_raw = simple_product(normed_ordered, in_full[:, mixer_width : 2 * mixer_width])
    state_raw = simple_product(normed_ordered, in_full[:, at["b"][0] : at["key"][0]])
    raw = {
        "z": (gate_raw, 0, mixer_width),
        "x": (x_raw, 0, mixer_width),
        "b": (state_raw, 0, state_size),
        "c": (state_raw, state_size, state_size),
        "misc": (state_raw, 2 * state_size, LANES),
    }

    pad_lanes = lambda vector: jnp.pad(vector, (0, LANES - heads))[None]
    bias, rate = (pad_lanes(delta_bias), pad_lanes(jnp.exp(decay_log)))
    skip = jnp.repeat(skip_gain, MIXER_HEAD_SIZE)[None]
    delta, cumulative, delta_row, cum_row, local_state, local_log = scan_first(raw, bias, rate)
    entry_states = from_earlier(pack_state(local_state, local_log))
    attended, attn_part, log_totals = attend(rank, queries, keys_values, pieces)
    scanned, gated, states = scan(
        raw, delta, cumulative, delta_row, cum_row, entry_states, skip, [attn_part]
    )
    mixers = reorder(ranks, [gated, attn_part])
    middle = x_float + scatter_rows(lambda rows: dot_last(mixers[rows], mix_t), half_span)
    middle_scaled = middle * inverse_rms(middle)
    normed_two = gather_rows((middle_scaled * gain_two).astype(low))
    ffn_gate = simple_product(normed_two, gate_full)
    ffn_up = simple_product(normed_two, up_full)
    ffn_sig = jax.nn.sigmoid(ffn_gate)
    hidden = (ffn_gate * ffn_sig * ffn_up).astype(low)

    d_hidden = simple_product(ffn_grad, down_t)
    d_ffn_gate = (d_hidden * ffn_up * (ffn_sig * (1.0 + ffn_gate * (1.0 - ffn_sig)))).astype(low)
    d_ffn_up = (d_hidden * (ffn_gate * ffn_sig)).astype(low)
    d_normed_two = scatter_rows(
        lambda rows: dot_last(d_ffn_gate[rows], gate_full) + dot_last(d_ffn_up[rows], up_full),
        half_span,
    )
    ffn_grad_t, normed_t = (ffn_grad.T, normed_ordered.T)
    ffn_grads = weight_grads(
        [(normed_two, [d_ffn_gate, d_ffn_up], False), (ffn_grad_t, [hidden], True)],
        3 * hidden_width,
        after=[normed_t],
    )
    ffn_sums = weight_sum(ffn_grads).astype(jnp.float32)
    grad_gate, grad_up, grad_down_t = split_columns(ffn_sums, (hidden_width,) * 3)
    grad_two_part = jnp.sum(grad_gate * w_gate + grad_up * w_up, axis=1, keepdims=True)
    gain_own = gain_part.astype(jnp.float32)
    grad_two_part = grad_two_part / gain_own[:, 1:2]
    d_middle = out_grad.astype(jnp.float32) + norm_back(middle, gain_two, d_normed_two)
    mix_grad = gather_rows(d_middle.astype(low))
    d_mixers = reorder(
        ranks, [simple_product(mix_grad, mix_t).astype(low)], inverse=True, after=[ffn_grads]
    )
    d_scanned, d_gate_z, d_entry = scan_back_first(d_mixers, raw, scanned, cumulative)
    d_entry = pack_state(d_entry, local_log)
    after_states = from_earlier(d_entry, -1)
    mix_width = mixed_width + mixer_width
    all_width = mixed_width + in_own.shape[1]
    mix_grads = weight_grads(
        [(mix_grad, [mixers], False), (normed_t, [d_gate_z], True)], all_width, after=[d_entry]
    )
    d_query, d_own, d_far = attend_back(
        rank, queries, keys_values, pieces, attended, log_totals, d_mixers, cosine, sine, [mix_grads, *after_states]
    )
    d_ssm_in, d_bmat, d_cmat, d_pre, sums = scan_back(
        raw,
        d_scanned,
        bias,
        rate,
        delta,
        cumulative,
        cum_row,
        states,
        after_states,
        skip,
        [d_query],
    )
    far_half = d_far.shape[0] // 2
    d_mine = lax.dynamic_slice_in_dim(d_own, core * half_span, half_span, 0)
    d_theirs = lax.dynamic_slice_in_dim(d_own, (1 - core) * half_span, half_span, 0)
    d_mine = d_mine + to_partner(d_theirs.astype(low)).astype(jnp.float32)
    d_far = d_far[:far_half].astype(jnp.float32) + to_partner(d_far[far_half:]).astype(jnp.float32)
    d_one, d_two, d_three = (
        d_far[k * half_span : (k + 1) * half_span] for k in range(d_far.shape[0] // half_span)
    )
    d_one = d_one + on_blocks(d_two.astype(low), -1).astype(jnp.float32)
    d_mine = d_mine + on_blocks(d_one.astype(low), -1).astype(jnp.float32)
    d_mine = d_mine + on_blocks(d_three.astype(low), -3).astype(jnp.float32)
    half_cos = lax.dynamic_slice_in_dim(cosine, core * half_span, half_span, 0)
    half_sin = lax.dynamic_slice_in_dim(sine, core * half_span, half_span, 0)
    d_key = d_mine[:, :HD]
    d_key = d_key * half_cos - jnp.roll(d_key, HD // 2, axis=1) * half_sin
    d_mine = jnp.concatenate([d_key, d_mine[:, HD:]], axis=1).astype(low)
    d_keys_values = lax.dynamic_update_slice_in_dim(
        jnp.zeros((span_length, 2 * HD), low), d_mine, core * half_span, 0
    )

    scan_rights = [d_ssm_in, d_bmat, d_cmat, d_pre]
    in_grads = weight_grads([(normed_t, scan_rights, True)], all_width, mix_width, mix_grads)
    late_rights = [d_keys_values, d_query]
    late_start = mix_width + sum(array.shape[1] for array in scan_rights)
    in_grads = weight_grads([(normed_t, late_rights, True)], all_width, late_start, in_grads)
    in_sums = weight_sum(in_grads)
    d_projected = reorder(
        ranks,
        [d_gate_z, d_ssm_in, d_query, d_bmat, d_cmat, d_pre, d_keys_values],
        after=[in_grads],
    )
    d_normed = scatter_rows(lambda rows: dot_last(d_projected[rows], in_full), half_span)
    input_grad = d_middle + norm_back(x_float, gain_one, d_normed)
    ffn_out = scatter_rows(lambda rows: dot_last(hidden[rows], down_t), half_span)
    activations = (middle + ffn_out).astype(low)
    sums_names = ("ssm_out", "attn_out", "z", "x", "b", "c", "misc", "key", "value", "query")
    sums_widths = [mixer_width, query_width] + [at[name][1] for name in sums_names[2:]]
    sums_starts = [sum(sums_widths[:k]) for k in range(len(sums_widths))]
    sums_at = dict(zip(sums_names, zip(sums_starts, sums_widths)))
    extra = jnp.concatenate([gain_own[:, 0:1], grad_two_part], axis=1)
    extra = jnp.pad(extra, ((0, 0), (0, LANES - 2)))
    grad_ssm_out, grad_attn_out, grad_gatez, grad_ssmx, grad_query, misc_sums, shared_parts = finish(
        turns,
        kv_index.astype(jnp.int32)[None],
        in_sums,
        in_own,
        extra,
        at,
        sums_at,
    )
    shared_sums = scatter_small(shared_parts)
    grad_key, grad_value, grad_bmat, grad_cmat, gain_sums = split_columns(
        shared_sums, (kv_width, kv_width, state_size, state_size, LANES)
    )
    small_sums = sum_blocks(sums)[:, :heads]
    return (
        activations,
        input_grad,
        gain_sums[:, 0],
        grad_query,
        grad_key,
        grad_value,
        grad_gatez,
        grad_ssmx,
        misc_sums[:, :heads],
        grad_bmat,
        grad_cmat,
        small_sums[0],
        small_sums[1],
        small_sums[2],
        grad_attn_out,
        grad_ssm_out,
        gain_sums[:, 1],
        grad_gate,
        grad_up,
        grad_down_t.T,
    )


def solution(mesh):
    placed = (
        P(("dp", "blk", "heads"), None),
        P(("dp", "blk", "heads"), None),
        P(("dp", "blk", "heads")),
        P(("dp", "blk"), "heads"),
        P(("dp", "blk", "heads"), None),
        P(("dp", "blk", "heads"), None),
        P(("dp", "blk"), "heads"),
        P(("dp", "blk"), "heads"),
        P(("dp", "blk"), "heads"),
        P(("dp", "blk", "heads"), None),
        P(("dp", "blk", "heads"), None),
        P("heads"),
        P("heads"),
        P("heads"),
        P("heads", ("dp", "blk")),
        P("heads", ("dp", "blk")),
        P(("dp", "blk", "heads")),
        P(("dp", "blk"), "heads"),
        P(("dp", "blk"), "heads"),
        P("heads", ("dp", "blk")),
    )
    return jax.shard_map(
        shards,
        mesh=mesh,
        in_specs=placed,
        out_specs=(
            P(("dp", "blk", "heads"), None),
            P(("dp", "blk", "heads"), None),
            P(("dp", "blk", "heads")),
            P(("dp", "blk"), "heads"),
            P(("dp", "blk", "heads"), None),
            P(("dp", "blk", "heads"), None),
            P(("dp", "blk"), "heads"),
            P(("dp", "blk"), "heads"),
            P(("dp", "blk"), "heads"),
            P(("dp", "blk", "heads"), None),
            P(("dp", "blk", "heads"), None),
            P("heads"),
            P("heads"),
            P("heads"),
            P("heads", ("dp", "blk")),
            P("heads", ("dp", "blk")),
            P(("dp", "blk", "heads")),
            P(("dp", "blk"), "heads"),
            P(("dp", "blk"), "heads"),
            P("heads", ("dp", "blk")),
        ),
        check_vma=False,
    )
```

```python
import functools

import jax
import jax.numpy as jnp
from jax import lax
from jax.experimental import pallas as pl
from jax.experimental.pallas import tpu as pltpu
from jax.sharding import PartitionSpec as P

QH = 8
KVH = 2
HD = 128
MIXER_HEAD_SIZE = 64
BLOCK = 256
LANES = 128
LOG2_E = 1.4426950408889634


HIGH_PRECISION = lax.Precision.HIGHEST
norm_eps = 1e-05
rope_base = 100000000000.0


def simple_product(left_side, right_side):
    return jnp.dot(left_side, right_side, preferred_element_type=jnp.float32)


def dot_last(left_side, right_side):
    return lax.dot_general(
        left_side, right_side, (((1,), (1,)), ((), ())), preferred_element_type=jnp.float32
    )


def dot_first(left_side, right_side):
    return lax.dot_general(
        left_side, right_side, (((0,), (0,)), ((), ())), preferred_element_type=jnp.float32
    )


def compiler_params(mebibytes=20):
    return pltpu.CompilerParams(vmem_limit_bytes=mebibytes * 1024 * 1024)


def small_cost():
    return pl.CostEstimate(flops=1000, bytes_accessed=1000, transcendentals=0)


def in_vmem(count):
    return [pl.BlockSpec(memory_space=pltpu.VMEM)] * count


def mul(left_side, right_side):
    return jnp.dot(left_side, right_side, preferred_element_type=jnp.float32)


def tile_scores(key_rows, query_rows, head_size):
    return dot_last(key_rows, query_rows) * (head_size**-0.5 * LOG2_E)


def causal(scores):
    key_at = lax.broadcasted_iota(jnp.int32, scores.shape, 0)
    query_at = lax.broadcasted_iota(jnp.int32, scores.shape, 1)
    return jnp.where(key_at <= query_at, scores, -1e30)


def enter_kernel(
    ranks_ref,
    heads_ref,
    x_ref,
    misc_ref,
    key_ref,
    value_ref,
    w_query_ref,
    cos_ref,
    sin_ref,
    _,
    __,
    ordered_ref,
    query_ref,
    kv_ref,
    gains_ref,
):
    head_size = query_ref.shape[1]

    @pl.when(pl.program_id(0) == 0)
    def _():
        lane = lax.broadcasted_iota(jnp.int32, misc_ref.shape, 1)
        for k in range(2):
            column = jnp.where(lane == heads_ref[0] + k, misc_ref[...].astype(jnp.float32), 0.0)
            gains_ref[k : k + 1, :] = jnp.sum(column.T, axis=0, keepdims=True)

    cosine, sine = (cos_ref[...], sin_ref[...])

    def turn(value):
        return (value * cosine + pltpu.roll(value, head_size // 2, 1) * sine).astype(jnp.bfloat16)

    rows = x_ref[...].astype(jnp.float32)
    normed = (rows * inverse_rms(rows) * gains_ref[0:1, :]).astype(jnp.bfloat16)
    ordered_ref[...] = normed
    kv_ref[:, :head_size] = turn(mul(normed, key_ref[...]))
    kv_ref[:, head_size:] = mul(normed, value_ref[...]).astype(jnp.bfloat16)
    query_ref[...] = turn(mul(normed, w_query_ref[...]))


def enter(ranks, heads, x_span, in_full, at, cosine, sine, after):
    count = ranks.shape[0]
    rows, width = x_span.shape
    head_size = cosine.shape[1]
    here = lambda columns: pl.BlockSpec((rows // count, columns), lambda k, r, h: (k, 0))
    there = lambda columns: pl.BlockSpec((rows // count, columns), lambda k, r, h: (r[k], 0))
    weight = lambda name: pl.BlockSpec(
        (width, at[name][1]), lambda k, r, h: (0, at[name][0] // at[name][1])
    )
    return pl.pallas_call(
        enter_kernel,
        grid_spec=pltpu.PrefetchScalarGridSpec(
            num_scalar_prefetch=2,
            grid=(count,),
            in_specs=[
                here(width),
                weight("misc"),
                weight("key"),
                weight("value"),
                weight("query"),
                there(head_size),
                there(head_size),
            ]
            + [pl.BlockSpec(memory_space=pl.ANY)] * 2,
            out_specs=(
                there(width),
                there(head_size),
                there(2 * head_size),
                pl.BlockSpec((8, width), lambda k, r, h: (0, 0)),
            ),
        ),
        out_shape=(
            jax.ShapeDtypeStruct((rows, width), jnp.bfloat16),
            jax.ShapeDtypeStruct((rows, head_size), jnp.bfloat16),
            jax.ShapeDtypeStruct((rows, 2 * head_size), jnp.bfloat16),
            jax.ShapeDtypeStruct((8, width), jnp.float32),
        ),
        compiler_params=compiler_params(),
        cost_estimate=small_cost(),
        name="enter",
    )(ranks, heads, x_span, in_full, in_full, in_full, in_full, cosine, sine, *after)


def weight_grads_kernel(*refs, counts):
    out_ref = refs[-1]
    start, used = (0, len(counts))
    for k, count in enumerate(counts):
        left = refs[k][...].T
        for ref in refs[used : used + count]:
            out_ref[:, start : start + ref.shape[1]] = mul(left, ref[...]).astype(jnp.bfloat16)
            start += ref.shape[1]
        used += count


def weight_grads(groups, width, start=0, buffer=None, after=()):
    rights = [right for _, group in groups for right in group]
    columns = sum(right.shape[1] for right in rights)
    depth = rights[0].shape[0]
    rows = groups[0][0].shape[1]
    operands = [left for left, _ in groups] + rights
    count = len(operands)
    extra = list(after) if buffer is None else [buffer] + list(after)

    def call(*refs):
        weight_grads_kernel(
            *refs[:count],
            refs[-1],
            counts=tuple(len(group) for _, group in groups),
        )

    return pl.pallas_call(
        call,
        grid=(rows // BLOCK,),
        out_shape=jax.ShapeDtypeStruct((rows, width), jnp.bfloat16),
        in_specs=[pl.BlockSpec((depth, BLOCK), lambda k: (0, k)) for _ in groups]
        + [pl.BlockSpec(right.shape, lambda k: (0, 0)) for right in rights]
        + [pl.BlockSpec(memory_space=pl.ANY)] * len(extra),
        out_specs=pl.BlockSpec(
            (pl.Element(BLOCK), pl.Element(columns)), lambda k: (k * BLOCK, start)
        ),
        input_output_aliases={} if buffer is None else {count: 0},
        compiler_params=compiler_params(),
        cost_estimate=pl.CostEstimate(
            flops=2 * rows * depth * columns,
            bytes_accessed=2 * (depth * (2 * rows + columns) + rows * columns),
            transcendentals=0,
        ),
        name="weight_grads",
    )(*operands, *extra)


def pack_kernel(*refs, turned):
    out_ref = refs[-1]
    start = 0
    for ref, turn in zip(refs, turned):
        piece = ref[...].T if turn else ref[...]
        out_ref[:, start : start + piece.shape[1]] = piece
        start += piece.shape[1]


def pack(pieces, turned, after):
    sizes = [piece.shape[::-1] if turn else piece.shape for piece, turn in zip(pieces, turned)]
    return pl.pallas_call(
        functools.partial(pack_kernel, turned=turned),
        out_shape=jax.ShapeDtypeStruct(
            (sizes[0][0], sum(size[1] for size in sizes)), jnp.bfloat16
        ),
        in_specs=in_vmem(len(pieces)) + [pl.BlockSpec(memory_space=pl.ANY)],
        out_specs=pl.BlockSpec(memory_space=pltpu.VMEM),
        compiler_params=compiler_params(),
        name="pack",
    )(*pieces, after)


def finish_kernel(
    ranks_ref,
    kv_ref,
    sums_ref,
    weight_ref,
    extra_ref,
    ssm_out_ref,
    attn_out_ref,
    gate_ref,
    ssm_ref,
    query_ref,
    misc_ref,
    shared_ref,
    whole_ref,
    *,
    at,
    sums_at,
):
    def of(name):
        start, size = sums_at[name]
        return sums_ref[:, start : start + size].astype(jnp.float32)

    ssm_out_ref[...] = of("ssm_out").T
    attn_out_ref[...] = of("attn_out").T
    gate_ref[...] = of("z")
    ssm_ref[...] = of("x")
    query_ref[...] = of("query")
    misc_ref[...] = of("misc")
    total = 0.0
    for name, (start, size) in at.items():
        product = of(name) * weight_ref[:, start : start + size].astype(jnp.float32)
        total += jnp.sum(product, axis=1, keepdims=True)
    total = total / extra_ref[:, 0:1]
    lane = lax.broadcasted_iota(jnp.int32, misc_ref.shape, 1)
    gains = jnp.where(lane == 0, total, jnp.where(lane == 1, extra_ref[:, 1:2], 0.0))
    zero = jnp.zeros_like(gains)
    first = kv_ref[0] == 0
    key, value = (of("key"), of("value"))
    pieces = (
        jnp.where(first, key, zero),
        jnp.where(first, zero, key),
        jnp.where(first, value, zero),
        jnp.where(first, zero, value),
        of("b"),
        of("c"),
        gains,
    )
    start = 0
    for piece in pieces:
        whole_ref[:, start : start + piece.shape[1]] = piece
        start += piece.shape[1]
    count = ranks_ref.shape[0]
    size = shared_ref.shape[0] // count
    for k in range(count):
        rows = pl.ds(pl.multiple_of(ranks_ref[k] * size, size), size)
        shared_ref[k * size : (k + 1) * size, :] = whole_ref[rows, :].astype(jnp.bfloat16)


def finish(ranks, kv_index, sums, weights, extra, at, sums_at):
    rows = weights.shape[0]
    shape = lambda *sizes: jax.ShapeDtypeStruct(sizes, jnp.float32)
    width = lambda name: sums_at[name][1]
    shared = 2 * (width("key") + width("value")) + width("b") + width("c") + LANES
    return pl.pallas_call(
        functools.partial(finish_kernel, at=at, sums_at=sums_at),
        out_shape=(
            shape(width("ssm_out"), rows),
            shape(width("attn_out"), rows),
            shape(rows, width("z")),
            shape(rows, width("x")),
            shape(rows, width("query")),
            shape(rows, width("misc")),
            jax.ShapeDtypeStruct((rows, shared), jnp.bfloat16),
        ),
        in_specs=[pl.BlockSpec(memory_space=pltpu.SMEM)] * 2 + in_vmem(3),
        out_specs=tuple(in_vmem(7)),
        scratch_shapes=[pltpu.VMEM((rows, shared), jnp.float32)],
        compiler_params=compiler_params(),
        name="finish",
    )(ranks, kv_index, sums, weights, extra)


def attend_kernel(rank_ref, query_ref, own_ref, *refs):
    pieces, (out_ref, low_ref, log_ref) = (refs[:-3], refs[-3:])
    span_length, head_size = query_ref.shape
    tile = own_ref.shape[0] // 2
    for block in range(span_length // tile):
        here = slice(block * tile, (block + 1) * tile)
        query_rows = query_ref[here, :]

        def step(kv_rows, carried, masked=False):
            top, total, summed = carried
            scores = tile_scores(kv_rows[:, :head_size], query_rows, head_size)
            if masked:
                scores = causal(scores)
            new_top = jnp.maximum(top, jnp.max(scores, axis=0, keepdims=True))
            probs = jnp.exp2(scores - new_top)
            scale = jnp.exp2(top - new_top)
            total = total * scale + jnp.sum(probs, axis=0, keepdims=True)
            summed = summed * scale + dot_first(kv_rows[:, head_size:], probs.astype(jnp.bfloat16))
            return (new_top, total, summed)

        carried = (
            jnp.full((1, tile), -1e30, jnp.float32),
            jnp.zeros((1, tile), jnp.float32),
            jnp.zeros((head_size, tile), jnp.float32),
        )
        carried = step(own_ref[here, :], carried, True)
        for earlier in range(block):
            carried = step(own_ref[earlier * tile : (earlier + 1) * tile, :], carried)
        for distance in range(1, 1 + len(pieces) // 2):
            pair = pieces[2 * distance - 2 : 2 * distance]

            def both(_, carried, pair=pair):
                return step(pair[1][...], step(pair[0][...], carried))

            valid = (rank_ref[0] >= distance).astype(jnp.int32)
            carried = lax.fori_loop(0, valid, both, carried)
        top, total, summed = carried
        result = summed / total
        out_ref[:, here] = result
        low_ref[here, :] = result.T.astype(jnp.bfloat16)
        log_ref[:, here] = top + jnp.log2(total)


def attend(rank, queries, own, pieces):
    span_length, head_size = queries.shape
    return pl.pallas_call(
        attend_kernel,
        out_shape=(
            jax.ShapeDtypeStruct((head_size, span_length), jnp.float32),
            jax.ShapeDtypeStruct((span_length, head_size), jnp.bfloat16),
            jax.ShapeDtypeStruct((1, span_length), jnp.float32),
        ),
        in_specs=[pl.BlockSpec(memory_space=pltpu.SMEM)] + in_vmem(2 + len(pieces)),
        out_specs=tuple(in_vmem(3)),
        compiler_params=compiler_params(),
        cost_estimate=small_cost(),
        name="attend",
    )(rank, queries, own, *pieces)


def attend_back_kernel(rank_ref, query_ref, own_ref, *refs):
    pieces, refs = (refs[:-13], refs[-13:])
    out_ref, log_ref, grad_ref, cos_ref, sin_ref, *_, d_query_ref, d_own_ref, d_far_ref, sums_ref = refs
    span_length, head_size = query_ref.shape
    tile = own_ref.shape[0] // 2
    score_scale = head_size**-0.5
    sums_ref[...] = jnp.zeros_like(sums_ref)
    for block in range(span_length // tile):
        here = slice(block * tile, (block + 1) * tile)
        query_rows = query_ref[here, :]
        grad_rows = grad_ref[here, grad_ref.shape[1] - head_size :]
        log_total = log_ref[:, here]
        delta_row = jnp.sum(
            grad_rows.astype(jnp.float32).T * out_ref[:, here], axis=0, keepdims=True
        )

        def step(kv_ref, start, at, d_query, masked=False):
            key_rows = kv_ref[start : start + tile, :head_size]
            scores = tile_scores(key_rows, query_rows, head_size)
            if masked:
                scores = causal(scores)
            probs = jnp.exp2(scores - log_total)
            d_probs = dot_last(kv_ref[start : start + tile, head_size:], grad_rows)
            d_scores = (probs * (d_probs - delta_row)).astype(jnp.bfloat16)
            rows = slice(at * tile, (at + 1) * tile)
            sums_ref[rows, head_size:] += mul(probs.astype(jnp.bfloat16), grad_rows)
            sums_ref[rows, :head_size] += mul(d_scores, query_rows)
            return d_query + dot_first(key_rows, d_scores)

        d_query = jnp.zeros((head_size, tile), jnp.float32)
        d_query = step(own_ref, block * tile, block, d_query, True)
        for earlier in range(block):
            d_query = step(own_ref, earlier * tile, earlier, d_query)
        for distance in range(1, 1 + len(pieces) // 2):

            def both(_, d_query, distance=distance):
                for k in (2 * distance - 2, 2 * distance - 1):
                    d_query = step(pieces[k], 0, 2 + k, d_query)
                return d_query

            valid = (rank_ref[0] >= distance).astype(jnp.int32)
            d_query = lax.fori_loop(0, valid, both, d_query)
        turned = d_query.T * score_scale
        d_query_ref[here, :] = (
            turned * cos_ref[here, :] - pltpu.roll(turned, head_size // 2, 1) * sin_ref[here, :]
        ).astype(jnp.bfloat16)
    lane = lax.broadcasted_iota(jnp.int32, (tile, 2 * head_size), 1)
    scale = jnp.where(lane < head_size, score_scale, 1.0)
    for at in range(2):
        rows = slice(at * tile, (at + 1) * tile)
        d_own_ref[rows, :] = sums_ref[rows, :] * scale
    for k in range(len(pieces)):
        rows = slice((2 + k) * tile, (3 + k) * tile)
        into = (k % 2) * (len(pieces) // 2) + k // 2
        d_far_ref[into * tile : (into + 1) * tile, :] = (sums_ref[rows, :] * scale).astype(
            jnp.bfloat16
        )


def attend_back(rank, queries, own, pieces, attended, log_totals, d_attn, cosine, sine, after):
    tile = own.shape[0] // 2
    return pl.pallas_call(
        attend_back_kernel,
        out_shape=(
            jax.ShapeDtypeStruct(queries.shape, jnp.bfloat16),
            jax.ShapeDtypeStruct(own.shape, jnp.float32),
            jax.ShapeDtypeStruct((len(pieces) * tile, own.shape[1]), jnp.bfloat16),
        ),
        in_specs=[pl.BlockSpec(memory_space=pltpu.SMEM)]
        + in_vmem(7 + len(pieces))
        + [pl.BlockSpec(memory_space=pl.ANY)] * len(after),
        out_specs=tuple(in_vmem(3)),
        scratch_shapes=[pltpu.VMEM(((2 + len(pieces)) * tile, own.shape[1]), jnp.float32)],
        compiler_params=compiler_params(),
        cost_estimate=small_cost(),
        name="attend_back",
    )(rank, queries, own, *pieces, attended, log_totals, d_attn, cosine, sine, *after)


def reorder_kernel(ranks_ref, *refs, count):
    out_ref = refs[-1]
    start = 0
    for ref in refs[:count]:
        out_ref[:, start : start + ref.shape[1]] = ref[...].astype(out_ref.dtype)
        start += ref.shape[1]


def reorder(ranks, pieces, inverse=False, after=()):
    count = ranks.shape[0]
    rows = pieces[0].shape[0] // count
    width = sum(piece.shape[1] for piece in pieces)
    there = lambda k, ranks: (ranks[k], 0)
    here = lambda k, ranks: (k, 0)
    return pl.pallas_call(
        functools.partial(reorder_kernel, count=len(pieces)),
        grid_spec=pltpu.PrefetchScalarGridSpec(
            num_scalar_prefetch=1,
            grid=(count,),
            in_specs=[
                pl.BlockSpec((rows, piece.shape[1]), here if inverse else there)
                for piece in pieces
            ]
            + [pl.BlockSpec(memory_space=pl.ANY)] * len(after),
            out_specs=pl.BlockSpec((rows, width), there if inverse else here),
        ),
        out_shape=jax.ShapeDtypeStruct((count * rows, width), jnp.bfloat16),
        compiler_params=compiler_params(),
        cost_estimate=small_cost(),
        name="reorder",
    )(ranks, *pieces, *after)


def lower_ones(size, dtype=jnp.float32):
    row = lax.broadcasted_iota(jnp.int32, (size, size), 0)
    column = lax.broadcasted_iota(jnp.int32, (size, size), 1)
    return (row >= column).astype(dtype)


def precise(left_side, right_side):
    return jnp.dot(
        left_side, right_side, precision=HIGH_PRECISION, preferred_element_type=jnp.float32
    )


def spread_heads(columns, head_size, width):
    lane = lax.broadcasted_iota(jnp.int32, (columns.shape[0], 2 * head_size), 1)
    pairs = [
        jnp.where(lane < head_size, columns[:, k : k + 1], columns[:, k + 1 : k + 2])
        for k in range(0, width // head_size, 2)
    ]
    return jnp.concatenate(pairs, axis=1)


def head_ones(width, head_size, lanes, dtype):
    at = lax.broadcasted_iota(jnp.int32, (width, lanes), 0)
    lane = lax.broadcasted_iota(jnp.int32, (width, lanes), 1)
    low = lane * head_size
    return ((at >= low) & (at < low + head_size)).astype(dtype)


def scan_first_kernel(
    pre_ref, bias_ref, rate_ref, x_ref, b_ref, delta_ref, cum_ref, delta_row_ref, cum_row_ref, state_ref, log_ref
):
    @pl.when(pl.program_id(0) == 0)
    def _():
        state_ref[...] = jnp.zeros_like(state_ref)
        log_ref[...] = jnp.zeros_like(log_ref)

    delta = jax.nn.softplus(pre_ref[...] + bias_ref[...])
    log_step = -delta * rate_ref[...]
    cumulative = precise(lower_ones(log_step.shape[0]), log_step)
    delta_ref[...] = delta
    cum_ref[...] = cumulative
    delta_row_ref[...] = delta.T[:8]
    cum_row_ref[...] = cumulative.T[:8]
    ending = cumulative[-1:, :]
    weight = jnp.exp(ending - cumulative + log_ref[...]) * delta
    width = x_ref.shape[1]
    x_low = x_ref[...].astype(jnp.bfloat16).astype(jnp.float32)
    weighted = (x_low * spread_heads(weight, MIXER_HEAD_SIZE, width)).astype(jnp.bfloat16)
    state_ref[...] += dot_first(b_ref[...].astype(jnp.bfloat16), weighted)
    log_ref[...] += ending


def part(projected, start, width, order=lambda c: c):
    at = start // width
    return (projected, pl.BlockSpec((BLOCK, width), lambda c: (order(c), at)))


def run_scan(kernel, chunks, operands, out_shape, out_specs, name, scratch=(), after=()):
    count = len(operands)
    operands = operands + [(array, pl.BlockSpec(memory_space=pl.ANY)) for array in after]

    def call(*refs):
        kernel(*refs[:count], *refs[count + len(after) :])

    return pl.pallas_call(
        call,
        grid=(chunks,),
        out_shape=out_shape,
        in_specs=[spec for _, spec in operands],
        out_specs=out_specs,
        scratch_shapes=list(scratch),
        compiler_params=compiler_params(),
        cost_estimate=small_cost(),
        name=name,
    )(*[array for array, _ in operands])


def whole(array):
    return (array, pl.BlockSpec(array.shape, lambda c: (0,) * array.ndim))


def scan_first(at, bias, rate):
    rows, lanes = (at["x"][0].shape[0], bias.shape[1])
    chunks = rows // BLOCK
    back = lambda c: chunks - 1 - c
    width, state_size = (at["x"][2], at["b"][2])
    by_chunk = pl.BlockSpec((BLOCK, lanes), lambda c: (back(c), 0))
    across = pl.BlockSpec((8, BLOCK), lambda c: (0, back(c)))
    shape = lambda *sizes: jax.ShapeDtypeStruct(sizes, jnp.float32)
    return run_scan(
        scan_first_kernel,
        chunks,
        [
            part(*at["misc"], back),
            whole(bias),
            whole(rate),
            part(*at["x"], back),
            part(*at["b"], back),
        ],
        (
            shape(rows, lanes),
            shape(rows, lanes),
            shape(8, rows),
            shape(8, rows),
            shape(state_size, width),
            shape(1, lanes),
        ),
        (
            by_chunk,
            by_chunk,
            across,
            across,
            pl.BlockSpec((state_size, width), lambda c: (0, 0)),
            pl.BlockSpec((1, lanes), lambda c: (0, 0)),
        ),
        "scan_first",
    )


def chained(refs, width):
    state = jnp.zeros((refs[0].shape[0] - 16, width), jnp.float32)
    for ref in reversed(refs):
        logs = ref[-16:, :LANES].astype(jnp.float32)
        decay = jnp.exp(jnp.sum(logs[:3], axis=0, keepdims=True))
        state = ref[:-16].astype(jnp.float32) + spread_heads(decay, MIXER_HEAD_SIZE, width) * state
    return state


def scan_kernel(
    x_ref,
    z_ref,
    b_ref,
    c_ref,
    delta_ref,
    cum_ref,
    delta_row_ref,
    cum_row_ref,
    near_ref,
    next_ref,
    far_ref,
    skip_ref,
    scanned_ref,
    gated_ref,
    states_ref,
    state_ref,
):
    @pl.when(pl.program_id(0) == 0)
    def _():
        state_ref[...] = chained((near_ref, next_ref, far_ref), x_ref.shape[1])

    head_size = MIXER_HEAD_SIZE
    pair = 2 * head_size
    size, width = x_ref.shape
    state = state_ref[...]
    states_ref[0] = state
    delta, cumulative = (delta_ref[...], cum_ref[...])
    delta_row, cum_row = (delta_row_ref[...], cum_row_ref[...])
    bmat, cmat = (b_ref[...].astype(jnp.bfloat16), c_ref[...].astype(jnp.bfloat16))
    x_all = x_ref[...].astype(jnp.bfloat16)
    inner = dot_last(cmat, bmat)
    row = lax.broadcasted_iota(jnp.int32, (size, size), 0)
    column = lax.broadcasted_iota(jnp.int32, (size, size), 1)
    allowed = row >= column
    lane = lax.broadcasted_iota(jnp.int32, (size, pair), 1)
    from_state = mul(cmat, state.astype(jnp.bfloat16))
    spread = spread_heads(jnp.exp(cumulative), head_size, width)
    for first in range(0, width // head_size, 2):
        here = slice(first * head_size, first * head_size + pair)
        x_pair = x_all[:, here]
        total = from_state[:, here] * spread[:, here]
        total += skip_ref[:, here] * x_pair.astype(jnp.float32)
        for head in (first, first + 1):
            gap = cumulative[:, head : head + 1] - cum_row[head : head + 1, :]
            decay = jnp.exp(jnp.where(allowed, gap, -1e30))
            mixing = inner * decay * delta_row[head : head + 1, :]
            x_head = jnp.where((lane >= head_size) == (head > first), x_pair, 0.0)
            total += mul(mixing.astype(jnp.bfloat16), x_head.astype(jnp.bfloat16))
        scanned_ref[:, here] = total
        gate = z_ref[:, here]
        gated_ref[:, here] = (total * (gate * jax.nn.sigmoid(gate))).astype(jnp.bfloat16)
    ending = cumulative[-1:, :]
    weight = spread_heads(jnp.exp(ending - cumulative) * delta, head_size, width)
    weighted = (x_all.astype(jnp.float32) * weight).astype(jnp.bfloat16)
    state_ref[...] = state * spread[-1:, :] + dot_first(bmat, weighted)


def scan(at, delta, cumulative, delta_row, cum_row, entry, skip, after):
    rows = delta.shape[0]
    state_size, width = (at["b"][2], at["x"][2])
    chunks = rows // BLOCK
    by_chunk = pl.BlockSpec((BLOCK, width), lambda c: (c, 0))
    lanes = delta.shape[1]
    across = pl.BlockSpec((8, BLOCK), lambda c: (0, c))
    return run_scan(
        scan_kernel,
        chunks,
        [
            part(*at["x"]),
            part(*at["z"]),
            part(*at["b"]),
            part(*at["c"]),
            part(delta, 0, lanes),
            part(cumulative, 0, lanes),
            (delta_row, across),
            (cum_row, across),
            *[whole(packed) for packed in entry],
            whole(skip),
        ],
        (
            jax.ShapeDtypeStruct((rows, width), jnp.float32),
            jax.ShapeDtypeStruct((rows, width), jnp.bfloat16),
            jax.ShapeDtypeStruct((chunks, state_size, width), jnp.float32),
        ),
        (by_chunk, by_chunk, pl.BlockSpec((1, state_size, width), lambda c: (c, 0, 0))),
        "scan",
        [pltpu.VMEM((state_size, width), jnp.float32)],
        after,
    )


def scan_back_first_kernel(
    grad_ref, z_ref, scanned_ref, c_ref, cum_ref, d_scanned_ref, d_gate_ref, state_ref, log_ref
):
    @pl.when(pl.program_id(0) == 0)
    def _():
        state_ref[...] = jnp.zeros_like(state_ref)
        log_ref[...] = jnp.zeros_like(log_ref)

    gate = z_ref[...]
    chance = jax.nn.sigmoid(gate)
    grad = grad_ref[:, : z_ref.shape[1]].astype(jnp.float32)
    d_scanned = grad * (gate * chance)
    d_scanned_ref[...] = d_scanned
    d_gate_ref[...] = (
        grad * scanned_ref[...] * (chance * (1.0 + gate * (1.0 - chance)))
    ).astype(jnp.bfloat16)
    cumulative = cum_ref[...]
    decay = spread_heads(jnp.exp(cumulative + log_ref[...]), MIXER_HEAD_SIZE, z_ref.shape[1])
    state_ref[...] += dot_first(
        c_ref[...].astype(jnp.bfloat16), (d_scanned * decay).astype(jnp.bfloat16)
    )
    log_ref[...] += cumulative[-1:, :]


def scan_back_first(grads, at, scanned, cumulative):
    rows, width = scanned.shape
    state_size, lanes = (at["c"][2], cumulative.shape[1])
    by_chunk = pl.BlockSpec((BLOCK, width), lambda c: (c, 0))
    return run_scan(
        scan_back_first_kernel,
        rows // BLOCK,
        [
            part(grads, 0, grads.shape[1]),
            part(*at["z"]),
            part(scanned, 0, width),
            part(*at["c"]),
            part(cumulative, 0, lanes),
        ],
        (
            jax.ShapeDtypeStruct((rows, width), jnp.float32),
            jax.ShapeDtypeStruct((rows, width), jnp.bfloat16),
            jax.ShapeDtypeStruct((state_size, width), jnp.float32),
        ),
        (by_chunk, by_chunk, pl.BlockSpec((state_size, width), lambda c: (0, 0))),
        "scan_back_first",
        [pltpu.VMEM((1, lanes), jnp.float32)],
    )


def scan_back_kernel(
    x_ref,
    grad_ref,
    b_ref,
    c_ref,
    pre_ref,
    bias_ref,
    rate_ref,
    delta_ref,
    cum_ref,
    cum_row_ref,
    states_ref,
    near_ref,
    next_ref,
    far_ref,
    skip_ref,
    d_x_ref,
    d_b_ref,
    d_c_ref,
    d_pre_ref,
    sums_ref,
    state_ref,
):
    @pl.when(pl.program_id(0) == 0)
    def _():
        state_ref[...] = chained((near_ref, next_ref, far_ref), x_ref.shape[1])
        sums_ref[...] = jnp.zeros_like(sums_ref)

    head_size = MIXER_HEAD_SIZE
    pair = 2 * head_size
    size, width = x_ref.shape
    lanes = delta_ref.shape[1]
    low = jnp.bfloat16
    delta, cumulative, cum_row = (delta_ref[...], cum_ref[...], cum_row_ref[...])
    bmat, cmat = (b_ref[...].astype(low), c_ref[...].astype(low))
    x_all = x_ref[...].astype(low)
    x_single = x_all.astype(jnp.float32)
    grad = grad_ref[...]
    grad_low = grad.astype(low)
    state = states_ref[0]
    state_low = state.astype(low)
    after = state_ref[...]
    after_low = after.astype(low)
    ending = cumulative[-1:, :]
    row = lax.broadcasted_iota(jnp.int32, (size, size), 0)
    column = lax.broadcasted_iota(jnp.int32, (size, size), 1)
    later = column >= row
    before = (row > column).astype(low)
    onward = later.astype(low)
    lane = lax.broadcasted_iota(jnp.int32, (size, pair), 1)
    head_lane = lax.broadcasted_iota(jnp.int32, (size, lanes), 1)
    sum_heads = head_ones(width, head_size, lanes, low)

    inner = dot_last(bmat, cmat)
    from_after = mul(bmat, after_low)
    weight = jnp.exp(ending - cumulative)
    spread_weight = spread_heads(weight * delta, head_size, width)
    spread = spread_heads(jnp.exp(cumulative), head_size, width)
    to_end = mul((x_single * from_after).astype(low), sum_heads)
    through = jnp.exp(cumulative) * mul((grad * mul(cmat, state_low)).astype(low), sum_heads)
    carried = jnp.sum(state * after, axis=0, keepdims=True) * spread[-1:, :]
    carried = precise(carried, sum_heads.astype(jnp.float32))
    d_delta = weight * to_end
    d_log = (
        mul(onward, through.astype(low)) + mul(before, (d_delta * delta).astype(low)) + carried
    )

    d_inner = jnp.zeros((size, size), jnp.float32)
    for first in range(0, width // head_size, 2):
        here = slice(first * head_size, first * head_size + pair)
        x_pair, grad_pair = (x_all[:, here], grad_low[:, here])
        d_x = from_after[:, here] * spread_weight[:, here] + skip_ref[:, here] * grad[:, here]
        for head in (first, first + 1):
            mine = (lane >= head_size) == (head > first)
            gap = cum_row[head : head + 1, :] - cumulative[:, head : head + 1]
            decay = jnp.exp(jnp.where(later, gap, -1e30))
            delta_column = delta[:, head : head + 1]
            d_mixing = dot_last(jnp.where(mine, x_pair, 0.0).astype(low), grad_pair) * decay
            d_inner += d_mixing * delta_column
            flow = d_mixing * inner
            mixing = inner * decay * delta_column
            d_x += mul(mixing.astype(low), jnp.where(mine, grad_pair, 0.0).astype(low))
            d_delta_head = jnp.sum(flow, axis=1, keepdims=True)
            passing = mul(before, (flow * delta_column).astype(low))
            d_log_head = jnp.sum(jnp.where(later, passing, 0.0), axis=1, keepdims=True)
            d_delta += jnp.where(head_lane == head, d_delta_head, 0.0)
            d_log += jnp.where(head_lane == head, d_log_head, 0.0)
        d_x_ref[:, here] = d_x.astype(low)

    d_inner_low = d_inner.astype(low)
    scaled_grad = (grad * spread).astype(low)
    weighted = (x_single * spread_weight).astype(low)
    d_b_ref[...] = (mul(d_inner_low, cmat) + dot_last(weighted, after_low)).astype(low)
    d_c_ref[...] = (dot_first(d_inner_low, bmat) + dot_last(scaled_grad, state_low)).astype(low)
    state_ref[...] = after * spread[-1:, :] + dot_first(cmat, scaled_grad)
    rate = rate_ref[...]
    d_pre = (d_delta - d_log * rate) * jax.nn.sigmoid(pre_ref[...] + bias_ref[...])
    d_pre = jnp.where(head_lane < width // head_size, d_pre, 0.0)
    d_pre_ref[...] = d_pre.astype(low)
    skip_sum = precise(
        jnp.sum(grad * x_single, axis=0, keepdims=True), sum_heads.astype(jnp.float32)
    )
    sums_ref[0:1, :] += jnp.sum(d_pre, axis=0, keepdims=True)
    sums_ref[1:2, :] += jnp.sum(d_log * (-delta * rate), axis=0, keepdims=True)
    sums_ref[2:3, :] += skip_sum


def scan_back(
    at, d_scanned, bias, rate, delta, cumulative, cum_row, states, entry, skip, after
):
    rows, width = d_scanned.shape
    state_size, lanes = (at["b"][2], delta.shape[1])
    chunks = rows // BLOCK
    back = lambda c: chunks - 1 - c
    by_chunk = lambda columns: pl.BlockSpec((BLOCK, columns), lambda c: (back(c), 0))
    shape = lambda columns: jax.ShapeDtypeStruct((rows, columns), jnp.bfloat16)
    return run_scan(
        scan_back_kernel,
        chunks,
        [
            part(*at["x"], back),
            part(d_scanned, 0, width, back),
            part(*at["b"], back),
            part(*at["c"], back),
            part(*at["misc"], back),
            whole(bias),
            whole(rate),
            part(delta, 0, lanes, back),
            part(cumulative, 0, lanes, back),
            (cum_row, pl.BlockSpec((8, BLOCK), lambda c: (0, back(c)))),
            (states, pl.BlockSpec((1, state_size, width), lambda c: (back(c), 0, 0))),
            *[whole(packed) for packed in entry],
            whole(skip),
        ],
        (
            shape(width),
            shape(state_size),
            shape(state_size),
            shape(lanes),
            jax.ShapeDtypeStruct((8, lanes), jnp.float32),
        ),
        (
            by_chunk(width),
            by_chunk(state_size),
            by_chunk(state_size),
            by_chunk(lanes),
            pl.BlockSpec((8, lanes), lambda c: (0, 0)),
        ),
        "scan_back",
        [pltpu.VMEM((state_size, width), jnp.float32)],
        after,
    )


def on_heads(value, move):
    devices = lax.axis_size("heads")
    pairs = []
    for at in range(devices):
        z, core = move(at // 2, at % 2)
        pairs.append((at, 2 * (z % (devices // 2)) + core))
    return lax.ppermute(value, "heads", pairs)


def to_partner(value):
    return on_heads(value, lambda z, core: (z, 1 - core))


def along(value):
    return on_heads(value, lambda z, core: (z + 1 - 2 * core, core))


def against(value):
    return on_heads(value, lambda z, core: (z - 1 + 2 * core, core))


def chunk_ranks():
    devices = lax.axis_size("heads")
    z, core = (lax.axis_index("heads") // 2, lax.axis_index("heads") % 2)
    step, other = (1 - 2 * core, 1 - core)
    owners = (
        (z, core),
        (z + 2, core),
        (z - step, core),
        (z - step, other),
        (z, other),
        (z + 2, other),
        (z + step, other),
        (z + step, core),
    )
    return jnp.stack([2 * ((at + devices) % (devices // 2)) + side for at, side in owners])


def gather_rows(own):
    partner = to_partner(own)
    near = along(own)
    near_other = along(partner)
    far = along(near)
    mine = (own, far, near, near_other)
    theirs = (partner, to_partner(far), to_partner(near), to_partner(near_other))
    return jnp.concatenate(mine + theirs, axis=0)


def scatter_rows(product, half):
    chunk = half // 4
    got = to_partner(product(slice(half, 2 * half)).astype(jnp.bfloat16))
    summed = product(slice(0, half)) + got.astype(jnp.float32)
    low = summed[chunk:].astype(jnp.bfloat16)
    far = against(low[:chunk])
    near_other = against(low[2 * chunk :])
    near = against((low[chunk : 2 * chunk].astype(jnp.float32) + far).astype(jnp.bfloat16))
    return summed[:chunk] + near.astype(jnp.float32) + to_partner(near_other).astype(jnp.float32)


def across(value, bit):
    devices = lax.axis_size("heads")
    return lax.ppermute(value, "heads", [(at, at ^ bit) for at in range(devices)])


def gather_small(value):
    for bit in (1, 2, 4):
        value = jnp.concatenate([value, across(value, bit)], axis=0)
    return value


def scatter_small(value):
    for bit in (4, 2, 1):
        half = value.shape[0] // 2
        got = across(value[half:].astype(jnp.bfloat16), bit)
        value = value[:half].astype(jnp.float32) + got.astype(jnp.float32)
    return value


def on_blocks(value, step):
    devices = lax.axis_size("blk")
    pairs = [(at, at + step) for at in range(devices) if 0 <= at + step < devices]
    return lax.ppermute(value, "blk", pairs)


def from_earlier(value, step=1):
    return tuple(on_blocks(value, distance * step) for distance in (1, 2, 3))


def pack_state(state, log_total):
    high = log_total.astype(jnp.bfloat16)
    rest = log_total - high.astype(jnp.float32)
    middle = rest.astype(jnp.bfloat16)
    low = (rest - middle.astype(jnp.float32)).astype(jnp.bfloat16)
    logs = jnp.concatenate([high, middle, low], axis=0)
    logs = jnp.pad(logs, ((0, 16 - logs.shape[0]), (0, state.shape[1] - logs.shape[1])))
    return jnp.concatenate([state.astype(jnp.bfloat16), logs], axis=0)


def sum_blocks(value):
    for axis in ("dp", "blk"):
        for bit in (1, 2):
            value = value + lax.ppermute(
                value, axis, [(at, at ^ bit) for at in range(lax.axis_size(axis))]
            )
    return value


def weight_sum(grads):
    return lax.psum_scatter(grads, ("dp", "blk"), scatter_dimension=0, tiled=True)


def split_columns(value_in, widths):
    pieces, start = [], 0
    for width in widths:
        pieces.append(value_in[:, start : start + width])
        start += width
    return pieces


def inverse_rms(rows_in):
    return lax.rsqrt(jnp.mean(rows_in * rows_in, axis=-1, keepdims=True) + norm_eps)


def norm_back(rows_in, gain_in, cotangent):
    inverse = inverse_rms(rows_in)
    scaled = rows_in * inverse
    weighted = cotangent * gain_in
    return inverse * (weighted - scaled * jnp.mean(weighted * scaled, axis=-1, keepdims=True))


def shards(
    x_in,
    out_grad,
    norm_one,
    w_query,
    w_key,
    w_value,
    output_gate_weight,
    mixer_input_weight,
    w_delta,
    w_bmat,
    w_cmat,
    delta_bias,
    decay_log,
    skip_gain,
    w_attn_out,
    mixer_output_weight,
    norm_two,
    w_gate,
    w_up,
    w_down,
):
    heads_count = lax.axis_size("heads")
    head_rank = lax.axis_index("heads")
    core = head_rank % 2
    block_rank = lax.axis_index("blk")
    rank = block_rank.astype(jnp.int32)[None]
    own_rows = x_in.shape[0]
    span_length = own_rows * heads_count
    half_span = span_length // 2
    span_start = block_rank * span_length
    query_width = w_query.shape[1]
    mixer_width = mixer_input_weight.shape[1]
    heads = mixer_width // MIXER_HEAD_SIZE
    state_size = w_bmat.shape[1]
    hidden_width = w_gate.shape[1]
    rows_of = w_query.shape[0]
    kv_index = head_rank * (query_width // HD) // (QH // KVH)
    kv_width = KVH * HD
    low = jnp.bfloat16
    ranks = chunk_ranks().astype(jnp.int32)
    turns = (head_rank ^ jnp.arange(heads_count)).astype(jnp.int32)

    gains = jnp.stack([norm_one, norm_two], axis=1)
    gains = jnp.pad(gains, ((0, 0), (0, LANES - 2)))
    shared = jnp.concatenate([w_key, w_value, w_bmat, w_cmat, gains], axis=1)
    shared = reorder(turns, [gather_small(shared)], inverse=True)
    key_part = lax.dynamic_slice_in_dim(shared, kv_index * HD, HD, 1)
    value_part = lax.dynamic_slice_in_dim(shared, kv_width + kv_index * HD, HD, 1)
    state_part = shared[:, 2 * kv_width : 2 * kv_width + 2 * state_size]
    gain_part = shared[:, 2 * kv_width + 2 * state_size :][:, :2]
    misc_part = jnp.concatenate(
        [w_delta, gain_part, jnp.zeros((rows_of, LANES - heads - 2), low)], axis=1
    )
    in_names = ("z", "x", "query", "b", "c", "misc", "key", "value")
    in_widths = (mixer_width, mixer_width, query_width, state_size, state_size, LANES, HD, HD)
    starts = [sum(in_widths[:k]) for k in range(len(in_widths))]
    at = dict(zip(in_names, zip(starts, in_widths)))
    in_first = jnp.concatenate([output_gate_weight, mixer_input_weight, w_query], axis=1)
    in_second = jnp.concatenate([state_part, misc_part, key_part, value_part], axis=1)
    in_own = jnp.concatenate([in_first, in_second], axis=1)
    mix_own = pack((mixer_output_weight, w_attn_out), (True, True), w_gate)
    first_own = jnp.concatenate([in_own, mix_own], axis=1)
    first_full = lax.all_gather(first_own, ("dp", "blk"), axis=0, tiled=True)
    in_full, mix_t = (first_full[:, : in_own.shape[1]], first_full[:, in_own.shape[1] :])
    x_float = x_in.astype(jnp.float32)
    zero = 0.0 * in_own[0, 0]
    x_span = gather_rows(x_in + zero)
    ffn_grad = gather_rows(out_grad + 0.0 * x_span[0, 0])
    ffn_own = pack((w_gate, w_up, w_down), (False, False, True), x_span)
    ffn_full = lax.all_gather(ffn_own, ("dp", "blk"), axis=0, tiled=True)
    mixed_width = query_width + mixer_width
    gate_full, up_full, down_t = split_columns(ffn_full, (hidden_width,) * 3)
    positions = (span_start + jnp.arange(span_length)).astype(jnp.float32)
    freqs = rope_base ** (-2.0 * jnp.arange(HD // 2, dtype=jnp.float32) / HD)
    angles = positions[:, None] * freqs[None, :]
    cosine, sine = (jnp.cos(angles), jnp.sin(angles))
    cosine = jnp.concatenate([cosine, cosine], axis=1)
    sine = jnp.concatenate([-sine, sine], axis=1)
    normed_ordered, queries, keys_values, gain_rows = enter(
        ranks, jnp.full((1,), heads, jnp.int32), x_span, first_full, at, cosine, sine, [ffn_grad, ffn_own]
    )
    gain_one, gain_two = (gain_rows[0:1], gain_rows[1:2])
    mine = lax.dynamic_slice_in_dim(keys_values, core * half_span, half_span, 0)
    pieces = []
    for piece in from_earlier(mine):
        pieces += [piece, to_partner(piece)]
    gate_raw = simple_product(normed_ordered, in_full[:, :mixer_width])
    x_raw = simple_product(normed_ordered, in_full[:, mixer_width : 2 * mixer_width])
    state_raw = simple_product(normed_ordered, in_full[:, at["b"][0] : at["key"][0]])
    raw = {
        "z": (gate_raw, 0, mixer_width),
        "x": (x_raw, 0, mixer_width),
        "b": (state_raw, 0, state_size),
        "c": (state_raw, state_size, state_size),
        "misc": (state_raw, 2 * state_size, LANES),
    }

    pad_lanes = lambda vector: jnp.pad(vector, (0, LANES - heads))[None]
    bias, rate = (pad_lanes(delta_bias), pad_lanes(jnp.exp(decay_log)))
    skip = jnp.repeat(skip_gain, MIXER_HEAD_SIZE)[None]
    delta, cumulative, delta_row, cum_row, local_state, local_log = scan_first(raw, bias, rate)
    entry_states = from_earlier(pack_state(local_state, local_log))
    attended, attn_part, log_totals = attend(rank, queries, keys_values, pieces)
    scanned, gated, states = scan(
        raw, delta, cumulative, delta_row, cum_row, entry_states, skip, [attn_part]
    )
    mixers = reorder(ranks, [gated, attn_part], after=[ffn_full])
    middle = x_float + scatter_rows(lambda rows: dot_last(mixers[rows], mix_t), half_span)
    middle_scaled = middle * inverse_rms(middle)
    normed_two = gather_rows((middle_scaled * gain_two).astype(low))
    ffn_gate = simple_product(normed_two, gate_full)
    ffn_up = simple_product(normed_two, up_full)
    ffn_sig = jax.nn.sigmoid(ffn_gate)
    hidden = (ffn_gate * ffn_sig * ffn_up).astype(low)

    d_hidden = simple_product(ffn_grad, down_t)
    d_ffn_gate = (d_hidden * ffn_up * (ffn_sig * (1.0 + ffn_gate * (1.0 - ffn_sig)))).astype(low)
    d_ffn_up = (d_hidden * (ffn_gate * ffn_sig)).astype(low)
    d_normed_two = scatter_rows(
        lambda rows: dot_last(d_ffn_gate[rows], gate_full) + dot_last(d_ffn_up[rows], up_full),
        half_span,
    )
    ffn_grads = weight_grads(
        [(normed_two, [d_ffn_gate, d_ffn_up]), (ffn_grad, [hidden])], 3 * hidden_width
    )
    ffn_sums = weight_sum(ffn_grads).astype(jnp.float32)
    grad_gate, grad_up, grad_down_t = split_columns(ffn_sums, (hidden_width,) * 3)
    grad_two_part = jnp.sum(grad_gate * w_gate + grad_up * w_up, axis=1, keepdims=True)
    gain_own = gain_part.astype(jnp.float32)
    grad_two_part = grad_two_part / gain_own[:, 1:2]
    d_middle = out_grad.astype(jnp.float32) + norm_back(middle, gain_two, d_normed_two)
    mix_grad = gather_rows(d_middle.astype(low))
    d_mixers = reorder(
        ranks, [simple_product(mix_grad, mix_t).astype(low)], inverse=True, after=[ffn_grads]
    )
    d_scanned, d_gate_z, d_entry = scan_back_first(d_mixers, raw, scanned, cumulative)
    d_entry = pack_state(d_entry, local_log)
    after_states = from_earlier(d_entry, -1)
    mix_width = mixed_width + mixer_width
    all_width = mixed_width + in_own.shape[1]
    mix_grads = weight_grads(
        [(mix_grad, [mixers]), (normed_ordered, [d_gate_z])], all_width, after=[d_entry]
    )
    d_query, d_own, d_far = attend_back(
        rank, queries, keys_values, pieces, attended, log_totals, d_mixers, cosine, sine, [mix_grads, *after_states]
    )
    d_ssm_in, d_bmat, d_cmat, d_pre, sums = scan_back(
        raw,
        d_scanned,
        bias,
        rate,
        delta,
        cumulative,
        cum_row,
        states,
        after_states,
        skip,
        [d_query],
    )
    far_half = d_far.shape[0] // 2
    d_mine = lax.dynamic_slice_in_dim(d_own, core * half_span, half_span, 0)
    d_theirs = lax.dynamic_slice_in_dim(d_own, (1 - core) * half_span, half_span, 0)
    d_mine = d_mine + to_partner(d_theirs.astype(low)).astype(jnp.float32)
    d_far = d_far[:far_half].astype(jnp.float32) + to_partner(d_far[far_half:]).astype(jnp.float32)
    d_one, d_two, d_three = (
        d_far[k * half_span : (k + 1) * half_span] for k in range(d_far.shape[0] // half_span)
    )
    d_one = d_one + on_blocks(d_two.astype(low), -1).astype(jnp.float32)
    d_mine = d_mine + on_blocks(d_one.astype(low), -1).astype(jnp.float32)
    d_mine = d_mine + on_blocks(d_three.astype(low), -3).astype(jnp.float32)
    half_cos = lax.dynamic_slice_in_dim(cosine, core * half_span, half_span, 0)
    half_sin = lax.dynamic_slice_in_dim(sine, core * half_span, half_span, 0)
    d_key = d_mine[:, :HD]
    d_key = d_key * half_cos - jnp.roll(d_key, HD // 2, axis=1) * half_sin
    d_mine = jnp.concatenate([d_key, d_mine[:, HD:]], axis=1).astype(low)
    d_keys_values = lax.dynamic_update_slice_in_dim(
        jnp.zeros((span_length, 2 * HD), low), d_mine, core * half_span, 0
    )

    scan_rights = [d_ssm_in, d_bmat, d_cmat, d_pre]
    in_grads = weight_grads([(normed_ordered, scan_rights)], all_width, mix_width, mix_grads)
    late_rights = [d_keys_values, d_query]
    late_start = mix_width + sum(array.shape[1] for array in scan_rights)
    in_grads = weight_grads([(normed_ordered, late_rights)], all_width, late_start, in_grads)
    in_sums = weight_sum(in_grads)
    d_projected = reorder(
        ranks,
        [d_gate_z, d_ssm_in, d_query, d_bmat, d_cmat, d_pre, d_keys_values],
        after=[in_grads],
    )
    d_normed = scatter_rows(lambda rows: dot_last(d_projected[rows], in_full), half_span)
    input_grad = d_middle + norm_back(x_float, gain_one, d_normed)
    ffn_out = scatter_rows(lambda rows: dot_last(hidden[rows], down_t), half_span)
    activations = (middle + ffn_out).astype(low)
    sums_names = ("ssm_out", "attn_out", "z", "x", "b", "c", "misc", "key", "value", "query")
    sums_widths = [mixer_width, query_width] + [at[name][1] for name in sums_names[2:]]
    sums_starts = [sum(sums_widths[:k]) for k in range(len(sums_widths))]
    sums_at = dict(zip(sums_names, zip(sums_starts, sums_widths)))
    extra = jnp.concatenate([gain_own[:, 0:1], grad_two_part], axis=1)
    extra = jnp.pad(extra, ((0, 0), (0, LANES - 2)))
    grad_ssm_out, grad_attn_out, grad_gatez, grad_ssmx, grad_query, misc_sums, shared_parts = finish(
        turns,
        kv_index.astype(jnp.int32)[None],
        in_sums,
        in_own,
        extra,
        at,
        sums_at,
    )
    shared_sums = scatter_small(shared_parts)
    grad_key, grad_value, grad_bmat, grad_cmat, gain_sums = split_columns(
        shared_sums, (kv_width, kv_width, state_size, state_size, LANES)
    )
    small_sums = sum_blocks(sums)[:, :heads]
    return (
        activations,
        input_grad,
        gain_sums[:, 0],
        grad_query,
        grad_key,
        grad_value,
        grad_gatez,
        grad_ssmx,
        misc_sums[:, :heads],
        grad_bmat,
        grad_cmat,
        small_sums[0],
        small_sums[1],
        small_sums[2],
        grad_attn_out,
        grad_ssm_out,
        gain_sums[:, 1],
        grad_gate,
        grad_up,
        grad_down_t.T,
    )


def solution(mesh):
    placed = (
        P(("dp", "blk", "heads"), None),
        P(("dp", "blk", "heads"), None),
        P(("dp", "blk", "heads")),
        P(("dp", "blk"), "heads"),
        P(("dp", "blk", "heads"), None),
        P(("dp", "blk", "heads"), None),
        P(("dp", "blk"), "heads"),
        P(("dp", "blk"), "heads"),
        P(("dp", "blk"), "heads"),
        P(("dp", "blk", "heads"), None),
        P(("dp", "blk", "heads"), None),
        P("heads"),
        P("heads"),
        P("heads"),
        P("heads", ("dp", "blk")),
        P("heads", ("dp", "blk")),
        P(("dp", "blk", "heads")),
        P(("dp", "blk"), "heads"),
        P(("dp", "blk"), "heads"),
        P("heads", ("dp", "blk")),
    )
    return jax.shard_map(
        shards,
        mesh=mesh,
        in_specs=placed,
        out_specs=(
            P(("dp", "blk", "heads"), None),
            P(("dp", "blk", "heads"), None),
            P(("dp", "blk", "heads")),
            P(("dp", "blk"), "heads"),
            P(("dp", "blk", "heads"), None),
            P(("dp", "blk", "heads"), None),
            P(("dp", "blk"), "heads"),
            P(("dp", "blk"), "heads"),
            P(("dp", "blk"), "heads"),
            P(("dp", "blk", "heads"), None),
            P(("dp", "blk", "heads"), None),
            P("heads"),
            P("heads"),
            P("heads"),
            P("heads", ("dp", "blk")),
            P("heads", ("dp", "blk")),
            P(("dp", "blk", "heads")),
            P(("dp", "blk"), "heads"),
            P(("dp", "blk"), "heads"),
            P("heads", ("dp", "blk")),
        ),
        check_vma=False,
    )
```

```python
import functools

import jax
import jax.numpy as jnp
from jax import lax
from jax.experimental import pallas as pl
from jax.experimental.pallas import tpu as pltpu
from jax.sharding import PartitionSpec as P

QH = 8
KVH = 2
HD = 128
MIXER_HEAD_SIZE = 64
BLOCK = 256
LANES = 128
LOG2_E = 1.4426950408889634


HIGH_PRECISION = lax.Precision.HIGHEST
norm_eps = 1e-05
rope_base = 100000000000.0


def simple_product(left_side, right_side):
    return jnp.dot(left_side, right_side, preferred_element_type=jnp.float32)


def dot_last(left_side, right_side):
    return lax.dot_general(
        left_side, right_side, (((1,), (1,)), ((), ())), preferred_element_type=jnp.float32
    )


def dot_first(left_side, right_side):
    return lax.dot_general(
        left_side, right_side, (((0,), (0,)), ((), ())), preferred_element_type=jnp.float32
    )


def compiler_params(mebibytes=20):
    return pltpu.CompilerParams(vmem_limit_bytes=mebibytes * 1024 * 1024)


def ends(gathered):
    chunk = gathered.shape[0] // 8
    return [corner(gathered[k * chunk :]) for k in (5, 6, 7)]


def small_cost():
    return pl.CostEstimate(flops=1000, bytes_accessed=1000, transcendentals=0)


def corner(value):
    return value[:16, :LANES]


def in_vmem(count):
    return [pl.BlockSpec(memory_space=pltpu.VMEM)] * count


def mul(left_side, right_side):
    return jnp.dot(left_side, right_side, preferred_element_type=jnp.float32)


def tile_scores(key_rows, query_rows, head_size):
    return dot_last(key_rows, query_rows) * (head_size**-0.5 * LOG2_E)


def causal(scores):
    key_at = lax.broadcasted_iota(jnp.int32, scores.shape, 0)
    query_at = lax.broadcasted_iota(jnp.int32, scores.shape, 1)
    return jnp.where(key_at <= query_at, scores, -1e30)


def enter_kernel(
    ranks_ref, heads_ref, x_ref, misc_ref, key_ref, value_ref, w_query_ref, cos_ref, sin_ref, *refs
):
    ordered_ref, query_ref, kv_ref, gains_ref = refs[-4:]
    head_size = query_ref.shape[1]

    @pl.when(pl.program_id(0) == 0)
    def _():
        lane = lax.broadcasted_iota(jnp.int32, misc_ref.shape, 1)
        for k in range(2):
            column = jnp.where(lane == heads_ref[0] + k, misc_ref[...].astype(jnp.float32), 0.0)
            gains_ref[k : k + 1, :] = jnp.sum(column.T, axis=0, keepdims=True)

    cosine, sine = (cos_ref[...], sin_ref[...])

    def turn(value):
        return (value * cosine + pltpu.roll(value, head_size // 2, 1) * sine).astype(jnp.bfloat16)

    rows = x_ref[...].astype(jnp.float32)
    normed = (rows * inverse_rms(rows) * gains_ref[0:1, :]).astype(jnp.bfloat16)
    ordered_ref[...] = normed
    kv_ref[:, :head_size] = turn(mul(normed, key_ref[...]))
    kv_ref[:, head_size:] = mul(normed, value_ref[...]).astype(jnp.bfloat16)
    query_ref[...] = turn(mul(normed, w_query_ref[...]))


def enter(ranks, heads, x_span, in_full, at, cosine, sine, after):
    count = ranks.shape[0]
    rows, width = x_span.shape
    head_size = cosine.shape[1]
    here = lambda columns: pl.BlockSpec((rows // count, columns), lambda k, r, h: (k, 0))
    there = lambda columns: pl.BlockSpec((rows // count, columns), lambda k, r, h: (r[k], 0))
    weight = lambda name: pl.BlockSpec(
        (width, at[name][1]), lambda k, r, h: (0, at[name][0] // at[name][1])
    )
    return pl.pallas_call(
        enter_kernel,
        grid_spec=pltpu.PrefetchScalarGridSpec(
            num_scalar_prefetch=2,
            grid=(count,),
            in_specs=[
                here(width),
                weight("misc"),
                weight("key"),
                weight("value"),
                weight("query"),
                there(head_size),
                there(head_size),
            ]
            + [pl.BlockSpec(memory_space=pl.ANY)] * len(after),
            out_specs=(
                there(width),
                there(head_size),
                there(2 * head_size),
                pl.BlockSpec((8, width), lambda k, r, h: (0, 0)),
            ),
        ),
        out_shape=(
            jax.ShapeDtypeStruct((rows, width), jnp.bfloat16),
            jax.ShapeDtypeStruct((rows, head_size), jnp.bfloat16),
            jax.ShapeDtypeStruct((rows, 2 * head_size), jnp.bfloat16),
            jax.ShapeDtypeStruct((8, width), jnp.float32),
        ),
        compiler_params=compiler_params(),
        cost_estimate=small_cost(),
        name="enter",
    )(ranks, heads, x_span, in_full, in_full, in_full, in_full, cosine, sine, *after)


def weight_grads_kernel(*refs, counts):
    out_ref = refs[-1]
    start, used = (0, len(counts))
    for k, count in enumerate(counts):
        left = refs[k][...].T
        for ref in refs[used : used + count]:
            out_ref[:, start : start + ref.shape[1]] = mul(left, ref[...]).astype(jnp.bfloat16)
            start += ref.shape[1]
        used += count


def weight_grads(groups, width, start=0, buffer=None, after=()):
    rights = [right for _, group in groups for right in group]
    columns = sum(right.shape[1] for right in rights)
    depth = rights[0].shape[0]
    rows = groups[0][0].shape[1]
    operands = [left for left, _ in groups] + rights
    count = len(operands)
    extra = list(after) if buffer is None else [buffer] + list(after)

    def call(*refs):
        weight_grads_kernel(
            *refs[:count],
            refs[-1],
            counts=tuple(len(group) for _, group in groups),
        )

    return pl.pallas_call(
        call,
        grid=(rows // BLOCK,),
        out_shape=pltpu.HBM((rows, width), jnp.bfloat16),
        in_specs=[pl.BlockSpec((depth, BLOCK), lambda k: (0, k)) for _ in groups]
        + [pl.BlockSpec(right.shape, lambda k: (0, 0)) for right in rights]
        + [pl.BlockSpec(memory_space=pl.ANY)] * len(extra),
        out_specs=pl.BlockSpec(
            (pl.Element(BLOCK), pl.Element(columns)), lambda k: (k * BLOCK, start)
        ),
        input_output_aliases={} if buffer is None else {count: 0},
        compiler_params=compiler_params(),
        cost_estimate=pl.CostEstimate(
            flops=2 * rows * depth * columns,
            bytes_accessed=2 * (depth * (2 * rows + columns) + rows * columns),
            transcendentals=0,
        ),
        name="weight_grads",
    )(*operands, *extra)


def pack_kernel(*refs, turned):
    out_ref = refs[-1]
    start = 0
    for ref, turn in zip(refs, turned):
        piece = ref[...].T if turn else ref[...]
        out_ref[:, start : start + piece.shape[1]] = piece
        start += piece.shape[1]


def pack(pieces, turned, after):
    sizes = [piece.shape[::-1] if turn else piece.shape for piece, turn in zip(pieces, turned)]
    return pl.pallas_call(
        functools.partial(pack_kernel, turned=turned),
        out_shape=jax.ShapeDtypeStruct(
            (sizes[0][0], sum(size[1] for size in sizes)), jnp.bfloat16
        ),
        in_specs=in_vmem(len(pieces)) + [pl.BlockSpec(memory_space=pl.ANY)],
        out_specs=pl.BlockSpec(memory_space=pltpu.VMEM),
        compiler_params=compiler_params(),
        name="pack",
    )(*pieces, after)


def finish_kernel(
    ranks_ref,
    kv_ref,
    sums_ref,
    weight_ref,
    extra_ref,
    ssm_out_ref,
    attn_out_ref,
    gate_ref,
    ssm_ref,
    query_ref,
    misc_ref,
    shared_ref,
    whole_ref,
    *,
    at,
    sums_at,
):
    def of(name):
        start, size = sums_at[name]
        return sums_ref[:, start : start + size].astype(jnp.float32)

    ssm_out_ref[...] = of("ssm_out").T
    attn_out_ref[...] = of("attn_out").T
    gate_ref[...] = of("z")
    ssm_ref[...] = of("x")
    query_ref[...] = of("query")
    misc_ref[...] = of("misc")
    total = 0.0
    for name, (start, size) in at.items():
        product = of(name) * weight_ref[:, start : start + size].astype(jnp.float32)
        total += jnp.sum(product, axis=1, keepdims=True)
    total = total / extra_ref[:, 0:1]
    lane = lax.broadcasted_iota(jnp.int32, misc_ref.shape, 1)
    gains = jnp.where(lane == 0, total, jnp.where(lane == 1, extra_ref[:, 1:2], 0.0))
    zero = jnp.zeros_like(gains)
    first = kv_ref[0] == 0
    key, value = (of("key"), of("value"))
    pieces = (
        jnp.where(first, key, zero),
        jnp.where(first, zero, key),
        jnp.where(first, value, zero),
        jnp.where(first, zero, value),
        of("b"),
        of("c"),
        gains,
    )
    start = 0
    for piece in pieces:
        whole_ref[:, start : start + piece.shape[1]] = piece
        start += piece.shape[1]
    count = ranks_ref.shape[0]
    size = shared_ref.shape[0] // count
    for k in range(count):
        rows = pl.ds(pl.multiple_of(ranks_ref[k] * size, size), size)
        shared_ref[k * size : (k + 1) * size, :] = whole_ref[rows, :].astype(jnp.bfloat16)


def finish(ranks, kv_index, sums, weights, extra, at, sums_at):
    rows = weights.shape[0]
    shape = lambda *sizes: jax.ShapeDtypeStruct(sizes, jnp.float32)
    width = lambda name: sums_at[name][1]
    shared = 2 * (width("key") + width("value")) + width("b") + width("c") + LANES
    return pl.pallas_call(
        functools.partial(finish_kernel, at=at, sums_at=sums_at),
        out_shape=(
            shape(width("ssm_out"), rows),
            shape(width("attn_out"), rows),
            shape(rows, width("z")),
            shape(rows, width("x")),
            shape(rows, width("query")),
            shape(rows, width("misc")),
            jax.ShapeDtypeStruct((rows, shared), jnp.bfloat16),
        ),
        in_specs=[pl.BlockSpec(memory_space=pltpu.SMEM)] * 2 + in_vmem(3),
        out_specs=tuple(in_vmem(7)),
        scratch_shapes=[pltpu.VMEM((rows, shared), jnp.float32)],
        compiler_params=compiler_params(),
        name="finish",
    )(ranks, kv_index, sums, weights, extra)


def attend_kernel(rank_ref, query_ref, own_ref, *refs):
    pieces, (out_ref, low_ref, log_ref) = (refs[:-3], refs[-3:])
    span_length, head_size = query_ref.shape
    tile = own_ref.shape[0] // 2
    for block in range(span_length // tile):
        here = slice(block * tile, (block + 1) * tile)
        query_rows = query_ref[here, :]

        def step(kv_rows, carried, masked=False):
            top, total, summed = carried
            scores = tile_scores(kv_rows[:, :head_size], query_rows, head_size)
            if masked:
                scores = causal(scores)
            new_top = jnp.maximum(top, jnp.max(scores, axis=0, keepdims=True))
            probs = jnp.exp2(scores - new_top)
            scale = jnp.exp2(top - new_top)
            total = total * scale + jnp.sum(probs, axis=0, keepdims=True)
            summed = summed * scale + dot_first(kv_rows[:, head_size:], probs.astype(jnp.bfloat16))
            return (new_top, total, summed)

        carried = (
            jnp.full((1, tile), -1e30, jnp.float32),
            jnp.zeros((1, tile), jnp.float32),
            jnp.zeros((head_size, tile), jnp.float32),
        )
        carried = step(own_ref[here, :], carried, True)
        for earlier in range(block):
            carried = step(own_ref[earlier * tile : (earlier + 1) * tile, :], carried)
        for distance in range(1, 1 + len(pieces) // 2):
            pair = pieces[2 * distance - 2 : 2 * distance]

            def both(_, carried, pair=pair):
                return step(pair[1][...], step(pair[0][...], carried))

            valid = (rank_ref[0] >= distance).astype(jnp.int32)
            carried = lax.fori_loop(0, valid, both, carried)
        top, total, summed = carried
        result = summed / total
        out_ref[:, here] = result
        low_ref[here, :] = result.T.astype(jnp.bfloat16)
        log_ref[:, here] = top + jnp.log2(total)


def attend(rank, queries, own, pieces):
    span_length, head_size = queries.shape
    return pl.pallas_call(
        attend_kernel,
        out_shape=(
            jax.ShapeDtypeStruct((head_size, span_length), jnp.float32),
            jax.ShapeDtypeStruct((span_length, head_size), jnp.bfloat16),
            jax.ShapeDtypeStruct((1, span_length), jnp.float32),
        ),
        in_specs=[pl.BlockSpec(memory_space=pltpu.SMEM)] + in_vmem(2 + len(pieces)),
        out_specs=tuple(in_vmem(3)),
        compiler_params=compiler_params(),
        cost_estimate=small_cost(),
        name="attend",
    )(rank, queries, own, *pieces)


def attend_back_kernel(rank_ref, query_ref, own_ref, *refs):
    pieces, refs = (refs[:-13], refs[-13:])
    out_ref, log_ref, grad_ref, cos_ref, sin_ref, *_, d_query_ref, d_own_ref, d_far_ref, sums_ref = refs
    span_length, head_size = query_ref.shape
    tile = own_ref.shape[0] // 2
    score_scale = head_size**-0.5
    sums_ref[...] = jnp.zeros_like(sums_ref)
    for block in range(span_length // tile):
        here = slice(block * tile, (block + 1) * tile)
        query_rows = query_ref[here, :]
        grad_rows = grad_ref[here, grad_ref.shape[1] - head_size :]
        log_total = log_ref[:, here]
        delta_row = jnp.sum(
            grad_rows.astype(jnp.float32).T * out_ref[:, here], axis=0, keepdims=True
        )

        def step(kv_ref, start, at, d_query, masked=False):
            key_rows = kv_ref[start : start + tile, :head_size]
            scores = tile_scores(key_rows, query_rows, head_size)
            if masked:
                scores = causal(scores)
            probs = jnp.exp2(scores - log_total)
            d_probs = dot_last(kv_ref[start : start + tile, head_size:], grad_rows)
            d_scores = (probs * (d_probs - delta_row)).astype(jnp.bfloat16)
            rows = slice(at * tile, (at + 1) * tile)
            sums_ref[rows, head_size:] += mul(probs.astype(jnp.bfloat16), grad_rows)
            sums_ref[rows, :head_size] += mul(d_scores, query_rows)
            return d_query + dot_first(key_rows, d_scores)

        d_query = jnp.zeros((head_size, tile), jnp.float32)
        d_query = step(own_ref, block * tile, block, d_query, True)
        for earlier in range(block):
            d_query = step(own_ref, earlier * tile, earlier, d_query)
        for distance in range(1, 1 + len(pieces) // 2):

            def both(_, d_query, distance=distance):
                for k in (2 * distance - 2, 2 * distance - 1):
                    d_query = step(pieces[k], 0, 2 + k, d_query)
                return d_query

            valid = (rank_ref[0] >= distance).astype(jnp.int32)
            d_query = lax.fori_loop(0, valid, both, d_query)
        turned = d_query.T * score_scale
        d_query_ref[here, :] = (
            turned * cos_ref[here, :] - pltpu.roll(turned, head_size // 2, 1) * sin_ref[here, :]
        ).astype(jnp.bfloat16)
    lane = lax.broadcasted_iota(jnp.int32, (tile, 2 * head_size), 1)
    scale = jnp.where(lane < head_size, score_scale, 1.0)
    for at in range(2):
        rows = slice(at * tile, (at + 1) * tile)
        d_own_ref[rows, :] = sums_ref[rows, :] * scale
    for k in range(len(pieces)):
        rows = slice((2 + k) * tile, (3 + k) * tile)
        into = (k % 2) * (len(pieces) // 2) + k // 2
        d_far_ref[into * tile : (into + 1) * tile, :] = (sums_ref[rows, :] * scale).astype(
            jnp.bfloat16
        )


def attend_back(rank, queries, own, pieces, attended, log_totals, d_attn, cosine, sine, after):
    tile = own.shape[0] // 2
    return pl.pallas_call(
        attend_back_kernel,
        out_shape=(
            jax.ShapeDtypeStruct(queries.shape, jnp.bfloat16),
            jax.ShapeDtypeStruct(own.shape, jnp.float32),
            jax.ShapeDtypeStruct((len(pieces) * tile, own.shape[1]), jnp.bfloat16),
        ),
        in_specs=[pl.BlockSpec(memory_space=pltpu.SMEM)]
        + in_vmem(7 + len(pieces))
        + [pl.BlockSpec(memory_space=pl.ANY)] * len(after),
        out_specs=tuple(in_vmem(3)),
        scratch_shapes=[pltpu.VMEM(((2 + len(pieces)) * tile, own.shape[1]), jnp.float32)],
        compiler_params=compiler_params(),
        cost_estimate=small_cost(),
        name="attend_back",
    )(rank, queries, own, *pieces, attended, log_totals, d_attn, cosine, sine, *after)


def reorder_kernel(ranks_ref, *refs, count):
    out_ref = refs[-1]
    start = 0
    for ref in refs[:count]:
        out_ref[:, start : start + ref.shape[1]] = ref[...].astype(out_ref.dtype)
        start += ref.shape[1]


def reorder(ranks, pieces, inverse=False, after=()):
    count = ranks.shape[0]
    rows = pieces[0].shape[0] // count
    width = sum(piece.shape[1] for piece in pieces)
    there = lambda k, ranks: (ranks[k], 0)
    here = lambda k, ranks: (k, 0)
    return pl.pallas_call(
        functools.partial(reorder_kernel, count=len(pieces)),
        grid_spec=pltpu.PrefetchScalarGridSpec(
            num_scalar_prefetch=1,
            grid=(count,),
            in_specs=[
                pl.BlockSpec((rows, piece.shape[1]), here if inverse else there)
                for piece in pieces
            ]
            + [pl.BlockSpec(memory_space=pl.ANY)] * len(after),
            out_specs=pl.BlockSpec((rows, width), there if inverse else here),
        ),
        out_shape=jax.ShapeDtypeStruct((count * rows, width), jnp.bfloat16),
        compiler_params=compiler_params(),
        cost_estimate=small_cost(),
        name="reorder",
    )(ranks, *pieces, *after)


def lower_ones(size, dtype=jnp.float32):
    row = lax.broadcasted_iota(jnp.int32, (size, size), 0)
    column = lax.broadcasted_iota(jnp.int32, (size, size), 1)
    return (row >= column).astype(dtype)


def precise(left_side, right_side):
    return jnp.dot(
        left_side, right_side, precision=HIGH_PRECISION, preferred_element_type=jnp.float32
    )


def spread_heads(columns, head_size, width):
    lane = lax.broadcasted_iota(jnp.int32, (columns.shape[0], 2 * head_size), 1)
    pairs = [
        jnp.where(lane < head_size, columns[:, k : k + 1], columns[:, k + 1 : k + 2])
        for k in range(0, width // head_size, 2)
    ]
    return jnp.concatenate(pairs, axis=1)


def head_ones(width, head_size, lanes, dtype):
    at = lax.broadcasted_iota(jnp.int32, (width, lanes), 0)
    lane = lax.broadcasted_iota(jnp.int32, (width, lanes), 1)
    low = lane * head_size
    return ((at >= low) & (at < low + head_size)).astype(dtype)


def scan_first_kernel(
    pre_ref, bias_ref, rate_ref, x_ref, b_ref, delta_ref, cum_ref, delta_row_ref, cum_row_ref, state_ref, log_ref
):
    @pl.when(pl.program_id(0) == 0)
    def _():
        state_ref[...] = jnp.zeros_like(state_ref)
        log_ref[...] = jnp.zeros_like(log_ref)

    delta = jax.nn.softplus(pre_ref[...] + bias_ref[...])
    log_step = -delta * rate_ref[...]
    cumulative = precise(lower_ones(log_step.shape[0]), log_step)
    delta_ref[...] = delta
    cum_ref[...] = cumulative
    delta_row_ref[...] = delta.T[:8]
    cum_row_ref[...] = cumulative.T[:8]
    ending = cumulative[-1:, :]
    weight = jnp.exp(ending - cumulative + log_ref[...]) * delta
    width = x_ref.shape[1]
    x_low = x_ref[...].astype(jnp.bfloat16).astype(jnp.float32)
    weighted = (x_low * spread_heads(weight, MIXER_HEAD_SIZE, width)).astype(jnp.bfloat16)
    state_ref[...] += dot_first(b_ref[...].astype(jnp.bfloat16), weighted)
    log_ref[...] += ending


def part(projected, start, width, order=lambda c: c):
    at = start // width
    return (projected, pl.BlockSpec((BLOCK, width), lambda c: (order(c), at)))


def run_scan(
    kernel, chunks, operands, out_shape, out_specs, name, scratch=(), after=(), mebibytes=20
):
    count = len(operands)
    operands = operands + [(array, pl.BlockSpec(memory_space=pl.ANY)) for array in after]

    def call(*refs):
        kernel(*refs[:count], *refs[count + len(after) :])

    return pl.pallas_call(
        call,
        grid=(chunks,),
        out_shape=out_shape,
        in_specs=[spec for _, spec in operands],
        out_specs=out_specs,
        scratch_shapes=list(scratch),
        compiler_params=compiler_params(mebibytes),
        cost_estimate=small_cost(),
        name=name,
    )(*[array for array, _ in operands])


def whole(array):
    return (array, pl.BlockSpec(array.shape, lambda c: (0,) * array.ndim))


def scan_first(at, bias, rate):
    rows, lanes = (at["x"][0].shape[0], bias.shape[1])
    chunks = rows // BLOCK
    back = lambda c: chunks - 1 - c
    width, state_size = (at["x"][2], at["b"][2])
    by_chunk = pl.BlockSpec((BLOCK, lanes), lambda c: (back(c), 0))
    across = pl.BlockSpec((8, BLOCK), lambda c: (0, back(c)))
    shape = lambda *sizes: jax.ShapeDtypeStruct(sizes, jnp.float32)
    return run_scan(
        scan_first_kernel,
        chunks,
        [
            part(*at["misc"], back),
            whole(bias),
            whole(rate),
            part(*at["x"], back),
            part(*at["b"], back),
        ],
        (
            shape(rows, lanes),
            shape(rows, lanes),
            shape(8, rows),
            shape(8, rows),
            shape(state_size, width),
            shape(1, lanes),
        ),
        (
            by_chunk,
            by_chunk,
            across,
            across,
            pl.BlockSpec((state_size, width), lambda c: (0, 0)),
            pl.BlockSpec((1, lanes), lambda c: (0, 0)),
        ),
        "scan_first",
    )


def chained(refs, width):
    state = jnp.zeros((refs[0].shape[0] - 16, width), jnp.float32)
    for ref in reversed(refs):
        logs = ref[-16:, :LANES].astype(jnp.float32)
        decay = jnp.exp(jnp.sum(logs[:3], axis=0, keepdims=True))
        state = ref[:-16].astype(jnp.float32) + spread_heads(decay, MIXER_HEAD_SIZE, width) * state
    return state


def scan_kernel(
    x_ref,
    z_ref,
    b_ref,
    c_ref,
    delta_ref,
    cum_ref,
    delta_row_ref,
    cum_row_ref,
    near_ref,
    next_ref,
    far_ref,
    skip_ref,
    scanned_ref,
    gated_ref,
    states_ref,
    state_ref,
):
    @pl.when(pl.program_id(0) == 0)
    def _():
        state_ref[...] = chained((near_ref, next_ref, far_ref), x_ref.shape[1])

    head_size = MIXER_HEAD_SIZE
    pair = 2 * head_size
    size, width = x_ref.shape
    state = state_ref[...]
    states_ref[0] = state
    delta, cumulative = (delta_ref[...], cum_ref[...])
    delta_row, cum_row = (delta_row_ref[...], cum_row_ref[...])
    bmat, cmat = (b_ref[...].astype(jnp.bfloat16), c_ref[...].astype(jnp.bfloat16))
    x_all = x_ref[...].astype(jnp.bfloat16)
    inner = dot_last(cmat, bmat)
    row = lax.broadcasted_iota(jnp.int32, (size, size), 0)
    column = lax.broadcasted_iota(jnp.int32, (size, size), 1)
    allowed = row >= column
    lane = lax.broadcasted_iota(jnp.int32, (size, pair), 1)
    from_state = mul(cmat, state.astype(jnp.bfloat16))
    spread = spread_heads(jnp.exp(cumulative), head_size, width)
    for first in range(0, width // head_size, 2):
        here = slice(first * head_size, first * head_size + pair)
        x_pair = x_all[:, here]
        total = from_state[:, here] * spread[:, here]
        total += skip_ref[:, here] * x_pair.astype(jnp.float32)
        for head in (first, first + 1):
            gap = cumulative[:, head : head + 1] - cum_row[head : head + 1, :]
            decay = jnp.exp(jnp.where(allowed, gap, -1e30))
            mixing = inner * decay * delta_row[head : head + 1, :]
            x_head = jnp.where((lane >= head_size) == (head > first), x_pair, 0.0)
            total += mul(mixing.astype(jnp.bfloat16), x_head.astype(jnp.bfloat16))
        scanned_ref[:, here] = total
        gate = z_ref[:, here]
        gated_ref[:, here] = (total * (gate * jax.nn.sigmoid(gate))).astype(jnp.bfloat16)
    ending = cumulative[-1:, :]
    weight = spread_heads(jnp.exp(ending - cumulative) * delta, head_size, width)
    weighted = (x_all.astype(jnp.float32) * weight).astype(jnp.bfloat16)
    state_ref[...] = state * spread[-1:, :] + dot_first(bmat, weighted)


def scan(at, delta, cumulative, delta_row, cum_row, entry, skip, after):
    rows = delta.shape[0]
    state_size, width = (at["b"][2], at["x"][2])
    chunks = rows // BLOCK
    by_chunk = pl.BlockSpec((BLOCK, width), lambda c: (c, 0))
    lanes = delta.shape[1]
    across = pl.BlockSpec((8, BLOCK), lambda c: (0, c))
    return run_scan(
        scan_kernel,
        chunks,
        [
            part(*at["x"]),
            part(*at["z"]),
            part(*at["b"]),
            part(*at["c"]),
            part(delta, 0, lanes),
            part(cumulative, 0, lanes),
            (delta_row, across),
            (cum_row, across),
            *[whole(packed) for packed in entry],
            whole(skip),
        ],
        (
            jax.ShapeDtypeStruct((rows, width), jnp.float32),
            jax.ShapeDtypeStruct((rows, width), jnp.bfloat16),
            jax.ShapeDtypeStruct((chunks, state_size, width), jnp.float32),
        ),
        (by_chunk, by_chunk, pl.BlockSpec((1, state_size, width), lambda c: (c, 0, 0))),
        "scan",
        [pltpu.VMEM((state_size, width), jnp.float32)],
        after,
    )


def scan_back_first_kernel(
    grad_ref, z_ref, scanned_ref, c_ref, cum_ref, d_scanned_ref, d_gate_ref, state_ref, log_ref
):
    @pl.when(pl.program_id(0) == 0)
    def _():
        state_ref[...] = jnp.zeros_like(state_ref)
        log_ref[...] = jnp.zeros_like(log_ref)

    gate = z_ref[...]
    chance = jax.nn.sigmoid(gate)
    grad = grad_ref[:, : z_ref.shape[1]].astype(jnp.float32)
    d_scanned = grad * (gate * chance)
    d_scanned_ref[...] = d_scanned
    d_gate_ref[...] = (
        grad * scanned_ref[...] * (chance * (1.0 + gate * (1.0 - chance)))
    ).astype(jnp.bfloat16)
    cumulative = cum_ref[...]
    decay = spread_heads(jnp.exp(cumulative + log_ref[...]), MIXER_HEAD_SIZE, z_ref.shape[1])
    state_ref[...] += dot_first(
        c_ref[...].astype(jnp.bfloat16), (d_scanned * decay).astype(jnp.bfloat16)
    )
    log_ref[...] += cumulative[-1:, :]


def scan_back_first(grads, at, scanned, cumulative):
    rows, width = scanned.shape
    state_size, lanes = (at["c"][2], cumulative.shape[1])
    by_chunk = pl.BlockSpec((BLOCK, width), lambda c: (c, 0))
    return run_scan(
        scan_back_first_kernel,
        rows // BLOCK,
        [
            part(grads, 0, grads.shape[1]),
            part(*at["z"]),
            part(scanned, 0, width),
            part(*at["c"]),
            part(cumulative, 0, lanes),
        ],
        (
            jax.ShapeDtypeStruct((rows, width), jnp.float32),
            jax.ShapeDtypeStruct((rows, width), jnp.bfloat16),
            jax.ShapeDtypeStruct((state_size, width), jnp.float32),
        ),
        (by_chunk, by_chunk, pl.BlockSpec((state_size, width), lambda c: (0, 0))),
        "scan_back_first",
        [pltpu.VMEM((1, lanes), jnp.float32)],
    )


def scan_back_kernel(
    x_ref,
    grad_ref,
    b_ref,
    c_ref,
    pre_ref,
    bias_ref,
    rate_ref,
    delta_ref,
    cum_ref,
    cum_row_ref,
    states_ref,
    near_ref,
    next_ref,
    far_ref,
    skip_ref,
    d_x_ref,
    d_b_ref,
    d_c_ref,
    d_pre_ref,
    sums_ref,
    state_ref,
):
    @pl.when(pl.program_id(0) == 0)
    def _():
        state_ref[...] = chained((near_ref, next_ref, far_ref), x_ref.shape[1])
        sums_ref[...] = jnp.zeros_like(sums_ref)

    head_size = MIXER_HEAD_SIZE
    pair = 2 * head_size
    size, width = x_ref.shape
    lanes = delta_ref.shape[1]
    low = jnp.bfloat16
    delta, cumulative, cum_row = (delta_ref[...], cum_ref[...], cum_row_ref[...])
    bmat, cmat = (b_ref[...].astype(low), c_ref[...].astype(low))
    x_all = x_ref[...].astype(low)
    x_single = x_all.astype(jnp.float32)
    grad = grad_ref[...]
    grad_low = grad.astype(low)
    state = states_ref[0]
    state_low = state.astype(low)
    after = state_ref[...]
    after_low = after.astype(low)
    ending = cumulative[-1:, :]
    row = lax.broadcasted_iota(jnp.int32, (size, size), 0)
    column = lax.broadcasted_iota(jnp.int32, (size, size), 1)
    later = column >= row
    before = (row > column).astype(low)
    onward = later.astype(low)
    lane = lax.broadcasted_iota(jnp.int32, (size, pair), 1)
    head_lane = lax.broadcasted_iota(jnp.int32, (size, lanes), 1)
    sum_heads = head_ones(width, head_size, lanes, low)

    inner = dot_last(bmat, cmat)
    from_after = mul(bmat, after_low)
    weight = jnp.exp(ending - cumulative)
    spread_weight = spread_heads(weight * delta, head_size, width)
    spread = spread_heads(jnp.exp(cumulative), head_size, width)
    to_end = mul((x_single * from_after).astype(low), sum_heads)
    through = jnp.exp(cumulative) * mul((grad * mul(cmat, state_low)).astype(low), sum_heads)
    carried = jnp.sum(state * after, axis=0, keepdims=True) * spread[-1:, :]
    carried = precise(carried, sum_heads.astype(jnp.float32))
    d_delta = weight * to_end
    d_log = (
        mul(onward, through.astype(low)) + mul(before, (d_delta * delta).astype(low)) + carried
    )

    d_inner = jnp.zeros((size, size), jnp.float32)
    for first in range(0, width // head_size, 2):
        here = slice(first * head_size, first * head_size + pair)
        x_pair, grad_pair = (x_all[:, here], grad_low[:, here])
        d_x = from_after[:, here] * spread_weight[:, here] + skip_ref[:, here] * grad[:, here]
        for head in (first, first + 1):
            mine = (lane >= head_size) == (head > first)
            gap = cum_row[head : head + 1, :] - cumulative[:, head : head + 1]
            decay = jnp.exp(jnp.where(later, gap, -1e30))
            delta_column = delta[:, head : head + 1]
            d_mixing = dot_last(jnp.where(mine, x_pair, 0.0).astype(low), grad_pair) * decay
            d_inner += d_mixing * delta_column
            flow = d_mixing * inner
            mixing = inner * decay * delta_column
            d_x += mul(mixing.astype(low), jnp.where(mine, grad_pair, 0.0).astype(low))
            d_delta_head = jnp.sum(flow, axis=1, keepdims=True)
            passing = mul(before, (flow * delta_column).astype(low))
            d_log_head = jnp.sum(jnp.where(later, passing, 0.0), axis=1, keepdims=True)
            d_delta += jnp.where(head_lane == head, d_delta_head, 0.0)
            d_log += jnp.where(head_lane == head, d_log_head, 0.0)
        d_x_ref[:, here] = d_x.astype(low)

    d_inner_low = d_inner.astype(low)
    scaled_grad = (grad * spread).astype(low)
    weighted = (x_single * spread_weight).astype(low)
    d_b_ref[...] = (mul(d_inner_low, cmat) + dot_last(weighted, after_low)).astype(low)
    d_c_ref[...] = (dot_first(d_inner_low, bmat) + dot_last(scaled_grad, state_low)).astype(low)
    state_ref[...] = after * spread[-1:, :] + dot_first(cmat, scaled_grad)
    rate = rate_ref[...]
    d_pre = (d_delta - d_log * rate) * jax.nn.sigmoid(pre_ref[...] + bias_ref[...])
    d_pre = jnp.where(head_lane < width // head_size, d_pre, 0.0)
    d_pre_ref[...] = d_pre.astype(low)
    skip_sum = precise(
        jnp.sum(grad * x_single, axis=0, keepdims=True), sum_heads.astype(jnp.float32)
    )
    sums_ref[0:1, :] += jnp.sum(d_pre, axis=0, keepdims=True)
    sums_ref[1:2, :] += jnp.sum(d_log * (-delta * rate), axis=0, keepdims=True)
    sums_ref[2:3, :] += skip_sum


def scan_back(
    at, d_scanned, bias, rate, delta, cumulative, cum_row, states, entry, skip, after
):
    rows, width = d_scanned.shape
    state_size, lanes = (at["b"][2], delta.shape[1])
    chunks = rows // BLOCK
    back = lambda c: chunks - 1 - c
    by_chunk = lambda columns: pl.BlockSpec((BLOCK, columns), lambda c: (back(c), 0))
    shape = lambda columns: jax.ShapeDtypeStruct((rows, columns), jnp.bfloat16)
    return run_scan(
        scan_back_kernel,
        chunks,
        [
            part(*at["x"], back),
            part(d_scanned, 0, width, back),
            part(*at["b"], back),
            part(*at["c"], back),
            part(*at["misc"], back),
            whole(bias),
            whole(rate),
            part(delta, 0, lanes, back),
            part(cumulative, 0, lanes, back),
            (cum_row, pl.BlockSpec((8, BLOCK), lambda c: (0, back(c)))),
            (states, pl.BlockSpec((1, state_size, width), lambda c: (back(c), 0, 0))),
            *[whole(packed) for packed in entry],
            whole(skip),
        ],
        (
            shape(width),
            shape(state_size),
            shape(state_size),
            shape(lanes),
            jax.ShapeDtypeStruct((8, lanes), jnp.float32),
        ),
        (
            by_chunk(width),
            by_chunk(state_size),
            by_chunk(state_size),
            by_chunk(lanes),
            pl.BlockSpec((8, lanes), lambda c: (0, 0)),
        ),
        "scan_back",
        [pltpu.VMEM((state_size, width), jnp.float32)],
        after,
        44,
    )


def on_heads(value, move):
    devices = lax.axis_size("heads")
    pairs = []
    for at in range(devices):
        z, core = move(at // 2, at % 2)
        pairs.append((at, 2 * (z % (devices // 2)) + core))
    return lax.ppermute(value, "heads", pairs)


def to_partner(value):
    return on_heads(value, lambda z, core: (z, 1 - core))


def along(value):
    return on_heads(value, lambda z, core: (z + 1 - 2 * core, core))


def against(value):
    return on_heads(value, lambda z, core: (z - 1 + 2 * core, core))


def chunk_ranks():
    devices = lax.axis_size("heads")
    z, core = (lax.axis_index("heads") // 2, lax.axis_index("heads") % 2)
    step, other = (1 - 2 * core, 1 - core)
    owners = (
        (z, core),
        (z + 2, core),
        (z - step, core),
        (z - step, other),
        (z, other),
        (z + 2, other),
        (z + step, other),
        (z + step, core),
    )
    return jnp.stack([2 * ((at + devices) % (devices // 2)) + side for at, side in owners])


def gather_rows(own):
    partner = to_partner(own)
    near = along(own)
    near_other = along(partner)
    far = along(near)
    mine = (own, far, near, near_other)
    theirs = (partner, to_partner(far), to_partner(near), to_partner(near_other))
    return jnp.concatenate(mine + theirs, axis=0)


def scatter_rows(product, half, late=None):
    chunk = half // 4
    got = to_partner(product(slice(half, 2 * half)).astype(jnp.bfloat16))
    summed = product(slice(0, half)) + got.astype(jnp.float32)
    low = summed[chunk:].astype(jnp.bfloat16)
    far = against(low[:chunk])
    near_other = against(low[2 * chunk :])
    near = low[chunk : 2 * chunk].astype(jnp.float32) + far.astype(jnp.float32)
    near = against((near if late is None else near + late).astype(jnp.bfloat16))
    total = summed[:chunk] + near.astype(jnp.float32)
    return total + to_partner(near_other).astype(jnp.float32), far


def across(value, bit):
    devices = lax.axis_size("heads")
    return lax.ppermute(value, "heads", [(at, at ^ bit) for at in range(devices)])


def gather_small(value):
    for bit in (1, 2, 4):
        value = jnp.concatenate([value, across(value, bit)], axis=0)
    return value


def scatter_small(value):
    for bit in (4, 2, 1):
        half = value.shape[0] // 2
        got = across(value[half:].astype(jnp.bfloat16), bit)
        value = value[:half].astype(jnp.float32) + got.astype(jnp.float32)
    return value


def on_blocks(value, step):
    devices = lax.axis_size("blk")
    pairs = [(at, at + step) for at in range(devices) if 0 <= at + step < devices]
    return lax.ppermute(value, "blk", pairs)


def from_earlier(value, step=1):
    return tuple(on_blocks(value, distance * step) for distance in (1, 2, 3))


def pack_state(state, log_total):
    high = log_total.astype(jnp.bfloat16)
    rest = log_total - high.astype(jnp.float32)
    middle = rest.astype(jnp.bfloat16)
    low = (rest - middle.astype(jnp.float32)).astype(jnp.bfloat16)
    logs = jnp.concatenate([high, middle, low], axis=0)
    logs = jnp.pad(logs, ((0, 16 - logs.shape[0]), (0, state.shape[1] - logs.shape[1])))
    return jnp.concatenate([state.astype(jnp.bfloat16), logs], axis=0)


def sum_blocks(value):
    for axis in ("dp", "blk"):
        for bit in (1, 2):
            value = value + lax.ppermute(
                value, axis, [(at, at ^ bit) for at in range(lax.axis_size(axis))]
            )
    return value


def weight_sum(grads):
    return lax.psum_scatter(grads, ("dp", "blk"), scatter_dimension=0, tiled=True)


def split_columns(value_in, widths):
    pieces, start = [], 0
    for width in widths:
        pieces.append(value_in[:, start : start + width])
        start += width
    return pieces


def inverse_rms(rows_in):
    return lax.rsqrt(jnp.mean(rows_in * rows_in, axis=-1, keepdims=True) + norm_eps)


def norm_back(rows_in, gain_in, cotangent):
    inverse = inverse_rms(rows_in)
    scaled = rows_in * inverse
    weighted = cotangent * gain_in
    return inverse * (weighted - scaled * jnp.mean(weighted * scaled, axis=-1, keepdims=True))


def shards(
    x_in,
    out_grad,
    norm_one,
    w_query,
    w_key,
    w_value,
    output_gate_weight,
    mixer_input_weight,
    w_delta,
    w_bmat,
    w_cmat,
    delta_bias,
    decay_log,
    skip_gain,
    w_attn_out,
    mixer_output_weight,
    norm_two,
    w_gate,
    w_up,
    w_down,
):
    heads_count = lax.axis_size("heads")
    head_rank = lax.axis_index("heads")
    core = head_rank % 2
    block_rank = lax.axis_index("blk")
    rank = block_rank.astype(jnp.int32)[None]
    own_rows = x_in.shape[0]
    span_length = own_rows * heads_count
    half_span = span_length // 2
    span_start = block_rank * span_length
    query_width = w_query.shape[1]
    mixer_width = mixer_input_weight.shape[1]
    heads = mixer_width // MIXER_HEAD_SIZE
    state_size = w_bmat.shape[1]
    hidden_width = w_gate.shape[1]
    rows_of = w_query.shape[0]
    kv_index = head_rank * (query_width // HD) // (QH // KVH)
    kv_width = KVH * HD
    low = jnp.bfloat16
    ranks = chunk_ranks().astype(jnp.int32)
    turns = (head_rank ^ jnp.arange(heads_count)).astype(jnp.int32)

    gains = jnp.stack([norm_one, norm_two], axis=1)
    gains = jnp.pad(gains, ((0, 0), (0, LANES - 2)))
    shared = jnp.concatenate([w_key, w_value, w_bmat, w_cmat, gains], axis=1)
    shared = reorder(turns, [gather_small(shared)], inverse=True)
    key_part = lax.dynamic_slice_in_dim(shared, kv_index * HD, HD, 1)
    value_part = lax.dynamic_slice_in_dim(shared, kv_width + kv_index * HD, HD, 1)
    state_part = shared[:, 2 * kv_width : 2 * kv_width + 2 * state_size]
    gain_part = shared[:, 2 * kv_width + 2 * state_size :][:, :2]
    misc_part = jnp.concatenate(
        [w_delta, gain_part, jnp.zeros((rows_of, LANES - heads - 2), low)], axis=1
    )
    in_names = ("z", "x", "query", "b", "c", "misc", "key", "value")
    in_widths = (mixer_width, mixer_width, query_width, state_size, state_size, LANES, HD, HD)
    starts = [sum(in_widths[:k]) for k in range(len(in_widths))]
    at = dict(zip(in_names, zip(starts, in_widths)))
    in_first = jnp.concatenate([output_gate_weight, mixer_input_weight, w_query], axis=1)
    in_second = jnp.concatenate([state_part, misc_part, key_part, value_part], axis=1)
    in_own = jnp.concatenate([in_first, in_second], axis=1)
    mix_own = pack((mixer_output_weight, w_attn_out), (True, True), w_gate)
    first_own = jnp.concatenate([in_own, mix_own], axis=1)
    first_full = lax.all_gather(first_own, ("dp", "blk"), axis=0, tiled=True)
    in_full, mix_t = (first_full[:, : in_own.shape[1]], first_full[:, in_own.shape[1] :])
    x_float = x_in.astype(jnp.float32)
    zero = 0.0 * in_own[0, 0]
    x_span = gather_rows(x_in + zero)
    ffn_grad = gather_rows(out_grad + 0.0 * x_span[0, 0])
    ffn_own = pack((w_gate, w_up, w_down), (False, False, True), x_span)
    ffn_full = lax.all_gather(ffn_own, ("dp", "blk"), axis=0, tiled=True)
    mixed_width = query_width + mixer_width
    gate_full, up_full, down_t = split_columns(ffn_full, (hidden_width,) * 3)
    positions = (span_start + jnp.arange(span_length)).astype(jnp.float32)
    freqs = rope_base ** (-2.0 * jnp.arange(HD // 2, dtype=jnp.float32) / HD)
    angles = positions[:, None] * freqs[None, :]
    cosine, sine = (jnp.cos(angles), jnp.sin(angles))
    cosine = jnp.concatenate([cosine, cosine], axis=1)
    sine = jnp.concatenate([-sine, sine], axis=1)
    normed_ordered, queries, keys_values, gain_rows = enter(
        ranks, jnp.full((1,), heads, jnp.int32), x_span, first_full, at, cosine, sine, [corner(ffn_own)] + ends(ffn_grad)
    )
    gain_one, gain_two = (gain_rows[0:1], gain_rows[1:2])
    mine = lax.dynamic_slice_in_dim(keys_values, core * half_span, half_span, 0)
    pieces = []
    for piece in from_earlier(mine):
        pieces += [piece, to_partner(piece)]
    gate_raw = simple_product(normed_ordered, in_full[:, :mixer_width])
    x_raw = simple_product(normed_ordered, in_full[:, mixer_width : 2 * mixer_width])
    state_raw = simple_product(normed_ordered, in_full[:, at["b"][0] : at["key"][0]])
    raw = {
        "z": (gate_raw, 0, mixer_width),
        "x": (x_raw, 0, mixer_width),
        "b": (state_raw, 0, state_size),
        "c": (state_raw, state_size, state_size),
        "misc": (state_raw, 2 * state_size, LANES),
    }

    pad_lanes = lambda vector: jnp.pad(vector, (0, LANES - heads))[None]
    bias, rate = (pad_lanes(delta_bias), pad_lanes(jnp.exp(decay_log)))
    skip = jnp.repeat(skip_gain, MIXER_HEAD_SIZE)[None]
    delta, cumulative, delta_row, cum_row, local_state, local_log = scan_first(raw, bias, rate)
    entry_states = from_earlier(pack_state(local_state, local_log))
    attended, attn_part, log_totals = attend(rank, queries, keys_values, pieces)
    scanned, gated, states = scan(
        raw, delta, cumulative, delta_row, cum_row, entry_states, skip, [corner(attn_part)]
    )
    mixers = reorder(ranks, [gated, attn_part])
    ffn_zero = 0.0 * ffn_full[0, 0].astype(jnp.float32)
    mixed, _ = scatter_rows(lambda rows: dot_last(mixers[rows], mix_t), half_span, ffn_zero)
    middle = x_float + mixed
    middle_scaled = middle * inverse_rms(middle)
    normed_two = gather_rows((middle_scaled * gain_two).astype(low))
    ffn_gate = simple_product(normed_two, gate_full)
    ffn_up = simple_product(normed_two, up_full)
    ffn_sig = jax.nn.sigmoid(ffn_gate)
    hidden = (ffn_gate * ffn_sig * ffn_up).astype(low)

    d_hidden = simple_product(ffn_grad, down_t)
    d_ffn_gate = (d_hidden * ffn_up * (ffn_sig * (1.0 + ffn_gate * (1.0 - ffn_sig)))).astype(low)
    d_ffn_up = (d_hidden * (ffn_gate * ffn_sig)).astype(low)
    d_normed_two, d_two_far = scatter_rows(
        lambda rows: dot_last(d_ffn_gate[rows], gate_full) + dot_last(d_ffn_up[rows], up_full),
        half_span,
    )
    ffn_grads = weight_grads(
        [(normed_two, [d_ffn_gate, d_ffn_up]), (ffn_grad, [hidden])],
        3 * hidden_width,
        after=[corner(d_two_far)],
    )
    ffn_sums = weight_sum(ffn_grads).astype(jnp.float32)
    grad_gate, grad_up, grad_down_t = split_columns(ffn_sums, (hidden_width,) * 3)
    grad_two_part = jnp.sum(grad_gate * w_gate + grad_up * w_up, axis=1, keepdims=True)
    gain_own = gain_part.astype(jnp.float32)
    grad_two_part = grad_two_part / gain_own[:, 1:2]
    d_middle = out_grad.astype(jnp.float32) + norm_back(middle, gain_two, d_normed_two)
    mix_grad = gather_rows(d_middle.astype(low))
    d_mixers = reorder(
        ranks, [simple_product(mix_grad, mix_t).astype(low)], inverse=True, after=[corner(ffn_grads)]
    )
    d_scanned, d_gate_z, d_entry = scan_back_first(d_mixers, raw, scanned, cumulative)
    d_entry = pack_state(d_entry, local_log)
    after_states = from_earlier(d_entry, -1)
    mix_width = mixed_width + mixer_width
    all_width = mixed_width + in_own.shape[1]
    mix_grads = weight_grads(
        [(mix_grad, [mixers]), (normed_ordered, [d_gate_z])], all_width, after=[corner(d_entry)]
    )
    d_query, d_own, d_far = attend_back(
        rank, queries, keys_values, pieces, attended, log_totals, d_mixers, cosine, sine, [corner(mix_grads), *map(corner, after_states)]
    )
    d_ssm_in, d_bmat, d_cmat, d_pre, sums = scan_back(
        raw,
        d_scanned,
        bias,
        rate,
        delta,
        cumulative,
        cum_row,
        states,
        after_states,
        skip,
        [corner(d_query)],
    )
    far_half = d_far.shape[0] // 2
    d_mine = lax.dynamic_slice_in_dim(d_own, core * half_span, half_span, 0)
    d_theirs = lax.dynamic_slice_in_dim(d_own, (1 - core) * half_span, half_span, 0)
    d_mine = d_mine + to_partner(d_theirs.astype(low)).astype(jnp.float32)
    d_far = d_far[:far_half].astype(jnp.float32) + to_partner(d_far[far_half:]).astype(jnp.float32)
    d_one, d_two, d_three = (
        d_far[k * half_span : (k + 1) * half_span] for k in range(d_far.shape[0] // half_span)
    )
    d_one = d_one + on_blocks(d_two.astype(low), -1).astype(jnp.float32)
    d_mine = d_mine + on_blocks(d_one.astype(low), -1).astype(jnp.float32)
    d_mine = d_mine + on_blocks(d_three.astype(low), -3).astype(jnp.float32)
    half_cos = lax.dynamic_slice_in_dim(cosine, core * half_span, half_span, 0)
    half_sin = lax.dynamic_slice_in_dim(sine, core * half_span, half_span, 0)
    d_key = d_mine[:, :HD]
    d_key = d_key * half_cos - jnp.roll(d_key, HD // 2, axis=1) * half_sin
    d_mine = jnp.concatenate([d_key, d_mine[:, HD:]], axis=1).astype(low)
    d_keys_values = lax.dynamic_update_slice_in_dim(
        jnp.zeros((span_length, 2 * HD), low), d_mine, core * half_span, 0
    )

    scan_rights = [d_ssm_in, d_bmat, d_cmat, d_pre]
    in_grads = weight_grads([(normed_ordered, scan_rights)], all_width, mix_width, mix_grads)
    late_rights = [d_keys_values, d_query]
    late_start = mix_width + sum(array.shape[1] for array in scan_rights)
    in_grads = weight_grads([(normed_ordered, late_rights)], all_width, late_start, in_grads)
    in_sums = weight_sum(in_grads)
    d_projected = reorder(
        ranks,
        [d_gate_z, d_ssm_in, d_query, d_bmat, d_cmat, d_pre, d_keys_values],
        after=[corner(in_grads)],
    )
    d_normed, _ = scatter_rows(lambda rows: dot_last(d_projected[rows], in_full), half_span)
    input_grad = d_middle + norm_back(x_float, gain_one, d_normed)
    back_zero = 0.0 * d_query[0, 0].astype(jnp.float32)
    ffn_out, _ = scatter_rows(
        lambda rows: dot_last(hidden[rows], down_t) + back_zero, half_span
    )
    activations = (middle + ffn_out).astype(low)
    sums_names = ("ssm_out", "attn_out", "z", "x", "b", "c", "misc", "key", "value", "query")
    sums_widths = [mixer_width, query_width] + [at[name][1] for name in sums_names[2:]]
    sums_starts = [sum(sums_widths[:k]) for k in range(len(sums_widths))]
    sums_at = dict(zip(sums_names, zip(sums_starts, sums_widths)))
    extra = jnp.concatenate([gain_own[:, 0:1], grad_two_part], axis=1)
    extra = jnp.pad(extra, ((0, 0), (0, LANES - 2)))
    grad_ssm_out, grad_attn_out, grad_gatez, grad_ssmx, grad_query, misc_sums, shared_parts = finish(
        turns,
        kv_index.astype(jnp.int32)[None],
        in_sums,
        in_own,
        extra,
        at,
        sums_at,
    )
    shared_sums = scatter_small(shared_parts)
    grad_key, grad_value, grad_bmat, grad_cmat, gain_sums = split_columns(
        shared_sums, (kv_width, kv_width, state_size, state_size, LANES)
    )
    small_sums = sum_blocks(sums)[:, :heads]
    return (
        activations,
        input_grad,
        gain_sums[:, 0],
        grad_query,
        grad_key,
        grad_value,
        grad_gatez,
        grad_ssmx,
        misc_sums[:, :heads],
        grad_bmat,
        grad_cmat,
        small_sums[0],
        small_sums[1],
        small_sums[2],
        grad_attn_out,
        grad_ssm_out,
        gain_sums[:, 1],
        grad_gate,
        grad_up,
        grad_down_t.T,
    )


def solution(mesh):
    placed = (
        P(("dp", "blk", "heads"), None),
        P(("dp", "blk", "heads"), None),
        P(("dp", "blk", "heads")),
        P(("dp", "blk"), "heads"),
        P(("dp", "blk", "heads"), None),
        P(("dp", "blk", "heads"), None),
        P(("dp", "blk"), "heads"),
        P(("dp", "blk"), "heads"),
        P(("dp", "blk"), "heads"),
        P(("dp", "blk", "heads"), None),
        P(("dp", "blk", "heads"), None),
        P("heads"),
        P("heads"),
        P("heads"),
        P("heads", ("dp", "blk")),
        P("heads", ("dp", "blk")),
        P(("dp", "blk", "heads")),
        P(("dp", "blk"), "heads"),
        P(("dp", "blk"), "heads"),
        P("heads", ("dp", "blk")),
    )
    return jax.shard_map(
        shards,
        mesh=mesh,
        in_specs=placed,
        out_specs=(
            P(("dp", "blk", "heads"), None),
            P(("dp", "blk", "heads"), None),
            P(("dp", "blk", "heads")),
            P(("dp", "blk"), "heads"),
            P(("dp", "blk", "heads"), None),
            P(("dp", "blk", "heads"), None),
            P(("dp", "blk"), "heads"),
            P(("dp", "blk"), "heads"),
            P(("dp", "blk"), "heads"),
            P(("dp", "blk", "heads"), None),
            P(("dp", "blk", "heads"), None),
            P("heads"),
            P("heads"),
            P("heads"),
            P("heads", ("dp", "blk")),
            P("heads", ("dp", "blk")),
            P(("dp", "blk", "heads")),
            P(("dp", "blk"), "heads"),
            P(("dp", "blk"), "heads"),
            P("heads", ("dp", "blk")),
        ),
        check_vma=False,
    )
```

```python
import functools

import jax
import jax.numpy as jnp
from jax import lax
from jax.experimental import pallas as pl
from jax.experimental.pallas import tpu as pltpu
from jax.sharding import PartitionSpec as P

QH = 8
KVH = 2
HD = 128
MIXER_HEAD_SIZE = 64
BLOCK = 256
LANES = 128
LOG2_E = 1.4426950408889634


HIGH_PRECISION = lax.Precision.HIGHEST
norm_eps = 1e-05
rope_base = 100000000000.0


def simple_product(left_side, right_side):
    return jnp.dot(left_side, right_side, preferred_element_type=jnp.float32)


def dot_last(left_side, right_side):
    return lax.dot_general(
        left_side, right_side, (((1,), (1,)), ((), ())), preferred_element_type=jnp.float32
    )


def dot_first(left_side, right_side):
    return lax.dot_general(
        left_side, right_side, (((0,), (0,)), ((), ())), preferred_element_type=jnp.float32
    )


def compiler_params(mebibytes=20):
    return pltpu.CompilerParams(vmem_limit_bytes=mebibytes * 1024 * 1024)


def small_cost():
    return pl.CostEstimate(flops=1000, bytes_accessed=1000, transcendentals=0)


def in_hbm(value):
    return pltpu.with_memory_space_constraint(value, pltpu.HBM)


def corner(value):
    return value[:16, :LANES]


def in_vmem(count):
    return [pl.BlockSpec(memory_space=pltpu.VMEM)] * count


def mul(left_side, right_side):
    return jnp.dot(left_side, right_side, preferred_element_type=jnp.float32)


def tile_scores(key_rows, query_rows, head_size):
    return dot_last(key_rows, query_rows) * (head_size**-0.5 * LOG2_E)


def causal(scores):
    key_at = lax.broadcasted_iota(jnp.int32, scores.shape, 0)
    query_at = lax.broadcasted_iota(jnp.int32, scores.shape, 1)
    return jnp.where(key_at <= query_at, scores, -1e30)


def enter_kernel(
    ranks_ref, heads_ref, x_ref, misc_ref, key_ref, value_ref, w_query_ref, cos_ref, sin_ref, *refs
):
    ordered_ref, query_ref, kv_ref, gains_ref = refs[-4:]
    head_size = query_ref.shape[1]

    @pl.when(pl.program_id(0) == 0)
    def _():
        lane = lax.broadcasted_iota(jnp.int32, misc_ref.shape, 1)
        for k in range(2):
            column = jnp.where(lane == heads_ref[0] + k, misc_ref[...].astype(jnp.float32), 0.0)
            gains_ref[k : k + 1, :] = jnp.sum(column.T, axis=0, keepdims=True)

    cosine, sine = (cos_ref[...], sin_ref[...])

    def turn(value):
        return (value * cosine + pltpu.roll(value, head_size // 2, 1) * sine).astype(jnp.bfloat16)

    rows = x_ref[...].astype(jnp.float32)
    normed = (rows * inverse_rms(rows) * gains_ref[0:1, :]).astype(jnp.bfloat16)
    ordered_ref[...] = normed
    kv_ref[:, :head_size] = turn(mul(normed, key_ref[...]))
    kv_ref[:, head_size:] = mul(normed, value_ref[...]).astype(jnp.bfloat16)
    query_ref[...] = turn(mul(normed, w_query_ref[...]))


def enter(ranks, heads, x_span, in_full, at, cosine, sine, after):
    count = ranks.shape[0]
    rows, width = x_span.shape
    head_size = cosine.shape[1]
    here = lambda columns: pl.BlockSpec((rows // count, columns), lambda k, r, h: (k, 0))
    there = lambda columns: pl.BlockSpec((rows // count, columns), lambda k, r, h: (r[k], 0))
    weight = lambda name: pl.BlockSpec(
        (width, at[name][1]), lambda k, r, h: (0, at[name][0] // at[name][1])
    )
    return pl.pallas_call(
        enter_kernel,
        grid_spec=pltpu.PrefetchScalarGridSpec(
            num_scalar_prefetch=2,
            grid=(count,),
            in_specs=[
                here(width),
                weight("misc"),
                weight("key"),
                weight("value"),
                weight("query"),
                there(head_size),
                there(head_size),
            ]
            + [pl.BlockSpec(memory_space=pl.ANY)] * len(after),
            out_specs=(
                there(width),
                there(head_size),
                there(2 * head_size),
                pl.BlockSpec((8, width), lambda k, r, h: (0, 0)),
            ),
        ),
        out_shape=(
            jax.ShapeDtypeStruct((rows, width), jnp.bfloat16),
            jax.ShapeDtypeStruct((rows, head_size), jnp.bfloat16),
            jax.ShapeDtypeStruct((rows, 2 * head_size), jnp.bfloat16),
            jax.ShapeDtypeStruct((8, width), jnp.float32),
        ),
        compiler_params=compiler_params(),
        cost_estimate=small_cost(),
        name="enter",
    )(ranks, heads, x_span, in_full, in_full, in_full, in_full, cosine, sine, *after)


def weight_grads_kernel(*refs, counts):
    out_ref = refs[-1]
    start, used = (0, len(counts))
    for k, count in enumerate(counts):
        left = refs[k][...].T
        for ref in refs[used : used + count]:
            out_ref[:, start : start + ref.shape[1]] = mul(left, ref[...]).astype(jnp.bfloat16)
            start += ref.shape[1]
        used += count


def weight_grads(groups, width, start=0, buffer=None, after=()):
    rights = [right for _, group in groups for right in group]
    columns = sum(right.shape[1] for right in rights)
    depth = rights[0].shape[0]
    rows = groups[0][0].shape[1]
    operands = [left for left, _ in groups] + rights
    count = len(operands)
    extra = list(after) if buffer is None else [buffer] + list(after)

    def call(*refs):
        weight_grads_kernel(
            *refs[:count],
            refs[-1],
            counts=tuple(len(group) for _, group in groups),
        )

    return pl.pallas_call(
        call,
        grid=(rows // BLOCK,),
        out_shape=pltpu.HBM((rows, width), jnp.bfloat16),
        in_specs=[pl.BlockSpec((depth, BLOCK), lambda k: (0, k)) for _ in groups]
        + [pl.BlockSpec(right.shape, lambda k: (0, 0)) for right in rights]
        + [pl.BlockSpec(memory_space=pl.ANY)] * len(extra),
        out_specs=pl.BlockSpec(
            (pl.Element(BLOCK), pl.Element(columns)), lambda k: (k * BLOCK, start)
        ),
        input_output_aliases={} if buffer is None else {count: 0},
        compiler_params=compiler_params(),
        cost_estimate=pl.CostEstimate(
            flops=2 * rows * depth * columns,
            bytes_accessed=2 * (depth * (2 * rows + columns) + rows * columns),
            transcendentals=0,
        ),
        name="weight_grads",
    )(*operands, *extra)


def pack_kernel(*refs, turned):
    out_ref = refs[-1]
    start = 0
    for ref, turn in zip(refs, turned):
        piece = ref[...].T if turn else ref[...]
        out_ref[:, start : start + piece.shape[1]] = piece
        start += piece.shape[1]


def pack(pieces, turned, after):
    sizes = [piece.shape[::-1] if turn else piece.shape for piece, turn in zip(pieces, turned)]
    return pl.pallas_call(
        functools.partial(pack_kernel, turned=turned),
        out_shape=jax.ShapeDtypeStruct(
            (sizes[0][0], sum(size[1] for size in sizes)), jnp.bfloat16
        ),
        in_specs=in_vmem(len(pieces)) + [pl.BlockSpec(memory_space=pl.ANY)],
        out_specs=pl.BlockSpec(memory_space=pltpu.VMEM),
        compiler_params=compiler_params(),
        name="pack",
    )(*pieces, after)


def join_kernel(*refs):
    out_ref = refs[-1]
    start = 0
    for ref in refs[:-1]:
        out_ref[start : start + ref.shape[0], :] = ref[...]
        start += ref.shape[0]


def join(pieces):
    rows = sum(piece.shape[0] for piece in pieces)
    return pl.pallas_call(
        join_kernel,
        out_shape=jax.ShapeDtypeStruct((rows, pieces[0].shape[1]), pieces[0].dtype),
        in_specs=in_vmem(len(pieces)),
        out_specs=pl.BlockSpec(memory_space=pltpu.VMEM),
        compiler_params=compiler_params(),
        cost_estimate=small_cost(),
        name="join",
    )(*pieces)


def pack_first_kernel(
    turns_ref, kv_ref, shared_ref, delta_ref, z_ref, x_ref, query_ref, ssm_ref, attn_ref, out_ref, *, at
):
    def put(name, value, rows=slice(None)):
        start, size = at[name]
        out_ref[rows, start : start + size] = value

    put("z", z_ref[...])
    put("x", x_ref[...])
    put("query", query_ref[...])
    put("ssm_out", ssm_ref[...].T)
    put("attn_out", attn_ref[...].T)
    count = turns_ref.shape[0]
    size = shared_ref.shape[0] // count
    first = kv_ref[0] == 0
    for k in range(count):
        rows = pl.ds(pl.multiple_of(turns_ref[k] * size, size), size)
        chunk = shared_ref[k * size : (k + 1) * size, :]
        pieces, start = [], 0
        for width in (HD, HD, HD, HD, at["b"][1], at["c"][1], LANES):
            pieces.append(chunk[:, start : start + width])
            start += width
        put("key", jnp.where(first, pieces[0], pieces[1]), rows)
        put("value", jnp.where(first, pieces[2], pieces[3]), rows)
        put("b", pieces[4], rows)
        put("c", pieces[5], rows)
        put("misc", pieces[6] + delta_ref[rows, :], rows)


def pack_first(turns, kv_index, shared, delta, weights, at):
    rows = shared.shape[0]
    return pl.pallas_call(
        functools.partial(pack_first_kernel, at=at),
        out_shape=jax.ShapeDtypeStruct(
            (rows, max(start + size for start, size in at.values())), jnp.bfloat16
        ),
        in_specs=[pl.BlockSpec(memory_space=pltpu.SMEM)] * 2 + in_vmem(2 + len(weights)),
        out_specs=pl.BlockSpec(memory_space=pltpu.VMEM),
        compiler_params=compiler_params(),
        cost_estimate=small_cost(),
        name="pack_first",
    )(turns, kv_index, shared, delta, *weights)


def finish_kernel(
    ranks_ref,
    kv_ref,
    sums_ref,
    weight_ref,
    extra_ref,
    ssm_out_ref,
    attn_out_ref,
    gate_ref,
    ssm_ref,
    query_ref,
    misc_ref,
    shared_ref,
    whole_ref,
    *,
    at,
    sums_at,
):
    def of(name):
        start, size = sums_at[name]
        return sums_ref[:, start : start + size].astype(jnp.float32)

    ssm_out_ref[...] = of("ssm_out").T
    attn_out_ref[...] = of("attn_out").T
    gate_ref[...] = of("z")
    ssm_ref[...] = of("x")
    query_ref[...] = of("query")
    misc_ref[...] = of("misc")
    total = 0.0
    for name, (start, size) in at.items():
        product = of(name) * weight_ref[:, start : start + size].astype(jnp.float32)
        total += jnp.sum(product, axis=1, keepdims=True)
    total = total / extra_ref[:, 0:1]
    lane = lax.broadcasted_iota(jnp.int32, misc_ref.shape, 1)
    gains = jnp.where(lane == 0, total, jnp.where(lane == 1, extra_ref[:, 1:2], 0.0))
    zero = jnp.zeros_like(gains)
    first = kv_ref[0] == 0
    key, value = (of("key"), of("value"))
    pieces = (
        jnp.where(first, key, zero),
        jnp.where(first, zero, key),
        jnp.where(first, value, zero),
        jnp.where(first, zero, value),
        of("b"),
        of("c"),
        gains,
    )
    start = 0
    for piece in pieces:
        whole_ref[:, start : start + piece.shape[1]] = piece
        start += piece.shape[1]
    count = ranks_ref.shape[0]
    size = shared_ref.shape[0] // count
    for k in range(count):
        rows = pl.ds(pl.multiple_of(ranks_ref[k] * size, size), size)
        shared_ref[k * size : (k + 1) * size, :] = whole_ref[rows, :].astype(jnp.bfloat16)


def finish(ranks, kv_index, sums, weights, extra, at, sums_at):
    rows = weights.shape[0]
    shape = lambda *sizes: jax.ShapeDtypeStruct(sizes, jnp.float32)
    width = lambda name: sums_at[name][1]
    shared = 2 * (width("key") + width("value")) + width("b") + width("c") + LANES
    return pl.pallas_call(
        functools.partial(finish_kernel, at=at, sums_at=sums_at),
        out_shape=(
            shape(width("ssm_out"), rows),
            shape(width("attn_out"), rows),
            shape(rows, width("z")),
            shape(rows, width("x")),
            shape(rows, width("query")),
            shape(rows, width("misc")),
            jax.ShapeDtypeStruct((rows, shared), jnp.bfloat16),
        ),
        in_specs=[pl.BlockSpec(memory_space=pltpu.SMEM)] * 2 + in_vmem(3),
        out_specs=tuple(in_vmem(7)),
        scratch_shapes=[pltpu.VMEM((rows, shared), jnp.float32)],
        compiler_params=compiler_params(),
        name="finish",
    )(ranks, kv_index, sums, weights, extra)


def attend_kernel(rank_ref, query_ref, own_ref, *refs):
    pieces, (out_ref, low_ref, log_ref) = (refs[:-3], refs[-3:])
    span_length, head_size = query_ref.shape
    tile = own_ref.shape[0] // 2
    for block in range(span_length // tile):
        here = slice(block * tile, (block + 1) * tile)
        query_rows = query_ref[here, :]

        def step(kv_rows, carried, masked=False):
            top, total, summed = carried
            scores = tile_scores(kv_rows[:, :head_size], query_rows, head_size)
            if masked:
                scores = causal(scores)
            new_top = jnp.maximum(top, jnp.max(scores, axis=0, keepdims=True))
            probs = jnp.exp2(scores - new_top)
            scale = jnp.exp2(top - new_top)
            total = total * scale + jnp.sum(probs, axis=0, keepdims=True)
            summed = summed * scale + dot_first(kv_rows[:, head_size:], probs.astype(jnp.bfloat16))
            return (new_top, total, summed)

        carried = (
            jnp.full((1, tile), -1e30, jnp.float32),
            jnp.zeros((1, tile), jnp.float32),
            jnp.zeros((head_size, tile), jnp.float32),
        )
        carried = step(own_ref[here, :], carried, True)
        for earlier in range(block):
            carried = step(own_ref[earlier * tile : (earlier + 1) * tile, :], carried)
        for distance in range(1, 1 + len(pieces) // 2):
            pair = pieces[2 * distance - 2 : 2 * distance]

            def both(_, carried, pair=pair):
                return step(pair[1][...], step(pair[0][...], carried))

            valid = (rank_ref[0] >= distance).astype(jnp.int32)
            carried = lax.fori_loop(0, valid, both, carried)
        top, total, summed = carried
        result = summed / total
        out_ref[:, here] = result
        low_ref[here, :] = result.T.astype(jnp.bfloat16)
        log_ref[:, here] = top + jnp.log2(total)


def attend(rank, queries, own, pieces):
    span_length, head_size = queries.shape
    return pl.pallas_call(
        attend_kernel,
        out_shape=(
            jax.ShapeDtypeStruct((head_size, span_length), jnp.float32),
            jax.ShapeDtypeStruct((span_length, head_size), jnp.bfloat16),
            jax.ShapeDtypeStruct((1, span_length), jnp.float32),
        ),
        in_specs=[pl.BlockSpec(memory_space=pltpu.SMEM)] + in_vmem(2 + len(pieces)),
        out_specs=tuple(in_vmem(3)),
        compiler_params=compiler_params(),
        cost_estimate=small_cost(),
        name="attend",
    )(rank, queries, own, *pieces)


def attend_back_kernel(rank_ref, query_ref, own_ref, *refs):
    pieces, refs = (refs[:-13], refs[-13:])
    out_ref, log_ref, grad_ref, cos_ref, sin_ref, *_, d_query_ref, d_own_ref, d_far_ref, sums_ref = refs
    span_length, head_size = query_ref.shape
    tile = own_ref.shape[0] // 2
    score_scale = head_size**-0.5
    sums_ref[...] = jnp.zeros_like(sums_ref)
    for block in range(span_length // tile):
        here = slice(block * tile, (block + 1) * tile)
        query_rows = query_ref[here, :]
        grad_rows = grad_ref[here, grad_ref.shape[1] - head_size :]
        log_total = log_ref[:, here]
        delta_row = jnp.sum(
            grad_rows.astype(jnp.float32).T * out_ref[:, here], axis=0, keepdims=True
        )

        def step(kv_ref, start, at, d_query, masked=False):
            key_rows = kv_ref[start : start + tile, :head_size]
            scores = tile_scores(key_rows, query_rows, head_size)
            if masked:
                scores = causal(scores)
            probs = jnp.exp2(scores - log_total)
            d_probs = dot_last(kv_ref[start : start + tile, head_size:], grad_rows)
            d_scores = (probs * (d_probs - delta_row)).astype(jnp.bfloat16)
            rows = slice(at * tile, (at + 1) * tile)
            sums_ref[rows, head_size:] += mul(probs.astype(jnp.bfloat16), grad_rows)
            sums_ref[rows, :head_size] += mul(d_scores, query_rows)
            return d_query + dot_first(key_rows, d_scores)

        d_query = jnp.zeros((head_size, tile), jnp.float32)
        d_query = step(own_ref, block * tile, block, d_query, True)
        for earlier in range(block):
            d_query = step(own_ref, earlier * tile, earlier, d_query)
        for distance in range(1, 1 + len(pieces) // 2):

            def both(_, d_query, distance=distance):
                for k in (2 * distance - 2, 2 * distance - 1):
                    d_query = step(pieces[k], 0, 2 + k, d_query)
                return d_query

            valid = (rank_ref[0] >= distance).astype(jnp.int32)
            d_query = lax.fori_loop(0, valid, both, d_query)
        turned = d_query.T * score_scale
        d_query_ref[here, :] = (
            turned * cos_ref[here, :] - pltpu.roll(turned, head_size // 2, 1) * sin_ref[here, :]
        ).astype(jnp.bfloat16)
    lane = lax.broadcasted_iota(jnp.int32, (tile, 2 * head_size), 1)
    scale = jnp.where(lane < head_size, score_scale, 1.0)
    for at in range(2):
        rows = slice(at * tile, (at + 1) * tile)
        d_own_ref[rows, :] = sums_ref[rows, :] * scale
    for k in range(len(pieces)):
        rows = slice((2 + k) * tile, (3 + k) * tile)
        into = (k % 2) * (len(pieces) // 2) + k // 2
        d_far_ref[into * tile : (into + 1) * tile, :] = (sums_ref[rows, :] * scale).astype(
            jnp.bfloat16
        )


def attend_back(rank, queries, own, pieces, attended, log_totals, d_attn, cosine, sine, after):
    tile = own.shape[0] // 2
    return pl.pallas_call(
        attend_back_kernel,
        out_shape=(
            jax.ShapeDtypeStruct(queries.shape, jnp.bfloat16),
            jax.ShapeDtypeStruct(own.shape, jnp.float32),
            jax.ShapeDtypeStruct((len(pieces) * tile, own.shape[1]), jnp.bfloat16),
        ),
        in_specs=[pl.BlockSpec(memory_space=pltpu.SMEM)]
        + in_vmem(7 + len(pieces))
        + [pl.BlockSpec(memory_space=pl.ANY)] * len(after),
        out_specs=tuple(in_vmem(3)),
        scratch_shapes=[pltpu.VMEM(((2 + len(pieces)) * tile, own.shape[1]), jnp.float32)],
        compiler_params=compiler_params(),
        cost_estimate=small_cost(),
        name="attend_back",
    )(rank, queries, own, *pieces, attended, log_totals, d_attn, cosine, sine, *after)


def reorder_kernel(ranks_ref, *refs, count):
    out_ref = refs[-1]
    start = 0
    for ref in refs[:count]:
        out_ref[:, start : start + ref.shape[1]] = ref[...].astype(out_ref.dtype)
        start += ref.shape[1]


def reorder(ranks, pieces, inverse=False, after=()):
    count = ranks.shape[0]
    rows = pieces[0].shape[0] // count
    width = sum(piece.shape[1] for piece in pieces)
    there = lambda k, ranks: (ranks[k], 0)
    here = lambda k, ranks: (k, 0)
    return pl.pallas_call(
        functools.partial(reorder_kernel, count=len(pieces)),
        grid_spec=pltpu.PrefetchScalarGridSpec(
            num_scalar_prefetch=1,
            grid=(count,),
            in_specs=[
                pl.BlockSpec((rows, piece.shape[1]), here if inverse else there)
                for piece in pieces
            ]
            + [pl.BlockSpec(memory_space=pl.ANY)] * len(after),
            out_specs=pl.BlockSpec((rows, width), there if inverse else here),
        ),
        out_shape=jax.ShapeDtypeStruct((count * rows, width), jnp.bfloat16),
        compiler_params=compiler_params(),
        cost_estimate=small_cost(),
        name="reorder",
    )(ranks, *pieces, *after)


def lower_ones(size, dtype=jnp.float32):
    row = lax.broadcasted_iota(jnp.int32, (size, size), 0)
    column = lax.broadcasted_iota(jnp.int32, (size, size), 1)
    return (row >= column).astype(dtype)


def precise(left_side, right_side):
    return jnp.dot(
        left_side, right_side, precision=HIGH_PRECISION, preferred_element_type=jnp.float32
    )


def spread_heads(columns, head_size, width):
    lane = lax.broadcasted_iota(jnp.int32, (columns.shape[0], 2 * head_size), 1)
    pairs = [
        jnp.where(lane < head_size, columns[:, k : k + 1], columns[:, k + 1 : k + 2])
        for k in range(0, width // head_size, 2)
    ]
    return jnp.concatenate(pairs, axis=1)


def head_ones(width, head_size, lanes, dtype):
    at = lax.broadcasted_iota(jnp.int32, (width, lanes), 0)
    lane = lax.broadcasted_iota(jnp.int32, (width, lanes), 1)
    low = lane * head_size
    return ((at >= low) & (at < low + head_size)).astype(dtype)


def scan_first_kernel(
    pre_ref, bias_ref, rate_ref, x_ref, b_ref, delta_ref, cum_ref, delta_row_ref, cum_row_ref, state_ref, log_ref
):
    @pl.when(pl.program_id(0) == 0)
    def _():
        state_ref[...] = jnp.zeros_like(state_ref)
        log_ref[...] = jnp.zeros_like(log_ref)

    delta = jax.nn.softplus(pre_ref[...] + bias_ref[...])
    log_step = -delta * rate_ref[...]
    cumulative = precise(lower_ones(log_step.shape[0]), log_step)
    delta_ref[...] = delta
    cum_ref[...] = cumulative
    delta_row_ref[...] = delta.T[:8]
    cum_row_ref[...] = cumulative.T[:8]
    ending = cumulative[-1:, :]
    weight = jnp.exp(ending - cumulative + log_ref[...]) * delta
    width = x_ref.shape[1]
    x_low = x_ref[...].astype(jnp.bfloat16).astype(jnp.float32)
    weighted = (x_low * spread_heads(weight, MIXER_HEAD_SIZE, width)).astype(jnp.bfloat16)
    state_ref[...] += dot_first(b_ref[...].astype(jnp.bfloat16), weighted)
    log_ref[...] += ending


def part(projected, start, width, order=lambda c: c):
    at = start // width
    return (projected, pl.BlockSpec((BLOCK, width), lambda c: (order(c), at)))


def run_scan(
    kernel, chunks, operands, out_shape, out_specs, name, scratch=(), after=(), mebibytes=20
):
    count = len(operands)
    operands = operands + [(array, pl.BlockSpec(memory_space=pl.ANY)) for array in after]

    def call(*refs):
        kernel(*refs[:count], *refs[count + len(after) :])

    return pl.pallas_call(
        call,
        grid=(chunks,),
        out_shape=out_shape,
        in_specs=[spec for _, spec in operands],
        out_specs=out_specs,
        scratch_shapes=list(scratch),
        compiler_params=compiler_params(mebibytes),
        cost_estimate=small_cost(),
        name=name,
    )(*[array for array, _ in operands])


def whole(array):
    return (array, pl.BlockSpec(array.shape, lambda c: (0,) * array.ndim))


def scan_first(at, bias, rate):
    rows, lanes = (at["x"][0].shape[0], bias.shape[1])
    chunks = rows // BLOCK
    back = lambda c: chunks - 1 - c
    width, state_size = (at["x"][2], at["b"][2])
    by_chunk = pl.BlockSpec((BLOCK, lanes), lambda c: (back(c), 0))
    across = pl.BlockSpec((8, BLOCK), lambda c: (0, back(c)))
    shape = lambda *sizes: jax.ShapeDtypeStruct(sizes, jnp.float32)
    return run_scan(
        scan_first_kernel,
        chunks,
        [
            part(*at["misc"], back),
            whole(bias),
            whole(rate),
            part(*at["x"], back),
            part(*at["b"], back),
        ],
        (
            shape(rows, lanes),
            shape(rows, lanes),
            shape(8, rows),
            shape(8, rows),
            shape(state_size, width),
            shape(1, lanes),
        ),
        (
            by_chunk,
            by_chunk,
            across,
            across,
            pl.BlockSpec((state_size, width), lambda c: (0, 0)),
            pl.BlockSpec((1, lanes), lambda c: (0, 0)),
        ),
        "scan_first",
    )


def chained(refs, width):
    state = jnp.zeros((refs[0].shape[0] - 16, width), jnp.float32)
    for ref in reversed(refs):
        logs = ref[-16:, :LANES].astype(jnp.float32)
        decay = jnp.exp(jnp.sum(logs[:3], axis=0, keepdims=True))
        state = ref[:-16].astype(jnp.float32) + spread_heads(decay, MIXER_HEAD_SIZE, width) * state
    return state


def scan_kernel(
    x_ref,
    z_ref,
    b_ref,
    c_ref,
    delta_ref,
    cum_ref,
    delta_row_ref,
    cum_row_ref,
    near_ref,
    next_ref,
    far_ref,
    skip_ref,
    scanned_ref,
    gated_ref,
    states_ref,
    state_ref,
):
    @pl.when(pl.program_id(0) == 0)
    def _():
        state_ref[...] = chained((near_ref, next_ref, far_ref), x_ref.shape[1])

    head_size = MIXER_HEAD_SIZE
    pair = 2 * head_size
    size, width = x_ref.shape
    state = state_ref[...]
    states_ref[0] = state
    delta, cumulative = (delta_ref[...], cum_ref[...])
    delta_row, cum_row = (delta_row_ref[...], cum_row_ref[...])
    bmat, cmat = (b_ref[...].astype(jnp.bfloat16), c_ref[...].astype(jnp.bfloat16))
    x_all = x_ref[...].astype(jnp.bfloat16)
    inner = dot_last(cmat, bmat)
    row = lax.broadcasted_iota(jnp.int32, (size, size), 0)
    column = lax.broadcasted_iota(jnp.int32, (size, size), 1)
    allowed = row >= column
    lane = lax.broadcasted_iota(jnp.int32, (size, pair), 1)
    from_state = mul(cmat, state.astype(jnp.bfloat16))
    spread = spread_heads(jnp.exp(cumulative), head_size, width)
    for first in range(0, width // head_size, 2):
        here = slice(first * head_size, first * head_size + pair)
        x_pair = x_all[:, here]
        total = from_state[:, here] * spread[:, here]
        total += skip_ref[:, here] * x_pair.astype(jnp.float32)
        for head in (first, first + 1):
            gap = cumulative[:, head : head + 1] - cum_row[head : head + 1, :]
            decay = jnp.exp(jnp.where(allowed, gap, -1e30))
            mixing = inner * decay * delta_row[head : head + 1, :]
            x_head = jnp.where((lane >= head_size) == (head > first), x_pair, 0.0)
            total += mul(mixing.astype(jnp.bfloat16), x_head.astype(jnp.bfloat16))
        scanned_ref[:, here] = total
        gate = z_ref[:, here]
        gated_ref[:, here] = (total * (gate * jax.nn.sigmoid(gate))).astype(jnp.bfloat16)
    ending = cumulative[-1:, :]
    weight = spread_heads(jnp.exp(ending - cumulative) * delta, head_size, width)
    weighted = (x_all.astype(jnp.float32) * weight).astype(jnp.bfloat16)
    state_ref[...] = state * spread[-1:, :] + dot_first(bmat, weighted)


def scan(at, delta, cumulative, delta_row, cum_row, entry, skip, after):
    rows = delta.shape[0]
    state_size, width = (at["b"][2], at["x"][2])
    chunks = rows // BLOCK
    by_chunk = pl.BlockSpec((BLOCK, width), lambda c: (c, 0))
    lanes = delta.shape[1]
    across = pl.BlockSpec((8, BLOCK), lambda c: (0, c))
    return run_scan(
        scan_kernel,
        chunks,
        [
            part(*at["x"]),
            part(*at["z"]),
            part(*at["b"]),
            part(*at["c"]),
            part(delta, 0, lanes),
            part(cumulative, 0, lanes),
            (delta_row, across),
            (cum_row, across),
            *[whole(packed) for packed in entry],
            whole(skip),
        ],
        (
            jax.ShapeDtypeStruct((rows, width), jnp.float32),
            jax.ShapeDtypeStruct((rows, width), jnp.bfloat16),
            jax.ShapeDtypeStruct((chunks, state_size, width), jnp.float32),
        ),
        (by_chunk, by_chunk, pl.BlockSpec((1, state_size, width), lambda c: (c, 0, 0))),
        "scan",
        [pltpu.VMEM((state_size, width), jnp.float32)],
        after,
    )


def scan_back_first_kernel(
    grad_ref, z_ref, scanned_ref, c_ref, cum_ref, d_scanned_ref, d_gate_ref, state_ref, log_ref
):
    @pl.when(pl.program_id(0) == 0)
    def _():
        state_ref[...] = jnp.zeros_like(state_ref)
        log_ref[...] = jnp.zeros_like(log_ref)

    gate = z_ref[...]
    chance = jax.nn.sigmoid(gate)
    grad = grad_ref[:, : z_ref.shape[1]].astype(jnp.float32)
    d_scanned = grad * (gate * chance)
    d_scanned_ref[...] = d_scanned
    d_gate_ref[...] = (
        grad * scanned_ref[...] * (chance * (1.0 + gate * (1.0 - chance)))
    ).astype(jnp.bfloat16)
    cumulative = cum_ref[...]
    decay = spread_heads(jnp.exp(cumulative + log_ref[...]), MIXER_HEAD_SIZE, z_ref.shape[1])
    state_ref[...] += dot_first(
        c_ref[...].astype(jnp.bfloat16), (d_scanned * decay).astype(jnp.bfloat16)
    )
    log_ref[...] += cumulative[-1:, :]


def scan_back_first(grads, at, scanned, cumulative):
    rows, width = scanned.shape
    state_size, lanes = (at["c"][2], cumulative.shape[1])
    by_chunk = pl.BlockSpec((BLOCK, width), lambda c: (c, 0))
    return run_scan(
        scan_back_first_kernel,
        rows // BLOCK,
        [
            part(grads, 0, grads.shape[1]),
            part(*at["z"]),
            part(scanned, 0, width),
            part(*at["c"]),
            part(cumulative, 0, lanes),
        ],
        (
            jax.ShapeDtypeStruct((rows, width), jnp.float32),
            jax.ShapeDtypeStruct((rows, width), jnp.bfloat16),
            jax.ShapeDtypeStruct((state_size, width), jnp.float32),
        ),
        (by_chunk, by_chunk, pl.BlockSpec((state_size, width), lambda c: (0, 0))),
        "scan_back_first",
        [pltpu.VMEM((1, lanes), jnp.float32)],
    )


def scan_back_kernel(
    x_ref,
    grad_ref,
    b_ref,
    c_ref,
    pre_ref,
    bias_ref,
    rate_ref,
    delta_ref,
    cum_ref,
    cum_row_ref,
    states_ref,
    near_ref,
    next_ref,
    far_ref,
    skip_ref,
    d_x_ref,
    d_b_ref,
    d_c_ref,
    d_pre_ref,
    sums_ref,
    state_ref,
):
    @pl.when(pl.program_id(0) == 0)
    def _():
        state_ref[...] = chained((near_ref, next_ref, far_ref), x_ref.shape[1])
        sums_ref[...] = jnp.zeros_like(sums_ref)

    head_size = MIXER_HEAD_SIZE
    pair = 2 * head_size
    size, width = x_ref.shape
    lanes = delta_ref.shape[1]
    low = jnp.bfloat16
    delta, cumulative, cum_row = (delta_ref[...], cum_ref[...], cum_row_ref[...])
    bmat, cmat = (b_ref[...].astype(low), c_ref[...].astype(low))
    x_all = x_ref[...].astype(low)
    x_single = x_all.astype(jnp.float32)
    grad = grad_ref[...]
    grad_low = grad.astype(low)
    state = states_ref[0]
    state_low = state.astype(low)
    after = state_ref[...]
    after_low = after.astype(low)
    ending = cumulative[-1:, :]
    row = lax.broadcasted_iota(jnp.int32, (size, size), 0)
    column = lax.broadcasted_iota(jnp.int32, (size, size), 1)
    later = column >= row
    before = (row > column).astype(low)
    onward = later.astype(low)
    lane = lax.broadcasted_iota(jnp.int32, (size, pair), 1)
    head_lane = lax.broadcasted_iota(jnp.int32, (size, lanes), 1)
    sum_heads = head_ones(width, head_size, lanes, low)

    inner = dot_last(bmat, cmat)
    from_after = mul(bmat, after_low)
    weight = jnp.exp(ending - cumulative)
    spread_weight = spread_heads(weight * delta, head_size, width)
    spread = spread_heads(jnp.exp(cumulative), head_size, width)
    to_end = mul((x_single * from_after).astype(low), sum_heads)
    through = jnp.exp(cumulative) * mul((grad * mul(cmat, state_low)).astype(low), sum_heads)
    carried = jnp.sum(state * after, axis=0, keepdims=True) * spread[-1:, :]
    carried = precise(carried, sum_heads.astype(jnp.float32))
    d_delta = weight * to_end
    d_log = (
        mul(onward, through.astype(low)) + mul(before, (d_delta * delta).astype(low)) + carried
    )

    d_inner = jnp.zeros((size, size), jnp.float32)
    for first in range(0, width // head_size, 2):
        here = slice(first * head_size, first * head_size + pair)
        x_pair, grad_pair = (x_all[:, here], grad_low[:, here])
        d_x = from_after[:, here] * spread_weight[:, here] + skip_ref[:, here] * grad[:, here]
        for head in (first, first + 1):
            mine = (lane >= head_size) == (head > first)
            gap = cum_row[head : head + 1, :] - cumulative[:, head : head + 1]
            decay = jnp.exp(jnp.where(later, gap, -1e30))
            delta_column = delta[:, head : head + 1]
            d_mixing = dot_last(jnp.where(mine, x_pair, 0.0).astype(low), grad_pair) * decay
            d_inner += d_mixing * delta_column
            flow = d_mixing * inner
            mixing = inner * decay * delta_column
            d_x += mul(mixing.astype(low), jnp.where(mine, grad_pair, 0.0).astype(low))
            d_delta_head = jnp.sum(flow, axis=1, keepdims=True)
            passing = mul(before, (flow * delta_column).astype(low))
            d_log_head = jnp.sum(jnp.where(later, passing, 0.0), axis=1, keepdims=True)
            d_delta += jnp.where(head_lane == head, d_delta_head, 0.0)
            d_log += jnp.where(head_lane == head, d_log_head, 0.0)
        d_x_ref[:, here] = d_x.astype(low)

    d_inner_low = d_inner.astype(low)
    scaled_grad = (grad * spread).astype(low)
    weighted = (x_single * spread_weight).astype(low)
    d_b_ref[...] = (mul(d_inner_low, cmat) + dot_last(weighted, after_low)).astype(low)
    d_c_ref[...] = (dot_first(d_inner_low, bmat) + dot_last(scaled_grad, state_low)).astype(low)
    state_ref[...] = after * spread[-1:, :] + dot_first(cmat, scaled_grad)
    rate = rate_ref[...]
    d_pre = (d_delta - d_log * rate) * jax.nn.sigmoid(pre_ref[...] + bias_ref[...])
    d_pre = jnp.where(head_lane < width // head_size, d_pre, 0.0)
    d_pre_ref[...] = d_pre.astype(low)
    skip_sum = precise(
        jnp.sum(grad * x_single, axis=0, keepdims=True), sum_heads.astype(jnp.float32)
    )
    sums_ref[0:1, :] += jnp.sum(d_pre, axis=0, keepdims=True)
    sums_ref[1:2, :] += jnp.sum(d_log * (-delta * rate), axis=0, keepdims=True)
    sums_ref[2:3, :] += skip_sum


def scan_back(
    at, d_scanned, bias, rate, delta, cumulative, cum_row, states, entry, skip, after
):
    rows, width = d_scanned.shape
    state_size, lanes = (at["b"][2], delta.shape[1])
    chunks = rows // BLOCK
    back = lambda c: chunks - 1 - c
    by_chunk = lambda columns: pl.BlockSpec((BLOCK, columns), lambda c: (back(c), 0))
    shape = lambda columns: jax.ShapeDtypeStruct((rows, columns), jnp.bfloat16)
    return run_scan(
        scan_back_kernel,
        chunks,
        [
            part(*at["x"], back),
            part(in_hbm(d_scanned), 0, width, back),
            part(*at["b"], back),
            part(*at["c"], back),
            part(*at["misc"], back),
            whole(bias),
            whole(rate),
            part(delta, 0, lanes, back),
            part(cumulative, 0, lanes, back),
            (cum_row, pl.BlockSpec((8, BLOCK), lambda c: (0, back(c)))),
            (in_hbm(states), pl.BlockSpec((1, state_size, width), lambda c: (back(c), 0, 0))),
            *[whole(packed) for packed in entry],
            whole(skip),
        ],
        (
            shape(width),
            shape(state_size),
            shape(state_size),
            shape(lanes),
            jax.ShapeDtypeStruct((8, lanes), jnp.float32),
        ),
        (
            by_chunk(width),
            by_chunk(state_size),
            by_chunk(state_size),
            by_chunk(lanes),
            pl.BlockSpec((8, lanes), lambda c: (0, 0)),
        ),
        "scan_back",
        [pltpu.VMEM((state_size, width), jnp.float32)],
        after,
        44,
    )


def on_heads(value, move):
    devices = lax.axis_size("heads")
    pairs = []
    for at in range(devices):
        z, core = move(at // 2, at % 2)
        pairs.append((at, 2 * (z % (devices // 2)) + core))
    return lax.ppermute(value, "heads", pairs)


def to_partner(value):
    return on_heads(value, lambda z, core: (z, 1 - core))


def along(value):
    return on_heads(value, lambda z, core: (z + 1 - 2 * core, core))


def against(value):
    return on_heads(value, lambda z, core: (z - 1 + 2 * core, core))


def chunk_ranks():
    devices = lax.axis_size("heads")
    z, core = (lax.axis_index("heads") // 2, lax.axis_index("heads") % 2)
    step, other = (1 - 2 * core, 1 - core)
    owners = (
        (z, core),
        (z + 2, core),
        (z - step, core),
        (z - step, other),
        (z, other),
        (z + 2, other),
        (z + step, other),
        (z + step, core),
    )
    return jnp.stack([2 * ((at + devices) % (devices // 2)) + side for at, side in owners])


def gather_rows(own, joined=False):
    partner = to_partner(own)
    near = along(own)
    near_other = along(partner)
    far = along(near)
    mine = (own, far, near, near_other)
    theirs = (partner, to_partner(far), to_partner(near), to_partner(near_other))
    return join(mine + theirs) if joined else jnp.concatenate(mine + theirs, axis=0)


def scatter_rows(product, half, late=None):
    chunk = half // 4
    got = to_partner(product(slice(half, 2 * half)).astype(jnp.bfloat16))
    kept = lax.optimization_barrier(product(slice(0, half)))
    summed = kept + got.astype(jnp.float32)
    low = summed[chunk:].astype(jnp.bfloat16)
    far = against(low[:chunk])
    near_other = against(low[2 * chunk :])
    near = low[chunk : 2 * chunk].astype(jnp.float32) + far.astype(jnp.float32)
    near = against((near if late is None else near + late).astype(jnp.bfloat16))
    last = to_partner(near_other)
    total = summed[:chunk] + near.astype(jnp.float32)
    return total + last.astype(jnp.float32), last


def across(value, bit):
    devices = lax.axis_size("heads")
    return lax.ppermute(value, "heads", [(at, at ^ bit) for at in range(devices)])


def gather_small(value):
    for bit in (1, 2, 4):
        value = jnp.concatenate([value, across(value, bit)], axis=0)
    return value


def scatter_small(value):
    for bit in (4, 2, 1):
        half = value.shape[0] // 2
        got = across(value[half:].astype(jnp.bfloat16), bit)
        value = value[:half].astype(jnp.float32) + got.astype(jnp.float32)
    return value


def on_blocks(value, step):
    devices = lax.axis_size("blk")
    pairs = [(at, at + step) for at in range(devices) if 0 <= at + step < devices]
    return lax.ppermute(value, "blk", pairs)


def from_earlier(value, step=1):
    return tuple(on_blocks(value, distance * step) for distance in (1, 2, 3))


def pack_state(state, log_total):
    high = log_total.astype(jnp.bfloat16)
    rest = log_total - high.astype(jnp.float32)
    middle = rest.astype(jnp.bfloat16)
    low = (rest - middle.astype(jnp.float32)).astype(jnp.bfloat16)
    logs = jnp.concatenate([high, middle, low], axis=0)
    logs = jnp.pad(logs, ((0, 16 - logs.shape[0]), (0, state.shape[1] - logs.shape[1])))
    return jnp.concatenate([state.astype(jnp.bfloat16), logs], axis=0)


def sum_blocks(value):
    for axis in ("dp", "blk"):
        for bit in (1, 2):
            value = value + lax.ppermute(
                value, axis, [(at, at ^ bit) for at in range(lax.axis_size(axis))]
            )
    return value


def weight_sum(grads):
    return lax.psum_scatter(grads, ("dp", "blk"), scatter_dimension=0, tiled=True)


def split_columns(value_in, widths):
    pieces, start = [], 0
    for width in widths:
        pieces.append(value_in[:, start : start + width])
        start += width
    return pieces


def inverse_rms(rows_in):
    return lax.rsqrt(jnp.mean(rows_in * rows_in, axis=-1, keepdims=True) + norm_eps)


def norm_back(rows_in, gain_in, cotangent):
    inverse = inverse_rms(rows_in)
    scaled = rows_in * inverse
    weighted = cotangent * gain_in
    return inverse * (weighted - scaled * jnp.mean(weighted * scaled, axis=-1, keepdims=True))


def shards(
    x_in,
    out_grad,
    norm_one,
    w_query,
    w_key,
    w_value,
    output_gate_weight,
    mixer_input_weight,
    w_delta,
    w_bmat,
    w_cmat,
    delta_bias,
    decay_log,
    skip_gain,
    w_attn_out,
    mixer_output_weight,
    norm_two,
    w_gate,
    w_up,
    w_down,
):
    heads_count = lax.axis_size("heads")
    head_rank = lax.axis_index("heads")
    core = head_rank % 2
    block_rank = lax.axis_index("blk")
    rank = block_rank.astype(jnp.int32)[None]
    own_rows = x_in.shape[0]
    span_length = own_rows * heads_count
    half_span = span_length // 2
    span_start = block_rank * span_length
    query_width = w_query.shape[1]
    mixer_width = mixer_input_weight.shape[1]
    heads = mixer_width // MIXER_HEAD_SIZE
    state_size = w_bmat.shape[1]
    hidden_width = w_gate.shape[1]
    rows_of = w_query.shape[0]
    kv_index = head_rank * (query_width // HD) // (QH // KVH)
    kv_width = KVH * HD
    low = jnp.bfloat16
    ranks = chunk_ranks().astype(jnp.int32)
    turns = (head_rank ^ jnp.arange(heads_count)).astype(jnp.int32)

    gains = jnp.stack([norm_one, norm_two], axis=1)
    gains = jnp.pad(gains, ((0, 0), (heads, LANES - heads - 2)))
    shared = jnp.concatenate([w_key, w_value, w_bmat, w_cmat, gains], axis=1)
    delta_wide = jnp.pad(w_delta, ((0, 0), (0, LANES - heads)))
    in_names = ("z", "x", "query", "b", "c", "misc", "key", "value")
    in_widths = (mixer_width, mixer_width, query_width, state_size, state_size, LANES, HD, HD)
    in_width = sum(in_widths)
    starts = [sum(in_widths[:k]) for k in range(len(in_widths))]
    at = dict(zip(in_names, zip(starts, in_widths)))
    mix_at = {
        "ssm_out": (in_width, mixer_width),
        "attn_out": (in_width + mixer_width, query_width),
    }
    first_own = pack_first(
        turns,
        kv_index.astype(jnp.int32)[None],
        gather_small(shared),
        delta_wide,
        [output_gate_weight, mixer_input_weight, w_query, mixer_output_weight, w_attn_out],
        at | mix_at,
    )
    gain_part = first_own[:, at["misc"][0] + heads : at["misc"][0] + heads + 2]
    first_full = lax.all_gather(first_own, ("dp", "blk"), axis=0, tiled=True)
    in_full, mix_t = (first_full[:, :in_width], first_full[:, in_width:])
    x_float = x_in.astype(jnp.float32)
    zero = 0.0 * first_own[0, 0]
    x_span = gather_rows(x_in + zero)
    ffn_grad = gather_rows(out_grad + zero, joined=True)
    ffn_own = pack((w_gate, w_up, w_down), (False, False, True), x_span)
    ffn_full = lax.all_gather(ffn_own, ("dp", "blk"), axis=0, tiled=True)
    mixed_width = query_width + mixer_width
    gate_full, up_full, down_t = split_columns(ffn_full, (hidden_width,) * 3)
    positions = (span_start + jnp.arange(span_length)).astype(jnp.float32)
    freqs = rope_base ** (-2.0 * jnp.arange(HD // 2, dtype=jnp.float32) / HD)
    angles = positions[:, None] * freqs[None, :]
    cosine, sine = (jnp.cos(angles), jnp.sin(angles))
    cosine = jnp.concatenate([cosine, cosine], axis=1)
    sine = jnp.concatenate([-sine, sine], axis=1)
    normed_ordered, queries, keys_values, gain_rows = enter(
        ranks, jnp.full((1,), heads, jnp.int32), x_span, first_full, at, cosine, sine, [corner(ffn_own), corner(ffn_grad)]
    )
    gain_one, gain_two = (gain_rows[0:1], gain_rows[1:2])
    mine = lax.dynamic_slice_in_dim(keys_values, core * half_span, half_span, 0)
    pieces = []
    for piece in from_earlier(mine):
        pieces += [piece, to_partner(piece)]
    gate_raw = simple_product(normed_ordered, in_full[:, :mixer_width])
    x_raw = simple_product(normed_ordered, in_full[:, mixer_width : 2 * mixer_width])
    state_raw = simple_product(normed_ordered, in_full[:, at["b"][0] : at["key"][0]])
    raw = {
        "z": (gate_raw, 0, mixer_width),
        "x": (x_raw, 0, mixer_width),
        "b": (state_raw, 0, state_size),
        "c": (state_raw, state_size, state_size),
        "misc": (state_raw, 2 * state_size, LANES),
    }

    pad_lanes = lambda vector: jnp.pad(vector, (0, LANES - heads))[None]
    bias, rate = (pad_lanes(delta_bias), pad_lanes(jnp.exp(decay_log)))
    skip = jnp.repeat(skip_gain, MIXER_HEAD_SIZE)[None]
    delta, cumulative, delta_row, cum_row, local_state, local_log = scan_first(raw, bias, rate)
    entry_states = from_earlier(pack_state(local_state, local_log))
    attended, attn_part, log_totals = attend(rank, queries, keys_values, pieces)
    scanned, gated, states = scan(
        raw, delta, cumulative, delta_row, cum_row, entry_states, skip, [corner(attn_part)]
    )
    mixers = reorder(ranks, [gated, attn_part])
    ffn_zero = 0.0 * ffn_full[0, 0].astype(jnp.float32)
    mixed, _ = scatter_rows(lambda rows: dot_last(mixers[rows], mix_t), half_span, ffn_zero)
    middle = x_float + mixed
    middle_scaled = middle * inverse_rms(middle)
    normed_two = gather_rows((middle_scaled * gain_two).astype(low))
    ffn_gate = simple_product(normed_two, gate_full)
    ffn_up = simple_product(normed_two, up_full)
    ffn_sig = jax.nn.sigmoid(ffn_gate)
    hidden = (ffn_gate * ffn_sig * ffn_up).astype(low)

    d_hidden = simple_product(ffn_grad, down_t)
    d_ffn_gate = (d_hidden * ffn_up * (ffn_sig * (1.0 + ffn_gate * (1.0 - ffn_sig)))).astype(low)
    d_ffn_up = (d_hidden * (ffn_gate * ffn_sig)).astype(low)
    d_normed_two, d_two_last = scatter_rows(
        lambda rows: dot_last(d_ffn_gate[rows], gate_full) + dot_last(d_ffn_up[rows], up_full),
        half_span,
    )
    ffn_grads = weight_grads(
        [(normed_two, [d_ffn_gate, d_ffn_up]), (ffn_grad, [hidden])],
        3 * hidden_width,
        after=[corner(d_two_last)],
    )
    ffn_sums = weight_sum(ffn_grads).astype(jnp.float32)
    grad_gate, grad_up, grad_down_t = split_columns(ffn_sums, (hidden_width,) * 3)
    grad_two_part = jnp.sum(grad_gate * w_gate + grad_up * w_up, axis=1, keepdims=True)
    gain_own = gain_part.astype(jnp.float32)
    grad_two_part = grad_two_part / gain_own[:, 1:2]
    d_middle = out_grad.astype(jnp.float32) + norm_back(middle, gain_two, d_normed_two)
    mix_grad = gather_rows(d_middle.astype(low))
    d_mixers = reorder(
        ranks, [simple_product(mix_grad, mix_t).astype(low)], inverse=True, after=[corner(ffn_grads)]
    )
    d_scanned, d_gate_z, d_entry = scan_back_first(d_mixers, raw, scanned, cumulative)
    d_entry = pack_state(d_entry, local_log)
    after_states = from_earlier(d_entry, -1)
    mix_width = mixed_width + mixer_width
    all_width = mixed_width + in_width
    mix_grads = weight_grads(
        [(mix_grad, [mixers]), (normed_ordered, [d_gate_z])], all_width, after=[corner(d_entry)]
    )
    d_query, d_own, d_far = attend_back(
        rank, queries, keys_values, pieces, attended, log_totals, d_mixers, cosine, sine, [corner(mix_grads), *map(corner, after_states)]
    )
    d_ssm_in, d_bmat, d_cmat, d_pre, sums = scan_back(
        raw,
        d_scanned,
        bias,
        rate,
        delta,
        cumulative,
        cum_row,
        states,
        after_states,
        skip,
        [corner(d_query)],
    )
    far_half = d_far.shape[0] // 2
    d_mine = lax.dynamic_slice_in_dim(d_own, core * half_span, half_span, 0)
    d_theirs = lax.dynamic_slice_in_dim(d_own, (1 - core) * half_span, half_span, 0)
    d_mine = d_mine + to_partner(d_theirs.astype(low)).astype(jnp.float32)
    d_far = d_far[:far_half].astype(jnp.float32) + to_partner(d_far[far_half:]).astype(jnp.float32)
    d_one, d_two, d_three = (
        d_far[k * half_span : (k + 1) * half_span] for k in range(d_far.shape[0] // half_span)
    )
    d_one = d_one + on_blocks(d_two.astype(low), -1).astype(jnp.float32)
    d_mine = d_mine + on_blocks(d_one.astype(low), -1).astype(jnp.float32)
    d_mine = d_mine + on_blocks(d_three.astype(low), -3).astype(jnp.float32)
    half_cos = lax.dynamic_slice_in_dim(cosine, core * half_span, half_span, 0)
    half_sin = lax.dynamic_slice_in_dim(sine, core * half_span, half_span, 0)
    d_key = d_mine[:, :HD]
    d_key = d_key * half_cos - jnp.roll(d_key, HD // 2, axis=1) * half_sin
    d_mine = jnp.concatenate([d_key, d_mine[:, HD:]], axis=1).astype(low)
    d_keys_values = lax.dynamic_update_slice_in_dim(
        jnp.zeros((span_length, 2 * HD), low), d_mine, core * half_span, 0
    )

    scan_rights = [d_ssm_in, d_bmat, d_cmat, d_pre]
    in_grads = weight_grads([(normed_ordered, scan_rights)], all_width, mix_width, mix_grads)
    late_rights = [d_keys_values, d_query]
    late_start = mix_width + sum(array.shape[1] for array in scan_rights)
    in_grads = weight_grads([(normed_ordered, late_rights)], all_width, late_start, in_grads)
    in_sums = weight_sum(in_grads)
    d_projected = reorder(
        ranks,
        [d_gate_z, d_ssm_in, d_query, d_bmat, d_cmat, d_pre, d_keys_values],
        after=[corner(in_grads)],
    )
    d_normed, _ = scatter_rows(lambda rows: dot_last(d_projected[rows], in_full), half_span)
    input_grad = d_middle + norm_back(x_float, gain_one, d_normed)
    back_zero = 0.0 * d_query[0, 0].astype(jnp.float32)
    ffn_out, _ = scatter_rows(
        lambda rows: dot_last(hidden[rows], down_t) + back_zero, half_span
    )
    activations = (middle + ffn_out).astype(low)
    sums_names = ("ssm_out", "attn_out", "z", "x", "b", "c", "misc", "key", "value", "query")
    sums_widths = [mixer_width, query_width] + [at[name][1] for name in sums_names[2:]]
    sums_starts = [sum(sums_widths[:k]) for k in range(len(sums_widths))]
    sums_at = dict(zip(sums_names, zip(sums_starts, sums_widths)))
    extra = jnp.concatenate([gain_own[:, 0:1], grad_two_part], axis=1)
    extra = jnp.pad(extra, ((0, 0), (0, LANES - 2)))
    grad_ssm_out, grad_attn_out, grad_gatez, grad_ssmx, grad_query, misc_sums, shared_parts = finish(
        turns,
        kv_index.astype(jnp.int32)[None],
        in_sums,
        first_own,
        extra,
        at,
        sums_at,
    )
    shared_sums = scatter_small(shared_parts)
    grad_key, grad_value, grad_bmat, grad_cmat, gain_sums = split_columns(
        shared_sums, (kv_width, kv_width, state_size, state_size, LANES)
    )
    small_sums = sum_blocks(sums)[:, :heads]
    return (
        activations,
        input_grad,
        gain_sums[:, 0],
        grad_query,
        grad_key,
        grad_value,
        grad_gatez,
        grad_ssmx,
        misc_sums[:, :heads],
        grad_bmat,
        grad_cmat,
        small_sums[0],
        small_sums[1],
        small_sums[2],
        grad_attn_out,
        grad_ssm_out,
        gain_sums[:, 1],
        grad_gate,
        grad_up,
        grad_down_t.T,
    )


def solution(mesh):
    placed = (
        P(("dp", "blk", "heads"), None),
        P(("dp", "blk", "heads"), None),
        P(("dp", "blk", "heads")),
        P(("dp", "blk"), "heads"),
        P(("dp", "blk", "heads"), None),
        P(("dp", "blk", "heads"), None),
        P(("dp", "blk"), "heads"),
        P(("dp", "blk"), "heads"),
        P(("dp", "blk"), "heads"),
        P(("dp", "blk", "heads"), None),
        P(("dp", "blk", "heads"), None),
        P("heads"),
        P("heads"),
        P("heads"),
        P("heads", ("dp", "blk")),
        P("heads", ("dp", "blk")),
        P(("dp", "blk", "heads")),
        P(("dp", "blk"), "heads"),
        P(("dp", "blk"), "heads"),
        P("heads", ("dp", "blk")),
    )
    return jax.shard_map(
        shards,
        mesh=mesh,
        in_specs=placed,
        out_specs=(
            P(("dp", "blk", "heads"), None),
            P(("dp", "blk", "heads"), None),
            P(("dp", "blk", "heads")),
            P(("dp", "blk"), "heads"),
            P(("dp", "blk", "heads"), None),
            P(("dp", "blk", "heads"), None),
            P(("dp", "blk"), "heads"),
            P(("dp", "blk"), "heads"),
            P(("dp", "blk"), "heads"),
            P(("dp", "blk", "heads"), None),
            P(("dp", "blk", "heads"), None),
            P("heads"),
            P("heads"),
            P("heads"),
            P("heads", ("dp", "blk")),
            P("heads", ("dp", "blk")),
            P(("dp", "blk", "heads")),
            P(("dp", "blk"), "heads"),
            P(("dp", "blk"), "heads"),
            P("heads", ("dp", "blk")),
        ),
        check_vma=False,
    )
```

```python
import functools

import jax
import jax.numpy as jnp
from jax import lax
from jax.experimental import pallas as pl
from jax.experimental.pallas import tpu as pltpu
from jax.sharding import PartitionSpec as P

QH = 8
KVH = 2
HD = 128
MIXER_HEAD_SIZE = 64
BLOCK = 256
LANES = 128
LOG2_E = 1.4426950408889634


HIGH_PRECISION = lax.Precision.HIGHEST
norm_eps = 1e-05
rope_base = 100000000000.0


def simple_product(left_side, right_side):
    return jnp.dot(left_side, right_side, preferred_element_type=jnp.float32)


def dot_last(left_side, right_side):
    return lax.dot_general(
        left_side, right_side, (((1,), (1,)), ((), ())), preferred_element_type=jnp.float32
    )


def dot_first(left_side, right_side):
    return lax.dot_general(
        left_side, right_side, (((0,), (0,)), ((), ())), preferred_element_type=jnp.float32
    )


def compiler_params(mebibytes=20):
    return pltpu.CompilerParams(vmem_limit_bytes=mebibytes * 1024 * 1024)


def small_cost():
    return pl.CostEstimate(flops=1000, bytes_accessed=1000, transcendentals=0)


def in_hbm(value):
    return pltpu.with_memory_space_constraint(value, pltpu.HBM)


def corner(value):
    return value[:16, :LANES]


def in_vmem(count):
    return [pl.BlockSpec(memory_space=pltpu.VMEM)] * count


def mul(left_side, right_side):
    return jnp.dot(left_side, right_side, preferred_element_type=jnp.float32)


def tile_scores(key_rows, query_rows, head_size):
    return dot_last(key_rows, query_rows) * (head_size**-0.5 * LOG2_E)


def causal(scores):
    key_at = lax.broadcasted_iota(jnp.int32, scores.shape, 0)
    query_at = lax.broadcasted_iota(jnp.int32, scores.shape, 1)
    return jnp.where(key_at <= query_at, scores, -1e30)


def enter_kernel(
    ranks_ref, heads_ref, x_ref, misc_ref, key_ref, value_ref, w_query_ref, cos_ref, sin_ref, *refs
):
    ordered_ref, query_ref, kv_ref, gains_ref = refs[-4:]
    head_size = query_ref.shape[1]

    @pl.when(pl.program_id(0) == 0)
    def _():
        lane = lax.broadcasted_iota(jnp.int32, misc_ref.shape, 1)
        for k in range(2):
            column = jnp.where(lane == heads_ref[0] + k, misc_ref[...].astype(jnp.float32), 0.0)
            gains_ref[k : k + 1, :] = jnp.sum(column.T, axis=0, keepdims=True)

    cosine, sine = (cos_ref[...], sin_ref[...])

    def turn(value):
        return (value * cosine + pltpu.roll(value, head_size // 2, 1) * sine).astype(jnp.bfloat16)

    rows = x_ref[...].astype(jnp.float32)
    normed = (rows * inverse_rms(rows) * gains_ref[0:1, :]).astype(jnp.bfloat16)
    ordered_ref[...] = normed
    kv_ref[:, :head_size] = turn(mul(normed, key_ref[...]))
    kv_ref[:, head_size:] = mul(normed, value_ref[...]).astype(jnp.bfloat16)
    query_ref[...] = turn(mul(normed, w_query_ref[...]))


def enter(ranks, heads, x_span, in_full, at, cosine, sine, after):
    count = ranks.shape[0]
    rows, width = x_span.shape
    head_size = cosine.shape[1]
    here = lambda columns: pl.BlockSpec((rows // count, columns), lambda k, r, h: (k, 0))
    there = lambda columns: pl.BlockSpec((rows // count, columns), lambda k, r, h: (r[k], 0))
    weight = lambda name: pl.BlockSpec(
        (width, at[name][1]), lambda k, r, h: (0, at[name][0] // at[name][1])
    )
    return pl.pallas_call(
        enter_kernel,
        grid_spec=pltpu.PrefetchScalarGridSpec(
            num_scalar_prefetch=2,
            grid=(count,),
            in_specs=[
                here(width),
                weight("misc"),
                weight("key"),
                weight("value"),
                weight("query"),
                there(head_size),
                there(head_size),
            ]
            + [pl.BlockSpec(memory_space=pl.ANY)] * len(after),
            out_specs=(
                there(width),
                there(head_size),
                there(2 * head_size),
                pl.BlockSpec((8, width), lambda k, r, h: (0, 0)),
            ),
        ),
        out_shape=(
            jax.ShapeDtypeStruct((rows, width), jnp.bfloat16),
            jax.ShapeDtypeStruct((rows, head_size), jnp.bfloat16),
            jax.ShapeDtypeStruct((rows, 2 * head_size), jnp.bfloat16),
            jax.ShapeDtypeStruct((8, width), jnp.float32),
        ),
        compiler_params=compiler_params(),
        cost_estimate=small_cost(),
        name="enter",
    )(ranks, heads, in_hbm(x_span), in_full, in_full, in_full, in_full, cosine, sine, *after)


def weight_grads_kernel(*refs, counts):
    out_ref = refs[-1]
    start, used = (0, len(counts))
    for k, count in enumerate(counts):
        left = refs[k][...].T
        for ref in refs[used : used + count]:
            out_ref[:, start : start + ref.shape[1]] = mul(left, ref[...]).astype(jnp.bfloat16)
            start += ref.shape[1]
        used += count


def weight_grads(groups, width, start=0, buffer=None, after=()):
    rights = [right for _, group in groups for right in group]
    columns = sum(right.shape[1] for right in rights)
    depth = rights[0].shape[0]
    rows = groups[0][0].shape[1]
    operands = [left for left, _ in groups] + rights
    count = len(operands)
    extra = list(after) if buffer is None else [buffer] + list(after)

    def call(*refs):
        weight_grads_kernel(
            *refs[:count],
            refs[-1],
            counts=tuple(len(group) for _, group in groups),
        )

    return pl.pallas_call(
        call,
        grid=(rows // BLOCK,),
        out_shape=pltpu.HBM((rows, width), jnp.bfloat16),
        in_specs=[pl.BlockSpec((depth, BLOCK), lambda k: (0, k)) for _ in groups]
        + [pl.BlockSpec(right.shape, lambda k: (0, 0)) for right in rights]
        + [pl.BlockSpec(memory_space=pl.ANY)] * len(extra),
        out_specs=pl.BlockSpec(
            (pl.Element(BLOCK), pl.Element(columns)), lambda k: (k * BLOCK, start)
        ),
        input_output_aliases={} if buffer is None else {count: 0},
        compiler_params=compiler_params(),
        cost_estimate=pl.CostEstimate(
            flops=2 * rows * depth * columns,
            bytes_accessed=2 * (depth * (2 * rows + columns) + rows * columns),
            transcendentals=0,
        ),
        name="weight_grads",
    )(*operands, *extra)


def pack_kernel(*refs, turned):
    out_ref = refs[-1]
    start = 0
    for ref, turn in zip(refs, turned):
        piece = ref[...].T if turn else ref[...]
        out_ref[:, start : start + piece.shape[1]] = piece
        start += piece.shape[1]


def pack(pieces, turned, after):
    sizes = [piece.shape[::-1] if turn else piece.shape for piece, turn in zip(pieces, turned)]
    return pl.pallas_call(
        functools.partial(pack_kernel, turned=turned),
        out_shape=jax.ShapeDtypeStruct(
            (sizes[0][0], sum(size[1] for size in sizes)), jnp.bfloat16
        ),
        in_specs=in_vmem(len(pieces)) + [pl.BlockSpec(memory_space=pl.ANY)],
        out_specs=pl.BlockSpec(memory_space=pltpu.VMEM),
        compiler_params=compiler_params(),
        name="pack",
    )(*pieces, after)


def join_kernel(*refs):
    out_ref = refs[-1]
    start = 0
    for ref in refs[:-1]:
        out_ref[start : start + ref.shape[0], :] = ref[...]
        start += ref.shape[0]


def join(pieces):
    rows = sum(piece.shape[0] for piece in pieces)
    return pl.pallas_call(
        join_kernel,
        out_shape=jax.ShapeDtypeStruct((rows, pieces[0].shape[1]), pieces[0].dtype),
        in_specs=in_vmem(len(pieces)),
        out_specs=pl.BlockSpec(memory_space=pltpu.VMEM),
        compiler_params=compiler_params(),
        cost_estimate=small_cost(),
        name="join",
    )(*pieces)


def pack_first_kernel(
    turns_ref, kv_ref, shared_ref, delta_ref, z_ref, x_ref, query_ref, ssm_ref, attn_ref, out_ref, *, at
):
    def put(name, value, rows=slice(None)):
        start, size = at[name]
        out_ref[rows, start : start + size] = value

    put("z", z_ref[...])
    put("x", x_ref[...])
    put("query", query_ref[...])
    put("ssm_out", ssm_ref[...].T)
    put("attn_out", attn_ref[...].T)
    count = turns_ref.shape[0]
    size = shared_ref.shape[0] // count
    first = kv_ref[0] == 0
    for k in range(count):
        rows = pl.ds(pl.multiple_of(turns_ref[k] * size, size), size)
        chunk = shared_ref[k * size : (k + 1) * size, :]
        pieces, start = [], 0
        for width in (HD, HD, HD, HD, at["b"][1], at["c"][1], LANES):
            pieces.append(chunk[:, start : start + width])
            start += width
        put("key", jnp.where(first, pieces[0], pieces[1]), rows)
        put("value", jnp.where(first, pieces[2], pieces[3]), rows)
        put("b", pieces[4], rows)
        put("c", pieces[5], rows)
        put("misc", pieces[6] + delta_ref[rows, :], rows)


def pack_first(turns, kv_index, shared, delta, weights, at):
    rows = shared.shape[0]
    return pl.pallas_call(
        functools.partial(pack_first_kernel, at=at),
        out_shape=jax.ShapeDtypeStruct(
            (rows, max(start + size for start, size in at.values())), jnp.bfloat16
        ),
        in_specs=[pl.BlockSpec(memory_space=pltpu.SMEM)] * 2 + in_vmem(2 + len(weights)),
        out_specs=pl.BlockSpec(memory_space=pltpu.VMEM),
        compiler_params=compiler_params(50),
        cost_estimate=small_cost(),
        name="pack_first",
    )(turns, kv_index, shared, delta, *weights)


def finish_kernel(
    ranks_ref,
    kv_ref,
    sums_ref,
    weight_ref,
    extra_ref,
    ssm_out_ref,
    attn_out_ref,
    gate_ref,
    ssm_ref,
    query_ref,
    misc_ref,
    shared_ref,
    whole_ref,
    *,
    at,
    sums_at,
):
    def of(name):
        start, size = sums_at[name]
        return sums_ref[:, start : start + size].astype(jnp.float32)

    ssm_out_ref[...] = of("ssm_out").T
    attn_out_ref[...] = of("attn_out").T
    gate_ref[...] = of("z")
    ssm_ref[...] = of("x")
    query_ref[...] = of("query")
    misc_ref[...] = of("misc")
    total = 0.0
    for name, (start, size) in at.items():
        product = of(name) * weight_ref[:, start : start + size].astype(jnp.float32)
        total += jnp.sum(product, axis=1, keepdims=True)
    total = total / extra_ref[:, 0:1]
    lane = lax.broadcasted_iota(jnp.int32, misc_ref.shape, 1)
    gains = jnp.where(lane == 0, total, jnp.where(lane == 1, extra_ref[:, 1:2], 0.0))
    zero = jnp.zeros_like(gains)
    first = kv_ref[0] == 0
    key, value = (of("key"), of("value"))
    pieces = (
        jnp.where(first, key, zero),
        jnp.where(first, zero, key),
        jnp.where(first, value, zero),
        jnp.where(first, zero, value),
        of("b"),
        of("c"),
        gains,
    )
    start = 0
    for piece in pieces:
        whole_ref[:, start : start + piece.shape[1]] = piece
        start += piece.shape[1]
    count = ranks_ref.shape[0]
    size = shared_ref.shape[0] // count
    for k in range(count):
        rows = pl.ds(pl.multiple_of(ranks_ref[k] * size, size), size)
        shared_ref[k * size : (k + 1) * size, :] = whole_ref[rows, :].astype(jnp.bfloat16)


def finish(ranks, kv_index, sums, weights, extra, at, sums_at):
    rows = weights.shape[0]
    shape = lambda *sizes: jax.ShapeDtypeStruct(sizes, jnp.float32)
    width = lambda name: sums_at[name][1]
    shared = 2 * (width("key") + width("value")) + width("b") + width("c") + LANES
    return pl.pallas_call(
        functools.partial(finish_kernel, at=at, sums_at=sums_at),
        out_shape=(
            shape(width("ssm_out"), rows),
            shape(width("attn_out"), rows),
            shape(rows, width("z")),
            shape(rows, width("x")),
            shape(rows, width("query")),
            shape(rows, width("misc")),
            jax.ShapeDtypeStruct((rows, shared), jnp.bfloat16),
        ),
        in_specs=[pl.BlockSpec(memory_space=pltpu.SMEM)] * 2 + in_vmem(3),
        out_specs=tuple(in_vmem(7)),
        scratch_shapes=[pltpu.VMEM((rows, shared), jnp.float32)],
        compiler_params=compiler_params(),
        name="finish",
    )(ranks, kv_index, sums, weights, extra)


def attend_kernel(rank_ref, query_ref, own_ref, *refs):
    pieces, (out_ref, low_ref, log_ref) = (refs[:-3], refs[-3:])
    span_length, head_size = query_ref.shape
    tile = own_ref.shape[0] // 2
    for block in range(span_length // tile):
        here = slice(block * tile, (block + 1) * tile)
        query_rows = query_ref[here, :]

        def step(kv_rows, carried, masked=False):
            top, total, summed = carried
            scores = tile_scores(kv_rows[:, :head_size], query_rows, head_size)
            if masked:
                scores = causal(scores)
            new_top = jnp.maximum(top, jnp.max(scores, axis=0, keepdims=True))
            probs = jnp.exp2(scores - new_top)
            scale = jnp.exp2(top - new_top)
            total = total * scale + jnp.sum(probs, axis=0, keepdims=True)
            summed = summed * scale + dot_first(kv_rows[:, head_size:], probs.astype(jnp.bfloat16))
            return (new_top, total, summed)

        carried = (
            jnp.full((1, tile), -1e30, jnp.float32),
            jnp.zeros((1, tile), jnp.float32),
            jnp.zeros((head_size, tile), jnp.float32),
        )
        carried = step(own_ref[here, :], carried, True)
        for earlier in range(block):
            carried = step(own_ref[earlier * tile : (earlier + 1) * tile, :], carried)
        for distance in range(1, 1 + len(pieces) // 2):
            pair = pieces[2 * distance - 2 : 2 * distance]

            def both(_, carried, pair=pair):
                return step(pair[1][...], step(pair[0][...], carried))

            valid = (rank_ref[0] >= distance).astype(jnp.int32)
            carried = lax.fori_loop(0, valid, both, carried)
        top, total, summed = carried
        result = summed / total
        out_ref[:, here] = result
        low_ref[here, :] = result.T.astype(jnp.bfloat16)
        log_ref[:, here] = top + jnp.log2(total)


def attend(rank, queries, own, pieces):
    span_length, head_size = queries.shape
    return pl.pallas_call(
        attend_kernel,
        out_shape=(
            jax.ShapeDtypeStruct((head_size, span_length), jnp.float32),
            jax.ShapeDtypeStruct((span_length, head_size), jnp.bfloat16),
            jax.ShapeDtypeStruct((1, span_length), jnp.float32),
        ),
        in_specs=[pl.BlockSpec(memory_space=pltpu.SMEM)] + in_vmem(2 + len(pieces)),
        out_specs=tuple(in_vmem(3)),
        compiler_params=compiler_params(),
        cost_estimate=small_cost(),
        name="attend",
    )(rank, queries, own, *pieces)


def attend_back_kernel(rank_ref, query_ref, own_ref, *refs):
    pieces, refs = (refs[:-13], refs[-13:])
    out_ref, log_ref, grad_ref, cos_ref, sin_ref, *_, d_query_ref, d_own_ref, d_far_ref, sums_ref = refs
    span_length, head_size = query_ref.shape
    tile = own_ref.shape[0] // 2
    score_scale = head_size**-0.5
    sums_ref[...] = jnp.zeros_like(sums_ref)
    for block in range(span_length // tile):
        here = slice(block * tile, (block + 1) * tile)
        query_rows = query_ref[here, :]
        grad_rows = grad_ref[here, grad_ref.shape[1] - head_size :]
        log_total = log_ref[:, here]
        delta_row = jnp.sum(
            grad_rows.astype(jnp.float32).T * out_ref[:, here], axis=0, keepdims=True
        )

        def step(kv_ref, start, at, d_query, masked=False):
            key_rows = kv_ref[start : start + tile, :head_size]
            scores = tile_scores(key_rows, query_rows, head_size)
            if masked:
                scores = causal(scores)
            probs = jnp.exp2(scores - log_total)
            d_probs = dot_last(kv_ref[start : start + tile, head_size:], grad_rows)
            d_scores = (probs * (d_probs - delta_row)).astype(jnp.bfloat16)
            rows = slice(at * tile, (at + 1) * tile)
            sums_ref[rows, head_size:] += mul(probs.astype(jnp.bfloat16), grad_rows)
            sums_ref[rows, :head_size] += mul(d_scores, query_rows)
            return d_query + dot_first(key_rows, d_scores)

        d_query = jnp.zeros((head_size, tile), jnp.float32)
        d_query = step(own_ref, block * tile, block, d_query, True)
        for earlier in range(block):
            d_query = step(own_ref, earlier * tile, earlier, d_query)
        for distance in range(1, 1 + len(pieces) // 2):

            def both(_, d_query, distance=distance):
                for k in (2 * distance - 2, 2 * distance - 1):
                    d_query = step(pieces[k], 0, 2 + k, d_query)
                return d_query

            valid = (rank_ref[0] >= distance).astype(jnp.int32)
            d_query = lax.fori_loop(0, valid, both, d_query)
        turned = d_query.T * score_scale
        d_query_ref[here, :] = (
            turned * cos_ref[here, :] - pltpu.roll(turned, head_size // 2, 1) * sin_ref[here, :]
        ).astype(jnp.bfloat16)
    lane = lax.broadcasted_iota(jnp.int32, (tile, 2 * head_size), 1)
    scale = jnp.where(lane < head_size, score_scale, 1.0)
    for at in range(2):
        rows = slice(at * tile, (at + 1) * tile)
        d_own_ref[rows, :] = sums_ref[rows, :] * scale
    for k in range(len(pieces)):
        rows = slice((2 + k) * tile, (3 + k) * tile)
        into = (k % 2) * (len(pieces) // 2) + k // 2
        d_far_ref[into * tile : (into + 1) * tile, :] = (sums_ref[rows, :] * scale).astype(
            jnp.bfloat16
        )


def attend_back(rank, queries, own, pieces, attended, log_totals, d_attn, cosine, sine, after):
    tile = own.shape[0] // 2
    return pl.pallas_call(
        attend_back_kernel,
        out_shape=(
            jax.ShapeDtypeStruct(queries.shape, jnp.bfloat16),
            jax.ShapeDtypeStruct(own.shape, jnp.float32),
            jax.ShapeDtypeStruct((len(pieces) * tile, own.shape[1]), jnp.bfloat16),
        ),
        in_specs=[pl.BlockSpec(memory_space=pltpu.SMEM)]
        + in_vmem(7 + len(pieces))
        + [pl.BlockSpec(memory_space=pl.ANY)] * len(after),
        out_specs=tuple(in_vmem(3)),
        scratch_shapes=[pltpu.VMEM(((2 + len(pieces)) * tile, own.shape[1]), jnp.float32)],
        compiler_params=compiler_params(),
        cost_estimate=small_cost(),
        name="attend_back",
    )(rank, queries, own, *pieces, attended, log_totals, d_attn, cosine, sine, *after)


def reorder_kernel(ranks_ref, *refs, count):
    out_ref = refs[-1]
    start = 0
    for ref in refs[:count]:
        out_ref[:, start : start + ref.shape[1]] = ref[...].astype(out_ref.dtype)
        start += ref.shape[1]


def reorder(ranks, pieces, inverse=False, after=()):
    count = ranks.shape[0]
    rows = pieces[0].shape[0] // count
    width = sum(piece.shape[1] for piece in pieces)
    there = lambda k, ranks: (ranks[k], 0)
    here = lambda k, ranks: (k, 0)
    return pl.pallas_call(
        functools.partial(reorder_kernel, count=len(pieces)),
        grid_spec=pltpu.PrefetchScalarGridSpec(
            num_scalar_prefetch=1,
            grid=(count,),
            in_specs=[
                pl.BlockSpec((rows, piece.shape[1]), here if inverse else there)
                for piece in pieces
            ]
            + [pl.BlockSpec(memory_space=pl.ANY)] * len(after),
            out_specs=pl.BlockSpec((rows, width), there if inverse else here),
        ),
        out_shape=jax.ShapeDtypeStruct((count * rows, width), jnp.bfloat16),
        compiler_params=compiler_params(),
        cost_estimate=small_cost(),
        name="reorder",
    )(ranks, *pieces, *after)


def lower_ones(size, dtype=jnp.float32):
    row = lax.broadcasted_iota(jnp.int32, (size, size), 0)
    column = lax.broadcasted_iota(jnp.int32, (size, size), 1)
    return (row >= column).astype(dtype)


def precise(left_side, right_side):
    return jnp.dot(
        left_side, right_side, precision=HIGH_PRECISION, preferred_element_type=jnp.float32
    )


def spread_heads(columns, head_size, width):
    lane = lax.broadcasted_iota(jnp.int32, (columns.shape[0], 2 * head_size), 1)
    pairs = [
        jnp.where(lane < head_size, columns[:, k : k + 1], columns[:, k + 1 : k + 2])
        for k in range(0, width // head_size, 2)
    ]
    return jnp.concatenate(pairs, axis=1)


def head_ones(width, head_size, lanes, dtype):
    at = lax.broadcasted_iota(jnp.int32, (width, lanes), 0)
    lane = lax.broadcasted_iota(jnp.int32, (width, lanes), 1)
    low = lane * head_size
    return ((at >= low) & (at < low + head_size)).astype(dtype)


def scan_first_kernel(
    pre_ref, bias_ref, rate_ref, x_ref, b_ref, delta_ref, cum_ref, delta_row_ref, cum_row_ref, state_ref, log_ref
):
    @pl.when(pl.program_id(0) == 0)
    def _():
        state_ref[...] = jnp.zeros_like(state_ref)
        log_ref[...] = jnp.zeros_like(log_ref)

    delta = jax.nn.softplus(pre_ref[...] + bias_ref[...])
    log_step = -delta * rate_ref[...]
    cumulative = precise(lower_ones(log_step.shape[0]), log_step)
    delta_ref[...] = delta
    cum_ref[...] = cumulative
    delta_row_ref[...] = delta.T[:8]
    cum_row_ref[...] = cumulative.T[:8]
    ending = cumulative[-1:, :]
    weight = jnp.exp(ending - cumulative + log_ref[...]) * delta
    width = x_ref.shape[1]
    x_low = x_ref[...].astype(jnp.bfloat16).astype(jnp.float32)
    weighted = (x_low * spread_heads(weight, MIXER_HEAD_SIZE, width)).astype(jnp.bfloat16)
    state_ref[...] += dot_first(b_ref[...].astype(jnp.bfloat16), weighted)
    log_ref[...] += ending


def part(projected, start, width, order=lambda c: c):
    at = start // width
    return (projected, pl.BlockSpec((BLOCK, width), lambda c: (order(c), at)))


def run_scan(
    kernel, chunks, operands, out_shape, out_specs, name, scratch=(), after=(), mebibytes=20
):
    count = len(operands)
    operands = operands + [(array, pl.BlockSpec(memory_space=pl.ANY)) for array in after]

    def call(*refs):
        kernel(*refs[:count], *refs[count + len(after) :])

    return pl.pallas_call(
        call,
        grid=(chunks,),
        out_shape=out_shape,
        in_specs=[spec for _, spec in operands],
        out_specs=out_specs,
        scratch_shapes=list(scratch),
        compiler_params=compiler_params(mebibytes),
        cost_estimate=small_cost(),
        name=name,
    )(*[array for array, _ in operands])


def whole(array):
    return (array, pl.BlockSpec(array.shape, lambda c: (0,) * array.ndim))


def scan_first(at, bias, rate):
    rows, lanes = (at["x"][0].shape[0], bias.shape[1])
    chunks = rows // BLOCK
    back = lambda c: chunks - 1 - c
    width, state_size = (at["x"][2], at["b"][2])
    by_chunk = pl.BlockSpec((BLOCK, lanes), lambda c: (back(c), 0))
    across = pl.BlockSpec((8, BLOCK), lambda c: (0, back(c)))
    shape = lambda *sizes: jax.ShapeDtypeStruct(sizes, jnp.float32)
    return run_scan(
        scan_first_kernel,
        chunks,
        [
            part(*at["misc"], back),
            whole(bias),
            whole(rate),
            part(*at["x"], back),
            part(*at["b"], back),
        ],
        (
            shape(rows, lanes),
            shape(rows, lanes),
            shape(8, rows),
            shape(8, rows),
            shape(state_size, width),
            shape(1, lanes),
        ),
        (
            by_chunk,
            by_chunk,
            across,
            across,
            pl.BlockSpec((state_size, width), lambda c: (0, 0)),
            pl.BlockSpec((1, lanes), lambda c: (0, 0)),
        ),
        "scan_first",
    )


def chained(refs, width):
    state = jnp.zeros((refs[0].shape[0] - 16, width), jnp.float32)
    for ref in reversed(refs):
        logs = ref[-16:, :LANES].astype(jnp.float32)
        decay = jnp.exp(jnp.sum(logs[:3], axis=0, keepdims=True))
        state = ref[:-16].astype(jnp.float32) + spread_heads(decay, MIXER_HEAD_SIZE, width) * state
    return state


def scan_kernel(
    x_ref,
    z_ref,
    b_ref,
    c_ref,
    delta_ref,
    cum_ref,
    delta_row_ref,
    cum_row_ref,
    near_ref,
    next_ref,
    far_ref,
    skip_ref,
    scanned_ref,
    gated_ref,
    states_ref,
    state_ref,
):
    @pl.when(pl.program_id(0) == 0)
    def _():
        state_ref[...] = chained((near_ref, next_ref, far_ref), x_ref.shape[1])

    head_size = MIXER_HEAD_SIZE
    pair = 2 * head_size
    size, width = x_ref.shape
    state = state_ref[...]
    states_ref[0] = state
    delta, cumulative = (delta_ref[...], cum_ref[...])
    delta_row, cum_row = (delta_row_ref[...], cum_row_ref[...])
    bmat, cmat = (b_ref[...].astype(jnp.bfloat16), c_ref[...].astype(jnp.bfloat16))
    x_all = x_ref[...].astype(jnp.bfloat16)
    inner = dot_last(cmat, bmat)
    row = lax.broadcasted_iota(jnp.int32, (size, size), 0)
    column = lax.broadcasted_iota(jnp.int32, (size, size), 1)
    allowed = row >= column
    lane = lax.broadcasted_iota(jnp.int32, (size, pair), 1)
    from_state = mul(cmat, state.astype(jnp.bfloat16))
    spread = spread_heads(jnp.exp(cumulative), head_size, width)
    for first in range(0, width // head_size, 2):
        here = slice(first * head_size, first * head_size + pair)
        x_pair = x_all[:, here]
        total = from_state[:, here] * spread[:, here]
        total += skip_ref[:, here] * x_pair.astype(jnp.float32)
        for head in (first, first + 1):
            gap = cumulative[:, head : head + 1] - cum_row[head : head + 1, :]
            decay = jnp.exp(jnp.where(allowed, gap, -1e30))
            mixing = inner * decay * delta_row[head : head + 1, :]
            x_head = jnp.where((lane >= head_size) == (head > first), x_pair, 0.0)
            total += mul(mixing.astype(jnp.bfloat16), x_head.astype(jnp.bfloat16))
        scanned_ref[:, here] = total
        gate = z_ref[:, here]
        gated_ref[:, here] = (total * (gate * jax.nn.sigmoid(gate))).astype(jnp.bfloat16)
    ending = cumulative[-1:, :]
    weight = spread_heads(jnp.exp(ending - cumulative) * delta, head_size, width)
    weighted = (x_all.astype(jnp.float32) * weight).astype(jnp.bfloat16)
    state_ref[...] = state * spread[-1:, :] + dot_first(bmat, weighted)


def scan(at, delta, cumulative, delta_row, cum_row, entry, skip, after):
    rows = delta.shape[0]
    state_size, width = (at["b"][2], at["x"][2])
    chunks = rows // BLOCK
    by_chunk = pl.BlockSpec((BLOCK, width), lambda c: (c, 0))
    lanes = delta.shape[1]
    across = pl.BlockSpec((8, BLOCK), lambda c: (0, c))
    return run_scan(
        scan_kernel,
        chunks,
        [
            part(*at["x"]),
            part(*at["z"]),
            part(*at["b"]),
            part(*at["c"]),
            part(delta, 0, lanes),
            part(cumulative, 0, lanes),
            (delta_row, across),
            (cum_row, across),
            *[whole(packed) for packed in entry],
            whole(skip),
        ],
        (
            jax.ShapeDtypeStruct((rows, width), jnp.float32),
            jax.ShapeDtypeStruct((rows, width), jnp.bfloat16),
            jax.ShapeDtypeStruct((chunks, state_size, width), jnp.float32),
        ),
        (by_chunk, by_chunk, pl.BlockSpec((1, state_size, width), lambda c: (c, 0, 0))),
        "scan",
        [pltpu.VMEM((state_size, width), jnp.float32)],
        after,
    )


def scan_back_first_kernel(
    grad_ref, z_ref, scanned_ref, c_ref, cum_ref, d_scanned_ref, d_gate_ref, state_ref, log_ref
):
    @pl.when(pl.program_id(0) == 0)
    def _():
        state_ref[...] = jnp.zeros_like(state_ref)
        log_ref[...] = jnp.zeros_like(log_ref)

    gate = z_ref[...]
    chance = jax.nn.sigmoid(gate)
    grad = grad_ref[:, : z_ref.shape[1]].astype(jnp.float32)
    d_scanned = grad * (gate * chance)
    d_scanned_ref[...] = d_scanned
    d_gate_ref[...] = (
        grad * scanned_ref[...] * (chance * (1.0 + gate * (1.0 - chance)))
    ).astype(jnp.bfloat16)
    cumulative = cum_ref[...]
    decay = spread_heads(jnp.exp(cumulative + log_ref[...]), MIXER_HEAD_SIZE, z_ref.shape[1])
    state_ref[...] += dot_first(
        c_ref[...].astype(jnp.bfloat16), (d_scanned * decay).astype(jnp.bfloat16)
    )
    log_ref[...] += cumulative[-1:, :]


def scan_back_first(grads, at, scanned, cumulative):
    rows, width = scanned.shape
    state_size, lanes = (at["c"][2], cumulative.shape[1])
    by_chunk = pl.BlockSpec((BLOCK, width), lambda c: (c, 0))
    return run_scan(
        scan_back_first_kernel,
        rows // BLOCK,
        [
            part(grads, 0, grads.shape[1]),
            part(*at["z"]),
            part(scanned, 0, width),
            part(*at["c"]),
            part(cumulative, 0, lanes),
        ],
        (
            jax.ShapeDtypeStruct((rows, width), jnp.float32),
            jax.ShapeDtypeStruct((rows, width), jnp.bfloat16),
            jax.ShapeDtypeStruct((state_size, width), jnp.float32),
        ),
        (by_chunk, by_chunk, pl.BlockSpec((state_size, width), lambda c: (0, 0))),
        "scan_back_first",
        [pltpu.VMEM((1, lanes), jnp.float32)],
    )


def scan_back_kernel(
    x_ref,
    grad_ref,
    b_ref,
    c_ref,
    pre_ref,
    bias_ref,
    rate_ref,
    delta_ref,
    cum_ref,
    cum_row_ref,
    states_ref,
    near_ref,
    next_ref,
    far_ref,
    skip_ref,
    d_x_ref,
    d_b_ref,
    d_c_ref,
    d_pre_ref,
    sums_ref,
    state_ref,
):
    @pl.when(pl.program_id(0) == 0)
    def _():
        state_ref[...] = chained((near_ref, next_ref, far_ref), x_ref.shape[1])
        sums_ref[...] = jnp.zeros_like(sums_ref)

    head_size = MIXER_HEAD_SIZE
    pair = 2 * head_size
    size, width = x_ref.shape
    lanes = delta_ref.shape[1]
    low = jnp.bfloat16
    delta, cumulative, cum_row = (delta_ref[...], cum_ref[...], cum_row_ref[...])
    bmat, cmat = (b_ref[...].astype(low), c_ref[...].astype(low))
    x_all = x_ref[...].astype(low)
    x_single = x_all.astype(jnp.float32)
    grad = grad_ref[...]
    grad_low = grad.astype(low)
    state = states_ref[0]
    state_low = state.astype(low)
    after = state_ref[...]
    after_low = after.astype(low)
    ending = cumulative[-1:, :]
    row = lax.broadcasted_iota(jnp.int32, (size, size), 0)
    column = lax.broadcasted_iota(jnp.int32, (size, size), 1)
    later = column >= row
    before = (row > column).astype(low)
    onward = later.astype(low)
    lane = lax.broadcasted_iota(jnp.int32, (size, pair), 1)
    head_lane = lax.broadcasted_iota(jnp.int32, (size, lanes), 1)
    sum_heads = head_ones(width, head_size, lanes, low)

    inner = dot_last(bmat, cmat)
    from_after = mul(bmat, after_low)
    weight = jnp.exp(ending - cumulative)
    spread_weight = spread_heads(weight * delta, head_size, width)
    spread = spread_heads(jnp.exp(cumulative), head_size, width)
    to_end = mul((x_single * from_after).astype(low), sum_heads)
    through = jnp.exp(cumulative) * mul((grad * mul(cmat, state_low)).astype(low), sum_heads)
    carried = jnp.sum(state * after, axis=0, keepdims=True) * spread[-1:, :]
    carried = precise(carried, sum_heads.astype(jnp.float32))
    d_delta = weight * to_end
    d_log = (
        mul(onward, through.astype(low)) + mul(before, (d_delta * delta).astype(low)) + carried
    )

    d_inner = jnp.zeros((size, size), jnp.float32)
    for first in range(0, width // head_size, 2):
        here = slice(first * head_size, first * head_size + pair)
        x_pair, grad_pair = (x_all[:, here], grad_low[:, here])
        d_x = from_after[:, here] * spread_weight[:, here] + skip_ref[:, here] * grad[:, here]
        for head in (first, first + 1):
            mine = (lane >= head_size) == (head > first)
            gap = cum_row[head : head + 1, :] - cumulative[:, head : head + 1]
            decay = jnp.exp(jnp.where(later, gap, -1e30))
            delta_column = delta[:, head : head + 1]
            d_mixing = dot_last(jnp.where(mine, x_pair, 0.0).astype(low), grad_pair) * decay
            d_inner += d_mixing * delta_column
            flow = d_mixing * inner
            mixing = inner * decay * delta_column
            d_x += mul(mixing.astype(low), jnp.where(mine, grad_pair, 0.0).astype(low))
            d_delta_head = jnp.sum(flow, axis=1, keepdims=True)
            passing = mul(before, (flow * delta_column).astype(low))
            d_log_head = jnp.sum(jnp.where(later, passing, 0.0), axis=1, keepdims=True)
            d_delta += jnp.where(head_lane == head, d_delta_head, 0.0)
            d_log += jnp.where(head_lane == head, d_log_head, 0.0)
        d_x_ref[:, here] = d_x.astype(low)

    d_inner_low = d_inner.astype(low)
    scaled_grad = (grad * spread).astype(low)
    weighted = (x_single * spread_weight).astype(low)
    d_b_ref[...] = (mul(d_inner_low, cmat) + dot_last(weighted, after_low)).astype(low)
    d_c_ref[...] = (dot_first(d_inner_low, bmat) + dot_last(scaled_grad, state_low)).astype(low)
    state_ref[...] = after * spread[-1:, :] + dot_first(cmat, scaled_grad)
    rate = rate_ref[...]
    d_pre = (d_delta - d_log * rate) * jax.nn.sigmoid(pre_ref[...] + bias_ref[...])
    d_pre = jnp.where(head_lane < width // head_size, d_pre, 0.0)
    d_pre_ref[...] = d_pre.astype(low)
    skip_sum = precise(
        jnp.sum(grad * x_single, axis=0, keepdims=True), sum_heads.astype(jnp.float32)
    )
    sums_ref[0:1, :] += jnp.sum(d_pre, axis=0, keepdims=True)
    sums_ref[1:2, :] += jnp.sum(d_log * (-delta * rate), axis=0, keepdims=True)
    sums_ref[2:3, :] += skip_sum


def scan_back(
    at, d_scanned, bias, rate, delta, cumulative, cum_row, states, entry, skip, after
):
    rows, width = d_scanned.shape
    state_size, lanes = (at["b"][2], delta.shape[1])
    chunks = rows // BLOCK
    back = lambda c: chunks - 1 - c
    by_chunk = lambda columns: pl.BlockSpec((BLOCK, columns), lambda c: (back(c), 0))
    shape = lambda columns: jax.ShapeDtypeStruct((rows, columns), jnp.bfloat16)
    return run_scan(
        scan_back_kernel,
        chunks,
        [
            part(*at["x"], back),
            part(in_hbm(d_scanned), 0, width, back),
            part(*at["b"], back),
            part(*at["c"], back),
            part(*at["misc"], back),
            whole(bias),
            whole(rate),
            part(delta, 0, lanes, back),
            part(cumulative, 0, lanes, back),
            (cum_row, pl.BlockSpec((8, BLOCK), lambda c: (0, back(c)))),
            (in_hbm(states), pl.BlockSpec((1, state_size, width), lambda c: (back(c), 0, 0))),
            *[whole(packed) for packed in entry],
            whole(skip),
        ],
        (
            shape(width),
            shape(state_size),
            shape(state_size),
            shape(lanes),
            jax.ShapeDtypeStruct((8, lanes), jnp.float32),
        ),
        (
            by_chunk(width),
            by_chunk(state_size),
            by_chunk(state_size),
            by_chunk(lanes),
            pl.BlockSpec((8, lanes), lambda c: (0, 0)),
        ),
        "scan_back",
        [pltpu.VMEM((state_size, width), jnp.float32)],
        after,
        44,
    )


def on_heads(value, move):
    devices = lax.axis_size("heads")
    pairs = []
    for at in range(devices):
        z, core = move(at // 2, at % 2)
        pairs.append((at, 2 * (z % (devices // 2)) + core))
    return lax.ppermute(value, "heads", pairs)


def to_partner(value):
    return on_heads(value, lambda z, core: (z, 1 - core))


def along(value):
    return on_heads(value, lambda z, core: (z + 1 - 2 * core, core))


def against(value):
    return on_heads(value, lambda z, core: (z - 1 + 2 * core, core))


def chunk_ranks():
    devices = lax.axis_size("heads")
    z, core = (lax.axis_index("heads") // 2, lax.axis_index("heads") % 2)
    step, other = (1 - 2 * core, 1 - core)
    owners = (
        (z, core),
        (z + 2, core),
        (z - step, core),
        (z - step, other),
        (z, other),
        (z + 2, other),
        (z + step, other),
        (z + step, core),
    )
    return jnp.stack([2 * ((at + devices) % (devices // 2)) + side for at, side in owners])


def along_other(value):
    return on_heads(value, lambda z, core: (z - 1 + 2 * core, 1 - core))


def against_other(value):
    return on_heads(value, lambda z, core: (z - 1 + 2 * core, 1 - core))


def gather_rows(own, joined=False):
    near = along(own)
    near_other = along_other(own)
    partner = to_partner(own)
    far = along(near)
    mine = (own, far, near, near_other)
    theirs = (partner, to_partner(far), to_partner(near), to_partner(near_other))
    rows = join(mine + theirs) if joined else jnp.concatenate(mine + theirs, axis=0)
    return rows, partner


def scatter_rows(product, half, late=None):
    chunk = half // 4
    got = to_partner(product(slice(half, 2 * half)).astype(jnp.bfloat16))
    kept = lax.optimization_barrier(product(slice(0, half)))
    summed = kept + got.astype(jnp.float32)
    low = summed[chunk:].astype(jnp.bfloat16)
    far = against(low[:chunk])
    near_other = against_other(low[2 * chunk :])
    near = low[chunk : 2 * chunk].astype(jnp.float32) + far.astype(jnp.float32)
    near = against((near if late is None else near + late).astype(jnp.bfloat16))
    return summed[:chunk] + near.astype(jnp.float32) + near_other.astype(jnp.float32)


def across(value, bit):
    devices = lax.axis_size("heads")
    return lax.ppermute(value, "heads", [(at, at ^ bit) for at in range(devices)])


def gather_small(value):
    for bit in (1, 2, 4):
        value = jnp.concatenate([value, across(value, bit)], axis=0)
    return value


def scatter_small(value):
    for bit in (4, 2, 1):
        half = value.shape[0] // 2
        got = across(value[half:].astype(jnp.bfloat16), bit)
        value = value[:half].astype(jnp.float32) + got.astype(jnp.float32)
    return value


def on_blocks(value, step):
    devices = lax.axis_size("blk")
    pairs = [(at, at + step) for at in range(devices) if 0 <= at + step < devices]
    return lax.ppermute(value, "blk", pairs)


def from_earlier(value, step=1):
    return tuple(on_blocks(value, distance * step) for distance in (1, 2, 3))


def pack_state(state, log_total):
    high = log_total.astype(jnp.bfloat16)
    rest = log_total - high.astype(jnp.float32)
    middle = rest.astype(jnp.bfloat16)
    low = (rest - middle.astype(jnp.float32)).astype(jnp.bfloat16)
    logs = jnp.concatenate([high, middle, low], axis=0)
    logs = jnp.pad(logs, ((0, 16 - logs.shape[0]), (0, state.shape[1] - logs.shape[1])))
    return jnp.concatenate([state.astype(jnp.bfloat16), logs], axis=0)


def sum_blocks(value):
    for axis in ("dp", "blk"):
        for bit in (1, 2):
            value = value + lax.ppermute(
                value, axis, [(at, at ^ bit) for at in range(lax.axis_size(axis))]
            )
    return value


def weight_sum(grads):
    return lax.psum_scatter(grads, ("dp", "blk"), scatter_dimension=0, tiled=True)


def split_columns(value_in, widths):
    pieces, start = [], 0
    for width in widths:
        pieces.append(value_in[:, start : start + width])
        start += width
    return pieces


def inverse_rms(rows_in):
    return lax.rsqrt(jnp.mean(rows_in * rows_in, axis=-1, keepdims=True) + norm_eps)


def norm_back(rows_in, gain_in, cotangent):
    inverse = inverse_rms(rows_in)
    scaled = rows_in * inverse
    weighted = cotangent * gain_in
    return inverse * (weighted - scaled * jnp.mean(weighted * scaled, axis=-1, keepdims=True))


def shards(
    x_in,
    out_grad,
    norm_one,
    w_query,
    w_key,
    w_value,
    output_gate_weight,
    mixer_input_weight,
    w_delta,
    w_bmat,
    w_cmat,
    delta_bias,
    decay_log,
    skip_gain,
    w_attn_out,
    mixer_output_weight,
    norm_two,
    w_gate,
    w_up,
    w_down,
):
    heads_count = lax.axis_size("heads")
    head_rank = lax.axis_index("heads")
    core = head_rank % 2
    block_rank = lax.axis_index("blk")
    rank = block_rank.astype(jnp.int32)[None]
    own_rows = x_in.shape[0]
    span_length = own_rows * heads_count
    half_span = span_length // 2
    span_start = block_rank * span_length
    query_width = w_query.shape[1]
    mixer_width = mixer_input_weight.shape[1]
    heads = mixer_width // MIXER_HEAD_SIZE
    state_size = w_bmat.shape[1]
    hidden_width = w_gate.shape[1]
    rows_of = w_query.shape[0]
    kv_index = head_rank * (query_width // HD) // (QH // KVH)
    kv_width = KVH * HD
    low = jnp.bfloat16
    ranks = chunk_ranks().astype(jnp.int32)
    turns = (head_rank ^ jnp.arange(heads_count)).astype(jnp.int32)

    gains = jnp.stack([norm_one, norm_two], axis=1)
    gains = jnp.pad(gains, ((0, 0), (heads, LANES - heads - 2)))
    shared = jnp.concatenate([w_key, w_value, w_bmat, w_cmat, gains], axis=1)
    delta_wide = jnp.pad(w_delta, ((0, 0), (0, LANES - heads)))
    in_names = ("z", "x", "query", "b", "c", "misc", "key", "value")
    in_widths = (mixer_width, mixer_width, query_width, state_size, state_size, LANES, HD, HD)
    in_width = sum(in_widths)
    starts = [sum(in_widths[:k]) for k in range(len(in_widths))]
    at = dict(zip(in_names, zip(starts, in_widths)))
    mix_at = {
        "ssm_out": (in_width, mixer_width),
        "attn_out": (in_width + mixer_width, query_width),
    }
    first_own = pack_first(
        turns,
        kv_index.astype(jnp.int32)[None],
        gather_small(shared),
        delta_wide,
        [output_gate_weight, mixer_input_weight, w_query, mixer_output_weight, w_attn_out],
        at | mix_at,
    )
    gain_part = first_own[:, at["misc"][0] + heads : at["misc"][0] + heads + 2]
    first_full = lax.all_gather(first_own, ("dp", "blk"), axis=0, tiled=True)
    in_full, mix_t = (first_full[:, :in_width], first_full[:, in_width:])
    x_float = x_in.astype(jnp.float32)
    zero = 0.0 * first_own[0, 0]
    x_span, _ = gather_rows(x_in + zero, joined=True)
    ffn_grad, _ = gather_rows(out_grad + zero, joined=True)
    ffn_own = pack((w_gate, w_up, w_down), (False, False, True), x_span)
    ffn_full = lax.all_gather(ffn_own, ("dp", "blk"), axis=0, tiled=True)
    mixed_width = query_width + mixer_width
    gate_full, up_full, down_t = split_columns(ffn_full, (hidden_width,) * 3)
    positions = (span_start + jnp.arange(span_length)).astype(jnp.float32)
    freqs = rope_base ** (-2.0 * jnp.arange(HD // 2, dtype=jnp.float32) / HD)
    angles = positions[:, None] * freqs[None, :]
    cosine, sine = (jnp.cos(angles), jnp.sin(angles))
    cosine = jnp.concatenate([cosine, cosine], axis=1)
    sine = jnp.concatenate([-sine, sine], axis=1)
    normed_ordered, queries, keys_values, gain_rows = enter(
        ranks, jnp.full((1,), heads, jnp.int32), x_span, first_full, at, cosine, sine, [corner(ffn_own), corner(ffn_grad)]
    )
    gain_one, gain_two = (gain_rows[0:1], gain_rows[1:2])
    mine = lax.dynamic_slice_in_dim(keys_values, core * half_span, half_span, 0)
    pieces = []
    for piece in from_earlier(mine):
        pieces += [piece, to_partner(piece)]
    gate_raw = simple_product(normed_ordered, in_full[:, :mixer_width])
    x_raw = simple_product(normed_ordered, in_full[:, mixer_width : 2 * mixer_width])
    state_raw = simple_product(normed_ordered, in_full[:, at["b"][0] : at["key"][0]])
    raw = {
        "z": (gate_raw, 0, mixer_width),
        "x": (x_raw, 0, mixer_width),
        "b": (state_raw, 0, state_size),
        "c": (state_raw, state_size, state_size),
        "misc": (state_raw, 2 * state_size, LANES),
    }

    pad_lanes = lambda vector: jnp.pad(vector, (0, LANES - heads))[None]
    bias, rate = (pad_lanes(delta_bias), pad_lanes(jnp.exp(decay_log)))
    skip = jnp.repeat(skip_gain, MIXER_HEAD_SIZE)[None]
    delta, cumulative, delta_row, cum_row, local_state, local_log = scan_first(raw, bias, rate)
    entry_states = from_earlier(pack_state(local_state, local_log))
    attended, attn_part, log_totals = attend(rank, queries, keys_values, pieces)
    scanned, gated, states = scan(
        raw, delta, cumulative, delta_row, cum_row, entry_states, skip, [corner(attn_part)]
    )
    mixers = reorder(ranks, [gated, attn_part])
    ffn_zero = 0.0 * ffn_full[0, 0].astype(jnp.float32)
    mixed = scatter_rows(lambda rows: dot_last(mixers[rows], mix_t), half_span, ffn_zero)
    middle = x_float + mixed
    middle_scaled = middle * inverse_rms(middle)
    normed_two, _ = gather_rows((middle_scaled * gain_two).astype(low))
    ffn_gate = simple_product(normed_two, gate_full)
    ffn_up = simple_product(normed_two, up_full)
    ffn_sig = jax.nn.sigmoid(ffn_gate)
    hidden = (ffn_gate * ffn_sig * ffn_up).astype(low)

    d_hidden = simple_product(ffn_grad, down_t)
    d_ffn_gate = (d_hidden * ffn_up * (ffn_sig * (1.0 + ffn_gate * (1.0 - ffn_sig)))).astype(low)
    d_ffn_up = (d_hidden * (ffn_gate * ffn_sig)).astype(low)
    d_normed_two = scatter_rows(
        lambda rows: dot_last(d_ffn_gate[rows], gate_full) + dot_last(d_ffn_up[rows], up_full),
        half_span,
    )
    d_middle = out_grad.astype(jnp.float32) + norm_back(middle, gain_two, d_normed_two)
    mix_grad, mix_partner = gather_rows(d_middle.astype(low))
    ffn_grads = weight_grads(
        [(normed_two, [d_ffn_gate, d_ffn_up]), (ffn_grad, [hidden])],
        3 * hidden_width,
        after=[corner(mix_partner)],
    )
    ffn_sums = weight_sum(ffn_grads).astype(jnp.float32)
    grad_gate, grad_up, grad_down_t = split_columns(ffn_sums, (hidden_width,) * 3)
    grad_two_part = jnp.sum(grad_gate * w_gate + grad_up * w_up, axis=1, keepdims=True)
    gain_own = gain_part.astype(jnp.float32)
    grad_two_part = grad_two_part / gain_own[:, 1:2]
    d_mixers = reorder(
        ranks, [simple_product(mix_grad, mix_t).astype(low)], inverse=True, after=[corner(ffn_grads)]
    )
    d_scanned, d_gate_z, d_entry = scan_back_first(d_mixers, raw, scanned, cumulative)
    d_entry = pack_state(d_entry, local_log)
    after_states = from_earlier(d_entry, -1)
    mix_width = mixed_width + mixer_width
    all_width = mixed_width + in_width
    mix_grads = weight_grads(
        [(mix_grad, [mixers]), (normed_ordered, [d_gate_z])], all_width, after=[corner(d_entry)]
    )
    d_query, d_own, d_far = attend_back(
        rank, queries, keys_values, pieces, attended, log_totals, d_mixers, cosine, sine, [corner(mix_grads), *map(corner, after_states)]
    )
    d_ssm_in, d_bmat, d_cmat, d_pre, sums = scan_back(
        raw,
        d_scanned,
        bias,
        rate,
        delta,
        cumulative,
        cum_row,
        states,
        after_states,
        skip,
        [corner(d_query)],
    )
    far_half = d_far.shape[0] // 2
    d_mine = lax.dynamic_slice_in_dim(d_own, core * half_span, half_span, 0)
    d_theirs = lax.dynamic_slice_in_dim(d_own, (1 - core) * half_span, half_span, 0)
    d_mine = d_mine + to_partner(d_theirs.astype(low)).astype(jnp.float32)
    d_far = d_far[:far_half].astype(jnp.float32) + to_partner(d_far[far_half:]).astype(jnp.float32)
    d_one, d_two, d_three = (
        d_far[k * half_span : (k + 1) * half_span] for k in range(d_far.shape[0] // half_span)
    )
    d_one = d_one + on_blocks(d_two.astype(low), -1).astype(jnp.float32)
    d_mine = d_mine + on_blocks(d_one.astype(low), -1).astype(jnp.float32)
    d_mine = d_mine + on_blocks(d_three.astype(low), -3).astype(jnp.float32)
    half_cos = lax.dynamic_slice_in_dim(cosine, core * half_span, half_span, 0)
    half_sin = lax.dynamic_slice_in_dim(sine, core * half_span, half_span, 0)
    d_key = d_mine[:, :HD]
    d_key = d_key * half_cos - jnp.roll(d_key, HD // 2, axis=1) * half_sin
    d_mine = jnp.concatenate([d_key, d_mine[:, HD:]], axis=1).astype(low)
    d_keys_values = lax.dynamic_update_slice_in_dim(
        jnp.zeros((span_length, 2 * HD), low), d_mine, core * half_span, 0
    )

    scan_rights = [d_ssm_in, d_bmat, d_cmat, d_pre]
    in_grads = weight_grads([(normed_ordered, scan_rights)], all_width, mix_width, mix_grads)
    late_rights = [d_keys_values, d_query]
    late_start = mix_width + sum(array.shape[1] for array in scan_rights)
    in_grads = weight_grads([(normed_ordered, late_rights)], all_width, late_start, in_grads)
    in_sums = weight_sum(in_grads)
    d_projected = reorder(
        ranks,
        [d_gate_z, d_ssm_in, d_query, d_bmat, d_cmat, d_pre, d_keys_values],
        after=[corner(in_grads)],
    )
    d_normed = scatter_rows(lambda rows: dot_last(d_projected[rows], in_full), half_span)
    input_grad = d_middle + norm_back(x_float, gain_one, d_normed)
    back_zero = 0.0 * d_query[0, 0].astype(jnp.float32)
    ffn_out = scatter_rows(
        lambda rows: dot_last(hidden[rows], down_t) + back_zero, half_span
    )
    activations = (middle + ffn_out).astype(low)
    sums_names = ("ssm_out", "attn_out", "z", "x", "b", "c", "misc", "key", "value", "query")
    sums_widths = [mixer_width, query_width] + [at[name][1] for name in sums_names[2:]]
    sums_starts = [sum(sums_widths[:k]) for k in range(len(sums_widths))]
    sums_at = dict(zip(sums_names, zip(sums_starts, sums_widths)))
    extra = jnp.concatenate([gain_own[:, 0:1], grad_two_part], axis=1)
    extra = jnp.pad(extra, ((0, 0), (0, LANES - 2)))
    grad_ssm_out, grad_attn_out, grad_gatez, grad_ssmx, grad_query, misc_sums, shared_parts = finish(
        turns,
        kv_index.astype(jnp.int32)[None],
        in_sums,
        first_own,
        extra,
        at,
        sums_at,
    )
    shared_sums = scatter_small(shared_parts)
    grad_key, grad_value, grad_bmat, grad_cmat, gain_sums = split_columns(
        shared_sums, (kv_width, kv_width, state_size, state_size, LANES)
    )
    small_sums = sum_blocks(sums)[:, :heads]
    return (
        activations,
        input_grad,
        gain_sums[:, 0],
        grad_query,
        grad_key,
        grad_value,
        grad_gatez,
        grad_ssmx,
        misc_sums[:, :heads],
        grad_bmat,
        grad_cmat,
        small_sums[0],
        small_sums[1],
        small_sums[2],
        grad_attn_out,
        grad_ssm_out,
        gain_sums[:, 1],
        grad_gate,
        grad_up,
        grad_down_t.T,
    )


def solution(mesh):
    placed = (
        P(("dp", "blk", "heads"), None),
        P(("dp", "blk", "heads"), None),
        P(("dp", "blk", "heads")),
        P(("dp", "blk"), "heads"),
        P(("dp", "blk", "heads"), None),
        P(("dp", "blk", "heads"), None),
        P(("dp", "blk"), "heads"),
        P(("dp", "blk"), "heads"),
        P(("dp", "blk"), "heads"),
        P(("dp", "blk", "heads"), None),
        P(("dp", "blk", "heads"), None),
        P("heads"),
        P("heads"),
        P("heads"),
        P("heads", ("dp", "blk")),
        P("heads", ("dp", "blk")),
        P(("dp", "blk", "heads")),
        P(("dp", "blk"), "heads"),
        P(("dp", "blk"), "heads"),
        P("heads", ("dp", "blk")),
    )
    return jax.shard_map(
        shards,
        mesh=mesh,
        in_specs=placed,
        out_specs=(
            P(("dp", "blk", "heads"), None),
            P(("dp", "blk", "heads"), None),
            P(("dp", "blk", "heads")),
            P(("dp", "blk"), "heads"),
            P(("dp", "blk", "heads"), None),
            P(("dp", "blk", "heads"), None),
            P(("dp", "blk"), "heads"),
            P(("dp", "blk"), "heads"),
            P(("dp", "blk"), "heads"),
            P(("dp", "blk", "heads"), None),
            P(("dp", "blk", "heads"), None),
            P("heads"),
            P("heads"),
            P("heads"),
            P("heads", ("dp", "blk")),
            P("heads", ("dp", "blk")),
            P(("dp", "blk", "heads")),
            P(("dp", "blk"), "heads"),
            P(("dp", "blk"), "heads"),
            P("heads", ("dp", "blk")),
        ),
        check_vma=False,
    )
```

```python
import functools

import jax
import jax.numpy as jnp
from jax import lax
from jax.experimental import pallas as pl
from jax.experimental.pallas import tpu as pltpu
from jax.sharding import PartitionSpec as P

QH = 8
KVH = 2
HD = 128
MIXER_HEAD_SIZE = 64
BLOCK = 256
LANES = 128
LOG2_E = 1.4426950408889634


HIGH_PRECISION = lax.Precision.HIGHEST
norm_eps = 1e-05
rope_base = 100000000000.0


def simple_product(left_side, right_side):
    return jnp.dot(left_side, right_side, preferred_element_type=jnp.float32)


def dot_last(left_side, right_side):
    return lax.dot_general(
        left_side, right_side, (((1,), (1,)), ((), ())), preferred_element_type=jnp.float32
    )


def dot_first(left_side, right_side):
    return lax.dot_general(
        left_side, right_side, (((0,), (0,)), ((), ())), preferred_element_type=jnp.float32
    )


def compiler_params(mebibytes=20):
    return pltpu.CompilerParams(vmem_limit_bytes=mebibytes * 1024 * 1024)


def small_cost():
    return pl.CostEstimate(flops=1000, bytes_accessed=1000, transcendentals=0)


def in_hbm(value):
    return pltpu.with_memory_space_constraint(value, pltpu.HBM)


def corner(value):
    return value[:16, :LANES]


def in_vmem(count):
    return [pl.BlockSpec(memory_space=pltpu.VMEM)] * count


def mul(left_side, right_side):
    return jnp.dot(left_side, right_side, preferred_element_type=jnp.float32)


def tile_scores(key_rows, query_rows, head_size):
    return dot_last(key_rows, query_rows) * (head_size**-0.5 * LOG2_E)


def causal(scores):
    key_at = lax.broadcasted_iota(jnp.int32, scores.shape, 0)
    query_at = lax.broadcasted_iota(jnp.int32, scores.shape, 1)
    return jnp.where(key_at <= query_at, scores, -1e30)


def enter_kernel(
    ranks_ref, heads_ref, x_ref, misc_ref, key_ref, value_ref, w_query_ref, cos_ref, sin_ref, *refs
):
    ordered_ref, query_ref, kv_ref, gains_ref = refs[-4:]
    head_size = query_ref.shape[1]

    @pl.when(pl.program_id(0) == 0)
    def _():
        lane = lax.broadcasted_iota(jnp.int32, misc_ref.shape, 1)
        for k in range(2):
            column = jnp.where(lane == heads_ref[0] + k, misc_ref[...].astype(jnp.float32), 0.0)
            gains_ref[k : k + 1, :] = jnp.sum(column.T, axis=0, keepdims=True)

    cosine, sine = (cos_ref[...], sin_ref[...])

    def turn(value):
        return (value * cosine + pltpu.roll(value, head_size // 2, 1) * sine).astype(jnp.bfloat16)

    rows = x_ref[...].astype(jnp.float32)
    normed = (rows * inverse_rms(rows) * gains_ref[0:1, :]).astype(jnp.bfloat16)
    ordered_ref[...] = normed
    kv_ref[:, :head_size] = turn(mul(normed, key_ref[...]))
    kv_ref[:, head_size:] = mul(normed, value_ref[...]).astype(jnp.bfloat16)
    query_ref[...] = turn(mul(normed, w_query_ref[...]))


def enter(ranks, heads, x_span, in_full, at, cosine, sine, after):
    count = ranks.shape[0]
    rows, width = x_span.shape
    head_size = cosine.shape[1]
    here = lambda columns: pl.BlockSpec((rows // count, columns), lambda k, r, h: (k, 0))
    there = lambda columns: pl.BlockSpec((rows // count, columns), lambda k, r, h: (r[k], 0))
    weight = lambda name: pl.BlockSpec(
        (width, at[name][1]), lambda k, r, h: (0, at[name][0] // at[name][1])
    )
    return pl.pallas_call(
        enter_kernel,
        grid_spec=pltpu.PrefetchScalarGridSpec(
            num_scalar_prefetch=2,
            grid=(count,),
            in_specs=[
                here(width),
                weight("misc"),
                weight("key"),
                weight("value"),
                weight("query"),
                there(head_size),
                there(head_size),
            ]
            + [pl.BlockSpec(memory_space=pl.ANY)] * len(after),
            out_specs=(
                there(width),
                there(head_size),
                there(2 * head_size),
                pl.BlockSpec((8, width), lambda k, r, h: (0, 0)),
            ),
        ),
        out_shape=(
            jax.ShapeDtypeStruct((rows, width), jnp.bfloat16),
            jax.ShapeDtypeStruct((rows, head_size), jnp.bfloat16),
            jax.ShapeDtypeStruct((rows, 2 * head_size), jnp.bfloat16),
            jax.ShapeDtypeStruct((8, width), jnp.float32),
        ),
        compiler_params=compiler_params(),
        cost_estimate=small_cost(),
        name="enter",
    )(ranks, heads, in_hbm(x_span), in_full, in_full, in_full, in_full, cosine, sine, *after)


def weight_grads_kernel(*refs, counts):
    out_ref = refs[-1]
    start, used = (0, len(counts))
    for k, count in enumerate(counts):
        left = refs[k][...].T
        for ref in refs[used : used + count]:
            out_ref[:, start : start + ref.shape[1]] = mul(left, ref[...]).astype(jnp.bfloat16)
            start += ref.shape[1]
        used += count


def weight_grads(groups, width, start=0, buffer=None, after=()):
    rights = [right for _, group in groups for right in group]
    columns = sum(right.shape[1] for right in rights)
    depth = rights[0].shape[0]
    rows = groups[0][0].shape[1]
    operands = [left for left, _ in groups] + rights
    count = len(operands)
    extra = list(after) if buffer is None else [buffer] + list(after)

    def call(*refs):
        weight_grads_kernel(
            *refs[:count],
            refs[-1],
            counts=tuple(len(group) for _, group in groups),
        )

    return pl.pallas_call(
        call,
        grid=(rows // BLOCK,),
        out_shape=pltpu.HBM((rows, width), jnp.bfloat16),
        in_specs=[pl.BlockSpec((depth, BLOCK), lambda k: (0, k)) for _ in groups]
        + [pl.BlockSpec(right.shape, lambda k: (0, 0)) for right in rights]
        + [pl.BlockSpec(memory_space=pl.ANY)] * len(extra),
        out_specs=pl.BlockSpec(
            (pl.Element(BLOCK), pl.Element(columns)), lambda k: (k * BLOCK, start)
        ),
        input_output_aliases={} if buffer is None else {count: 0},
        compiler_params=compiler_params(),
        cost_estimate=small_cost(),
        name="weight_grads",
    )(*operands, *extra)


def pack_kernel(*refs, turned):
    out_ref = refs[-1]
    start = 0
    for ref, turn in zip(refs, turned):
        piece = ref[...].T if turn else ref[...]
        out_ref[:, start : start + piece.shape[1]] = piece
        start += piece.shape[1]


def pack(pieces, turned, after=()):
    sizes = [piece.shape[::-1] if turn else piece.shape for piece, turn in zip(pieces, turned)]
    return pl.pallas_call(
        functools.partial(pack_kernel, turned=turned),
        out_shape=jax.ShapeDtypeStruct(
            (sizes[0][0], sum(size[1] for size in sizes)), jnp.bfloat16
        ),
        in_specs=in_vmem(len(pieces)) + [pl.BlockSpec(memory_space=pl.ANY)] * len(after),
        out_specs=pl.BlockSpec(memory_space=pltpu.VMEM),
        compiler_params=compiler_params(),
        cost_estimate=small_cost(),
        name="pack",
    )(*map(in_hbm, pieces), *after)


def join_kernel(*refs):
    out_ref = refs[-1]
    start = 0
    for ref in refs[:-1]:
        out_ref[start : start + ref.shape[0], :] = ref[...]
        start += ref.shape[0]


def join(pieces):
    rows = sum(piece.shape[0] for piece in pieces)
    return pl.pallas_call(
        join_kernel,
        out_shape=jax.ShapeDtypeStruct((rows, pieces[0].shape[1]), pieces[0].dtype),
        in_specs=in_vmem(len(pieces)),
        out_specs=pl.BlockSpec(memory_space=pltpu.VMEM),
        compiler_params=compiler_params(),
        cost_estimate=small_cost(),
        name="join",
    )(*pieces)


def pack_first_kernel(
    turns_ref, kv_ref, shared_ref, delta_ref, z_ref, x_ref, query_ref, ssm_ref, attn_ref, out_ref, *, at
):
    def put(name, value, rows=slice(None)):
        start, size = at[name]
        out_ref[rows, start : start + size] = value

    put("z", z_ref[...])
    put("x", x_ref[...])
    put("query", query_ref[...])
    put("ssm_out", ssm_ref[...].T)
    put("attn_out", attn_ref[...].T)
    count = turns_ref.shape[0]
    size = shared_ref.shape[0] // count
    first = kv_ref[0] == 0
    for k in range(count):
        rows = pl.ds(pl.multiple_of(turns_ref[k] * size, size), size)
        chunk = shared_ref[k * size : (k + 1) * size, :]
        pieces, start = [], 0
        for width in (HD, HD, HD, HD, at["b"][1], at["c"][1], LANES):
            pieces.append(chunk[:, start : start + width])
            start += width
        put("key", jnp.where(first, pieces[0], pieces[1]), rows)
        put("value", jnp.where(first, pieces[2], pieces[3]), rows)
        put("b", pieces[4], rows)
        put("c", pieces[5], rows)
        put("misc", pieces[6] + delta_ref[rows, :], rows)


def pack_first(turns, kv_index, shared, delta, weights, at):
    rows = shared.shape[0]
    return pl.pallas_call(
        functools.partial(pack_first_kernel, at=at),
        out_shape=jax.ShapeDtypeStruct(
            (rows, max(start + size for start, size in at.values())), jnp.bfloat16
        ),
        in_specs=[pl.BlockSpec(memory_space=pltpu.SMEM)] * 2 + in_vmem(2 + len(weights)),
        out_specs=pl.BlockSpec(memory_space=pltpu.VMEM),
        compiler_params=compiler_params(50),
        cost_estimate=small_cost(),
        name="pack_first",
    )(turns, kv_index, shared, delta, *map(in_hbm, weights))


def finish_kernel(
    ranks_ref,
    kv_ref,
    sums_ref,
    weight_ref,
    extra_ref,
    ssm_out_ref,
    attn_out_ref,
    gate_ref,
    ssm_ref,
    query_ref,
    misc_ref,
    shared_ref,
    whole_ref,
    *,
    at,
    sums_at,
):
    def of(name):
        start, size = sums_at[name]
        return sums_ref[:, start : start + size].astype(jnp.float32)

    ssm_out_ref[...] = of("ssm_out").T
    attn_out_ref[...] = of("attn_out").T
    gate_ref[...] = of("z")
    ssm_ref[...] = of("x")
    query_ref[...] = of("query")
    misc_ref[...] = of("misc")
    total = 0.0
    for name, (start, size) in at.items():
        product = of(name) * weight_ref[:, start : start + size].astype(jnp.float32)
        total += jnp.sum(product, axis=1, keepdims=True)
    total = total / extra_ref[:, 0:1]
    lane = lax.broadcasted_iota(jnp.int32, misc_ref.shape, 1)
    gains = jnp.where(lane == 0, total, jnp.where(lane == 1, extra_ref[:, 1:2], 0.0))
    zero = jnp.zeros_like(gains)
    first = kv_ref[0] == 0
    key, value = (of("key"), of("value"))
    pieces = (
        jnp.where(first, key, zero),
        jnp.where(first, zero, key),
        jnp.where(first, value, zero),
        jnp.where(first, zero, value),
        of("b"),
        of("c"),
        gains,
    )
    start = 0
    for piece in pieces:
        whole_ref[:, start : start + piece.shape[1]] = piece
        start += piece.shape[1]
    count = ranks_ref.shape[0]
    size = shared_ref.shape[0] // count
    for k in range(count):
        rows = pl.ds(pl.multiple_of(ranks_ref[k] * size, size), size)
        shared_ref[k * size : (k + 1) * size, :] = whole_ref[rows, :].astype(jnp.bfloat16)


def finish(ranks, kv_index, sums, weights, extra, at, sums_at):
    rows = weights.shape[0]
    shape = lambda *sizes: jax.ShapeDtypeStruct(sizes, jnp.float32)
    width = lambda name: sums_at[name][1]
    shared = 2 * (width("key") + width("value")) + width("b") + width("c") + LANES
    return pl.pallas_call(
        functools.partial(finish_kernel, at=at, sums_at=sums_at),
        out_shape=(
            shape(width("ssm_out"), rows),
            shape(width("attn_out"), rows),
            shape(rows, width("z")),
            shape(rows, width("x")),
            shape(rows, width("query")),
            shape(rows, width("misc")),
            jax.ShapeDtypeStruct((rows, shared), jnp.bfloat16),
        ),
        in_specs=[pl.BlockSpec(memory_space=pltpu.SMEM)] * 2 + in_vmem(3),
        out_specs=tuple(in_vmem(7)),
        scratch_shapes=[pltpu.VMEM((rows, shared), jnp.float32)],
        compiler_params=compiler_params(),
        name="finish",
    )(ranks, kv_index, sums, weights, extra)


def attend_kernel(rank_ref, query_ref, own_ref, *refs):
    pieces, (out_ref, low_ref, log_ref) = (refs[:-3], refs[-3:])
    span_length, head_size = query_ref.shape
    tile = own_ref.shape[0] // 2
    for block in range(span_length // tile):
        here = slice(block * tile, (block + 1) * tile)
        query_rows = query_ref[here, :]

        def step(kv_rows, carried, masked=False):
            top, total, summed = carried
            scores = tile_scores(kv_rows[:, :head_size], query_rows, head_size)
            if masked:
                scores = causal(scores)
            new_top = jnp.maximum(top, jnp.max(scores, axis=0, keepdims=True))
            probs = jnp.exp2(scores - new_top)
            scale = jnp.exp2(top - new_top)
            total = total * scale + jnp.sum(probs, axis=0, keepdims=True)
            summed = summed * scale + dot_first(kv_rows[:, head_size:], probs.astype(jnp.bfloat16))
            return (new_top, total, summed)

        carried = (
            jnp.full((1, tile), -1e30, jnp.float32),
            jnp.zeros((1, tile), jnp.float32),
            jnp.zeros((head_size, tile), jnp.float32),
        )
        carried = step(own_ref[here, :], carried, True)
        for earlier in range(block):
            carried = step(own_ref[earlier * tile : (earlier + 1) * tile, :], carried)
        for distance in range(1, 1 + len(pieces) // 2):
            pair = pieces[2 * distance - 2 : 2 * distance]

            def both(_, carried, pair=pair):
                return step(pair[1][...], step(pair[0][...], carried))

            valid = (rank_ref[0] >= distance).astype(jnp.int32)
            carried = lax.fori_loop(0, valid, both, carried)
        top, total, summed = carried
        result = summed / total
        out_ref[:, here] = result
        low_ref[here, :] = result.T.astype(jnp.bfloat16)
        log_ref[:, here] = top + jnp.log2(total)


def attend(rank, queries, own, pieces):
    span_length, head_size = queries.shape
    return pl.pallas_call(
        attend_kernel,
        out_shape=(
            jax.ShapeDtypeStruct((head_size, span_length), jnp.float32),
            jax.ShapeDtypeStruct((span_length, head_size), jnp.bfloat16),
            jax.ShapeDtypeStruct((1, span_length), jnp.float32),
        ),
        in_specs=[pl.BlockSpec(memory_space=pltpu.SMEM)] + in_vmem(2 + len(pieces)),
        out_specs=tuple(in_vmem(3)),
        compiler_params=compiler_params(),
        cost_estimate=small_cost(),
        name="attend",
    )(rank, queries, own, *pieces)


def attend_back_kernel(rank_ref, query_ref, own_ref, *refs):
    pieces, refs = (refs[:-13], refs[-13:])
    out_ref, log_ref, grad_ref, cos_ref, sin_ref, *_, d_query_ref, d_own_ref, d_far_ref, sums_ref = refs
    span_length, head_size = query_ref.shape
    tile = own_ref.shape[0] // 2
    score_scale = head_size**-0.5
    sums_ref[...] = jnp.zeros_like(sums_ref)
    for block in range(span_length // tile):
        here = slice(block * tile, (block + 1) * tile)
        query_rows = query_ref[here, :]
        grad_rows = grad_ref[here, grad_ref.shape[1] - head_size :]
        log_total = log_ref[:, here]
        delta_row = jnp.sum(
            grad_rows.astype(jnp.float32).T * out_ref[:, here], axis=0, keepdims=True
        )

        def step(kv_ref, start, at, d_query, masked=False):
            key_rows = kv_ref[start : start + tile, :head_size]
            scores = tile_scores(key_rows, query_rows, head_size)
            if masked:
                scores = causal(scores)
            probs = jnp.exp2(scores - log_total)
            d_probs = dot_last(kv_ref[start : start + tile, head_size:], grad_rows)
            d_scores = (probs * (d_probs - delta_row)).astype(jnp.bfloat16)
            rows = slice(at * tile, (at + 1) * tile)
            sums_ref[rows, head_size:] += mul(probs.astype(jnp.bfloat16), grad_rows)
            sums_ref[rows, :head_size] += mul(d_scores, query_rows)
            return d_query + dot_first(key_rows, d_scores)

        d_query = jnp.zeros((head_size, tile), jnp.float32)
        d_query = step(own_ref, block * tile, block, d_query, True)
        for earlier in range(block):
            d_query = step(own_ref, earlier * tile, earlier, d_query)
        for distance in range(1, 1 + len(pieces) // 2):

            def both(_, d_query, distance=distance):
                for k in (2 * distance - 2, 2 * distance - 1):
                    d_query = step(pieces[k], 0, 2 + k, d_query)
                return d_query

            valid = (rank_ref[0] >= distance).astype(jnp.int32)
            d_query = lax.fori_loop(0, valid, both, d_query)
        turned = d_query.T * score_scale
        d_query_ref[here, :] = (
            turned * cos_ref[here, :] - pltpu.roll(turned, head_size // 2, 1) * sin_ref[here, :]
        ).astype(jnp.bfloat16)
    lane = lax.broadcasted_iota(jnp.int32, (tile, 2 * head_size), 1)
    scale = jnp.where(lane < head_size, score_scale, 1.0)
    for at in range(2):
        rows = slice(at * tile, (at + 1) * tile)
        d_own_ref[rows, :] = sums_ref[rows, :] * scale
    for k in range(len(pieces)):
        rows = slice((2 + k) * tile, (3 + k) * tile)
        into = (k % 2) * (len(pieces) // 2) + k // 2
        d_far_ref[into * tile : (into + 1) * tile, :] = (sums_ref[rows, :] * scale).astype(
            jnp.bfloat16
        )


def attend_back(rank, queries, own, pieces, attended, log_totals, d_attn, cosine, sine, after):
    tile = own.shape[0] // 2
    return pl.pallas_call(
        attend_back_kernel,
        out_shape=(
            jax.ShapeDtypeStruct(queries.shape, jnp.bfloat16),
            jax.ShapeDtypeStruct(own.shape, jnp.float32),
            jax.ShapeDtypeStruct((len(pieces) * tile, own.shape[1]), jnp.bfloat16),
        ),
        in_specs=[pl.BlockSpec(memory_space=pltpu.SMEM)]
        + in_vmem(7 + len(pieces))
        + [pl.BlockSpec(memory_space=pl.ANY)] * len(after),
        out_specs=tuple(in_vmem(3)),
        scratch_shapes=[pltpu.VMEM(((2 + len(pieces)) * tile, own.shape[1]), jnp.float32)],
        compiler_params=compiler_params(),
        cost_estimate=small_cost(),
        name="attend_back",
    )(rank, queries, own, *pieces, attended, log_totals, d_attn, cosine, sine, *after)


def reorder_kernel(ranks_ref, *refs, count):
    out_ref = refs[-1]
    start = 0
    for ref in refs[:count]:
        out_ref[:, start : start + ref.shape[1]] = ref[...].astype(out_ref.dtype)
        start += ref.shape[1]


def reorder(ranks, pieces, inverse=False, after=()):
    count = ranks.shape[0]
    rows = pieces[0].shape[0] // count
    width = sum(piece.shape[1] for piece in pieces)
    there = lambda k, ranks: (ranks[k], 0)
    here = lambda k, ranks: (k, 0)
    return pl.pallas_call(
        functools.partial(reorder_kernel, count=len(pieces)),
        grid_spec=pltpu.PrefetchScalarGridSpec(
            num_scalar_prefetch=1,
            grid=(count,),
            in_specs=[
                pl.BlockSpec((rows, piece.shape[1]), here if inverse else there)
                for piece in pieces
            ]
            + [pl.BlockSpec(memory_space=pl.ANY)] * len(after),
            out_specs=pl.BlockSpec((rows, width), there if inverse else here),
        ),
        out_shape=jax.ShapeDtypeStruct((count * rows, width), jnp.bfloat16),
        compiler_params=compiler_params(),
        cost_estimate=small_cost(),
        name="reorder",
    )(ranks, *pieces, *after)


def lower_ones(size, dtype=jnp.float32):
    row = lax.broadcasted_iota(jnp.int32, (size, size), 0)
    column = lax.broadcasted_iota(jnp.int32, (size, size), 1)
    return (row >= column).astype(dtype)


def precise(left_side, right_side):
    return jnp.dot(
        left_side, right_side, precision=HIGH_PRECISION, preferred_element_type=jnp.float32
    )


def spread_heads(columns, head_size, width):
    lane = lax.broadcasted_iota(jnp.int32, (columns.shape[0], 2 * head_size), 1)
    pairs = [
        jnp.where(lane < head_size, columns[:, k : k + 1], columns[:, k + 1 : k + 2])
        for k in range(0, width // head_size, 2)
    ]
    return jnp.concatenate(pairs, axis=1)


def head_ones(width, head_size, lanes, dtype):
    at = lax.broadcasted_iota(jnp.int32, (width, lanes), 0)
    lane = lax.broadcasted_iota(jnp.int32, (width, lanes), 1)
    low = lane * head_size
    return ((at >= low) & (at < low + head_size)).astype(dtype)


def scan_first_kernel(
    pre_ref, bias_ref, rate_ref, x_ref, b_ref, delta_ref, cum_ref, delta_row_ref, cum_row_ref, state_ref, log_ref
):
    @pl.when(pl.program_id(0) == 0)
    def _():
        state_ref[...] = jnp.zeros_like(state_ref)
        log_ref[...] = jnp.zeros_like(log_ref)

    delta = jax.nn.softplus(pre_ref[...] + bias_ref[...])
    log_step = -delta * rate_ref[...]
    cumulative = precise(lower_ones(log_step.shape[0]), log_step)
    delta_ref[...] = delta
    cum_ref[...] = cumulative
    delta_row_ref[...] = delta.T[:8]
    cum_row_ref[...] = cumulative.T[:8]
    ending = cumulative[-1:, :]
    weight = jnp.exp(ending - cumulative + log_ref[...]) * delta
    width = x_ref.shape[1]
    x_low = x_ref[...].astype(jnp.bfloat16).astype(jnp.float32)
    weighted = (x_low * spread_heads(weight, MIXER_HEAD_SIZE, width)).astype(jnp.bfloat16)
    state_ref[...] += dot_first(b_ref[...].astype(jnp.bfloat16), weighted)
    log_ref[...] += ending


def part(projected, start, width, order=lambda c: c):
    at = start // width
    return (projected, pl.BlockSpec((BLOCK, width), lambda c: (order(c), at)))


def run_scan(
    kernel, chunks, operands, out_shape, out_specs, name, scratch=(), after=(), mebibytes=20
):
    count = len(operands)
    operands = operands + [(array, pl.BlockSpec(memory_space=pl.ANY)) for array in after]

    def call(*refs):
        kernel(*refs[:count], *refs[count + len(after) :])

    return pl.pallas_call(
        call,
        grid=(chunks,),
        out_shape=out_shape,
        in_specs=[spec for _, spec in operands],
        out_specs=out_specs,
        scratch_shapes=list(scratch),
        compiler_params=compiler_params(mebibytes),
        cost_estimate=small_cost(),
        name=name,
    )(*[array for array, _ in operands])


def whole(array):
    return (array, pl.BlockSpec(array.shape, lambda c: (0,) * array.ndim))


def scan_first(at, bias, rate):
    rows, lanes = (at["x"][0].shape[0], bias.shape[1])
    chunks = rows // BLOCK
    back = lambda c: chunks - 1 - c
    width, state_size = (at["x"][2], at["b"][2])
    by_chunk = pl.BlockSpec((BLOCK, lanes), lambda c: (back(c), 0))
    across = pl.BlockSpec((8, BLOCK), lambda c: (0, back(c)))
    shape = lambda *sizes: jax.ShapeDtypeStruct(sizes, jnp.float32)
    return run_scan(
        scan_first_kernel,
        chunks,
        [
            part(*at["misc"], back),
            whole(bias),
            whole(rate),
            part(*at["x"], back),
            part(*at["b"], back),
        ],
        (
            shape(rows, lanes),
            shape(rows, lanes),
            shape(8, rows),
            shape(8, rows),
            shape(state_size, width),
            shape(1, lanes),
        ),
        (
            by_chunk,
            by_chunk,
            across,
            across,
            pl.BlockSpec((state_size, width), lambda c: (0, 0)),
            pl.BlockSpec((1, lanes), lambda c: (0, 0)),
        ),
        "scan_first",
    )


def chained(refs, width):
    state = jnp.zeros((refs[0].shape[0] - 16, width), jnp.float32)
    for ref in reversed(refs):
        logs = ref[-16:, :LANES].astype(jnp.float32)
        decay = jnp.exp(jnp.sum(logs[:3], axis=0, keepdims=True))
        state = ref[:-16].astype(jnp.float32) + spread_heads(decay, MIXER_HEAD_SIZE, width) * state
    return state


def scan_kernel(
    x_ref,
    z_ref,
    b_ref,
    c_ref,
    delta_ref,
    cum_ref,
    delta_row_ref,
    cum_row_ref,
    near_ref,
    next_ref,
    far_ref,
    skip_ref,
    scanned_ref,
    gated_ref,
    states_ref,
    state_ref,
):
    @pl.when(pl.program_id(0) == 0)
    def _():
        state_ref[...] = chained((near_ref, next_ref, far_ref), x_ref.shape[1])

    head_size = MIXER_HEAD_SIZE
    pair = 2 * head_size
    size, width = x_ref.shape
    state = state_ref[...]
    states_ref[0] = state
    delta, cumulative = (delta_ref[...], cum_ref[...])
    delta_row, cum_row = (delta_row_ref[...], cum_row_ref[...])
    bmat, cmat = (b_ref[...].astype(jnp.bfloat16), c_ref[...].astype(jnp.bfloat16))
    x_all = x_ref[...].astype(jnp.bfloat16)
    inner = dot_last(cmat, bmat)
    row = lax.broadcasted_iota(jnp.int32, (size, size), 0)
    column = lax.broadcasted_iota(jnp.int32, (size, size), 1)
    allowed = row >= column
    lane = lax.broadcasted_iota(jnp.int32, (size, pair), 1)
    from_state = mul(cmat, state.astype(jnp.bfloat16))
    spread = spread_heads(jnp.exp(cumulative), head_size, width)
    for first in range(0, width // head_size, 2):
        here = slice(first * head_size, first * head_size + pair)
        x_pair = x_all[:, here]
        total = from_state[:, here] * spread[:, here]
        total += skip_ref[:, here] * x_pair.astype(jnp.float32)
        for head in (first, first + 1):
            gap = cumulative[:, head : head + 1] - cum_row[head : head + 1, :]
            decay = jnp.exp(jnp.where(allowed, gap, -1e30))
            mixing = inner * decay * delta_row[head : head + 1, :]
            x_head = jnp.where((lane >= head_size) == (head > first), x_pair, 0.0)
            total += mul(mixing.astype(jnp.bfloat16), x_head.astype(jnp.bfloat16))
        scanned_ref[:, here] = total
        gate = z_ref[:, here]
        gated_ref[:, here] = (total * (gate * jax.nn.sigmoid(gate))).astype(jnp.bfloat16)
    ending = cumulative[-1:, :]
    weight = spread_heads(jnp.exp(ending - cumulative) * delta, head_size, width)
    weighted = (x_all.astype(jnp.float32) * weight).astype(jnp.bfloat16)
    state_ref[...] = state * spread[-1:, :] + dot_first(bmat, weighted)


def scan(at, delta, cumulative, delta_row, cum_row, entry, skip, after):
    rows = delta.shape[0]
    state_size, width = (at["b"][2], at["x"][2])
    chunks = rows // BLOCK
    by_chunk = pl.BlockSpec((BLOCK, width), lambda c: (c, 0))
    lanes = delta.shape[1]
    across = pl.BlockSpec((8, BLOCK), lambda c: (0, c))
    return run_scan(
        scan_kernel,
        chunks,
        [
            part(*at["x"]),
            part(*at["z"]),
            part(*at["b"]),
            part(*at["c"]),
            part(delta, 0, lanes),
            part(cumulative, 0, lanes),
            (delta_row, across),
            (cum_row, across),
            *[whole(packed) for packed in entry],
            whole(skip),
        ],
        (
            jax.ShapeDtypeStruct((rows, width), jnp.float32),
            jax.ShapeDtypeStruct((rows, width), jnp.bfloat16),
            jax.ShapeDtypeStruct((chunks, state_size, width), jnp.float32),
        ),
        (by_chunk, by_chunk, pl.BlockSpec((1, state_size, width), lambda c: (c, 0, 0))),
        "scan",
        [pltpu.VMEM((state_size, width), jnp.float32)],
        after,
    )


def scan_back_first_kernel(
    grad_ref, z_ref, scanned_ref, c_ref, cum_ref, d_scanned_ref, d_gate_ref, state_ref, log_ref
):
    @pl.when(pl.program_id(0) == 0)
    def _():
        state_ref[...] = jnp.zeros_like(state_ref)
        log_ref[...] = jnp.zeros_like(log_ref)

    gate = z_ref[...]
    chance = jax.nn.sigmoid(gate)
    grad = grad_ref[:, : z_ref.shape[1]].astype(jnp.float32)
    d_scanned = grad * (gate * chance)
    d_scanned_ref[...] = d_scanned
    d_gate_ref[...] = (
        grad * scanned_ref[...] * (chance * (1.0 + gate * (1.0 - chance)))
    ).astype(jnp.bfloat16)
    cumulative = cum_ref[...]
    decay = spread_heads(jnp.exp(cumulative + log_ref[...]), MIXER_HEAD_SIZE, z_ref.shape[1])
    state_ref[...] += dot_first(
        c_ref[...].astype(jnp.bfloat16), (d_scanned * decay).astype(jnp.bfloat16)
    )
    log_ref[...] += cumulative[-1:, :]


def scan_back_first(grads, at, scanned, cumulative):
    rows, width = scanned.shape
    state_size, lanes = (at["c"][2], cumulative.shape[1])
    by_chunk = pl.BlockSpec((BLOCK, width), lambda c: (c, 0))
    return run_scan(
        scan_back_first_kernel,
        rows // BLOCK,
        [
            part(grads, 0, grads.shape[1]),
            part(*at["z"]),
            part(scanned, 0, width),
            part(*at["c"]),
            part(cumulative, 0, lanes),
        ],
        (
            jax.ShapeDtypeStruct((rows, width), jnp.float32),
            jax.ShapeDtypeStruct((rows, width), jnp.bfloat16),
            jax.ShapeDtypeStruct((state_size, width), jnp.float32),
        ),
        (by_chunk, by_chunk, pl.BlockSpec((state_size, width), lambda c: (0, 0))),
        "scan_back_first",
        [pltpu.VMEM((1, lanes), jnp.float32)],
    )


def scan_back_kernel(
    x_ref,
    grad_ref,
    b_ref,
    c_ref,
    pre_ref,
    bias_ref,
    rate_ref,
    delta_ref,
    cum_ref,
    cum_row_ref,
    states_ref,
    near_ref,
    next_ref,
    far_ref,
    skip_ref,
    d_x_ref,
    d_b_ref,
    d_c_ref,
    d_pre_ref,
    sums_ref,
    state_ref,
):
    @pl.when(pl.program_id(0) == 0)
    def _():
        state_ref[...] = chained((near_ref, next_ref, far_ref), x_ref.shape[1])
        sums_ref[...] = jnp.zeros_like(sums_ref)

    head_size = MIXER_HEAD_SIZE
    pair = 2 * head_size
    size, width = x_ref.shape
    lanes = delta_ref.shape[1]
    low = jnp.bfloat16
    delta, cumulative, cum_row = (delta_ref[...], cum_ref[...], cum_row_ref[...])
    bmat, cmat = (b_ref[...].astype(low), c_ref[...].astype(low))
    x_all = x_ref[...].astype(low)
    x_single = x_all.astype(jnp.float32)
    grad = grad_ref[...]
    grad_low = grad.astype(low)
    state = states_ref[0]
    state_low = state.astype(low)
    after = state_ref[...]
    after_low = after.astype(low)
    ending = cumulative[-1:, :]
    row = lax.broadcasted_iota(jnp.int32, (size, size), 0)
    column = lax.broadcasted_iota(jnp.int32, (size, size), 1)
    later = column >= row
    before = (row > column).astype(low)
    onward = later.astype(low)
    lane = lax.broadcasted_iota(jnp.int32, (size, pair), 1)
    head_lane = lax.broadcasted_iota(jnp.int32, (size, lanes), 1)
    sum_heads = head_ones(width, head_size, lanes, low)

    inner = dot_last(bmat, cmat)
    from_after = mul(bmat, after_low)
    weight = jnp.exp(ending - cumulative)
    spread_weight = spread_heads(weight * delta, head_size, width)
    spread = spread_heads(jnp.exp(cumulative), head_size, width)
    to_end = mul((x_single * from_after).astype(low), sum_heads)
    through = jnp.exp(cumulative) * mul((grad * mul(cmat, state_low)).astype(low), sum_heads)
    carried = jnp.sum(state * after, axis=0, keepdims=True) * spread[-1:, :]
    carried = precise(carried, sum_heads.astype(jnp.float32))
    d_delta = weight * to_end
    d_log = (
        mul(onward, through.astype(low)) + mul(before, (d_delta * delta).astype(low)) + carried
    )

    d_inner = jnp.zeros((size, size), jnp.float32)
    for first in range(0, width // head_size, 2):
        here = slice(first * head_size, first * head_size + pair)
        x_pair, grad_pair = (x_all[:, here], grad_low[:, here])
        d_x = from_after[:, here] * spread_weight[:, here] + skip_ref[:, here] * grad[:, here]
        for head in (first, first + 1):
            mine = (lane >= head_size) == (head > first)
            gap = cum_row[head : head + 1, :] - cumulative[:, head : head + 1]
            decay = jnp.exp(jnp.where(later, gap, -1e30))
            delta_column = delta[:, head : head + 1]
            d_mixing = dot_last(jnp.where(mine, x_pair, 0.0).astype(low), grad_pair) * decay
            d_inner += d_mixing * delta_column
            flow = d_mixing * inner
            mixing = inner * decay * delta_column
            d_x += mul(mixing.astype(low), jnp.where(mine, grad_pair, 0.0).astype(low))
            d_delta_head = jnp.sum(flow, axis=1, keepdims=True)
            passing = mul(before, (flow * delta_column).astype(low))
            d_log_head = jnp.sum(jnp.where(later, passing, 0.0), axis=1, keepdims=True)
            d_delta += jnp.where(head_lane == head, d_delta_head, 0.0)
            d_log += jnp.where(head_lane == head, d_log_head, 0.0)
        d_x_ref[:, here] = d_x.astype(low)

    d_inner_low = d_inner.astype(low)
    scaled_grad = (grad * spread).astype(low)
    weighted = (x_single * spread_weight).astype(low)
    d_b_ref[...] = (mul(d_inner_low, cmat) + dot_last(weighted, after_low)).astype(low)
    d_c_ref[...] = (dot_first(d_inner_low, bmat) + dot_last(scaled_grad, state_low)).astype(low)
    state_ref[...] = after * spread[-1:, :] + dot_first(cmat, scaled_grad)
    rate = rate_ref[...]
    d_pre = (d_delta - d_log * rate) * jax.nn.sigmoid(pre_ref[...] + bias_ref[...])
    d_pre = jnp.where(head_lane < width // head_size, d_pre, 0.0)
    d_pre_ref[...] = d_pre.astype(low)
    skip_sum = precise(
        jnp.sum(grad * x_single, axis=0, keepdims=True), sum_heads.astype(jnp.float32)
    )
    sums_ref[0:1, :] += jnp.sum(d_pre, axis=0, keepdims=True)
    sums_ref[1:2, :] += jnp.sum(d_log * (-delta * rate), axis=0, keepdims=True)
    sums_ref[2:3, :] += skip_sum


def scan_back(
    at, d_scanned, bias, rate, delta, cumulative, cum_row, states, entry, skip, after
):
    rows, width = d_scanned.shape
    state_size, lanes = (at["b"][2], delta.shape[1])
    chunks = rows // BLOCK
    back = lambda c: chunks - 1 - c
    by_chunk = lambda columns: pl.BlockSpec((BLOCK, columns), lambda c: (back(c), 0))
    shape = lambda columns: jax.ShapeDtypeStruct((rows, columns), jnp.bfloat16)
    return run_scan(
        scan_back_kernel,
        chunks,
        [
            part(in_hbm(at["x"][0]), *at["x"][1:], back),
            part(in_hbm(d_scanned), 0, width, back),
            part(in_hbm(at["b"][0]), *at["b"][1:], back),
            part(in_hbm(at["c"][0]), *at["c"][1:], back),
            part(in_hbm(at["misc"][0]), *at["misc"][1:], back),
            whole(bias),
            whole(rate),
            part(in_hbm(delta), 0, lanes, back),
            part(in_hbm(cumulative), 0, lanes, back),
            (in_hbm(cum_row), pl.BlockSpec((8, BLOCK), lambda c: (0, back(c)))),
            (in_hbm(states), pl.BlockSpec((1, state_size, width), lambda c: (back(c), 0, 0))),
            *[whole(in_hbm(packed)) for packed in entry],
            whole(skip),
        ],
        (
            shape(width),
            shape(state_size),
            shape(state_size),
            shape(lanes),
            jax.ShapeDtypeStruct((8, lanes), jnp.float32),
        ),
        (
            by_chunk(width),
            by_chunk(state_size),
            by_chunk(state_size),
            by_chunk(lanes),
            pl.BlockSpec((8, lanes), lambda c: (0, 0)),
        ),
        "scan_back",
        [pltpu.VMEM((state_size, width), jnp.float32)],
        after,
        44,
    )


def on_heads(value, move):
    devices = lax.axis_size("heads")
    pairs = []
    for at in range(devices):
        z, core = move(at // 2, at % 2)
        pairs.append((at, 2 * (z % (devices // 2)) + core))
    return lax.ppermute(value, "heads", pairs)


def to_partner(value):
    return on_heads(value, lambda z, core: (z, 1 - core))


def along(value):
    return on_heads(value, lambda z, core: (z + 1 - 2 * core, core))


def against(value):
    return on_heads(value, lambda z, core: (z - 1 + 2 * core, core))


def chunk_ranks():
    devices = lax.axis_size("heads")
    z, core = (lax.axis_index("heads") // 2, lax.axis_index("heads") % 2)
    step, other = (1 - 2 * core, 1 - core)
    owners = (
        (z, core),
        (z + 2, core),
        (z - step, core),
        (z - step, other),
        (z, other),
        (z + 2, other),
        (z + step, other),
        (z + step, core),
    )
    return jnp.stack([2 * ((at + devices) % (devices // 2)) + side for at, side in owners])


def along_other(value):
    return on_heads(value, lambda z, core: (z - 1 + 2 * core, 1 - core))


def against_other(value):
    return on_heads(value, lambda z, core: (z - 1 + 2 * core, 1 - core))


def gather_rows(own, joined=False):
    near = along(own)
    near_other = along_other(own)
    partner = to_partner(own)
    far = along(near)
    mine = (own, far, near, near_other)
    theirs = (partner, to_partner(far), to_partner(near), to_partner(near_other))
    rows = join(mine + theirs) if joined else jnp.concatenate(mine + theirs, axis=0)
    return rows, partner


def scatter_rows(product, half, late=None):
    chunk = half // 4
    got = to_partner(product(slice(half, 2 * half)).astype(jnp.bfloat16))
    kept = lax.optimization_barrier(product(slice(0, half)))

    summed = kept + got.astype(jnp.float32)
    low = summed[chunk:].astype(jnp.bfloat16)
    far = against(low[:chunk])
    near_other = against_other(low[2 * chunk :])
    near = low[chunk : 2 * chunk].astype(jnp.float32) + far.astype(jnp.float32)
    near = against(near.astype(jnp.bfloat16))
    total = summed[:chunk] + near.astype(jnp.float32) + near_other.astype(jnp.float32)
    return total if late is None else total + late


def across(value, bit):
    devices = lax.axis_size("heads")
    return lax.ppermute(value, "heads", [(at, at ^ bit) for at in range(devices)])


def gather_small(value):
    for bit in (1, 2, 4):
        value = jnp.concatenate([value, across(value, bit)], axis=0)
    return value


def scatter_small(value):
    for bit in (4, 2, 1):
        half = value.shape[0] // 2
        got = across(value[half:].astype(jnp.bfloat16), bit)
        value = value[:half].astype(jnp.float32) + got.astype(jnp.float32)
    return value


def on_blocks(value, step):
    devices = lax.axis_size("blk")
    pairs = [(at, at + step) for at in range(devices) if 0 <= at + step < devices]
    return lax.ppermute(value, "blk", pairs)


def from_earlier(value, step=1):
    return tuple(on_blocks(value, distance * step) for distance in (1, 2, 3))


def pack_state(state, log_total):
    high = log_total.astype(jnp.bfloat16)
    rest = log_total - high.astype(jnp.float32)
    middle = rest.astype(jnp.bfloat16)
    low = (rest - middle.astype(jnp.float32)).astype(jnp.bfloat16)
    logs = jnp.concatenate([high, middle, low], axis=0)
    logs = jnp.pad(logs, ((0, 16 - logs.shape[0]), (0, state.shape[1] - logs.shape[1])))
    return jnp.concatenate([state.astype(jnp.bfloat16), logs], axis=0)


def sum_blocks(value):
    for axis in ("dp", "blk"):
        for bit in (1, 2):
            value = value + lax.ppermute(
                value, axis, [(at, at ^ bit) for at in range(lax.axis_size(axis))]
            )
    return value


def weight_sum(grads):
    return lax.psum_scatter(grads, ("dp", "blk"), scatter_dimension=0, tiled=True)


def split_columns(value_in, widths):
    pieces, start = [], 0
    for width in widths:
        pieces.append(value_in[:, start : start + width])
        start += width
    return pieces


def inverse_rms(rows_in):
    return lax.rsqrt(jnp.mean(rows_in * rows_in, axis=-1, keepdims=True) + norm_eps)


def norm_back(rows_in, gain_in, cotangent):
    inverse = inverse_rms(rows_in)
    scaled = rows_in * inverse
    weighted = cotangent * gain_in
    return inverse * (weighted - scaled * jnp.mean(weighted * scaled, axis=-1, keepdims=True))


def shards(
    x_in,
    out_grad,
    norm_one,
    w_query,
    w_key,
    w_value,
    output_gate_weight,
    mixer_input_weight,
    w_delta,
    w_bmat,
    w_cmat,
    delta_bias,
    decay_log,
    skip_gain,
    w_attn_out,
    mixer_output_weight,
    norm_two,
    w_gate,
    w_up,
    w_down,
):
    heads_count = lax.axis_size("heads")
    head_rank = lax.axis_index("heads")
    core = head_rank % 2
    block_rank = lax.axis_index("blk")
    rank = block_rank.astype(jnp.int32)[None]
    own_rows = x_in.shape[0]
    span_length = own_rows * heads_count
    half_span = span_length // 2
    span_start = block_rank * span_length
    query_width = w_query.shape[1]
    mixer_width = mixer_input_weight.shape[1]
    heads = mixer_width // MIXER_HEAD_SIZE
    state_size = w_bmat.shape[1]
    hidden_width = w_gate.shape[1]
    rows_of = w_query.shape[0]
    kv_index = head_rank * (query_width // HD) // (QH // KVH)
    kv_width = KVH * HD
    low = jnp.bfloat16
    ranks = chunk_ranks().astype(jnp.int32)
    turns = (head_rank ^ jnp.arange(heads_count)).astype(jnp.int32)

    gains = jnp.stack([norm_one, norm_two], axis=1)
    gains = jnp.pad(gains, ((0, 0), (heads, LANES - heads - 2)))
    shared = pack((w_key, w_value, w_bmat, w_cmat, gains), (False,) * 5)
    delta_wide = jnp.pad(w_delta, ((0, 0), (0, LANES - heads)))
    in_names = ("z", "x", "query", "b", "c", "misc", "key", "value")
    in_widths = (mixer_width, mixer_width, query_width, state_size, state_size, LANES, HD, HD)
    in_width = sum(in_widths)
    starts = [sum(in_widths[:k]) for k in range(len(in_widths))]
    at = dict(zip(in_names, zip(starts, in_widths)))
    mix_at = {
        "ssm_out": (in_width, mixer_width),
        "attn_out": (in_width + mixer_width, query_width),
    }
    first_own = pack_first(
        turns,
        kv_index.astype(jnp.int32)[None],
        gather_small(shared),
        delta_wide,
        [output_gate_weight, mixer_input_weight, w_query, mixer_output_weight, w_attn_out],
        at | mix_at,
    )
    gain_part = first_own[:, at["misc"][0] + heads : at["misc"][0] + heads + 2]
    first_full = lax.all_gather(first_own, ("dp", "blk"), axis=0, tiled=True)
    in_full, mix_t = (first_full[:, :in_width], first_full[:, in_width:])
    x_float = x_in.astype(jnp.float32)
    zero = 0.0 * first_own[0, 0]
    x_span, _ = gather_rows(x_in + zero, joined=True)
    ffn_grad, _ = gather_rows(out_grad + zero, joined=True)
    ffn_own = pack((w_gate, w_up, w_down), (False, False, True), [corner(x_span)])
    ffn_full = lax.all_gather(ffn_own, ("dp", "blk"), axis=0, tiled=True)
    mixed_width = query_width + mixer_width
    gate_full, up_full, down_t = split_columns(ffn_full, (hidden_width,) * 3)
    positions = (span_start + jnp.arange(span_length)).astype(jnp.float32)
    freqs = rope_base ** (-2.0 * jnp.arange(HD // 2, dtype=jnp.float32) / HD)
    angles = positions[:, None] * freqs[None, :]
    cosine, sine = (jnp.cos(angles), jnp.sin(angles))
    cosine = jnp.concatenate([cosine, cosine], axis=1)
    sine = jnp.concatenate([-sine, sine], axis=1)
    normed_ordered, queries, keys_values, gain_rows = enter(
        ranks, jnp.full((1,), heads, jnp.int32), x_span, first_full, at, cosine, sine, [corner(ffn_own), corner(ffn_grad)]
    )
    gain_one, gain_two = (gain_rows[0:1], gain_rows[1:2])
    mine = lax.dynamic_slice_in_dim(keys_values, core * half_span, half_span, 0)
    pieces = []
    for piece in from_earlier(mine):
        pieces += [piece, to_partner(piece)]
    gate_raw = simple_product(normed_ordered, in_full[:, :mixer_width])
    x_raw = simple_product(normed_ordered, in_full[:, mixer_width : 2 * mixer_width])
    state_raw = simple_product(normed_ordered, in_full[:, at["b"][0] : at["key"][0]])
    raw = {
        "z": (gate_raw, 0, mixer_width),
        "x": (x_raw, 0, mixer_width),
        "b": (state_raw, 0, state_size),
        "c": (state_raw, state_size, state_size),
        "misc": (state_raw, 2 * state_size, LANES),
    }

    pad_lanes = lambda vector: jnp.pad(vector, (0, LANES - heads))[None]
    bias, rate = (pad_lanes(delta_bias), pad_lanes(jnp.exp(decay_log)))
    skip = jnp.repeat(skip_gain, MIXER_HEAD_SIZE)[None]
    delta, cumulative, delta_row, cum_row, local_state, local_log = scan_first(raw, bias, rate)
    entry_states = from_earlier(pack_state(local_state, local_log))
    attended, attn_part, log_totals = attend(rank, queries, keys_values, pieces)
    scanned, gated, states = scan(
        raw, delta, cumulative, delta_row, cum_row, entry_states, skip, [corner(attn_part)]
    )
    mixers = reorder(ranks, [gated, attn_part])
    ffn_zero = 0.0 * ffn_full[0, 0].astype(jnp.float32)
    mixed = scatter_rows(lambda rows: dot_last(mixers[rows], mix_t), half_span, ffn_zero)
    middle = x_float + mixed
    middle_scaled = middle * inverse_rms(middle)
    normed_two, _ = gather_rows((middle_scaled * gain_two).astype(low))
    ffn_gate = simple_product(normed_two, gate_full)
    ffn_up = simple_product(normed_two, up_full)
    ffn_sig = jax.nn.sigmoid(ffn_gate)
    hidden = (ffn_gate * ffn_sig * ffn_up).astype(low)

    d_hidden = simple_product(ffn_grad, down_t)
    d_ffn_gate = (d_hidden * ffn_up * (ffn_sig * (1.0 + ffn_gate * (1.0 - ffn_sig)))).astype(low)
    d_ffn_up = (d_hidden * (ffn_gate * ffn_sig)).astype(low)
    d_normed_two = scatter_rows(
        lambda rows: dot_last(d_ffn_gate[rows], gate_full) + dot_last(d_ffn_up[rows], up_full),
        half_span,
    )
    d_middle = out_grad.astype(jnp.float32) + norm_back(middle, gain_two, d_normed_two)
    mix_grad, mix_partner = gather_rows(d_middle.astype(low))
    ffn_grads = weight_grads(
        [(normed_two, [d_ffn_gate, d_ffn_up]), (ffn_grad, [hidden])],
        3 * hidden_width,
        after=[corner(mix_partner)],
    )
    ffn_sums = weight_sum(ffn_grads).astype(jnp.float32)
    grad_gate, grad_up, grad_down_t = split_columns(ffn_sums, (hidden_width,) * 3)
    grad_two_part = jnp.sum(grad_gate * w_gate + grad_up * w_up, axis=1, keepdims=True)
    gain_own = gain_part.astype(jnp.float32)
    grad_two_part = grad_two_part / gain_own[:, 1:2]
    d_mixers = reorder(
        ranks, [simple_product(mix_grad, mix_t).astype(low)], inverse=True, after=[corner(ffn_grads)]
    )
    d_scanned, d_gate_z, d_entry = scan_back_first(d_mixers, raw, scanned, cumulative)
    d_entry = pack_state(d_entry, local_log)
    after_states = from_earlier(d_entry, -1)
    mix_width = mixed_width + mixer_width
    all_width = mixed_width + in_width
    mix_grads = weight_grads(
        [(mix_grad, [mixers]), (normed_ordered, [d_gate_z])], all_width, after=[corner(d_entry)]
    )
    d_query, d_own, d_far = attend_back(
        rank, queries, keys_values, pieces, attended, log_totals, d_mixers, cosine, sine, [corner(mix_grads), *map(corner, after_states)]
    )
    d_ssm_in, d_bmat, d_cmat, d_pre, sums = scan_back(
        raw,
        d_scanned,
        bias,
        rate,
        delta,
        cumulative,
        cum_row,
        states,
        after_states,
        skip,
        [corner(d_query)],
    )
    far_half = d_far.shape[0] // 2
    d_mine = lax.dynamic_slice_in_dim(d_own, core * half_span, half_span, 0)
    d_theirs = lax.dynamic_slice_in_dim(d_own, (1 - core) * half_span, half_span, 0)
    d_mine = d_mine + to_partner(d_theirs.astype(low)).astype(jnp.float32)
    d_far = d_far[:far_half].astype(jnp.float32) + to_partner(d_far[far_half:]).astype(jnp.float32)
    d_one, d_two, d_three = (
        d_far[k * half_span : (k + 1) * half_span] for k in range(d_far.shape[0] // half_span)
    )
    d_one = d_one + on_blocks(d_two.astype(low), -1).astype(jnp.float32)
    d_mine = d_mine + on_blocks(d_one.astype(low), -1).astype(jnp.float32)
    d_mine = d_mine + on_blocks(d_three.astype(low), -3).astype(jnp.float32)
    half_cos = lax.dynamic_slice_in_dim(cosine, core * half_span, half_span, 0)
    half_sin = lax.dynamic_slice_in_dim(sine, core * half_span, half_span, 0)
    d_key = d_mine[:, :HD]
    d_key = d_key * half_cos - jnp.roll(d_key, HD // 2, axis=1) * half_sin
    d_mine = jnp.concatenate([d_key, d_mine[:, HD:]], axis=1).astype(low)
    d_keys_values = lax.dynamic_update_slice_in_dim(
        jnp.zeros((span_length, 2 * HD), low), d_mine, core * half_span, 0
    )

    scan_rights = [d_ssm_in, d_bmat, d_cmat, d_pre]
    in_grads = weight_grads([(normed_ordered, scan_rights)], all_width, mix_width, mix_grads)
    late_rights = [d_keys_values, d_query]
    late_start = mix_width + sum(array.shape[1] for array in scan_rights)
    in_grads = weight_grads([(normed_ordered, late_rights)], all_width, late_start, in_grads)
    in_sums = weight_sum(in_grads)
    d_projected = reorder(
        ranks,
        [d_gate_z, d_ssm_in, d_query, d_bmat, d_cmat, d_pre, d_keys_values],
        after=[corner(in_grads)],
    )
    d_normed = scatter_rows(lambda rows: dot_last(d_projected[rows], in_full), half_span)
    input_grad = d_middle + norm_back(x_float, gain_one, d_normed)
    back_zero = 0.0 * d_query[0, 0].astype(jnp.float32)
    ffn_out = scatter_rows(
        lambda rows: dot_last(hidden[rows], down_t) + back_zero, half_span
    )
    activations = (middle + ffn_out).astype(low)
    sums_names = ("ssm_out", "attn_out", "z", "x", "b", "c", "misc", "key", "value", "query")
    sums_widths = [mixer_width, query_width] + [at[name][1] for name in sums_names[2:]]
    sums_starts = [sum(sums_widths[:k]) for k in range(len(sums_widths))]
    sums_at = dict(zip(sums_names, zip(sums_starts, sums_widths)))
    extra = jnp.concatenate([gain_own[:, 0:1], grad_two_part], axis=1)
    extra = jnp.pad(extra, ((0, 0), (0, LANES - 2)))
    grad_ssm_out, grad_attn_out, grad_gatez, grad_ssmx, grad_query, misc_sums, shared_parts = finish(
        turns,
        kv_index.astype(jnp.int32)[None],
        in_sums,
        first_own,
        extra,
        at,
        sums_at,
    )
    shared_sums = scatter_small(shared_parts)
    grad_key, grad_value, grad_bmat, grad_cmat, gain_sums = split_columns(
        shared_sums, (kv_width, kv_width, state_size, state_size, LANES)
    )
    small_sums = sum_blocks(sums)[:, :heads]
    return (
        activations,
        input_grad,
        gain_sums[:, 0],
        grad_query,
        grad_key,
        grad_value,
        grad_gatez,
        grad_ssmx,
        misc_sums[:, :heads],
        grad_bmat,
        grad_cmat,
        small_sums[0],
        small_sums[1],
        small_sums[2],
        grad_attn_out,
        grad_ssm_out,
        gain_sums[:, 1],
        grad_gate,
        grad_up,
        grad_down_t.T,
    )


def solution(mesh):
    placed = (
        P(("dp", "blk", "heads"), None),
        P(("dp", "blk", "heads"), None),
        P(("dp", "blk", "heads")),
        P(("dp", "blk"), "heads"),
        P(("dp", "blk", "heads"), None),
        P(("dp", "blk", "heads"), None),
        P(("dp", "blk"), "heads"),
        P(("dp", "blk"), "heads"),
        P(("dp", "blk"), "heads"),
        P(("dp", "blk", "heads"), None),
        P(("dp", "blk", "heads"), None),
        P("heads"),
        P("heads"),
        P("heads"),
        P("heads", ("dp", "blk")),
        P("heads", ("dp", "blk")),
        P(("dp", "blk", "heads")),
        P(("dp", "blk"), "heads"),
        P(("dp", "blk"), "heads"),
        P("heads", ("dp", "blk")),
    )
    return jax.shard_map(
        shards,
        mesh=mesh,
        in_specs=placed,
        out_specs=(
            P(("dp", "blk", "heads"), None),
            P(("dp", "blk", "heads"), None),
            P(("dp", "blk", "heads")),
            P(("dp", "blk"), "heads"),
            P(("dp", "blk", "heads"), None),
            P(("dp", "blk", "heads"), None),
            P(("dp", "blk"), "heads"),
            P(("dp", "blk"), "heads"),
            P(("dp", "blk"), "heads"),
            P(("dp", "blk", "heads"), None),
            P(("dp", "blk", "heads"), None),
            P("heads"),
            P("heads"),
            P("heads"),
            P("heads", ("dp", "blk")),
            P("heads", ("dp", "blk")),
            P(("dp", "blk", "heads")),
            P(("dp", "blk"), "heads"),
            P(("dp", "blk"), "heads"),
            P("heads", ("dp", "blk")),
        ),
        check_vma=False,
    )
```

```python
import functools

import jax
import jax.numpy as jnp
from jax import lax
from jax.experimental import pallas as pl
from jax.experimental.pallas import tpu as pltpu
from jax.sharding import PartitionSpec as P

QH = 8
KVH = 2
HD = 128
MIXER_HEAD_SIZE = 64
BLOCK = 256
LANES = 128
LOG2_E = 1.4426950408889634


HIGH_PRECISION = lax.Precision.HIGHEST
norm_eps = 1e-05
rope_base = 100000000000.0


def simple_product(left_side, right_side):
    return jnp.dot(left_side, right_side, preferred_element_type=jnp.float32)


def dot_last(left_side, right_side):
    return lax.dot_general(
        left_side, right_side, (((1,), (1,)), ((), ())), preferred_element_type=jnp.float32
    )


def dot_first(left_side, right_side):
    return lax.dot_general(
        left_side, right_side, (((0,), (0,)), ((), ())), preferred_element_type=jnp.float32
    )


def compiler_params(mebibytes=20):
    return pltpu.CompilerParams(vmem_limit_bytes=mebibytes * 1024 * 1024)


def small_cost():
    return pl.CostEstimate(flops=1000, bytes_accessed=1000, transcendentals=0)


def in_hbm(value):
    return pltpu.with_memory_space_constraint(value, pltpu.HBM)


def corner(value):
    return value[:16, :LANES]


def in_vmem(count):
    return [pl.BlockSpec(memory_space=pltpu.VMEM)] * count


def mul(left_side, right_side):
    return jnp.dot(left_side, right_side, preferred_element_type=jnp.float32)


def tile_scores(key_rows, query_rows, head_size):
    return dot_last(key_rows, query_rows) * (head_size**-0.5 * LOG2_E)


def causal(scores):
    key_at = lax.broadcasted_iota(jnp.int32, scores.shape, 0)
    query_at = lax.broadcasted_iota(jnp.int32, scores.shape, 1)
    return jnp.where(key_at <= query_at, scores, -1e30)


def enter_kernel(
    ranks_ref, heads_ref, x_ref, misc_ref, key_ref, value_ref, w_query_ref, cos_ref, sin_ref, *refs
):
    ordered_ref, query_ref, kv_ref, gains_ref = refs[-4:]
    head_size = query_ref.shape[1]

    @pl.when(pl.program_id(0) == 0)
    def _():
        lane = lax.broadcasted_iota(jnp.int32, misc_ref.shape, 1)
        for k in range(2):
            column = jnp.where(lane == heads_ref[0] + k, misc_ref[...].astype(jnp.float32), 0.0)
            gains_ref[k : k + 1, :] = jnp.sum(column.T, axis=0, keepdims=True)

    cosine, sine = (cos_ref[...], sin_ref[...])

    def turn(value):
        return (value * cosine + pltpu.roll(value, head_size // 2, 1) * sine).astype(jnp.bfloat16)

    rows = x_ref[...].astype(jnp.float32)
    normed = (rows * inverse_rms(rows) * gains_ref[0:1, :]).astype(jnp.bfloat16)
    ordered_ref[...] = normed
    kv_ref[:, :head_size] = turn(mul(normed, key_ref[...]))
    kv_ref[:, head_size:] = mul(normed, value_ref[...]).astype(jnp.bfloat16)
    query_ref[...] = turn(mul(normed, w_query_ref[...]))


def enter(ranks, heads, x_span, in_full, at, cosine, sine, after):
    count = ranks.shape[0]
    rows, width = x_span.shape
    head_size = cosine.shape[1]
    here = lambda columns: pl.BlockSpec((rows // count, columns), lambda k, r, h: (k, 0))
    there = lambda columns: pl.BlockSpec((rows // count, columns), lambda k, r, h: (r[k], 0))
    weight = lambda name: pl.BlockSpec(
        (width, at[name][1]), lambda k, r, h: (0, at[name][0] // at[name][1])
    )
    return pl.pallas_call(
        enter_kernel,
        grid_spec=pltpu.PrefetchScalarGridSpec(
            num_scalar_prefetch=2,
            grid=(count,),
            in_specs=[
                here(width),
                weight("misc"),
                weight("key"),
                weight("value"),
                weight("query"),
                there(head_size),
                there(head_size),
            ]
            + [pl.BlockSpec(memory_space=pl.ANY)] * len(after),
            out_specs=(
                there(width),
                there(head_size),
                there(2 * head_size),
                pl.BlockSpec((8, width), lambda k, r, h: (0, 0)),
            ),
        ),
        out_shape=(
            jax.ShapeDtypeStruct((rows, width), jnp.bfloat16),
            jax.ShapeDtypeStruct((rows, head_size), jnp.bfloat16),
            jax.ShapeDtypeStruct((rows, 2 * head_size), jnp.bfloat16),
            jax.ShapeDtypeStruct((8, width), jnp.float32),
        ),
        compiler_params=compiler_params(),
        cost_estimate=small_cost(),
        name="enter",
    )(ranks, heads, in_hbm(x_span), *[in_hbm(in_full)] * 4, cosine, sine, *after)


def weight_grads_kernel(*refs, counts):
    out_ref = refs[-1]
    start, used = (0, len(counts))
    for k, count in enumerate(counts):
        left = refs[k][...].T
        for ref in refs[used : used + count]:
            out_ref[:, start : start + ref.shape[1]] = mul(left, ref[...]).astype(jnp.bfloat16)
            start += ref.shape[1]
        used += count


def weight_grads(groups, width, start=0, buffer=None, after=()):
    rights = [right for _, group in groups for right in group]
    columns = sum(right.shape[1] for right in rights)
    depth = rights[0].shape[0]
    rows = groups[0][0].shape[1]
    operands = [left for left, _ in groups] + rights
    count = len(operands)
    extra = list(after) if buffer is None else [buffer] + list(after)

    def call(*refs):
        weight_grads_kernel(
            *refs[:count],
            refs[-1],
            counts=tuple(len(group) for _, group in groups),
        )

    return pl.pallas_call(
        call,
        grid=(rows // BLOCK,),
        out_shape=pltpu.HBM((rows, width), jnp.bfloat16),
        in_specs=[pl.BlockSpec((depth, BLOCK), lambda k: (0, k)) for _ in groups]
        + [pl.BlockSpec(right.shape, lambda k: (0, 0)) for right in rights]
        + [pl.BlockSpec(memory_space=pl.ANY)] * len(extra),
        out_specs=pl.BlockSpec(
            (pl.Element(BLOCK), pl.Element(columns)), lambda k: (k * BLOCK, start)
        ),
        input_output_aliases={} if buffer is None else {count: 0},
        compiler_params=compiler_params(),
        cost_estimate=small_cost(),
        name="weight_grads",
    )(*operands, *extra)


def pack_kernel(*refs, turned):
    out_ref = refs[-1]
    start = 0
    for ref, turn in zip(refs, turned):
        piece = ref[...].T if turn else ref[...]
        out_ref[:, start : start + piece.shape[1]] = piece
        start += piece.shape[1]


def pack(pieces, turned, after=()):
    sizes = [piece.shape[::-1] if turn else piece.shape for piece, turn in zip(pieces, turned)]
    return pl.pallas_call(
        functools.partial(pack_kernel, turned=turned),
        out_shape=jax.ShapeDtypeStruct(
            (sizes[0][0], sum(size[1] for size in sizes)), jnp.bfloat16
        ),
        in_specs=in_vmem(len(pieces)) + [pl.BlockSpec(memory_space=pl.ANY)] * len(after),
        out_specs=pl.BlockSpec(memory_space=pltpu.VMEM),
        compiler_params=compiler_params(),
        cost_estimate=small_cost(),
        name="pack",
    )(*map(in_hbm, pieces), *after)


def join_kernel(*refs):
    out_ref = refs[-1]
    start = 0
    for ref in refs[:-1]:
        out_ref[start : start + ref.shape[0], :] = ref[...]
        start += ref.shape[0]


def join(pieces):
    rows = sum(piece.shape[0] for piece in pieces)
    return pl.pallas_call(
        join_kernel,
        out_shape=jax.ShapeDtypeStruct((rows, pieces[0].shape[1]), pieces[0].dtype),
        in_specs=in_vmem(len(pieces)),
        out_specs=pl.BlockSpec(memory_space=pltpu.VMEM),
        compiler_params=compiler_params(),
        cost_estimate=small_cost(),
        name="join",
    )(*pieces)


def pack_first_kernel(
    turns_ref, kv_ref, shared_ref, delta_ref, z_ref, x_ref, query_ref, ssm_ref, attn_ref, out_ref, *, at
):
    def put(name, value, rows=slice(None)):
        start, size = at[name]
        out_ref[rows, start : start + size] = value

    put("z", z_ref[...])
    put("x", x_ref[...])
    put("query", query_ref[...])
    put("ssm_out", ssm_ref[...].T)
    put("attn_out", attn_ref[...].T)
    count = turns_ref.shape[0]
    size = shared_ref.shape[0] // count
    first = kv_ref[0] == 0
    for k in range(count):
        rows = pl.ds(pl.multiple_of(turns_ref[k] * size, size), size)
        chunk = shared_ref[k * size : (k + 1) * size, :]
        pieces, start = [], 0
        for width in (HD, HD, HD, HD, at["b"][1], at["c"][1], LANES):
            pieces.append(chunk[:, start : start + width])
            start += width
        put("key", jnp.where(first, pieces[0], pieces[1]), rows)
        put("value", jnp.where(first, pieces[2], pieces[3]), rows)
        put("b", pieces[4], rows)
        put("c", pieces[5], rows)
        put("misc", pieces[6] + delta_ref[rows, :], rows)


def pack_first(turns, kv_index, shared, delta, weights, at):
    rows = shared.shape[0]
    return pl.pallas_call(
        functools.partial(pack_first_kernel, at=at),
        out_shape=jax.ShapeDtypeStruct(
            (rows, max(start + size for start, size in at.values())), jnp.bfloat16
        ),
        in_specs=[pl.BlockSpec(memory_space=pltpu.SMEM)] * 2 + in_vmem(2 + len(weights)),
        out_specs=pl.BlockSpec(memory_space=pltpu.VMEM),
        compiler_params=compiler_params(50),
        cost_estimate=small_cost(),
        name="pack_first",
    )(turns, kv_index, shared, delta, *map(in_hbm, weights))


def finish_kernel(
    ranks_ref,
    kv_ref,
    sums_ref,
    weight_ref,
    extra_ref,
    ssm_out_ref,
    attn_out_ref,
    gate_ref,
    ssm_ref,
    query_ref,
    misc_ref,
    shared_ref,
    whole_ref,
    *,
    at,
    sums_at,
):
    def of(name):
        start, size = sums_at[name]
        return sums_ref[:, start : start + size].astype(jnp.float32)

    ssm_out_ref[...] = of("ssm_out").T
    attn_out_ref[...] = of("attn_out").T
    gate_ref[...] = of("z")
    ssm_ref[...] = of("x")
    query_ref[...] = of("query")
    misc_ref[...] = of("misc")
    total = 0.0
    for name, (start, size) in at.items():
        product = of(name) * weight_ref[:, start : start + size].astype(jnp.float32)
        total += jnp.sum(product, axis=1, keepdims=True)
    total = total / extra_ref[:, 0:1]
    lane = lax.broadcasted_iota(jnp.int32, misc_ref.shape, 1)
    gains = jnp.where(lane == 0, total, jnp.where(lane == 1, extra_ref[:, 1:2], 0.0))
    zero = jnp.zeros_like(gains)
    first = kv_ref[0] == 0
    key, value = (of("key"), of("value"))
    pieces = (
        jnp.where(first, key, zero),
        jnp.where(first, zero, key),
        jnp.where(first, value, zero),
        jnp.where(first, zero, value),
        of("b"),
        of("c"),
        gains,
    )
    start = 0
    for piece in pieces:
        whole_ref[:, start : start + piece.shape[1]] = piece
        start += piece.shape[1]
    count = ranks_ref.shape[0]
    size = shared_ref.shape[0] // count
    for k in range(count):
        rows = pl.ds(pl.multiple_of(ranks_ref[k] * size, size), size)
        shared_ref[k * size : (k + 1) * size, :] = whole_ref[rows, :].astype(jnp.bfloat16)


def finish(ranks, kv_index, sums, weights, extra, at, sums_at):
    rows = weights.shape[0]
    shape = lambda *sizes: jax.ShapeDtypeStruct(sizes, jnp.float32)
    width = lambda name: sums_at[name][1]
    shared = 2 * (width("key") + width("value")) + width("b") + width("c") + LANES
    return pl.pallas_call(
        functools.partial(finish_kernel, at=at, sums_at=sums_at),
        out_shape=(
            shape(width("ssm_out"), rows),
            shape(width("attn_out"), rows),
            shape(rows, width("z")),
            shape(rows, width("x")),
            shape(rows, width("query")),
            shape(rows, width("misc")),
            jax.ShapeDtypeStruct((rows, shared), jnp.bfloat16),
        ),
        in_specs=[pl.BlockSpec(memory_space=pltpu.SMEM)] * 2 + in_vmem(3),
        out_specs=tuple(in_vmem(7)),
        scratch_shapes=[pltpu.VMEM((rows, shared), jnp.float32)],
        compiler_params=compiler_params(),
        name="finish",
    )(ranks, kv_index, sums, weights, extra)


def attend_kernel(rank_ref, query_ref, own_ref, *refs):
    pieces, (out_ref, low_ref, log_ref) = (refs[:-3], refs[-3:])
    span_length, head_size = query_ref.shape
    tile = own_ref.shape[0] // 2
    for block in range(span_length // tile):
        here = slice(block * tile, (block + 1) * tile)
        query_rows = query_ref[here, :]

        def step(kv_rows, carried, masked=False):
            top, total, summed = carried
            scores = tile_scores(kv_rows[:, :head_size], query_rows, head_size)
            if masked:
                scores = causal(scores)
            new_top = jnp.maximum(top, jnp.max(scores, axis=0, keepdims=True))
            probs = jnp.exp2(scores - new_top)
            scale = jnp.exp2(top - new_top)
            total = total * scale + jnp.sum(probs, axis=0, keepdims=True)
            summed = summed * scale + dot_first(kv_rows[:, head_size:], probs.astype(jnp.bfloat16))
            return (new_top, total, summed)

        carried = (
            jnp.full((1, tile), -1e30, jnp.float32),
            jnp.zeros((1, tile), jnp.float32),
            jnp.zeros((head_size, tile), jnp.float32),
        )
        carried = step(own_ref[here, :], carried, True)
        for earlier in range(block):
            carried = step(own_ref[earlier * tile : (earlier + 1) * tile, :], carried)
        for distance in range(1, 1 + len(pieces) // 2):
            pair = pieces[2 * distance - 2 : 2 * distance]

            def both(_, carried, pair=pair):
                return step(pair[1][...], step(pair[0][...], carried))

            valid = (rank_ref[0] >= distance).astype(jnp.int32)
            carried = lax.fori_loop(0, valid, both, carried)
        top, total, summed = carried
        result = summed / total
        out_ref[:, here] = result
        low_ref[here, :] = result.T.astype(jnp.bfloat16)
        log_ref[:, here] = top + jnp.log2(total)


def attend(rank, queries, own, pieces):
    span_length, head_size = queries.shape
    return pl.pallas_call(
        attend_kernel,
        out_shape=(
            jax.ShapeDtypeStruct((head_size, span_length), jnp.float32),
            jax.ShapeDtypeStruct((span_length, head_size), jnp.bfloat16),
            jax.ShapeDtypeStruct((1, span_length), jnp.float32),
        ),
        in_specs=[pl.BlockSpec(memory_space=pltpu.SMEM)] + in_vmem(2 + len(pieces)),
        out_specs=tuple(in_vmem(3)),
        compiler_params=compiler_params(),
        cost_estimate=small_cost(),
        name="attend",
    )(rank, queries, own, *pieces)


def attend_back_kernel(rank_ref, query_ref, own_ref, *refs):
    pieces, refs = (refs[:-13], refs[-13:])
    out_ref, log_ref, grad_ref, cos_ref, sin_ref, *_, d_query_ref, d_own_ref, d_far_ref, sums_ref = refs
    span_length, head_size = query_ref.shape
    tile = own_ref.shape[0] // 2
    score_scale = head_size**-0.5
    sums_ref[...] = jnp.zeros_like(sums_ref)
    for block in range(span_length // tile):
        here = slice(block * tile, (block + 1) * tile)
        query_rows = query_ref[here, :]
        grad_rows = grad_ref[here, grad_ref.shape[1] - head_size :]
        log_total = log_ref[:, here]
        delta_row = jnp.sum(
            grad_rows.astype(jnp.float32).T * out_ref[:, here], axis=0, keepdims=True
        )

        def step(kv_ref, start, at, d_query, masked=False):
            key_rows = kv_ref[start : start + tile, :head_size]
            scores = tile_scores(key_rows, query_rows, head_size)
            if masked:
                scores = causal(scores)
            probs = jnp.exp2(scores - log_total)
            d_probs = dot_last(kv_ref[start : start + tile, head_size:], grad_rows)
            d_scores = (probs * (d_probs - delta_row)).astype(jnp.bfloat16)
            rows = slice(at * tile, (at + 1) * tile)
            sums_ref[rows, head_size:] += mul(probs.astype(jnp.bfloat16), grad_rows)
            sums_ref[rows, :head_size] += mul(d_scores, query_rows)
            return d_query + dot_first(key_rows, d_scores)

        d_query = jnp.zeros((head_size, tile), jnp.float32)
        d_query = step(own_ref, block * tile, block, d_query, True)
        for earlier in range(block):
            d_query = step(own_ref, earlier * tile, earlier, d_query)
        for distance in range(1, 1 + len(pieces) // 2):

            def both(_, d_query, distance=distance):
                for k in (2 * distance - 2, 2 * distance - 1):
                    d_query = step(pieces[k], 0, 2 + k, d_query)
                return d_query

            valid = (rank_ref[0] >= distance).astype(jnp.int32)
            d_query = lax.fori_loop(0, valid, both, d_query)
        turned = d_query.T * score_scale
        d_query_ref[here, :] = (
            turned * cos_ref[here, :] - pltpu.roll(turned, head_size // 2, 1) * sin_ref[here, :]
        ).astype(jnp.bfloat16)
    lane = lax.broadcasted_iota(jnp.int32, (tile, 2 * head_size), 1)
    scale = jnp.where(lane < head_size, score_scale, 1.0)
    for at in range(2):
        rows = slice(at * tile, (at + 1) * tile)
        d_own_ref[rows, :] = sums_ref[rows, :] * scale
    for k in range(len(pieces)):
        rows = slice((2 + k) * tile, (3 + k) * tile)
        into = (k % 2) * (len(pieces) // 2) + k // 2
        d_far_ref[into * tile : (into + 1) * tile, :] = (sums_ref[rows, :] * scale).astype(
            jnp.bfloat16
        )


def attend_back(rank, queries, own, pieces, attended, log_totals, d_attn, cosine, sine, after):
    tile = own.shape[0] // 2
    return pl.pallas_call(
        attend_back_kernel,
        out_shape=(
            jax.ShapeDtypeStruct(queries.shape, jnp.bfloat16),
            jax.ShapeDtypeStruct(own.shape, jnp.float32),
            jax.ShapeDtypeStruct((len(pieces) * tile, own.shape[1]), jnp.bfloat16),
        ),
        in_specs=[pl.BlockSpec(memory_space=pltpu.SMEM)]
        + in_vmem(7 + len(pieces))
        + [pl.BlockSpec(memory_space=pl.ANY)] * len(after),
        out_specs=tuple(in_vmem(3)),
        scratch_shapes=[pltpu.VMEM(((2 + len(pieces)) * tile, own.shape[1]), jnp.float32)],
        compiler_params=compiler_params(),
        cost_estimate=small_cost(),
        name="attend_back",
    )(rank, queries, own, *pieces, attended, log_totals, d_attn, cosine, sine, *after)


def reorder_kernel(ranks_ref, *refs, count):
    out_ref = refs[-1]
    start = 0
    for ref in refs[:count]:
        out_ref[:, start : start + ref.shape[1]] = ref[...].astype(out_ref.dtype)
        start += ref.shape[1]


def reorder(ranks, pieces, inverse=False, after=()):
    count = ranks.shape[0]
    rows = pieces[0].shape[0] // count
    width = sum(piece.shape[1] for piece in pieces)
    there = lambda k, ranks: (ranks[k], 0)
    here = lambda k, ranks: (k, 0)
    return pl.pallas_call(
        functools.partial(reorder_kernel, count=len(pieces)),
        grid_spec=pltpu.PrefetchScalarGridSpec(
            num_scalar_prefetch=1,
            grid=(count,),
            in_specs=[
                pl.BlockSpec((rows, piece.shape[1]), here if inverse else there)
                for piece in pieces
            ]
            + [pl.BlockSpec(memory_space=pl.ANY)] * len(after),
            out_specs=pl.BlockSpec((rows, width), there if inverse else here),
        ),
        out_shape=jax.ShapeDtypeStruct((count * rows, width), jnp.bfloat16),
        compiler_params=compiler_params(),
        cost_estimate=small_cost(),
        name="reorder",
    )(ranks, *pieces, *after)


def lower_ones(size, dtype=jnp.float32):
    row = lax.broadcasted_iota(jnp.int32, (size, size), 0)
    column = lax.broadcasted_iota(jnp.int32, (size, size), 1)
    return (row >= column).astype(dtype)


def precise(left_side, right_side):
    return jnp.dot(
        left_side, right_side, precision=HIGH_PRECISION, preferred_element_type=jnp.float32
    )


def spread_heads(columns, head_size, width):
    lane = lax.broadcasted_iota(jnp.int32, (columns.shape[0], 2 * head_size), 1)
    pairs = [
        jnp.where(lane < head_size, columns[:, k : k + 1], columns[:, k + 1 : k + 2])
        for k in range(0, width // head_size, 2)
    ]
    return jnp.concatenate(pairs, axis=1)


def head_ones(width, head_size, lanes, dtype):
    at = lax.broadcasted_iota(jnp.int32, (width, lanes), 0)
    lane = lax.broadcasted_iota(jnp.int32, (width, lanes), 1)
    low = lane * head_size
    return ((at >= low) & (at < low + head_size)).astype(dtype)


def scan_first_kernel(
    pre_ref, bias_ref, rate_ref, x_ref, b_ref, delta_ref, cum_ref, delta_row_ref, cum_row_ref, state_ref, log_ref
):
    @pl.when(pl.program_id(0) == 0)
    def _():
        state_ref[...] = jnp.zeros_like(state_ref)
        log_ref[...] = jnp.zeros_like(log_ref)

    delta = jax.nn.softplus(pre_ref[...] + bias_ref[...])
    log_step = -delta * rate_ref[...]
    cumulative = precise(lower_ones(log_step.shape[0]), log_step)
    delta_ref[...] = delta
    cum_ref[...] = cumulative
    delta_row_ref[...] = delta.T[:8]
    cum_row_ref[...] = cumulative.T[:8]
    ending = cumulative[-1:, :]
    weight = jnp.exp(ending - cumulative + log_ref[...]) * delta
    width = x_ref.shape[1]
    x_low = x_ref[...].astype(jnp.bfloat16).astype(jnp.float32)
    weighted = (x_low * spread_heads(weight, MIXER_HEAD_SIZE, width)).astype(jnp.bfloat16)
    state_ref[...] += dot_first(b_ref[...].astype(jnp.bfloat16), weighted)
    log_ref[...] += ending


def part(projected, start, width, order=lambda c: c):
    at = start // width
    return (projected, pl.BlockSpec((BLOCK, width), lambda c: (order(c), at)))


def run_scan(
    kernel, chunks, operands, out_shape, out_specs, name, scratch=(), after=(), mebibytes=20
):
    count = len(operands)
    operands = operands + [(array, pl.BlockSpec(memory_space=pl.ANY)) for array in after]

    def call(*refs):
        kernel(*refs[:count], *refs[count + len(after) :])

    return pl.pallas_call(
        call,
        grid=(chunks,),
        out_shape=out_shape,
        in_specs=[spec for _, spec in operands],
        out_specs=out_specs,
        scratch_shapes=list(scratch),
        compiler_params=compiler_params(mebibytes),
        cost_estimate=small_cost(),
        name=name,
    )(*[array for array, _ in operands])


def whole(array):
    return (array, pl.BlockSpec(array.shape, lambda c: (0,) * array.ndim))


def scan_first(at, bias, rate):
    rows, lanes = (at["x"][0].shape[0], bias.shape[1])
    chunks = rows // BLOCK
    back = lambda c: chunks - 1 - c
    width, state_size = (at["x"][2], at["b"][2])
    by_chunk = pl.BlockSpec((BLOCK, lanes), lambda c: (back(c), 0))
    across = pl.BlockSpec((8, BLOCK), lambda c: (0, back(c)))
    shape = lambda *sizes: jax.ShapeDtypeStruct(sizes, jnp.float32)
    return run_scan(
        scan_first_kernel,
        chunks,
        [
            part(*at["misc"], back),
            whole(bias),
            whole(rate),
            part(*at["x"], back),
            part(*at["b"], back),
        ],
        (
            shape(rows, lanes),
            shape(rows, lanes),
            shape(8, rows),
            shape(8, rows),
            shape(state_size, width),
            shape(1, lanes),
        ),
        (
            by_chunk,
            by_chunk,
            across,
            across,
            pl.BlockSpec((state_size, width), lambda c: (0, 0)),
            pl.BlockSpec((1, lanes), lambda c: (0, 0)),
        ),
        "scan_first",
    )


def chained(refs, width):
    state = jnp.zeros((refs[0].shape[0] - 16, width), jnp.float32)
    for ref in reversed(refs):
        logs = ref[-16:, :LANES].astype(jnp.float32)
        decay = jnp.exp(jnp.sum(logs[:3], axis=0, keepdims=True))
        state = ref[:-16].astype(jnp.float32) + spread_heads(decay, MIXER_HEAD_SIZE, width) * state
    return state


def scan_kernel(
    x_ref,
    z_ref,
    b_ref,
    c_ref,
    delta_ref,
    cum_ref,
    delta_row_ref,
    cum_row_ref,
    near_ref,
    next_ref,
    far_ref,
    skip_ref,
    scanned_ref,
    gated_ref,
    states_ref,
    state_ref,
):
    @pl.when(pl.program_id(0) == 0)
    def _():
        state_ref[...] = chained((near_ref, next_ref, far_ref), x_ref.shape[1])

    head_size = MIXER_HEAD_SIZE
    pair = 2 * head_size
    size, width = x_ref.shape
    state = state_ref[...]
    states_ref[0] = state
    delta, cumulative = (delta_ref[...], cum_ref[...])
    delta_row, cum_row = (delta_row_ref[...], cum_row_ref[...])
    bmat, cmat = (b_ref[...].astype(jnp.bfloat16), c_ref[...].astype(jnp.bfloat16))
    x_all = x_ref[...].astype(jnp.bfloat16)
    inner = dot_last(cmat, bmat)
    row = lax.broadcasted_iota(jnp.int32, (size, size), 0)
    column = lax.broadcasted_iota(jnp.int32, (size, size), 1)
    allowed = row >= column
    lane = lax.broadcasted_iota(jnp.int32, (size, pair), 1)
    from_state = mul(cmat, state.astype(jnp.bfloat16))
    spread = spread_heads(jnp.exp(cumulative), head_size, width)
    for first in range(0, width // head_size, 2):
        here = slice(first * head_size, first * head_size + pair)
        x_pair = x_all[:, here]
        total = from_state[:, here] * spread[:, here]
        total += skip_ref[:, here] * x_pair.astype(jnp.float32)
        for head in (first, first + 1):
            gap = cumulative[:, head : head + 1] - cum_row[head : head + 1, :]
            decay = jnp.exp(jnp.where(allowed, gap, -1e30))
            mixing = inner * decay * delta_row[head : head + 1, :]
            x_head = jnp.where((lane >= head_size) == (head > first), x_pair, 0.0)
            total += mul(mixing.astype(jnp.bfloat16), x_head.astype(jnp.bfloat16))
        scanned_ref[:, here] = total
        gate = z_ref[:, here]
        gated_ref[:, here] = (total * (gate * jax.nn.sigmoid(gate))).astype(jnp.bfloat16)
    ending = cumulative[-1:, :]
    weight = spread_heads(jnp.exp(ending - cumulative) * delta, head_size, width)
    weighted = (x_all.astype(jnp.float32) * weight).astype(jnp.bfloat16)
    state_ref[...] = state * spread[-1:, :] + dot_first(bmat, weighted)


def scan(at, delta, cumulative, delta_row, cum_row, entry, skip, after):
    rows = delta.shape[0]
    state_size, width = (at["b"][2], at["x"][2])
    chunks = rows // BLOCK
    by_chunk = pl.BlockSpec((BLOCK, width), lambda c: (c, 0))
    lanes = delta.shape[1]
    across = pl.BlockSpec((8, BLOCK), lambda c: (0, c))
    return run_scan(
        scan_kernel,
        chunks,
        [
            part(*at["x"]),
            part(*at["z"]),
            part(*at["b"]),
            part(*at["c"]),
            part(delta, 0, lanes),
            part(cumulative, 0, lanes),
            (delta_row, across),
            (cum_row, across),
            *[whole(packed) for packed in entry],
            whole(skip),
        ],
        (
            jax.ShapeDtypeStruct((rows, width), jnp.float32),
            jax.ShapeDtypeStruct((rows, width), jnp.bfloat16),
            jax.ShapeDtypeStruct((chunks, state_size, width), jnp.float32),
        ),
        (by_chunk, by_chunk, pl.BlockSpec((1, state_size, width), lambda c: (c, 0, 0))),
        "scan",
        [pltpu.VMEM((state_size, width), jnp.float32)],
        after,
    )


def scan_back_first_kernel(
    grad_ref, z_ref, scanned_ref, c_ref, cum_ref, d_scanned_ref, d_gate_ref, state_ref, log_ref
):
    @pl.when(pl.program_id(0) == 0)
    def _():
        state_ref[...] = jnp.zeros_like(state_ref)
        log_ref[...] = jnp.zeros_like(log_ref)

    gate = z_ref[...]
    chance = jax.nn.sigmoid(gate)
    grad = grad_ref[:, : z_ref.shape[1]].astype(jnp.float32)
    d_scanned = grad * (gate * chance)
    d_scanned_ref[...] = d_scanned
    d_gate_ref[...] = (
        grad * scanned_ref[...] * (chance * (1.0 + gate * (1.0 - chance)))
    ).astype(jnp.bfloat16)
    cumulative = cum_ref[...]
    decay = spread_heads(jnp.exp(cumulative + log_ref[...]), MIXER_HEAD_SIZE, z_ref.shape[1])
    state_ref[...] += dot_first(
        c_ref[...].astype(jnp.bfloat16), (d_scanned * decay).astype(jnp.bfloat16)
    )
    log_ref[...] += cumulative[-1:, :]


def scan_back_first(grads, at, scanned, cumulative):
    rows, width = scanned.shape
    state_size, lanes = (at["c"][2], cumulative.shape[1])
    by_chunk = pl.BlockSpec((BLOCK, width), lambda c: (c, 0))
    return run_scan(
        scan_back_first_kernel,
        rows // BLOCK,
        [
            part(grads, 0, grads.shape[1]),
            part(*at["z"]),
            part(scanned, 0, width),
            part(*at["c"]),
            part(cumulative, 0, lanes),
        ],
        (
            jax.ShapeDtypeStruct((rows, width), jnp.float32),
            jax.ShapeDtypeStruct((rows, width), jnp.bfloat16),
            jax.ShapeDtypeStruct((state_size, width), jnp.float32),
        ),
        (by_chunk, by_chunk, pl.BlockSpec((state_size, width), lambda c: (0, 0))),
        "scan_back_first",
        [pltpu.VMEM((1, lanes), jnp.float32)],
    )


def scan_back_kernel(
    x_ref,
    grad_ref,
    b_ref,
    c_ref,
    pre_ref,
    bias_ref,
    rate_ref,
    delta_ref,
    cum_ref,
    cum_row_ref,
    states_ref,
    near_ref,
    next_ref,
    far_ref,
    skip_ref,
    d_x_ref,
    d_b_ref,
    d_c_ref,
    d_pre_ref,
    sums_ref,
    state_ref,
):
    @pl.when(pl.program_id(0) == 0)
    def _():
        state_ref[...] = chained((near_ref, next_ref, far_ref), x_ref.shape[1])
        sums_ref[...] = jnp.zeros_like(sums_ref)

    head_size = MIXER_HEAD_SIZE
    pair = 2 * head_size
    size, width = x_ref.shape
    lanes = delta_ref.shape[1]
    low = jnp.bfloat16
    delta, cumulative, cum_row = (delta_ref[...], cum_ref[...], cum_row_ref[...])
    bmat, cmat = (b_ref[...].astype(low), c_ref[...].astype(low))
    x_all = x_ref[...].astype(low)
    x_single = x_all.astype(jnp.float32)
    grad = grad_ref[...]
    grad_low = grad.astype(low)
    state = states_ref[0]
    state_low = state.astype(low)
    after = state_ref[...]
    after_low = after.astype(low)
    ending = cumulative[-1:, :]
    row = lax.broadcasted_iota(jnp.int32, (size, size), 0)
    column = lax.broadcasted_iota(jnp.int32, (size, size), 1)
    later = column >= row
    before = (row > column).astype(low)
    onward = later.astype(low)
    lane = lax.broadcasted_iota(jnp.int32, (size, pair), 1)
    head_lane = lax.broadcasted_iota(jnp.int32, (size, lanes), 1)
    sum_heads = head_ones(width, head_size, lanes, low)

    inner = dot_last(bmat, cmat)
    from_after = mul(bmat, after_low)
    weight = jnp.exp(ending - cumulative)
    spread_weight = spread_heads(weight * delta, head_size, width)
    spread = spread_heads(jnp.exp(cumulative), head_size, width)
    to_end = mul((x_single * from_after).astype(low), sum_heads)
    through = jnp.exp(cumulative) * mul((grad * mul(cmat, state_low)).astype(low), sum_heads)
    carried = jnp.sum(state * after, axis=0, keepdims=True) * spread[-1:, :]
    carried = precise(carried, sum_heads.astype(jnp.float32))
    d_delta = weight * to_end
    d_log = (
        mul(onward, through.astype(low)) + mul(before, (d_delta * delta).astype(low)) + carried
    )

    d_inner = jnp.zeros((size, size), jnp.float32)
    for first in range(0, width // head_size, 2):
        here = slice(first * head_size, first * head_size + pair)
        x_pair, grad_pair = (x_all[:, here], grad_low[:, here])
        d_x = from_after[:, here] * spread_weight[:, here] + skip_ref[:, here] * grad[:, here]
        for head in (first, first + 1):
            mine = (lane >= head_size) == (head > first)
            gap = cum_row[head : head + 1, :] - cumulative[:, head : head + 1]
            decay = jnp.exp(jnp.where(later, gap, -1e30))
            delta_column = delta[:, head : head + 1]
            d_mixing = dot_last(jnp.where(mine, x_pair, 0.0).astype(low), grad_pair) * decay
            d_inner += d_mixing * delta_column
            flow = d_mixing * inner
            mixing = inner * decay * delta_column
            d_x += mul(mixing.astype(low), jnp.where(mine, grad_pair, 0.0).astype(low))
            d_delta_head = jnp.sum(flow, axis=1, keepdims=True)
            passing = mul(before, (flow * delta_column).astype(low))
            d_log_head = jnp.sum(jnp.where(later, passing, 0.0), axis=1, keepdims=True)
            d_delta += jnp.where(head_lane == head, d_delta_head, 0.0)
            d_log += jnp.where(head_lane == head, d_log_head, 0.0)
        d_x_ref[:, here] = d_x.astype(low)

    d_inner_low = d_inner.astype(low)
    scaled_grad = (grad * spread).astype(low)
    weighted = (x_single * spread_weight).astype(low)
    d_b_ref[...] = (mul(d_inner_low, cmat) + dot_last(weighted, after_low)).astype(low)
    d_c_ref[...] = (dot_first(d_inner_low, bmat) + dot_last(scaled_grad, state_low)).astype(low)
    state_ref[...] = after * spread[-1:, :] + dot_first(cmat, scaled_grad)
    rate = rate_ref[...]
    d_pre = (d_delta - d_log * rate) * jax.nn.sigmoid(pre_ref[...] + bias_ref[...])
    d_pre = jnp.where(head_lane < width // head_size, d_pre, 0.0)
    d_pre_ref[...] = d_pre.astype(low)
    skip_sum = precise(
        jnp.sum(grad * x_single, axis=0, keepdims=True), sum_heads.astype(jnp.float32)
    )
    sums_ref[0:1, :] += jnp.sum(d_pre, axis=0, keepdims=True)
    sums_ref[1:2, :] += jnp.sum(d_log * (-delta * rate), axis=0, keepdims=True)
    sums_ref[2:3, :] += skip_sum


def scan_back(
    at, d_scanned, bias, rate, delta, cumulative, cum_row, states, entry, skip, after
):
    rows, width = d_scanned.shape
    state_size, lanes = (at["b"][2], delta.shape[1])
    chunks = rows // BLOCK
    back = lambda c: chunks - 1 - c
    by_chunk = lambda columns: pl.BlockSpec((BLOCK, columns), lambda c: (back(c), 0))
    shape = lambda columns: jax.ShapeDtypeStruct((rows, columns), jnp.bfloat16)
    return run_scan(
        scan_back_kernel,
        chunks,
        [
            part(in_hbm(at["x"][0]), *at["x"][1:], back),
            part(in_hbm(d_scanned), 0, width, back),
            part(in_hbm(at["b"][0]), *at["b"][1:], back),
            part(in_hbm(at["c"][0]), *at["c"][1:], back),
            part(in_hbm(at["misc"][0]), *at["misc"][1:], back),
            whole(bias),
            whole(rate),
            part(in_hbm(delta), 0, lanes, back),
            part(in_hbm(cumulative), 0, lanes, back),
            (in_hbm(cum_row), pl.BlockSpec((8, BLOCK), lambda c: (0, back(c)))),
            (in_hbm(states), pl.BlockSpec((1, state_size, width), lambda c: (back(c), 0, 0))),
            *[whole(in_hbm(packed)) for packed in entry],
            whole(skip),
        ],
        (
            shape(width),
            shape(state_size),
            shape(state_size),
            shape(lanes),
            jax.ShapeDtypeStruct((8, lanes), jnp.float32),
        ),
        (
            by_chunk(width),
            by_chunk(state_size),
            by_chunk(state_size),
            by_chunk(lanes),
            pl.BlockSpec((8, lanes), lambda c: (0, 0)),
        ),
        "scan_back",
        [pltpu.VMEM((state_size, width), jnp.float32)],
        after,
        44,
    )


def on_heads(value, move):
    devices = lax.axis_size("heads")
    pairs = []
    for at in range(devices):
        z, core = move(at // 2, at % 2)
        pairs.append((at, 2 * (z % (devices // 2)) + core))
    return lax.ppermute(value, "heads", pairs)


def to_partner(value):
    return on_heads(value, lambda z, core: (z, 1 - core))


def along(value):
    return on_heads(value, lambda z, core: (z + 1 - 2 * core, core))


def against(value):
    return on_heads(value, lambda z, core: (z - 1 + 2 * core, core))


def chunk_ranks():
    devices = lax.axis_size("heads")
    z, core = (lax.axis_index("heads") // 2, lax.axis_index("heads") % 2)
    step, other = (1 - 2 * core, 1 - core)
    owners = (
        (z, core),
        (z + 2, core),
        (z - step, core),
        (z - step, other),
        (z, other),
        (z + 2, other),
        (z + step, other),
        (z + step, core),
    )
    return jnp.stack([2 * ((at + devices) % (devices // 2)) + side for at, side in owners])


def against_other(value):
    return on_heads(value, lambda z, core: (z - 1 + 2 * core, 1 - core))


def gather_rows(own, joined=False):
    partner = to_partner(own)
    near = along(own)
    near_other = along(partner)
    far = along(near)
    last = to_partner(near_other)
    mine = (own, far, near, near_other)
    theirs = (partner, to_partner(far), to_partner(near), last)
    rows = join(mine + theirs) if joined else jnp.concatenate(mine + theirs, axis=0)
    return rows, last


def scatter_rows(product, half, late=None):
    chunk = half // 4
    got = to_partner(product(slice(half, 2 * half)).astype(jnp.bfloat16))
    kept = lax.optimization_barrier(product(slice(0, half)))

    summed = kept + got.astype(jnp.float32)
    low = summed[chunk:].astype(jnp.bfloat16)
    far = against(low[:chunk])
    near_other = against_other(low[2 * chunk :])
    near = low[chunk : 2 * chunk].astype(jnp.float32) + far.astype(jnp.float32)
    near = against(near.astype(jnp.bfloat16))
    total = summed[:chunk] + near.astype(jnp.float32) + near_other.astype(jnp.float32)
    return total if late is None else total + late


def across(value, bit):
    devices = lax.axis_size("heads")
    return lax.ppermute(value, "heads", [(at, at ^ bit) for at in range(devices)])


def gather_small(value):
    for bit in (1, 2, 4):
        value = jnp.concatenate([value, across(value, bit)], axis=0)
    return value


def scatter_small(value):
    for bit in (4, 2, 1):
        half = value.shape[0] // 2
        got = across(value[half:].astype(jnp.bfloat16), bit)
        value = value[:half].astype(jnp.float32) + got.astype(jnp.float32)
    return value


def on_blocks(value, step):
    devices = lax.axis_size("blk")
    pairs = [(at, at + step) for at in range(devices) if 0 <= at + step < devices]
    return lax.ppermute(value, "blk", pairs)


def from_earlier(value, step=1):
    return tuple(on_blocks(value, distance * step) for distance in (1, 2, 3))


def pack_state(state, log_total):
    high = log_total.astype(jnp.bfloat16)
    rest = log_total - high.astype(jnp.float32)
    middle = rest.astype(jnp.bfloat16)
    low = (rest - middle.astype(jnp.float32)).astype(jnp.bfloat16)
    logs = jnp.concatenate([high, middle, low], axis=0)
    logs = jnp.pad(logs, ((0, 16 - logs.shape[0]), (0, state.shape[1] - logs.shape[1])))
    return jnp.concatenate([state.astype(jnp.bfloat16), logs], axis=0)


def sum_blocks(value):
    for axis in ("dp", "blk"):
        for bit in (1, 2):
            value = value + lax.ppermute(
                value, axis, [(at, at ^ bit) for at in range(lax.axis_size(axis))]
            )
    return value


def weight_sum(grads):
    return lax.psum_scatter(grads, ("dp", "blk"), scatter_dimension=0, tiled=True)


def split_columns(value_in, widths):
    pieces, start = [], 0
    for width in widths:
        pieces.append(value_in[:, start : start + width])
        start += width
    return pieces


def inverse_rms(rows_in):
    return lax.rsqrt(jnp.mean(rows_in * rows_in, axis=-1, keepdims=True) + norm_eps)


def norm_back(rows_in, gain_in, cotangent):
    inverse = inverse_rms(rows_in)
    scaled = rows_in * inverse
    weighted = cotangent * gain_in
    return inverse * (weighted - scaled * jnp.mean(weighted * scaled, axis=-1, keepdims=True))


def shards(
    x_in,
    out_grad,
    norm_one,
    w_query,
    w_key,
    w_value,
    output_gate_weight,
    mixer_input_weight,
    w_delta,
    w_bmat,
    w_cmat,
    delta_bias,
    decay_log,
    skip_gain,
    w_attn_out,
    mixer_output_weight,
    norm_two,
    w_gate,
    w_up,
    w_down,
):
    heads_count = lax.axis_size("heads")
    head_rank = lax.axis_index("heads")
    core = head_rank % 2
    block_rank = lax.axis_index("blk")
    rank = block_rank.astype(jnp.int32)[None]
    own_rows = x_in.shape[0]
    span_length = own_rows * heads_count
    half_span = span_length // 2
    span_start = block_rank * span_length
    query_width = w_query.shape[1]
    mixer_width = mixer_input_weight.shape[1]
    heads = mixer_width // MIXER_HEAD_SIZE
    state_size = w_bmat.shape[1]
    hidden_width = w_gate.shape[1]
    rows_of = w_query.shape[0]
    kv_index = head_rank * (query_width // HD) // (QH // KVH)
    kv_width = KVH * HD
    low = jnp.bfloat16
    ranks = chunk_ranks().astype(jnp.int32)
    turns = (head_rank ^ jnp.arange(heads_count)).astype(jnp.int32)

    gains = jnp.stack([norm_one, norm_two], axis=1)
    gains = jnp.pad(gains, ((0, 0), (heads, LANES - heads - 2)))
    shared = pack((w_key, w_value, w_bmat, w_cmat, gains), (False,) * 5)
    delta_wide = jnp.pad(w_delta, ((0, 0), (0, LANES - heads)))
    in_names = ("z", "x", "query", "b", "c", "misc", "key", "value")
    in_widths = (mixer_width, mixer_width, query_width, state_size, state_size, LANES, HD, HD)
    in_width = sum(in_widths)
    starts = [sum(in_widths[:k]) for k in range(len(in_widths))]
    at = dict(zip(in_names, zip(starts, in_widths)))
    mix_at = {
        "ssm_out": (in_width, mixer_width),
        "attn_out": (in_width + mixer_width, query_width),
    }
    first_own = pack_first(
        turns,
        kv_index.astype(jnp.int32)[None],
        gather_small(shared),
        delta_wide,
        [output_gate_weight, mixer_input_weight, w_query, mixer_output_weight, w_attn_out],
        at | mix_at,
    )
    gain_part = first_own[:, at["misc"][0] + heads : at["misc"][0] + heads + 2]
    first_full = lax.all_gather(first_own, ("dp", "blk"), axis=0, tiled=True)
    in_full, mix_t = (first_full[:, :in_width], first_full[:, in_width:])
    x_float = x_in.astype(jnp.float32)
    zero = 0.0 * first_own[0, 0]
    x_span, _ = gather_rows(x_in + zero, joined=True)
    ffn_grad, _ = gather_rows(out_grad + zero, joined=True)
    ffn_own = pack((w_gate, w_up, w_down), (False, False, True), [corner(x_span)])
    ffn_full = lax.all_gather(ffn_own, ("dp", "blk"), axis=0, tiled=True)
    mixed_width = query_width + mixer_width
    gate_full, up_full, down_t = split_columns(ffn_full, (hidden_width,) * 3)
    positions = (span_start + jnp.arange(span_length)).astype(jnp.float32)
    freqs = rope_base ** (-2.0 * jnp.arange(HD // 2, dtype=jnp.float32) / HD)
    angles = positions[:, None] * freqs[None, :]
    cosine, sine = (jnp.cos(angles), jnp.sin(angles))
    cosine = jnp.concatenate([cosine, cosine], axis=1)
    sine = jnp.concatenate([-sine, sine], axis=1)
    normed_ordered, queries, keys_values, gain_rows = enter(
        ranks, jnp.full((1,), heads, jnp.int32), x_span, first_full, at, cosine, sine, [corner(ffn_own), corner(ffn_grad)]
    )
    gain_one, gain_two = (gain_rows[0:1], gain_rows[1:2])
    mine = lax.dynamic_slice_in_dim(keys_values, core * half_span, half_span, 0)
    pieces = []
    for piece in from_earlier(mine):
        pieces += [piece, to_partner(piece)]
    gate_raw = simple_product(normed_ordered, in_full[:, :mixer_width])
    x_raw = simple_product(normed_ordered, in_full[:, mixer_width : 2 * mixer_width])
    state_raw = simple_product(normed_ordered, in_full[:, at["b"][0] : at["key"][0]])
    raw = {
        "z": (gate_raw, 0, mixer_width),
        "x": (x_raw, 0, mixer_width),
        "b": (state_raw, 0, state_size),
        "c": (state_raw, state_size, state_size),
        "misc": (state_raw, 2 * state_size, LANES),
    }

    pad_lanes = lambda vector: jnp.pad(vector, (0, LANES - heads))[None]
    bias, rate = (pad_lanes(delta_bias), pad_lanes(jnp.exp(decay_log)))
    skip = jnp.repeat(skip_gain, MIXER_HEAD_SIZE)[None]
    delta, cumulative, delta_row, cum_row, local_state, local_log = scan_first(raw, bias, rate)
    entry_states = from_earlier(pack_state(local_state, local_log))
    attended, attn_part, log_totals = attend(rank, queries, keys_values, pieces)
    scanned, gated, states = scan(
        raw, delta, cumulative, delta_row, cum_row, entry_states, skip, [corner(attn_part)]
    )
    mixers = reorder(ranks, [gated, attn_part])
    ffn_zero = 0.0 * ffn_full[0, 0].astype(jnp.float32)
    mixed = scatter_rows(lambda rows: dot_last(mixers[rows], mix_t), half_span, ffn_zero)
    middle = x_float + mixed
    middle_scaled = middle * inverse_rms(middle)
    normed_two, _ = gather_rows((middle_scaled * gain_two).astype(low))
    ffn_gate = simple_product(normed_two, gate_full)
    ffn_up = simple_product(normed_two, up_full)
    ffn_sig = jax.nn.sigmoid(ffn_gate)
    hidden = (ffn_gate * ffn_sig * ffn_up).astype(low)

    d_hidden = simple_product(ffn_grad, down_t)
    d_ffn_gate = (d_hidden * ffn_up * (ffn_sig * (1.0 + ffn_gate * (1.0 - ffn_sig)))).astype(low)
    d_ffn_up = (d_hidden * (ffn_gate * ffn_sig)).astype(low)
    d_normed_two = scatter_rows(
        lambda rows: dot_last(d_ffn_gate[rows], gate_full) + dot_last(d_ffn_up[rows], up_full),
        half_span,
    )
    d_middle = out_grad.astype(jnp.float32) + norm_back(middle, gain_two, d_normed_two)
    mix_grad, mix_last = gather_rows(d_middle.astype(low))
    ffn_grads = weight_grads(
        [(normed_two, [d_ffn_gate, d_ffn_up]), (ffn_grad, [hidden])],
        3 * hidden_width,
        after=[corner(mix_last)],
    )
    ffn_sums = weight_sum(ffn_grads).astype(jnp.float32)
    grad_gate, grad_up, grad_down_t = split_columns(ffn_sums, (hidden_width,) * 3)
    grad_two_part = jnp.sum(grad_gate * w_gate + grad_up * w_up, axis=1, keepdims=True)
    gain_own = gain_part.astype(jnp.float32)
    grad_two_part = grad_two_part / gain_own[:, 1:2]
    d_mixers = reorder(
        ranks, [simple_product(mix_grad, mix_t).astype(low)], inverse=True, after=[corner(ffn_grads)]
    )
    d_scanned, d_gate_z, d_entry = scan_back_first(d_mixers, raw, scanned, cumulative)
    d_entry = pack_state(d_entry, local_log)
    after_states = from_earlier(d_entry, -1)
    mix_width = mixed_width + mixer_width
    all_width = mixed_width + in_width
    mix_grads = weight_grads(
        [(mix_grad, [mixers]), (normed_ordered, [d_gate_z])], all_width, after=[corner(d_entry)]
    )
    d_query, d_own, d_far = attend_back(
        rank, queries, keys_values, pieces, attended, log_totals, d_mixers, cosine, sine, [corner(mix_grads), *map(corner, after_states)]
    )
    d_ssm_in, d_bmat, d_cmat, d_pre, sums = scan_back(
        raw,
        d_scanned,
        bias,
        rate,
        delta,
        cumulative,
        cum_row,
        states,
        after_states,
        skip,
        [corner(d_query)],
    )
    far_half = d_far.shape[0] // 2
    d_mine = lax.dynamic_slice_in_dim(d_own, core * half_span, half_span, 0)
    d_theirs = lax.dynamic_slice_in_dim(d_own, (1 - core) * half_span, half_span, 0)
    d_mine = d_mine + to_partner(d_theirs.astype(low)).astype(jnp.float32)
    d_far = d_far[:far_half].astype(jnp.float32) + to_partner(d_far[far_half:]).astype(jnp.float32)
    d_one, d_two, d_three = (
        d_far[k * half_span : (k + 1) * half_span] for k in range(d_far.shape[0] // half_span)
    )
    scan_zero = 0.0 * d_pre[0, 0].astype(jnp.float32)
    d_one = d_one + on_blocks(d_two.astype(low), -1).astype(jnp.float32) + scan_zero
    d_mine = d_mine + on_blocks(d_one.astype(low), -1).astype(jnp.float32)
    d_mine = d_mine + on_blocks(d_three.astype(low), -3).astype(jnp.float32)
    half_cos = lax.dynamic_slice_in_dim(cosine, core * half_span, half_span, 0)
    half_sin = lax.dynamic_slice_in_dim(sine, core * half_span, half_span, 0)
    d_key = d_mine[:, :HD]
    d_key = d_key * half_cos - jnp.roll(d_key, HD // 2, axis=1) * half_sin
    d_mine = jnp.concatenate([d_key, d_mine[:, HD:]], axis=1).astype(low)
    d_keys_values = lax.dynamic_update_slice_in_dim(
        jnp.zeros((span_length, 2 * HD), low), d_mine, core * half_span, 0
    )

    scan_rights = [d_ssm_in, d_bmat, d_cmat, d_pre]
    in_grads = weight_grads([(normed_ordered, scan_rights)], all_width, mix_width, mix_grads)
    late_rights = [d_keys_values, d_query]
    late_start = mix_width + sum(array.shape[1] for array in scan_rights)
    in_grads = weight_grads([(normed_ordered, late_rights)], all_width, late_start, in_grads)
    in_sums = weight_sum(in_grads)
    d_projected = reorder(
        ranks,
        [d_gate_z, d_ssm_in, d_query, d_bmat, d_cmat, d_pre, d_keys_values],
        after=[corner(in_grads)],
    )
    d_normed = scatter_rows(lambda rows: dot_last(d_projected[rows], in_full), half_span)
    input_grad = d_middle + norm_back(x_float, gain_one, d_normed)
    back_zero = 0.0 * d_query[0, 0].astype(jnp.float32)
    ffn_out = scatter_rows(
        lambda rows: dot_last(hidden[rows], down_t) + back_zero, half_span
    )
    activations = (middle + ffn_out).astype(low)
    sums_names = ("ssm_out", "attn_out", "z", "x", "b", "c", "misc", "key", "value", "query")
    sums_widths = [mixer_width, query_width] + [at[name][1] for name in sums_names[2:]]
    sums_starts = [sum(sums_widths[:k]) for k in range(len(sums_widths))]
    sums_at = dict(zip(sums_names, zip(sums_starts, sums_widths)))
    extra = jnp.concatenate([gain_own[:, 0:1], grad_two_part], axis=1)
    extra = jnp.pad(extra, ((0, 0), (0, LANES - 2)))
    grad_ssm_out, grad_attn_out, grad_gatez, grad_ssmx, grad_query, misc_sums, shared_parts = finish(
        turns,
        kv_index.astype(jnp.int32)[None],
        in_sums,
        first_own,
        extra,
        at,
        sums_at,
    )
    shared_sums = scatter_small(shared_parts)
    grad_key, grad_value, grad_bmat, grad_cmat, gain_sums = split_columns(
        shared_sums, (kv_width, kv_width, state_size, state_size, LANES)
    )
    small_sums = sum_blocks(sums)[:, :heads]
    return (
        activations,
        input_grad,
        gain_sums[:, 0],
        grad_query,
        grad_key,
        grad_value,
        grad_gatez,
        grad_ssmx,
        misc_sums[:, :heads],
        grad_bmat,
        grad_cmat,
        small_sums[0],
        small_sums[1],
        small_sums[2],
        grad_attn_out,
        grad_ssm_out,
        gain_sums[:, 1],
        grad_gate,
        grad_up,
        grad_down_t.T,
    )


def solution(mesh):
    placed = (
        P(("dp", "blk", "heads"), None),
        P(("dp", "blk", "heads"), None),
        P(("dp", "blk", "heads")),
        P(("dp", "blk"), "heads"),
        P(("dp", "blk", "heads"), None),
        P(("dp", "blk", "heads"), None),
        P(("dp", "blk"), "heads"),
        P(("dp", "blk"), "heads"),
        P(("dp", "blk"), "heads"),
        P(("dp", "blk", "heads"), None),
        P(("dp", "blk", "heads"), None),
        P("heads"),
        P("heads"),
        P("heads"),
        P("heads", ("dp", "blk")),
        P("heads", ("dp", "blk")),
        P(("dp", "blk", "heads")),
        P(("dp", "blk"), "heads"),
        P(("dp", "blk"), "heads"),
        P("heads", ("dp", "blk")),
    )
    return jax.shard_map(
        shards,
        mesh=mesh,
        in_specs=placed,
        out_specs=(
            P(("dp", "blk", "heads"), None),
            P(("dp", "blk", "heads"), None),
            P(("dp", "blk", "heads")),
            P(("dp", "blk"), "heads"),
            P(("dp", "blk", "heads"), None),
            P(("dp", "blk", "heads"), None),
            P(("dp", "blk"), "heads"),
            P(("dp", "blk"), "heads"),
            P(("dp", "blk"), "heads"),
            P(("dp", "blk", "heads"), None),
            P(("dp", "blk", "heads"), None),
            P("heads"),
            P("heads"),
            P("heads"),
            P("heads", ("dp", "blk")),
            P("heads", ("dp", "blk")),
            P(("dp", "blk", "heads")),
            P(("dp", "blk"), "heads"),
            P(("dp", "blk"), "heads"),
            P("heads", ("dp", "blk")),
        ),
        check_vma=False,
    )
```

```python
import functools

import jax
import jax.numpy as jnp
from jax import lax
from jax.experimental import pallas as pl
from jax.experimental.pallas import tpu as pltpu
from jax.sharding import PartitionSpec as P

QH = 8
KVH = 2
HD = 128
MIXER_HEAD_SIZE = 64
BLOCK = 256
LANES = 128
LOG2_E = 1.4426950408889634


HIGH_PRECISION = lax.Precision.HIGHEST
norm_eps = 1e-05
rope_base = 100000000000.0


def simple_product(left_side, right_side):
    return jnp.dot(left_side, right_side, preferred_element_type=jnp.float32)


def dot_last(left_side, right_side):
    return lax.dot_general(
        left_side, right_side, (((1,), (1,)), ((), ())), preferred_element_type=jnp.float32
    )


def dot_first(left_side, right_side):
    return lax.dot_general(
        left_side, right_side, (((0,), (0,)), ((), ())), preferred_element_type=jnp.float32
    )


def compiler_params(mebibytes=20):
    return pltpu.CompilerParams(vmem_limit_bytes=mebibytes * 1024 * 1024)


def small_cost():
    return pl.CostEstimate(flops=1000, bytes_accessed=1000, transcendentals=0)


def in_hbm(value):
    return pltpu.with_memory_space_constraint(value, pltpu.HBM)


def corner(value):
    return value[:16, :LANES]


def in_vmem(count):
    return [pl.BlockSpec(memory_space=pltpu.VMEM)] * count


def mul(left_side, right_side):
    return jnp.dot(left_side, right_side, preferred_element_type=jnp.float32)


def tile_scores(key_rows, query_rows, head_size):
    return dot_last(key_rows, query_rows) * (head_size**-0.5 * LOG2_E)


def causal(scores):
    key_at = lax.broadcasted_iota(jnp.int32, scores.shape, 0)
    query_at = lax.broadcasted_iota(jnp.int32, scores.shape, 1)
    return jnp.where(key_at <= query_at, scores, -1e30)


def enter_kernel(
    ranks_ref, heads_ref, x_ref, misc_ref, key_ref, value_ref, w_query_ref, cos_ref, sin_ref, *refs
):
    ordered_ref, query_ref, kv_ref, gains_ref = refs[-4:]
    head_size = query_ref.shape[1]

    @pl.when(pl.program_id(0) == 0)
    def _():
        lane = lax.broadcasted_iota(jnp.int32, misc_ref.shape, 1)
        for k in range(2):
            column = jnp.where(lane == heads_ref[0] + k, misc_ref[...].astype(jnp.float32), 0.0)
            gains_ref[k : k + 1, :] = jnp.sum(column.T, axis=0, keepdims=True)

    cosine, sine = (cos_ref[...], sin_ref[...])

    def turn(value):
        return (value * cosine + pltpu.roll(value, head_size // 2, 1) * sine).astype(jnp.bfloat16)

    rows = x_ref[...].astype(jnp.float32)
    normed = (rows * inverse_rms(rows) * gains_ref[0:1, :]).astype(jnp.bfloat16)
    ordered_ref[...] = normed
    kv_ref[:, :head_size] = turn(mul(normed, key_ref[...]))
    kv_ref[:, head_size:] = mul(normed, value_ref[...]).astype(jnp.bfloat16)
    query_ref[...] = turn(mul(normed, w_query_ref[...]))


def enter(ranks, heads, x_span, in_full, at, cosine, sine, after):
    count = ranks.shape[0]
    rows, width = x_span.shape
    head_size = cosine.shape[1]
    here = lambda columns: pl.BlockSpec((rows // count, columns), lambda k, r, h: (k, 0))
    there = lambda columns: pl.BlockSpec((rows // count, columns), lambda k, r, h: (r[k], 0))
    weight = lambda name: pl.BlockSpec(
        (width, at[name][1]), lambda k, r, h: (0, at[name][0] // at[name][1])
    )
    return pl.pallas_call(
        enter_kernel,
        grid_spec=pltpu.PrefetchScalarGridSpec(
            num_scalar_prefetch=2,
            grid=(count,),
            in_specs=[
                here(width),
                weight("misc"),
                weight("key"),
                weight("value"),
                weight("query"),
                there(head_size),
                there(head_size),
            ]
            + [pl.BlockSpec(memory_space=pl.ANY)] * len(after),
            out_specs=(
                there(width),
                there(head_size),
                there(2 * head_size),
                pl.BlockSpec((8, width), lambda k, r, h: (0, 0)),
            ),
        ),
        out_shape=(
            jax.ShapeDtypeStruct((rows, width), jnp.bfloat16),
            jax.ShapeDtypeStruct((rows, head_size), jnp.bfloat16),
            jax.ShapeDtypeStruct((rows, 2 * head_size), jnp.bfloat16),
            jax.ShapeDtypeStruct((8, width), jnp.float32),
        ),
        compiler_params=compiler_params(),
        cost_estimate=small_cost(),
        name="enter",
    )(ranks, heads, in_hbm(x_span), *[in_hbm(in_full)] * 4, cosine, sine, *after)


def weight_grads_kernel(*refs, counts):
    out_ref = refs[-1]
    start, used = (0, len(counts))
    for k, count in enumerate(counts):
        left = refs[k][...].T
        for ref in refs[used : used + count]:
            out_ref[:, start : start + ref.shape[1]] = mul(left, ref[...]).astype(jnp.bfloat16)
            start += ref.shape[1]
        used += count


def weight_grads(groups, width, start=0, buffer=None, after=()):
    rights = [right for _, group in groups for right in group]
    columns = sum(right.shape[1] for right in rights)
    depth = rights[0].shape[0]
    rows = groups[0][0].shape[1]
    operands = [left for left, _ in groups] + rights
    count = len(operands)
    extra = list(after) if buffer is None else [buffer] + list(after)

    def call(*refs):
        weight_grads_kernel(
            *refs[:count],
            refs[-1],
            counts=tuple(len(group) for _, group in groups),
        )

    return pl.pallas_call(
        call,
        grid=(rows // BLOCK,),
        out_shape=pltpu.HBM((rows, width), jnp.bfloat16),
        in_specs=[pl.BlockSpec((depth, BLOCK), lambda k: (0, k)) for _ in groups]
        + [pl.BlockSpec(right.shape, lambda k: (0, 0)) for right in rights]
        + [pl.BlockSpec(memory_space=pl.ANY)] * len(extra),
        out_specs=pl.BlockSpec(
            (pl.Element(BLOCK), pl.Element(columns)), lambda k: (k * BLOCK, start)
        ),
        input_output_aliases={} if buffer is None else {count: 0},
        compiler_params=compiler_params(),
        cost_estimate=small_cost(),
        name="weight_grads",
    )(*operands, *extra)


def pack_kernel(*refs, turned):
    out_ref = refs[-1]
    start = 0
    for ref, turn in zip(refs, turned):
        piece = ref[...].T if turn else ref[...]
        out_ref[:, start : start + piece.shape[1]] = piece
        start += piece.shape[1]


def pack(pieces, turned, after=()):
    sizes = [piece.shape[::-1] if turn else piece.shape for piece, turn in zip(pieces, turned)]
    return pl.pallas_call(
        functools.partial(pack_kernel, turned=turned),
        out_shape=jax.ShapeDtypeStruct(
            (sizes[0][0], sum(size[1] for size in sizes)), jnp.bfloat16
        ),
        in_specs=in_vmem(len(pieces)) + [pl.BlockSpec(memory_space=pl.ANY)] * len(after),
        out_specs=pl.BlockSpec(memory_space=pltpu.VMEM),
        compiler_params=compiler_params(),
        cost_estimate=small_cost(),
        name="pack",
    )(*map(in_hbm, pieces), *after)


def join_kernel(*refs):
    out_ref = refs[-1]
    start = 0
    for ref in refs[:-1]:
        out_ref[start : start + ref.shape[0], :] = ref[...]
        start += ref.shape[0]


def join(pieces):
    rows = sum(piece.shape[0] for piece in pieces)
    return pl.pallas_call(
        join_kernel,
        out_shape=jax.ShapeDtypeStruct((rows, pieces[0].shape[1]), pieces[0].dtype),
        in_specs=in_vmem(len(pieces)),
        out_specs=pl.BlockSpec(memory_space=pltpu.VMEM),
        compiler_params=compiler_params(),
        cost_estimate=small_cost(),
        name="join",
    )(*pieces)


def pack_first_kernel(
    turns_ref, kv_ref, shared_ref, delta_ref, z_ref, x_ref, query_ref, ssm_ref, attn_ref, out_ref, *, at
):
    def put(name, value, rows=slice(None)):
        start, size = at[name]
        out_ref[rows, start : start + size] = value

    put("z", z_ref[...])
    put("x", x_ref[...])
    put("query", query_ref[...])
    put("ssm_out", ssm_ref[...].T)
    put("attn_out", attn_ref[...].T)
    count = turns_ref.shape[0]
    size = shared_ref.shape[0] // count
    first = kv_ref[0] == 0
    for k in range(count):
        rows = pl.ds(pl.multiple_of(turns_ref[k] * size, size), size)
        chunk = shared_ref[k * size : (k + 1) * size, :]
        pieces, start = [], 0
        for width in (HD, HD, HD, HD, at["b"][1], at["c"][1], LANES):
            pieces.append(chunk[:, start : start + width])
            start += width
        put("key", jnp.where(first, pieces[0], pieces[1]), rows)
        put("value", jnp.where(first, pieces[2], pieces[3]), rows)
        put("b", pieces[4], rows)
        put("c", pieces[5], rows)
        put("misc", pieces[6] + delta_ref[rows, :], rows)


def pack_first(turns, kv_index, shared, delta, weights, at):
    rows = shared.shape[0]
    return pl.pallas_call(
        functools.partial(pack_first_kernel, at=at),
        out_shape=jax.ShapeDtypeStruct(
            (rows, max(start + size for start, size in at.values())), jnp.bfloat16
        ),
        in_specs=[pl.BlockSpec(memory_space=pltpu.SMEM)] * 2 + in_vmem(2 + len(weights)),
        out_specs=pl.BlockSpec(memory_space=pltpu.VMEM),
        compiler_params=compiler_params(50),
        cost_estimate=small_cost(),
        name="pack_first",
    )(turns, kv_index, shared, delta, *map(in_hbm, weights))


def finish_kernel(
    ranks_ref,
    kv_ref,
    sums_ref,
    weight_ref,
    extra_ref,
    ssm_out_ref,
    attn_out_ref,
    gate_ref,
    ssm_ref,
    query_ref,
    misc_ref,
    shared_ref,
    whole_ref,
    *,
    at,
    sums_at,
):
    def of(name):
        start, size = sums_at[name]
        return sums_ref[:, start : start + size].astype(jnp.float32)

    ssm_out_ref[...] = of("ssm_out").T
    attn_out_ref[...] = of("attn_out").T
    gate_ref[...] = of("z")
    ssm_ref[...] = of("x")
    query_ref[...] = of("query")
    misc_ref[...] = of("misc")
    total = 0.0
    for name, (start, size) in at.items():
        product = of(name) * weight_ref[:, start : start + size].astype(jnp.float32)
        total += jnp.sum(product, axis=1, keepdims=True)
    total = total / extra_ref[:, 0:1]
    lane = lax.broadcasted_iota(jnp.int32, misc_ref.shape, 1)
    gains = jnp.where(lane == 0, total, jnp.where(lane == 1, extra_ref[:, 1:2], 0.0))
    zero = jnp.zeros_like(gains)
    first = kv_ref[0] == 0
    key, value = (of("key"), of("value"))
    pieces = (
        jnp.where(first, key, zero),
        jnp.where(first, zero, key),
        jnp.where(first, value, zero),
        jnp.where(first, zero, value),
        of("b"),
        of("c"),
        gains,
    )
    start = 0
    for piece in pieces:
        whole_ref[:, start : start + piece.shape[1]] = piece
        start += piece.shape[1]
    count = ranks_ref.shape[0]
    size = shared_ref.shape[0] // count
    for k in range(count):
        rows = pl.ds(pl.multiple_of(ranks_ref[k] * size, size), size)
        shared_ref[k * size : (k + 1) * size, :] = whole_ref[rows, :].astype(jnp.bfloat16)


def finish(ranks, kv_index, sums, weights, extra, at, sums_at):
    rows = weights.shape[0]
    shape = lambda *sizes: jax.ShapeDtypeStruct(sizes, jnp.float32)
    width = lambda name: sums_at[name][1]
    shared = 2 * (width("key") + width("value")) + width("b") + width("c") + LANES
    return pl.pallas_call(
        functools.partial(finish_kernel, at=at, sums_at=sums_at),
        out_shape=(
            shape(width("ssm_out"), rows),
            shape(width("attn_out"), rows),
            shape(rows, width("z")),
            shape(rows, width("x")),
            shape(rows, width("query")),
            shape(rows, width("misc")),
            jax.ShapeDtypeStruct((rows, shared), jnp.bfloat16),
        ),
        in_specs=[pl.BlockSpec(memory_space=pltpu.SMEM)] * 2 + in_vmem(3),
        out_specs=tuple(in_vmem(7)),
        scratch_shapes=[pltpu.VMEM((rows, shared), jnp.float32)],
        compiler_params=compiler_params(),
        name="finish",
    )(ranks, kv_index, sums, weights, extra)


def attend_kernel(rank_ref, query_ref, own_ref, *refs):
    pieces, (out_ref, low_ref, log_ref) = (refs[:-3], refs[-3:])
    span_length, head_size = query_ref.shape
    tile = own_ref.shape[0] // 2
    for block in range(span_length // tile):
        here = slice(block * tile, (block + 1) * tile)
        query_rows = query_ref[here, :]

        def step(kv_rows, carried, masked=False):
            top, total, summed = carried
            scores = tile_scores(kv_rows[:, :head_size], query_rows, head_size)
            if masked:
                scores = causal(scores)
            new_top = jnp.maximum(top, jnp.max(scores, axis=0, keepdims=True))
            probs = jnp.exp2(scores - new_top)
            scale = jnp.exp2(top - new_top)
            total = total * scale + jnp.sum(probs, axis=0, keepdims=True)
            summed = summed * scale + dot_first(kv_rows[:, head_size:], probs.astype(jnp.bfloat16))
            return (new_top, total, summed)

        carried = (
            jnp.full((1, tile), -1e30, jnp.float32),
            jnp.zeros((1, tile), jnp.float32),
            jnp.zeros((head_size, tile), jnp.float32),
        )
        carried = step(own_ref[here, :], carried, True)
        for earlier in range(block):
            carried = step(own_ref[earlier * tile : (earlier + 1) * tile, :], carried)
        for distance in range(1, 1 + len(pieces) // 2):
            pair = pieces[2 * distance - 2 : 2 * distance]

            def both(_, carried, pair=pair):
                return step(pair[1][...], step(pair[0][...], carried))

            valid = (rank_ref[0] >= distance).astype(jnp.int32)
            carried = lax.fori_loop(0, valid, both, carried)
        top, total, summed = carried
        result = summed / total
        out_ref[:, here] = result
        low_ref[here, :] = result.T.astype(jnp.bfloat16)
        log_ref[:, here] = top + jnp.log2(total)


def attend(rank, queries, own, pieces):
    span_length, head_size = queries.shape
    return pl.pallas_call(
        attend_kernel,
        out_shape=(
            jax.ShapeDtypeStruct((head_size, span_length), jnp.float32),
            jax.ShapeDtypeStruct((span_length, head_size), jnp.bfloat16),
            jax.ShapeDtypeStruct((1, span_length), jnp.float32),
        ),
        in_specs=[pl.BlockSpec(memory_space=pltpu.SMEM)] + in_vmem(2 + len(pieces)),
        out_specs=tuple(in_vmem(3)),
        compiler_params=compiler_params(),
        cost_estimate=small_cost(),
        name="attend",
    )(rank, queries, own, *pieces)


def attend_back_kernel(rank_ref, query_ref, own_ref, *refs):
    pieces, refs = (refs[:-13], refs[-13:])
    out_ref, log_ref, grad_ref, cos_ref, sin_ref, *_, d_query_ref, d_own_ref, d_far_ref, sums_ref = refs
    span_length, head_size = query_ref.shape
    tile = own_ref.shape[0] // 2
    score_scale = head_size**-0.5
    sums_ref[...] = jnp.zeros_like(sums_ref)
    for block in range(span_length // tile):
        here = slice(block * tile, (block + 1) * tile)
        query_rows = query_ref[here, :]
        grad_rows = grad_ref[here, grad_ref.shape[1] - head_size :]
        log_total = log_ref[:, here]
        delta_row = jnp.sum(
            grad_rows.astype(jnp.float32).T * out_ref[:, here], axis=0, keepdims=True
        )

        def step(kv_ref, start, at, d_query, masked=False):
            key_rows = kv_ref[start : start + tile, :head_size]
            scores = tile_scores(key_rows, query_rows, head_size)
            if masked:
                scores = causal(scores)
            probs = jnp.exp2(scores - log_total)
            d_probs = dot_last(kv_ref[start : start + tile, head_size:], grad_rows)
            d_scores = (probs * (d_probs - delta_row)).astype(jnp.bfloat16)
            rows = slice(at * tile, (at + 1) * tile)
            sums_ref[rows, head_size:] += mul(probs.astype(jnp.bfloat16), grad_rows)
            sums_ref[rows, :head_size] += mul(d_scores, query_rows)
            return d_query + dot_first(key_rows, d_scores)

        d_query = jnp.zeros((head_size, tile), jnp.float32)
        d_query = step(own_ref, block * tile, block, d_query, True)
        for earlier in range(block):
            d_query = step(own_ref, earlier * tile, earlier, d_query)
        for distance in range(1, 1 + len(pieces) // 2):

            def both(_, d_query, distance=distance):
                for k in (2 * distance - 2, 2 * distance - 1):
                    d_query = step(pieces[k], 0, 2 + k, d_query)
                return d_query

            valid = (rank_ref[0] >= distance).astype(jnp.int32)
            d_query = lax.fori_loop(0, valid, both, d_query)
        turned = d_query.T * score_scale
        d_query_ref[here, :] = (
            turned * cos_ref[here, :] - pltpu.roll(turned, head_size // 2, 1) * sin_ref[here, :]
        ).astype(jnp.bfloat16)
    lane = lax.broadcasted_iota(jnp.int32, (tile, 2 * head_size), 1)
    scale = jnp.where(lane < head_size, score_scale, 1.0)
    for at in range(2):
        rows = slice(at * tile, (at + 1) * tile)
        d_own_ref[rows, :] = sums_ref[rows, :] * scale
    for k in range(len(pieces)):
        rows = slice((2 + k) * tile, (3 + k) * tile)
        into = (k % 2) * (len(pieces) // 2) + k // 2
        d_far_ref[into * tile : (into + 1) * tile, :] = (sums_ref[rows, :] * scale).astype(
            jnp.bfloat16
        )


def attend_back(rank, queries, own, pieces, attended, log_totals, d_attn, cosine, sine, after):
    tile = own.shape[0] // 2
    return pl.pallas_call(
        attend_back_kernel,
        out_shape=(
            jax.ShapeDtypeStruct(queries.shape, jnp.bfloat16),
            jax.ShapeDtypeStruct(own.shape, jnp.float32),
            jax.ShapeDtypeStruct((len(pieces) * tile, own.shape[1]), jnp.bfloat16),
        ),
        in_specs=[pl.BlockSpec(memory_space=pltpu.SMEM)]
        + in_vmem(7 + len(pieces))
        + [pl.BlockSpec(memory_space=pl.ANY)] * len(after),
        out_specs=tuple(in_vmem(3)),
        scratch_shapes=[pltpu.VMEM(((2 + len(pieces)) * tile, own.shape[1]), jnp.float32)],
        compiler_params=compiler_params(),
        cost_estimate=small_cost(),
        name="attend_back",
    )(rank, queries, own, *pieces, attended, log_totals, d_attn, cosine, sine, *after)


def reorder_kernel(ranks_ref, *refs, count):
    out_ref = refs[-1]
    start = 0
    for ref in refs[:count]:
        out_ref[:, start : start + ref.shape[1]] = ref[...].astype(out_ref.dtype)
        start += ref.shape[1]


def reorder(ranks, pieces, inverse=False, after=()):
    count = ranks.shape[0]
    rows = pieces[0].shape[0] // count
    width = sum(piece.shape[1] for piece in pieces)
    there = lambda k, ranks: (ranks[k], 0)
    here = lambda k, ranks: (k, 0)
    return pl.pallas_call(
        functools.partial(reorder_kernel, count=len(pieces)),
        grid_spec=pltpu.PrefetchScalarGridSpec(
            num_scalar_prefetch=1,
            grid=(count,),
            in_specs=[
                pl.BlockSpec((rows, piece.shape[1]), here if inverse else there)
                for piece in pieces
            ]
            + [pl.BlockSpec(memory_space=pl.ANY)] * len(after),
            out_specs=pl.BlockSpec((rows, width), there if inverse else here),
        ),
        out_shape=jax.ShapeDtypeStruct((count * rows, width), jnp.bfloat16),
        compiler_params=compiler_params(),
        cost_estimate=small_cost(),
        name="reorder",
    )(ranks, *pieces, *after)


def lower_ones(size, dtype=jnp.float32):
    row = lax.broadcasted_iota(jnp.int32, (size, size), 0)
    column = lax.broadcasted_iota(jnp.int32, (size, size), 1)
    return (row >= column).astype(dtype)


def precise(left_side, right_side):
    return jnp.dot(
        left_side, right_side, precision=HIGH_PRECISION, preferred_element_type=jnp.float32
    )


def spread_heads(columns, head_size, width):
    lane = lax.broadcasted_iota(jnp.int32, (columns.shape[0], 2 * head_size), 1)
    pairs = [
        jnp.where(lane < head_size, columns[:, k : k + 1], columns[:, k + 1 : k + 2])
        for k in range(0, width // head_size, 2)
    ]
    return jnp.concatenate(pairs, axis=1)


def head_ones(width, head_size, lanes, dtype):
    at = lax.broadcasted_iota(jnp.int32, (width, lanes), 0)
    lane = lax.broadcasted_iota(jnp.int32, (width, lanes), 1)
    low = lane * head_size
    return ((at >= low) & (at < low + head_size)).astype(dtype)


def scan_first_kernel(
    pre_ref, bias_ref, rate_ref, x_ref, b_ref, delta_ref, cum_ref, delta_row_ref, cum_row_ref, state_ref, log_ref
):
    @pl.when(pl.program_id(0) == 0)
    def _():
        state_ref[...] = jnp.zeros_like(state_ref)
        log_ref[...] = jnp.zeros_like(log_ref)

    delta = jax.nn.softplus(pre_ref[...] + bias_ref[...])
    log_step = -delta * rate_ref[...]
    cumulative = precise(lower_ones(log_step.shape[0]), log_step)
    delta_ref[...] = delta
    cum_ref[...] = cumulative
    delta_row_ref[...] = delta.T[:8]
    cum_row_ref[...] = cumulative.T[:8]
    ending = cumulative[-1:, :]
    weight = jnp.exp(ending - cumulative + log_ref[...]) * delta
    width = x_ref.shape[1]
    x_low = x_ref[...].astype(jnp.bfloat16).astype(jnp.float32)
    weighted = (x_low * spread_heads(weight, MIXER_HEAD_SIZE, width)).astype(jnp.bfloat16)
    state_ref[...] += dot_first(b_ref[...].astype(jnp.bfloat16), weighted)
    log_ref[...] += ending


def part(projected, start, width, order=lambda c: c):
    at = start // width
    return (projected, pl.BlockSpec((BLOCK, width), lambda c: (order(c), at)))


def run_scan(
    kernel, chunks, operands, out_shape, out_specs, name, scratch=(), after=(), mebibytes=20
):
    count = len(operands)
    operands = operands + [(array, pl.BlockSpec(memory_space=pl.ANY)) for array in after]

    def call(*refs):
        kernel(*refs[:count], *refs[count + len(after) :])

    return pl.pallas_call(
        call,
        grid=(chunks,),
        out_shape=out_shape,
        in_specs=[spec for _, spec in operands],
        out_specs=out_specs,
        scratch_shapes=list(scratch),
        compiler_params=compiler_params(mebibytes),
        cost_estimate=small_cost(),
        name=name,
    )(*[array for array, _ in operands])


def whole(array):
    return (array, pl.BlockSpec(array.shape, lambda c: (0,) * array.ndim))


def scan_first(at, bias, rate):
    rows, lanes = (at["x"][0].shape[0], bias.shape[1])
    chunks = rows // BLOCK
    back = lambda c: chunks - 1 - c
    width, state_size = (at["x"][2], at["b"][2])
    by_chunk = pl.BlockSpec((BLOCK, lanes), lambda c: (back(c), 0))
    across = pl.BlockSpec((8, BLOCK), lambda c: (0, back(c)))
    shape = lambda *sizes: jax.ShapeDtypeStruct(sizes, jnp.float32)
    return run_scan(
        scan_first_kernel,
        chunks,
        [
            part(*at["misc"], back),
            whole(bias),
            whole(rate),
            part(*at["x"], back),
            part(*at["b"], back),
        ],
        (
            shape(rows, lanes),
            shape(rows, lanes),
            shape(8, rows),
            shape(8, rows),
            shape(state_size, width),
            shape(1, lanes),
        ),
        (
            by_chunk,
            by_chunk,
            across,
            across,
            pl.BlockSpec((state_size, width), lambda c: (0, 0)),
            pl.BlockSpec((1, lanes), lambda c: (0, 0)),
        ),
        "scan_first",
    )


def chained(refs, width):
    state = jnp.zeros((refs[0].shape[0] - 16, width), jnp.float32)
    for ref in reversed(refs):
        logs = ref[-16:, :LANES].astype(jnp.float32)
        decay = jnp.exp(jnp.sum(logs[:3], axis=0, keepdims=True))
        state = ref[:-16].astype(jnp.float32) + spread_heads(decay, MIXER_HEAD_SIZE, width) * state
    return state


def scan_kernel(
    x_ref,
    z_ref,
    b_ref,
    c_ref,
    delta_ref,
    cum_ref,
    delta_row_ref,
    cum_row_ref,
    near_ref,
    next_ref,
    far_ref,
    skip_ref,
    scanned_ref,
    gated_ref,
    states_ref,
    state_ref,
):
    @pl.when(pl.program_id(0) == 0)
    def _():
        state_ref[...] = chained((near_ref, next_ref, far_ref), x_ref.shape[1])

    head_size = MIXER_HEAD_SIZE
    pair = 2 * head_size
    size, width = x_ref.shape
    state = state_ref[...]
    states_ref[0] = state
    delta, cumulative = (delta_ref[...], cum_ref[...])
    delta_row, cum_row = (delta_row_ref[...], cum_row_ref[...])
    bmat, cmat = (b_ref[...].astype(jnp.bfloat16), c_ref[...].astype(jnp.bfloat16))
    x_all = x_ref[...].astype(jnp.bfloat16)
    inner = dot_last(cmat, bmat)
    row = lax.broadcasted_iota(jnp.int32, (size, size), 0)
    column = lax.broadcasted_iota(jnp.int32, (size, size), 1)
    allowed = row >= column
    lane = lax.broadcasted_iota(jnp.int32, (size, pair), 1)
    from_state = mul(cmat, state.astype(jnp.bfloat16))
    spread = spread_heads(jnp.exp(cumulative), head_size, width)
    for first in range(0, width // head_size, 2):
        here = slice(first * head_size, first * head_size + pair)
        x_pair = x_all[:, here]
        total = from_state[:, here] * spread[:, here]
        total += skip_ref[:, here] * x_pair.astype(jnp.float32)
        for head in (first, first + 1):
            gap = cumulative[:, head : head + 1] - cum_row[head : head + 1, :]
            decay = jnp.exp(jnp.where(allowed, gap, -1e30))
            mixing = inner * decay * delta_row[head : head + 1, :]
            x_head = jnp.where((lane >= head_size) == (head > first), x_pair, 0.0)
            total += mul(mixing.astype(jnp.bfloat16), x_head.astype(jnp.bfloat16))
        scanned_ref[:, here] = total
        gate = z_ref[:, here]
        gated_ref[:, here] = (total * (gate * jax.nn.sigmoid(gate))).astype(jnp.bfloat16)
    ending = cumulative[-1:, :]
    weight = spread_heads(jnp.exp(ending - cumulative) * delta, head_size, width)
    weighted = (x_all.astype(jnp.float32) * weight).astype(jnp.bfloat16)
    state_ref[...] = state * spread[-1:, :] + dot_first(bmat, weighted)


def scan(at, delta, cumulative, delta_row, cum_row, entry, skip, after):
    rows = delta.shape[0]
    state_size, width = (at["b"][2], at["x"][2])
    chunks = rows // BLOCK
    by_chunk = pl.BlockSpec((BLOCK, width), lambda c: (c, 0))
    lanes = delta.shape[1]
    across = pl.BlockSpec((8, BLOCK), lambda c: (0, c))
    return run_scan(
        scan_kernel,
        chunks,
        [
            part(*at["x"]),
            part(*at["z"]),
            part(*at["b"]),
            part(*at["c"]),
            part(delta, 0, lanes),
            part(cumulative, 0, lanes),
            (delta_row, across),
            (cum_row, across),
            *[whole(packed) for packed in entry],
            whole(skip),
        ],
        (
            jax.ShapeDtypeStruct((rows, width), jnp.float32),
            jax.ShapeDtypeStruct((rows, width), jnp.bfloat16),
            jax.ShapeDtypeStruct((chunks, state_size, width), jnp.float32),
        ),
        (by_chunk, by_chunk, pl.BlockSpec((1, state_size, width), lambda c: (c, 0, 0))),
        "scan",
        [pltpu.VMEM((state_size, width), jnp.float32)],
        after,
    )


def scan_back_first_kernel(
    grad_ref, z_ref, scanned_ref, c_ref, cum_ref, d_scanned_ref, d_gate_ref, state_ref, log_ref
):
    @pl.when(pl.program_id(0) == 0)
    def _():
        state_ref[...] = jnp.zeros_like(state_ref)
        log_ref[...] = jnp.zeros_like(log_ref)

    gate = z_ref[...]
    chance = jax.nn.sigmoid(gate)
    grad = grad_ref[:, : z_ref.shape[1]].astype(jnp.float32)
    d_scanned = grad * (gate * chance)
    d_scanned_ref[...] = d_scanned
    d_gate_ref[...] = (
        grad * scanned_ref[...] * (chance * (1.0 + gate * (1.0 - chance)))
    ).astype(jnp.bfloat16)
    cumulative = cum_ref[...]
    decay = spread_heads(jnp.exp(cumulative + log_ref[...]), MIXER_HEAD_SIZE, z_ref.shape[1])
    state_ref[...] += dot_first(
        c_ref[...].astype(jnp.bfloat16), (d_scanned * decay).astype(jnp.bfloat16)
    )
    log_ref[...] += cumulative[-1:, :]


def scan_back_first(grads, at, scanned, cumulative):
    rows, width = scanned.shape
    state_size, lanes = (at["c"][2], cumulative.shape[1])
    by_chunk = pl.BlockSpec((BLOCK, width), lambda c: (c, 0))
    return run_scan(
        scan_back_first_kernel,
        rows // BLOCK,
        [
            part(grads, 0, grads.shape[1]),
            part(*at["z"]),
            part(scanned, 0, width),
            part(*at["c"]),
            part(cumulative, 0, lanes),
        ],
        (
            jax.ShapeDtypeStruct((rows, width), jnp.float32),
            jax.ShapeDtypeStruct((rows, width), jnp.bfloat16),
            jax.ShapeDtypeStruct((state_size, width), jnp.float32),
        ),
        (by_chunk, by_chunk, pl.BlockSpec((state_size, width), lambda c: (0, 0))),
        "scan_back_first",
        [pltpu.VMEM((1, lanes), jnp.float32)],
    )


def scan_back_kernel(
    x_ref,
    grad_ref,
    b_ref,
    c_ref,
    pre_ref,
    bias_ref,
    rate_ref,
    delta_ref,
    cum_ref,
    cum_row_ref,
    states_ref,
    near_ref,
    next_ref,
    far_ref,
    skip_ref,
    d_x_ref,
    d_b_ref,
    d_c_ref,
    d_pre_ref,
    sums_ref,
    state_ref,
):
    @pl.when(pl.program_id(0) == 0)
    def _():
        state_ref[...] = chained((near_ref, next_ref, far_ref), x_ref.shape[1])
        sums_ref[...] = jnp.zeros_like(sums_ref)

    head_size = MIXER_HEAD_SIZE
    pair = 2 * head_size
    size, width = x_ref.shape
    lanes = delta_ref.shape[1]
    low = jnp.bfloat16
    delta, cumulative, cum_row = (delta_ref[...], cum_ref[...], cum_row_ref[...])
    bmat, cmat = (b_ref[...].astype(low), c_ref[...].astype(low))
    x_all = x_ref[...].astype(low)
    x_single = x_all.astype(jnp.float32)
    grad = grad_ref[...]
    grad_low = grad.astype(low)
    state = states_ref[0]
    state_low = state.astype(low)
    after = state_ref[...]
    after_low = after.astype(low)
    ending = cumulative[-1:, :]
    row = lax.broadcasted_iota(jnp.int32, (size, size), 0)
    column = lax.broadcasted_iota(jnp.int32, (size, size), 1)
    later = column >= row
    before = (row > column).astype(low)
    onward = later.astype(low)
    lane = lax.broadcasted_iota(jnp.int32, (size, pair), 1)
    head_lane = lax.broadcasted_iota(jnp.int32, (size, lanes), 1)
    sum_heads = head_ones(width, head_size, lanes, low)

    inner = dot_last(bmat, cmat)
    from_after = mul(bmat, after_low)
    weight = jnp.exp(ending - cumulative)
    spread_weight = spread_heads(weight * delta, head_size, width)
    spread = spread_heads(jnp.exp(cumulative), head_size, width)
    to_end = mul((x_single * from_after).astype(low), sum_heads)
    through = jnp.exp(cumulative) * mul((grad * mul(cmat, state_low)).astype(low), sum_heads)
    carried = jnp.sum(state * after, axis=0, keepdims=True) * spread[-1:, :]
    carried = precise(carried, sum_heads.astype(jnp.float32))
    d_delta = weight * to_end
    d_log = (
        mul(onward, through.astype(low)) + mul(before, (d_delta * delta).astype(low)) + carried
    )

    d_inner = jnp.zeros((size, size), jnp.float32)
    for first in range(0, width // head_size, 2):
        here = slice(first * head_size, first * head_size + pair)
        x_pair, grad_pair = (x_all[:, here], grad_low[:, here])
        d_x = from_after[:, here] * spread_weight[:, here] + skip_ref[:, here] * grad[:, here]
        for head in (first, first + 1):
            mine = (lane >= head_size) == (head > first)
            gap = cum_row[head : head + 1, :] - cumulative[:, head : head + 1]
            decay = jnp.exp(jnp.where(later, gap, -1e30))
            delta_column = delta[:, head : head + 1]
            d_mixing = dot_last(jnp.where(mine, x_pair, 0.0).astype(low), grad_pair) * decay
            d_inner += d_mixing * delta_column
            flow = d_mixing * inner
            mixing = inner * decay * delta_column
            d_x += mul(mixing.astype(low), jnp.where(mine, grad_pair, 0.0).astype(low))
            d_delta_head = jnp.sum(flow, axis=1, keepdims=True)
            passing = mul(before, (flow * delta_column).astype(low))
            d_log_head = jnp.sum(jnp.where(later, passing, 0.0), axis=1, keepdims=True)
            d_delta += jnp.where(head_lane == head, d_delta_head, 0.0)
            d_log += jnp.where(head_lane == head, d_log_head, 0.0)
        d_x_ref[:, here] = d_x.astype(low)

    d_inner_low = d_inner.astype(low)
    scaled_grad = (grad * spread).astype(low)
    weighted = (x_single * spread_weight).astype(low)
    d_b_ref[...] = (mul(d_inner_low, cmat) + dot_last(weighted, after_low)).astype(low)
    d_c_ref[...] = (dot_first(d_inner_low, bmat) + dot_last(scaled_grad, state_low)).astype(low)
    state_ref[...] = after * spread[-1:, :] + dot_first(cmat, scaled_grad)
    rate = rate_ref[...]
    d_pre = (d_delta - d_log * rate) * jax.nn.sigmoid(pre_ref[...] + bias_ref[...])
    d_pre = jnp.where(head_lane < width // head_size, d_pre, 0.0)
    d_pre_ref[...] = d_pre.astype(low)
    skip_sum = precise(
        jnp.sum(grad * x_single, axis=0, keepdims=True), sum_heads.astype(jnp.float32)
    )
    sums_ref[0:1, :] += jnp.sum(d_pre, axis=0, keepdims=True)
    sums_ref[1:2, :] += jnp.sum(d_log * (-delta * rate), axis=0, keepdims=True)
    sums_ref[2:3, :] += skip_sum


def scan_back(
    at, d_scanned, bias, rate, delta, cumulative, cum_row, states, entry, skip, after
):
    rows, width = d_scanned.shape
    state_size, lanes = (at["b"][2], delta.shape[1])
    chunks = rows // BLOCK
    back = lambda c: chunks - 1 - c
    by_chunk = lambda columns: pl.BlockSpec((BLOCK, columns), lambda c: (back(c), 0))
    shape = lambda columns: jax.ShapeDtypeStruct((rows, columns), jnp.bfloat16)
    return run_scan(
        scan_back_kernel,
        chunks,
        [
            part(in_hbm(at["x"][0]), *at["x"][1:], back),
            part(in_hbm(d_scanned), 0, width, back),
            part(in_hbm(at["b"][0]), *at["b"][1:], back),
            part(in_hbm(at["c"][0]), *at["c"][1:], back),
            part(in_hbm(at["misc"][0]), *at["misc"][1:], back),
            whole(bias),
            whole(rate),
            part(in_hbm(delta), 0, lanes, back),
            part(in_hbm(cumulative), 0, lanes, back),
            (in_hbm(cum_row), pl.BlockSpec((8, BLOCK), lambda c: (0, back(c)))),
            (in_hbm(states), pl.BlockSpec((1, state_size, width), lambda c: (back(c), 0, 0))),
            *[whole(in_hbm(packed)) for packed in entry],
            whole(skip),
        ],
        (
            shape(width),
            shape(state_size),
            shape(state_size),
            shape(lanes),
            jax.ShapeDtypeStruct((8, lanes), jnp.float32),
        ),
        (
            by_chunk(width),
            by_chunk(state_size),
            by_chunk(state_size),
            by_chunk(lanes),
            pl.BlockSpec((8, lanes), lambda c: (0, 0)),
        ),
        "scan_back",
        [pltpu.VMEM((state_size, width), jnp.float32)],
        after,
        44,
    )


def on_heads(value, move):
    devices = lax.axis_size("heads")
    pairs = []
    for at in range(devices):
        z, core = move(at // 2, at % 2)
        pairs.append((at, 2 * (z % (devices // 2)) + core))
    return lax.ppermute(value, "heads", pairs)


def to_partner(value):
    return on_heads(value, lambda z, core: (z, 1 - core))


def along(value):
    return on_heads(value, lambda z, core: (z + 1 - 2 * core, core))


def against(value):
    return on_heads(value, lambda z, core: (z - 1 + 2 * core, core))


def chunk_ranks():
    devices = lax.axis_size("heads")
    z, core = (lax.axis_index("heads") // 2, lax.axis_index("heads") % 2)
    step, other = (1 - 2 * core, 1 - core)
    owners = (
        (z, core),
        (z + 2, core),
        (z - step, core),
        (z - step, other),
        (z, other),
        (z + 2, other),
        (z + step, other),
        (z + step, core),
    )
    return jnp.stack([2 * ((at + devices) % (devices // 2)) + side for at, side in owners])


def against_other(value):
    return on_heads(value, lambda z, core: (z - 1 + 2 * core, 1 - core))


def gather_rows(own, joined=False):
    partner = to_partner(own)
    near = along(own)
    near_other = along(partner)
    far = along(near)
    last = (to_partner(far), to_partner(near), to_partner(near_other))
    mine = (own, far, near, near_other)
    theirs = (partner,) + last
    rows = join(mine + theirs) if joined else jnp.concatenate(mine + theirs, axis=0)
    return rows, last


def scatter_rows(product, half, late=None):
    chunk = half // 4
    got = to_partner(product(slice(half, 2 * half)).astype(jnp.bfloat16))
    kept = lax.optimization_barrier(product(slice(0, half)))

    summed = kept + got.astype(jnp.float32)
    low = summed[chunk:].astype(jnp.bfloat16)
    far = against(low[:chunk])
    near_other = against_other(low[2 * chunk :])
    near = low[chunk : 2 * chunk].astype(jnp.float32) + far.astype(jnp.float32)
    near = against(near.astype(jnp.bfloat16))
    total = summed[:chunk] + near.astype(jnp.float32) + near_other.astype(jnp.float32)
    return total if late is None else total + late


def across(value, bit):
    devices = lax.axis_size("heads")
    return lax.ppermute(value, "heads", [(at, at ^ bit) for at in range(devices)])


def gather_small(value):
    for bit in (1, 2, 4):
        value = jnp.concatenate([value, across(value, bit)], axis=0)
    return value


def scatter_small(value):
    for bit in (4, 2, 1):
        half = value.shape[0] // 2
        got = across(value[half:].astype(jnp.bfloat16), bit)
        value = value[:half].astype(jnp.float32) + got.astype(jnp.float32)
    return value


def on_blocks(value, step):
    devices = lax.axis_size("blk")
    pairs = [(at, at + step) for at in range(devices) if 0 <= at + step < devices]
    return lax.ppermute(value, "blk", pairs)


def from_earlier(value, step=1):
    return tuple(on_blocks(value, distance * step) for distance in (1, 2, 3))


def pack_state(state, log_total):
    high = log_total.astype(jnp.bfloat16)
    rest = log_total - high.astype(jnp.float32)
    middle = rest.astype(jnp.bfloat16)
    low = (rest - middle.astype(jnp.float32)).astype(jnp.bfloat16)
    logs = jnp.concatenate([high, middle, low], axis=0)
    logs = jnp.pad(logs, ((0, 16 - logs.shape[0]), (0, state.shape[1] - logs.shape[1])))
    return jnp.concatenate([state.astype(jnp.bfloat16), logs], axis=0)


def sum_blocks(value):
    for axis in ("dp", "blk"):
        for bit in (1, 2):
            value = value + lax.ppermute(
                value, axis, [(at, at ^ bit) for at in range(lax.axis_size(axis))]
            )
    return value


def weight_sum(grads):
    return lax.psum_scatter(grads, ("dp", "blk"), scatter_dimension=0, tiled=True)


def split_columns(value_in, widths):
    pieces, start = [], 0
    for width in widths:
        pieces.append(value_in[:, start : start + width])
        start += width
    return pieces


def inverse_rms(rows_in):
    return lax.rsqrt(jnp.mean(rows_in * rows_in, axis=-1, keepdims=True) + norm_eps)


def norm_back(rows_in, gain_in, cotangent):
    inverse = inverse_rms(rows_in)
    scaled = rows_in * inverse
    weighted = cotangent * gain_in
    return inverse * (weighted - scaled * jnp.mean(weighted * scaled, axis=-1, keepdims=True))


def shards(
    x_in,
    out_grad,
    norm_one,
    w_query,
    w_key,
    w_value,
    output_gate_weight,
    mixer_input_weight,
    w_delta,
    w_bmat,
    w_cmat,
    delta_bias,
    decay_log,
    skip_gain,
    w_attn_out,
    mixer_output_weight,
    norm_two,
    w_gate,
    w_up,
    w_down,
):
    heads_count = lax.axis_size("heads")
    head_rank = lax.axis_index("heads")
    core = head_rank % 2
    block_rank = lax.axis_index("blk")
    rank = block_rank.astype(jnp.int32)[None]
    own_rows = x_in.shape[0]
    span_length = own_rows * heads_count
    half_span = span_length // 2
    span_start = block_rank * span_length
    query_width = w_query.shape[1]
    mixer_width = mixer_input_weight.shape[1]
    heads = mixer_width // MIXER_HEAD_SIZE
    state_size = w_bmat.shape[1]
    hidden_width = w_gate.shape[1]
    rows_of = w_query.shape[0]
    kv_index = head_rank * (query_width // HD) // (QH // KVH)
    kv_width = KVH * HD
    low = jnp.bfloat16
    ranks = chunk_ranks().astype(jnp.int32)
    turns = (head_rank ^ jnp.arange(heads_count)).astype(jnp.int32)

    gains = jnp.stack([norm_one, norm_two], axis=1)
    gains = jnp.pad(gains, ((0, 0), (heads, LANES - heads - 2)))
    shared = pack((w_key, w_value, w_bmat, w_cmat, gains), (False,) * 5)
    delta_wide = jnp.pad(w_delta, ((0, 0), (0, LANES - heads)))
    in_names = ("z", "x", "query", "b", "c", "misc", "key", "value")
    in_widths = (mixer_width, mixer_width, query_width, state_size, state_size, LANES, HD, HD)
    in_width = sum(in_widths)
    starts = [sum(in_widths[:k]) for k in range(len(in_widths))]
    at = dict(zip(in_names, zip(starts, in_widths)))
    mix_at = {
        "ssm_out": (in_width, mixer_width),
        "attn_out": (in_width + mixer_width, query_width),
    }
    first_own = pack_first(
        turns,
        kv_index.astype(jnp.int32)[None],
        gather_small(shared),
        delta_wide,
        [output_gate_weight, mixer_input_weight, w_query, mixer_output_weight, w_attn_out],
        at | mix_at,
    )
    gain_part = first_own[:, at["misc"][0] + heads : at["misc"][0] + heads + 2]
    first_full = lax.all_gather(first_own, ("dp", "blk"), axis=0, tiled=True)
    in_full, mix_t = (first_full[:, :in_width], first_full[:, in_width:])
    x_float = x_in.astype(jnp.float32)
    zero = 0.0 * first_own[0, 0]
    x_span, _ = gather_rows(x_in + zero, joined=True)
    ffn_grad, _ = gather_rows(out_grad + zero, joined=True)
    ffn_own = pack((w_gate, w_up, w_down), (False, False, True), [corner(x_span)])
    ffn_full = lax.all_gather(ffn_own, ("dp", "blk"), axis=0, tiled=True)
    mixed_width = query_width + mixer_width
    gate_full, up_full, down_t = split_columns(ffn_full, (hidden_width,) * 3)
    positions = (span_start + jnp.arange(span_length)).astype(jnp.float32)
    freqs = rope_base ** (-2.0 * jnp.arange(HD // 2, dtype=jnp.float32) / HD)
    angles = positions[:, None] * freqs[None, :]
    cosine, sine = (jnp.cos(angles), jnp.sin(angles))
    cosine = jnp.concatenate([cosine, cosine], axis=1)
    sine = jnp.concatenate([-sine, sine], axis=1)
    normed_ordered, queries, keys_values, gain_rows = enter(
        ranks, jnp.full((1,), heads, jnp.int32), x_span, first_full, at, cosine, sine, [corner(ffn_own), corner(ffn_grad)]
    )
    gain_one, gain_two = (gain_rows[0:1], gain_rows[1:2])
    mine = lax.dynamic_slice_in_dim(keys_values, core * half_span, half_span, 0)
    pieces = []
    for piece in from_earlier(mine):
        pieces += [piece, to_partner(piece)]
    gate_raw = simple_product(normed_ordered, in_full[:, :mixer_width])
    x_raw = simple_product(normed_ordered, in_full[:, mixer_width : 2 * mixer_width])
    state_raw = simple_product(normed_ordered, in_full[:, at["b"][0] : at["key"][0]])
    raw = {
        "z": (gate_raw, 0, mixer_width),
        "x": (x_raw, 0, mixer_width),
        "b": (state_raw, 0, state_size),
        "c": (state_raw, state_size, state_size),
        "misc": (state_raw, 2 * state_size, LANES),
    }

    pad_lanes = lambda vector: jnp.pad(vector, (0, LANES - heads))[None]
    bias, rate = (pad_lanes(delta_bias), pad_lanes(jnp.exp(decay_log)))
    skip = jnp.repeat(skip_gain, MIXER_HEAD_SIZE)[None]
    delta, cumulative, delta_row, cum_row, local_state, local_log = scan_first(raw, bias, rate)
    entry_states = from_earlier(pack_state(local_state, local_log))
    attended, attn_part, log_totals = attend(rank, queries, keys_values, pieces)
    scanned, gated, states = scan(
        raw, delta, cumulative, delta_row, cum_row, entry_states, skip, [corner(attn_part)]
    )
    mixers = reorder(ranks, [gated, attn_part])
    ffn_zero = 0.0 * ffn_full[0, 0].astype(jnp.float32)
    mixed = scatter_rows(lambda rows: dot_last(mixers[rows], mix_t), half_span, ffn_zero)
    middle = x_float + mixed
    middle_scaled = middle * inverse_rms(middle)
    normed_two, _ = gather_rows((middle_scaled * gain_two).astype(low))
    ffn_gate = simple_product(normed_two, gate_full)
    ffn_up = simple_product(normed_two, up_full)
    ffn_sig = jax.nn.sigmoid(ffn_gate)
    hidden = (ffn_gate * ffn_sig * ffn_up).astype(low)

    d_hidden = simple_product(ffn_grad, down_t)
    d_ffn_gate = (d_hidden * ffn_up * (ffn_sig * (1.0 + ffn_gate * (1.0 - ffn_sig)))).astype(low)
    d_ffn_up = (d_hidden * (ffn_gate * ffn_sig)).astype(low)
    d_normed_two = scatter_rows(
        lambda rows: dot_last(d_ffn_gate[rows], gate_full) + dot_last(d_ffn_up[rows], up_full),
        half_span,
    )
    d_middle = out_grad.astype(jnp.float32) + norm_back(middle, gain_two, d_normed_two)
    mix_grad, mix_last = gather_rows(d_middle.astype(low))
    ffn_grads = weight_grads(
        [(normed_two, [d_ffn_gate, d_ffn_up]), (ffn_grad, [hidden])],
        3 * hidden_width,
        after=list(map(corner, mix_last)),
    )
    ffn_sums = weight_sum(ffn_grads).astype(jnp.float32)
    grad_gate, grad_up, grad_down_t = split_columns(ffn_sums, (hidden_width,) * 3)
    grad_two_part = jnp.sum(grad_gate * w_gate + grad_up * w_up, axis=1, keepdims=True)
    gain_own = gain_part.astype(jnp.float32)
    grad_two_part = grad_two_part / gain_own[:, 1:2]
    d_mixers = reorder(
        ranks, [simple_product(mix_grad, mix_t).astype(low)], inverse=True, after=[corner(ffn_grads)]
    )
    d_scanned, d_gate_z, d_entry = scan_back_first(d_mixers, raw, scanned, cumulative)
    d_entry = pack_state(d_entry, local_log)
    after_states = from_earlier(d_entry, -1)
    mix_width = mixed_width + mixer_width
    all_width = mixed_width + in_width
    mix_grads = weight_grads(
        [(mix_grad, [mixers]), (normed_ordered, [d_gate_z])], all_width, after=[corner(d_entry)]
    )
    d_query, d_own, d_far = attend_back(
        rank, queries, keys_values, pieces, attended, log_totals, d_mixers, cosine, sine, [corner(mix_grads), *map(corner, after_states)]
    )
    d_ssm_in, d_bmat, d_cmat, d_pre, sums = scan_back(
        raw,
        d_scanned,
        bias,
        rate,
        delta,
        cumulative,
        cum_row,
        states,
        after_states,
        skip,
        [corner(d_query)],
    )
    far_half = d_far.shape[0] // 2
    d_mine = lax.dynamic_slice_in_dim(d_own, core * half_span, half_span, 0)
    d_theirs = lax.dynamic_slice_in_dim(d_own, (1 - core) * half_span, half_span, 0)
    d_mine = d_mine + to_partner(d_theirs.astype(low)).astype(jnp.float32)
    d_far = d_far[:far_half].astype(jnp.float32) + to_partner(d_far[far_half:]).astype(jnp.float32)
    d_one, d_two, d_three = (
        d_far[k * half_span : (k + 1) * half_span] for k in range(d_far.shape[0] // half_span)
    )
    scan_zero = 0.0 * d_pre[0, 0].astype(jnp.float32)
    d_one = d_one + on_blocks(d_two.astype(low), -1).astype(jnp.float32) + scan_zero
    d_mine = d_mine + on_blocks(d_one.astype(low), -1).astype(jnp.float32)
    d_mine = d_mine + on_blocks(d_three.astype(low), -3).astype(jnp.float32)
    half_cos = lax.dynamic_slice_in_dim(cosine, core * half_span, half_span, 0)
    half_sin = lax.dynamic_slice_in_dim(sine, core * half_span, half_span, 0)
    d_key = d_mine[:, :HD]
    d_key = d_key * half_cos - jnp.roll(d_key, HD // 2, axis=1) * half_sin
    d_mine = jnp.concatenate([d_key, d_mine[:, HD:]], axis=1).astype(low)
    d_keys_values = lax.dynamic_update_slice_in_dim(
        jnp.zeros((span_length, 2 * HD), low), d_mine, core * half_span, 0
    )

    scan_rights = [d_ssm_in, d_bmat, d_cmat, d_pre]
    in_grads = weight_grads([(normed_ordered, scan_rights)], all_width, mix_width, mix_grads)
    late_rights = [d_keys_values, d_query]
    late_start = mix_width + sum(array.shape[1] for array in scan_rights)
    in_grads = weight_grads([(normed_ordered, late_rights)], all_width, late_start, in_grads)
    in_sums = weight_sum(in_grads)
    d_projected = reorder(
        ranks,
        [d_gate_z, d_ssm_in, d_query, d_bmat, d_cmat, d_pre, d_keys_values],
        after=[corner(in_grads)],
    )
    d_normed = scatter_rows(lambda rows: dot_last(d_projected[rows], in_full), half_span)
    input_grad = d_middle + norm_back(x_float, gain_one, d_normed)
    back_zero = 0.0 * d_query[0, 0].astype(jnp.float32)
    ffn_out = scatter_rows(
        lambda rows: dot_last(hidden[rows], down_t) + back_zero, half_span
    )
    activations = (middle + ffn_out).astype(low)
    sums_names = ("ssm_out", "attn_out", "z", "x", "b", "c", "misc", "key", "value", "query")
    sums_widths = [mixer_width, query_width] + [at[name][1] for name in sums_names[2:]]
    sums_starts = [sum(sums_widths[:k]) for k in range(len(sums_widths))]
    sums_at = dict(zip(sums_names, zip(sums_starts, sums_widths)))
    extra = jnp.concatenate([gain_own[:, 0:1], grad_two_part], axis=1)
    extra = jnp.pad(extra, ((0, 0), (0, LANES - 2)))
    grad_ssm_out, grad_attn_out, grad_gatez, grad_ssmx, grad_query, misc_sums, shared_parts = finish(
        turns,
        kv_index.astype(jnp.int32)[None],
        in_sums,
        first_own,
        extra,
        at,
        sums_at,
    )
    shared_sums = scatter_small(shared_parts)
    grad_key, grad_value, grad_bmat, grad_cmat, gain_sums = split_columns(
        shared_sums, (kv_width, kv_width, state_size, state_size, LANES)
    )
    small_sums = sum_blocks(sums)[:, :heads]
    return (
        activations,
        input_grad,
        gain_sums[:, 0],
        grad_query,
        grad_key,
        grad_value,
        grad_gatez,
        grad_ssmx,
        misc_sums[:, :heads],
        grad_bmat,
        grad_cmat,
        small_sums[0],
        small_sums[1],
        small_sums[2],
        grad_attn_out,
        grad_ssm_out,
        gain_sums[:, 1],
        grad_gate,
        grad_up,
        grad_down_t.T,
    )


def solution(mesh):
    placed = (
        P(("dp", "blk", "heads"), None),
        P(("dp", "blk", "heads"), None),
        P(("dp", "blk", "heads")),
        P(("dp", "blk"), "heads"),
        P(("dp", "blk", "heads"), None),
        P(("dp", "blk", "heads"), None),
        P(("dp", "blk"), "heads"),
        P(("dp", "blk"), "heads"),
        P(("dp", "blk"), "heads"),
        P(("dp", "blk", "heads"), None),
        P(("dp", "blk", "heads"), None),
        P("heads"),
        P("heads"),
        P("heads"),
        P("heads", ("dp", "blk")),
        P("heads", ("dp", "blk")),
        P(("dp", "blk", "heads")),
        P(("dp", "blk"), "heads"),
        P(("dp", "blk"), "heads"),
        P("heads", ("dp", "blk")),
    )
    return jax.shard_map(
        shards,
        mesh=mesh,
        in_specs=placed,
        out_specs=(
            P(("dp", "blk", "heads"), None),
            P(("dp", "blk", "heads"), None),
            P(("dp", "blk", "heads")),
            P(("dp", "blk"), "heads"),
            P(("dp", "blk", "heads"), None),
            P(("dp", "blk", "heads"), None),
            P(("dp", "blk"), "heads"),
            P(("dp", "blk"), "heads"),
            P(("dp", "blk"), "heads"),
            P(("dp", "blk", "heads"), None),
            P(("dp", "blk", "heads"), None),
            P("heads"),
            P("heads"),
            P("heads"),
            P("heads", ("dp", "blk")),
            P("heads", ("dp", "blk")),
            P(("dp", "blk", "heads")),
            P(("dp", "blk"), "heads"),
            P(("dp", "blk"), "heads"),
            P("heads", ("dp", "blk")),
        ),
        check_vma=False,
    )
```

```python
import functools

import jax
import jax.numpy as jnp
from jax import lax
from jax.experimental import pallas as pl
from jax.experimental.pallas import tpu as pltpu
from jax.sharding import PartitionSpec as P

QH = 8
KVH = 2
HD = 128
MIXER_HEAD_SIZE = 64
BLOCK = 256
LANES = 128
LOG2_E = 1.4426950408889634


HIGH_PRECISION = lax.Precision.HIGHEST
norm_eps = 1e-05
rope_base = 100000000000.0


def simple_product(left_side, right_side):
    return jnp.dot(left_side, right_side, preferred_element_type=jnp.float32)


def dot_last(left_side, right_side):
    return lax.dot_general(
        left_side, right_side, (((1,), (1,)), ((), ())), preferred_element_type=jnp.float32
    )


def dot_first(left_side, right_side):
    return lax.dot_general(
        left_side, right_side, (((0,), (0,)), ((), ())), preferred_element_type=jnp.float32
    )


def compiler_params(mebibytes=20):
    return pltpu.CompilerParams(vmem_limit_bytes=mebibytes * 1024 * 1024)


def small_cost():
    return pl.CostEstimate(flops=1000, bytes_accessed=1000, transcendentals=0)


def in_hbm(value):
    return pltpu.with_memory_space_constraint(value, pltpu.HBM)


def corner(value):
    return value[:16, :LANES]


def in_vmem(count):
    return [pl.BlockSpec(memory_space=pltpu.VMEM)] * count


def mul(left_side, right_side):
    return jnp.dot(left_side, right_side, preferred_element_type=jnp.float32)


def tile_scores(key_rows, query_rows, head_size):
    return dot_last(key_rows, query_rows) * (head_size**-0.5 * LOG2_E)


def causal(scores):
    key_at = lax.broadcasted_iota(jnp.int32, scores.shape, 0)
    query_at = lax.broadcasted_iota(jnp.int32, scores.shape, 1)
    return jnp.where(key_at <= query_at, scores, -1e30)


def enter_kernel(
    ranks_ref, heads_ref, x_ref, misc_ref, key_ref, value_ref, w_query_ref, cos_ref, sin_ref, *refs
):
    ordered_ref, query_ref, kv_ref, gains_ref = refs[-4:]
    head_size = query_ref.shape[1]

    @pl.when(pl.program_id(0) == 0)
    def _():
        lane = lax.broadcasted_iota(jnp.int32, misc_ref.shape, 1)
        for k in range(2):
            column = jnp.where(lane == heads_ref[0] + k, misc_ref[...].astype(jnp.float32), 0.0)
            gains_ref[k : k + 1, :] = jnp.sum(column.T, axis=0, keepdims=True)

    cosine, sine = (cos_ref[...], sin_ref[...])

    def turn(value):
        return (value * cosine + pltpu.roll(value, head_size // 2, 1) * sine).astype(jnp.bfloat16)

    rows = x_ref[...].astype(jnp.float32)
    normed = (rows * inverse_rms(rows) * gains_ref[0:1, :]).astype(jnp.bfloat16)
    ordered_ref[...] = normed
    kv_ref[:, :head_size] = turn(mul(normed, key_ref[...]))
    kv_ref[:, head_size:] = mul(normed, value_ref[...]).astype(jnp.bfloat16)
    query_ref[...] = turn(mul(normed, w_query_ref[...]))


def enter(ranks, heads, x_span, in_full, at, cosine, sine, after):
    count = ranks.shape[0]
    rows, width = x_span.shape
    head_size = cosine.shape[1]
    here = lambda columns: pl.BlockSpec((rows // count, columns), lambda k, r, h: (k, 0))
    there = lambda columns: pl.BlockSpec((rows // count, columns), lambda k, r, h: (r[k], 0))
    weight = lambda name: pl.BlockSpec(
        (width, at[name][1]), lambda k, r, h: (0, at[name][0] // at[name][1])
    )
    return pl.pallas_call(
        enter_kernel,
        grid_spec=pltpu.PrefetchScalarGridSpec(
            num_scalar_prefetch=2,
            grid=(count,),
            in_specs=[
                here(width),
                weight("misc"),
                weight("key"),
                weight("value"),
                weight("query"),
                there(head_size),
                there(head_size),
            ]
            + [pl.BlockSpec(memory_space=pl.ANY)] * len(after),
            out_specs=(
                there(width),
                there(head_size),
                there(2 * head_size),
                pl.BlockSpec((8, width), lambda k, r, h: (0, 0)),
            ),
        ),
        out_shape=(
            jax.ShapeDtypeStruct((rows, width), jnp.bfloat16),
            jax.ShapeDtypeStruct((rows, head_size), jnp.bfloat16),
            jax.ShapeDtypeStruct((rows, 2 * head_size), jnp.bfloat16),
            jax.ShapeDtypeStruct((8, width), jnp.float32),
        ),
        compiler_params=compiler_params(),
        cost_estimate=small_cost(),
        name="enter",
    )(ranks, heads, in_hbm(x_span), *[in_hbm(in_full)] * 4, cosine, sine, *after)


def weight_grads_kernel(*refs, counts):
    out_ref = refs[-1]
    start, used = (0, len(counts))
    for k, count in enumerate(counts):
        left = refs[k][...].T
        for ref in refs[used : used + count]:
            out_ref[:, start : start + ref.shape[1]] = mul(left, ref[...]).astype(jnp.bfloat16)
            start += ref.shape[1]
        used += count


def weight_grads(groups, width, start=0, buffer=None, after=()):
    rights = [right for _, group in groups for right in group]
    columns = sum(right.shape[1] for right in rights)
    depth = rights[0].shape[0]
    rows = groups[0][0].shape[1]
    operands = [left for left, _ in groups] + rights
    count = len(operands)
    extra = list(after) if buffer is None else [buffer] + list(after)

    def call(*refs):
        weight_grads_kernel(
            *refs[:count],
            refs[-1],
            counts=tuple(len(group) for _, group in groups),
        )

    return pl.pallas_call(
        call,
        grid=(rows // BLOCK,),
        out_shape=pltpu.HBM((rows, width), jnp.bfloat16),
        in_specs=[pl.BlockSpec((depth, BLOCK), lambda k: (0, k)) for _ in groups]
        + [pl.BlockSpec(right.shape, lambda k: (0, 0)) for right in rights]
        + [pl.BlockSpec(memory_space=pl.ANY)] * len(extra),
        out_specs=pl.BlockSpec(
            (pl.Element(BLOCK), pl.Element(columns)), lambda k: (k * BLOCK, start)
        ),
        input_output_aliases={} if buffer is None else {count: 0},
        compiler_params=compiler_params(),
        cost_estimate=small_cost(),
        name="weight_grads",
    )(*operands, *extra)


def pack_kernel(*refs, turned):
    out_ref = refs[-1]
    start = 0
    for ref, turn in zip(refs, turned):
        piece = ref[...].T if turn else ref[...]
        out_ref[:, start : start + piece.shape[1]] = piece
        start += piece.shape[1]


def pack(pieces, turned, after=()):
    sizes = [piece.shape[::-1] if turn else piece.shape for piece, turn in zip(pieces, turned)]
    return pl.pallas_call(
        functools.partial(pack_kernel, turned=turned),
        out_shape=jax.ShapeDtypeStruct(
            (sizes[0][0], sum(size[1] for size in sizes)), jnp.bfloat16
        ),
        in_specs=in_vmem(len(pieces)) + [pl.BlockSpec(memory_space=pl.ANY)] * len(after),
        out_specs=pl.BlockSpec(memory_space=pltpu.VMEM),
        compiler_params=compiler_params(),
        cost_estimate=small_cost(),
        name="pack",
    )(*map(in_hbm, pieces), *after)


def join_kernel(*refs):
    out_ref = refs[-1]
    start = 0
    for ref in refs[:-1]:
        out_ref[start : start + ref.shape[0], :] = ref[...]
        start += ref.shape[0]


def join(pieces):
    rows = sum(piece.shape[0] for piece in pieces)
    return pl.pallas_call(
        join_kernel,
        out_shape=jax.ShapeDtypeStruct((rows, pieces[0].shape[1]), pieces[0].dtype),
        in_specs=in_vmem(len(pieces)),
        out_specs=pl.BlockSpec(memory_space=pltpu.VMEM),
        compiler_params=compiler_params(),
        cost_estimate=small_cost(),
        name="join",
    )(*pieces)


def pack_first_kernel(
    turns_ref, kv_ref, shared_ref, delta_ref, z_ref, x_ref, query_ref, ssm_ref, attn_ref, out_ref, *, at
):
    def put(name, value, rows=slice(None)):
        start, size = at[name]
        out_ref[rows, start : start + size] = value

    put("z", z_ref[...])
    put("x", x_ref[...])
    put("query", query_ref[...])
    put("ssm_out", ssm_ref[...].T)
    put("attn_out", attn_ref[...].T)
    count = turns_ref.shape[0]
    size = shared_ref.shape[0] // count
    first = kv_ref[0] == 0
    for k in range(count):
        rows = pl.ds(pl.multiple_of(turns_ref[k] * size, size), size)
        chunk = shared_ref[k * size : (k + 1) * size, :]
        pieces, start = [], 0
        for width in (HD, HD, HD, HD, at["b"][1], at["c"][1], LANES):
            pieces.append(chunk[:, start : start + width])
            start += width
        put("key", jnp.where(first, pieces[0], pieces[1]), rows)
        put("value", jnp.where(first, pieces[2], pieces[3]), rows)
        put("b", pieces[4], rows)
        put("c", pieces[5], rows)
        put("misc", pieces[6] + delta_ref[rows, :], rows)


def pack_first(turns, kv_index, shared, delta, weights, at):
    rows = shared.shape[0]
    return pl.pallas_call(
        functools.partial(pack_first_kernel, at=at),
        out_shape=jax.ShapeDtypeStruct(
            (rows, max(start + size for start, size in at.values())), jnp.bfloat16
        ),
        in_specs=[pl.BlockSpec(memory_space=pltpu.SMEM)] * 2 + in_vmem(2 + len(weights)),
        out_specs=pl.BlockSpec(memory_space=pltpu.VMEM),
        compiler_params=compiler_params(50),
        cost_estimate=small_cost(),
        name="pack_first",
    )(turns, kv_index, shared, delta, *map(in_hbm, weights))


def finish_kernel(
    ranks_ref,
    kv_ref,
    sums_ref,
    weight_ref,
    extra_ref,
    ssm_out_ref,
    attn_out_ref,
    gate_ref,
    ssm_ref,
    query_ref,
    misc_ref,
    shared_ref,
    whole_ref,
    *,
    at,
    sums_at,
):
    def of(name):
        start, size = sums_at[name]
        return sums_ref[:, start : start + size].astype(jnp.float32)

    ssm_out_ref[...] = of("ssm_out").T
    attn_out_ref[...] = of("attn_out").T
    gate_ref[...] = of("z")
    ssm_ref[...] = of("x")
    query_ref[...] = of("query")
    misc_ref[...] = of("misc")
    total = 0.0
    for name, (start, size) in at.items():
        product = of(name) * weight_ref[:, start : start + size].astype(jnp.float32)
        total += jnp.sum(product, axis=1, keepdims=True)
    total = total / extra_ref[:, 0:1]
    lane = lax.broadcasted_iota(jnp.int32, misc_ref.shape, 1)
    gains = jnp.where(lane == 0, total, jnp.where(lane == 1, extra_ref[:, 1:2], 0.0))
    zero = jnp.zeros_like(gains)
    first = kv_ref[0] == 0
    key, value = (of("key"), of("value"))
    pieces = (
        jnp.where(first, key, zero),
        jnp.where(first, zero, key),
        jnp.where(first, value, zero),
        jnp.where(first, zero, value),
        of("b"),
        of("c"),
        gains,
    )
    start = 0
    for piece in pieces:
        whole_ref[:, start : start + piece.shape[1]] = piece
        start += piece.shape[1]
    count = ranks_ref.shape[0]
    size = shared_ref.shape[0] // count
    for k in range(count):
        rows = pl.ds(pl.multiple_of(ranks_ref[k] * size, size), size)
        shared_ref[k * size : (k + 1) * size, :] = whole_ref[rows, :].astype(jnp.bfloat16)


def finish(ranks, kv_index, sums, weights, extra, at, sums_at):
    rows = weights.shape[0]
    shape = lambda *sizes: jax.ShapeDtypeStruct(sizes, jnp.float32)
    width = lambda name: sums_at[name][1]
    shared = 2 * (width("key") + width("value")) + width("b") + width("c") + LANES
    return pl.pallas_call(
        functools.partial(finish_kernel, at=at, sums_at=sums_at),
        out_shape=(
            shape(width("ssm_out"), rows),
            shape(width("attn_out"), rows),
            shape(rows, width("z")),
            shape(rows, width("x")),
            shape(rows, width("query")),
            shape(rows, width("misc")),
            jax.ShapeDtypeStruct((rows, shared), jnp.bfloat16),
        ),
        in_specs=[pl.BlockSpec(memory_space=pltpu.SMEM)] * 2 + in_vmem(3),
        out_specs=tuple(in_vmem(7)),
        scratch_shapes=[pltpu.VMEM((rows, shared), jnp.float32)],
        compiler_params=compiler_params(),
        name="finish",
    )(ranks, kv_index, sums, weights, extra)


def attend_kernel(rank_ref, query_ref, own_ref, *refs):
    pieces, (out_ref, low_ref, log_ref) = (refs[:-3], refs[-3:])
    span_length, head_size = query_ref.shape
    tile = own_ref.shape[0] // 2
    for block in range(span_length // tile):
        here = slice(block * tile, (block + 1) * tile)
        query_rows = query_ref[here, :]

        def step(kv_rows, carried, masked=False):
            top, total, summed = carried
            scores = tile_scores(kv_rows[:, :head_size], query_rows, head_size)
            if masked:
                scores = causal(scores)
            new_top = jnp.maximum(top, jnp.max(scores, axis=0, keepdims=True))
            probs = jnp.exp2(scores - new_top)
            scale = jnp.exp2(top - new_top)
            total = total * scale + jnp.sum(probs, axis=0, keepdims=True)
            summed = summed * scale + dot_first(kv_rows[:, head_size:], probs.astype(jnp.bfloat16))
            return (new_top, total, summed)

        carried = (
            jnp.full((1, tile), -1e30, jnp.float32),
            jnp.zeros((1, tile), jnp.float32),
            jnp.zeros((head_size, tile), jnp.float32),
        )
        carried = step(own_ref[here, :], carried, True)
        for earlier in range(block):
            carried = step(own_ref[earlier * tile : (earlier + 1) * tile, :], carried)
        for distance in range(1, 1 + len(pieces) // 2):
            pair = pieces[2 * distance - 2 : 2 * distance]

            def both(_, carried, pair=pair):
                return step(pair[1][...], step(pair[0][...], carried))

            valid = (rank_ref[0] >= distance).astype(jnp.int32)
            carried = lax.fori_loop(0, valid, both, carried)
        top, total, summed = carried
        result = summed / total
        out_ref[:, here] = result
        low_ref[here, :] = result.T.astype(jnp.bfloat16)
        log_ref[:, here] = top + jnp.log2(total)


def attend(rank, queries, own, pieces):
    span_length, head_size = queries.shape
    return pl.pallas_call(
        attend_kernel,
        out_shape=(
            jax.ShapeDtypeStruct((head_size, span_length), jnp.float32),
            jax.ShapeDtypeStruct((span_length, head_size), jnp.bfloat16),
            jax.ShapeDtypeStruct((1, span_length), jnp.float32),
        ),
        in_specs=[pl.BlockSpec(memory_space=pltpu.SMEM)] + in_vmem(2 + len(pieces)),
        out_specs=tuple(in_vmem(3)),
        compiler_params=compiler_params(),
        cost_estimate=small_cost(),
        name="attend",
    )(rank, queries, own, *pieces)


def attend_back_kernel(rank_ref, query_ref, own_ref, *refs):
    pieces, refs = (refs[:-13], refs[-13:])
    out_ref, log_ref, grad_ref, cos_ref, sin_ref, *_, d_query_ref, d_own_ref, d_far_ref, sums_ref = refs
    span_length, head_size = query_ref.shape
    tile = own_ref.shape[0] // 2
    score_scale = head_size**-0.5
    sums_ref[...] = jnp.zeros_like(sums_ref)
    for block in range(span_length // tile):
        here = slice(block * tile, (block + 1) * tile)
        query_rows = query_ref[here, :]
        grad_rows = grad_ref[here, grad_ref.shape[1] - head_size :]
        log_total = log_ref[:, here]
        delta_row = jnp.sum(
            grad_rows.astype(jnp.float32).T * out_ref[:, here], axis=0, keepdims=True
        )

        def step(kv_ref, start, at, d_query, masked=False):
            key_rows = kv_ref[start : start + tile, :head_size]
            scores = tile_scores(key_rows, query_rows, head_size)
            if masked:
                scores = causal(scores)
            probs = jnp.exp2(scores - log_total)
            d_probs = dot_last(kv_ref[start : start + tile, head_size:], grad_rows)
            d_scores = (probs * (d_probs - delta_row)).astype(jnp.bfloat16)
            rows = slice(at * tile, (at + 1) * tile)
            sums_ref[rows, head_size:] += mul(probs.astype(jnp.bfloat16), grad_rows)
            sums_ref[rows, :head_size] += mul(d_scores, query_rows)
            return d_query + dot_first(key_rows, d_scores)

        d_query = jnp.zeros((head_size, tile), jnp.float32)
        d_query = step(own_ref, block * tile, block, d_query, True)
        for earlier in range(block):
            d_query = step(own_ref, earlier * tile, earlier, d_query)
        for distance in range(1, 1 + len(pieces) // 2):

            def both(_, d_query, distance=distance):
                for k in (2 * distance - 2, 2 * distance - 1):
                    d_query = step(pieces[k], 0, 2 + k, d_query)
                return d_query

            valid = (rank_ref[0] >= distance).astype(jnp.int32)
            d_query = lax.fori_loop(0, valid, both, d_query)
        turned = d_query.T * score_scale
        d_query_ref[here, :] = (
            turned * cos_ref[here, :] - pltpu.roll(turned, head_size // 2, 1) * sin_ref[here, :]
        ).astype(jnp.bfloat16)
    lane = lax.broadcasted_iota(jnp.int32, (tile, 2 * head_size), 1)
    scale = jnp.where(lane < head_size, score_scale, 1.0)
    for at in range(2):
        rows = slice(at * tile, (at + 1) * tile)
        d_own_ref[rows, :] = sums_ref[rows, :] * scale
    for k in range(len(pieces)):
        rows = slice((2 + k) * tile, (3 + k) * tile)
        into = (k % 2) * (len(pieces) // 2) + k // 2
        d_far_ref[into * tile : (into + 1) * tile, :] = (sums_ref[rows, :] * scale).astype(
            jnp.bfloat16
        )


def attend_back(rank, queries, own, pieces, attended, log_totals, d_attn, cosine, sine, after):
    tile = own.shape[0] // 2
    return pl.pallas_call(
        attend_back_kernel,
        out_shape=(
            jax.ShapeDtypeStruct(queries.shape, jnp.bfloat16),
            jax.ShapeDtypeStruct(own.shape, jnp.float32),
            jax.ShapeDtypeStruct((len(pieces) * tile, own.shape[1]), jnp.bfloat16),
        ),
        in_specs=[pl.BlockSpec(memory_space=pltpu.SMEM)]
        + in_vmem(7 + len(pieces))
        + [pl.BlockSpec(memory_space=pl.ANY)] * len(after),
        out_specs=tuple(in_vmem(3)),
        scratch_shapes=[pltpu.VMEM(((2 + len(pieces)) * tile, own.shape[1]), jnp.float32)],
        compiler_params=compiler_params(),
        cost_estimate=small_cost(),
        name="attend_back",
    )(rank, queries, own, *pieces, attended, log_totals, d_attn, cosine, sine, *after)


def reorder_kernel(ranks_ref, *refs, count):
    out_ref = refs[-1]
    start = 0
    for ref in refs[:count]:
        out_ref[:, start : start + ref.shape[1]] = ref[...].astype(out_ref.dtype)
        start += ref.shape[1]


def reorder(ranks, pieces, inverse=False, after=()):
    count = ranks.shape[0]
    rows = pieces[0].shape[0] // count
    width = sum(piece.shape[1] for piece in pieces)
    there = lambda k, ranks: (ranks[k], 0)
    here = lambda k, ranks: (k, 0)
    return pl.pallas_call(
        functools.partial(reorder_kernel, count=len(pieces)),
        grid_spec=pltpu.PrefetchScalarGridSpec(
            num_scalar_prefetch=1,
            grid=(count,),
            in_specs=[
                pl.BlockSpec((rows, piece.shape[1]), here if inverse else there)
                for piece in pieces
            ]
            + [pl.BlockSpec(memory_space=pl.ANY)] * len(after),
            out_specs=pl.BlockSpec((rows, width), there if inverse else here),
        ),
        out_shape=jax.ShapeDtypeStruct((count * rows, width), jnp.bfloat16),
        compiler_params=compiler_params(),
        cost_estimate=small_cost(),
        name="reorder",
    )(ranks, *pieces, *after)


def lower_ones(size, dtype=jnp.float32):
    row = lax.broadcasted_iota(jnp.int32, (size, size), 0)
    column = lax.broadcasted_iota(jnp.int32, (size, size), 1)
    return (row >= column).astype(dtype)


def precise(left_side, right_side):
    return jnp.dot(
        left_side, right_side, precision=HIGH_PRECISION, preferred_element_type=jnp.float32
    )


def spread_heads(columns, head_size, width):
    lane = lax.broadcasted_iota(jnp.int32, (columns.shape[0], 2 * head_size), 1)
    pairs = [
        jnp.where(lane < head_size, columns[:, k : k + 1], columns[:, k + 1 : k + 2])
        for k in range(0, width // head_size, 2)
    ]
    return jnp.concatenate(pairs, axis=1)


def head_ones(width, head_size, lanes, dtype):
    at = lax.broadcasted_iota(jnp.int32, (width, lanes), 0)
    lane = lax.broadcasted_iota(jnp.int32, (width, lanes), 1)
    low = lane * head_size
    return ((at >= low) & (at < low + head_size)).astype(dtype)


def scan_first_kernel(
    pre_ref, bias_ref, rate_ref, x_ref, b_ref, delta_ref, cum_ref, delta_row_ref, cum_row_ref, state_ref, log_ref
):
    @pl.when(pl.program_id(0) == 0)
    def _():
        state_ref[...] = jnp.zeros_like(state_ref)
        log_ref[...] = jnp.zeros_like(log_ref)

    delta = jax.nn.softplus(pre_ref[...] + bias_ref[...])
    log_step = -delta * rate_ref[...]
    cumulative = precise(lower_ones(log_step.shape[0]), log_step)
    delta_ref[...] = delta
    cum_ref[...] = cumulative
    delta_row_ref[...] = delta.T[:8]
    cum_row_ref[...] = cumulative.T[:8]
    ending = cumulative[-1:, :]
    weight = jnp.exp(ending - cumulative + log_ref[...]) * delta
    width = x_ref.shape[1]
    x_low = x_ref[...].astype(jnp.bfloat16).astype(jnp.float32)
    weighted = (x_low * spread_heads(weight, MIXER_HEAD_SIZE, width)).astype(jnp.bfloat16)
    state_ref[...] += dot_first(b_ref[...].astype(jnp.bfloat16), weighted)
    log_ref[...] += ending


def part(projected, start, width, order=lambda c: c):
    at = start // width
    return (projected, pl.BlockSpec((BLOCK, width), lambda c: (order(c), at)))


def run_scan(
    kernel, chunks, operands, out_shape, out_specs, name, scratch=(), after=(), mebibytes=20
):
    count = len(operands)
    operands = operands + [(array, pl.BlockSpec(memory_space=pl.ANY)) for array in after]

    def call(*refs):
        kernel(*refs[:count], *refs[count + len(after) :])

    return pl.pallas_call(
        call,
        grid=(chunks,),
        out_shape=out_shape,
        in_specs=[spec for _, spec in operands],
        out_specs=out_specs,
        scratch_shapes=list(scratch),
        compiler_params=compiler_params(mebibytes),
        cost_estimate=small_cost(),
        name=name,
    )(*[array for array, _ in operands])


def whole(array):
    return (array, pl.BlockSpec(array.shape, lambda c: (0,) * array.ndim))


def scan_first(at, bias, rate):
    rows, lanes = (at["x"][0].shape[0], bias.shape[1])
    chunks = rows // BLOCK
    back = lambda c: chunks - 1 - c
    width, state_size = (at["x"][2], at["b"][2])
    by_chunk = pl.BlockSpec((BLOCK, lanes), lambda c: (back(c), 0))
    across = pl.BlockSpec((8, BLOCK), lambda c: (0, back(c)))
    shape = lambda *sizes: jax.ShapeDtypeStruct(sizes, jnp.float32)
    return run_scan(
        scan_first_kernel,
        chunks,
        [
            part(*at["misc"], back),
            whole(bias),
            whole(rate),
            part(*at["x"], back),
            part(*at["b"], back),
        ],
        (
            shape(rows, lanes),
            shape(rows, lanes),
            shape(8, rows),
            shape(8, rows),
            shape(state_size, width),
            shape(1, lanes),
        ),
        (
            by_chunk,
            by_chunk,
            across,
            across,
            pl.BlockSpec((state_size, width), lambda c: (0, 0)),
            pl.BlockSpec((1, lanes), lambda c: (0, 0)),
        ),
        "scan_first",
    )


def chained(refs, width):
    state = jnp.zeros((refs[0].shape[0] - 16, width), jnp.float32)
    for ref in reversed(refs):
        logs = ref[-16:, :LANES].astype(jnp.float32)
        decay = jnp.exp(jnp.sum(logs[:3], axis=0, keepdims=True))
        state = ref[:-16].astype(jnp.float32) + spread_heads(decay, MIXER_HEAD_SIZE, width) * state
    return state


def scan_kernel(
    x_ref,
    z_ref,
    b_ref,
    c_ref,
    delta_ref,
    cum_ref,
    delta_row_ref,
    cum_row_ref,
    near_ref,
    next_ref,
    far_ref,
    skip_ref,
    scanned_ref,
    gated_ref,
    states_ref,
    state_ref,
):
    @pl.when(pl.program_id(0) == 0)
    def _():
        state_ref[...] = chained((near_ref, next_ref, far_ref), x_ref.shape[1])

    head_size = MIXER_HEAD_SIZE
    pair = 2 * head_size
    size, width = x_ref.shape
    state = state_ref[...]
    states_ref[0] = state
    delta, cumulative = (delta_ref[...], cum_ref[...])
    delta_row, cum_row = (delta_row_ref[...], cum_row_ref[...])
    bmat, cmat = (b_ref[...].astype(jnp.bfloat16), c_ref[...].astype(jnp.bfloat16))
    x_all = x_ref[...].astype(jnp.bfloat16)
    inner = dot_last(cmat, bmat)
    row = lax.broadcasted_iota(jnp.int32, (size, size), 0)
    column = lax.broadcasted_iota(jnp.int32, (size, size), 1)
    allowed = row >= column
    lane = lax.broadcasted_iota(jnp.int32, (size, pair), 1)
    from_state = mul(cmat, state.astype(jnp.bfloat16))
    spread = spread_heads(jnp.exp(cumulative), head_size, width)
    for first in range(0, width // head_size, 2):
        here = slice(first * head_size, first * head_size + pair)
        x_pair = x_all[:, here]
        total = from_state[:, here] * spread[:, here]
        total += skip_ref[:, here] * x_pair.astype(jnp.float32)
        for head in (first, first + 1):
            gap = cumulative[:, head : head + 1] - cum_row[head : head + 1, :]
            decay = jnp.exp(jnp.where(allowed, gap, -1e30))
            mixing = inner * decay * delta_row[head : head + 1, :]
            x_head = jnp.where((lane >= head_size) == (head > first), x_pair, 0.0)
            total += mul(mixing.astype(jnp.bfloat16), x_head.astype(jnp.bfloat16))
        scanned_ref[:, here] = total
        gate = z_ref[:, here]
        gated_ref[:, here] = (total * (gate * jax.nn.sigmoid(gate))).astype(jnp.bfloat16)
    ending = cumulative[-1:, :]
    weight = spread_heads(jnp.exp(ending - cumulative) * delta, head_size, width)
    weighted = (x_all.astype(jnp.float32) * weight).astype(jnp.bfloat16)
    state_ref[...] = state * spread[-1:, :] + dot_first(bmat, weighted)


def scan(at, delta, cumulative, delta_row, cum_row, entry, skip, after):
    rows = delta.shape[0]
    state_size, width = (at["b"][2], at["x"][2])
    chunks = rows // BLOCK
    by_chunk = pl.BlockSpec((BLOCK, width), lambda c: (c, 0))
    lanes = delta.shape[1]
    across = pl.BlockSpec((8, BLOCK), lambda c: (0, c))
    return run_scan(
        scan_kernel,
        chunks,
        [
            part(*at["x"]),
            part(*at["z"]),
            part(*at["b"]),
            part(*at["c"]),
            part(delta, 0, lanes),
            part(cumulative, 0, lanes),
            (delta_row, across),
            (cum_row, across),
            *[whole(packed) for packed in entry],
            whole(skip),
        ],
        (
            jax.ShapeDtypeStruct((rows, width), jnp.float32),
            jax.ShapeDtypeStruct((rows, width), jnp.bfloat16),
            jax.ShapeDtypeStruct((chunks, state_size, width), jnp.float32),
        ),
        (by_chunk, by_chunk, pl.BlockSpec((1, state_size, width), lambda c: (c, 0, 0))),
        "scan",
        [pltpu.VMEM((state_size, width), jnp.float32)],
        after,
    )


def scan_back_first_kernel(
    grad_ref, z_ref, scanned_ref, c_ref, cum_ref, d_scanned_ref, d_gate_ref, state_ref, log_ref
):
    @pl.when(pl.program_id(0) == 0)
    def _():
        state_ref[...] = jnp.zeros_like(state_ref)
        log_ref[...] = jnp.zeros_like(log_ref)

    gate = z_ref[...]
    chance = jax.nn.sigmoid(gate)
    grad = grad_ref[:, : z_ref.shape[1]].astype(jnp.float32)
    d_scanned = grad * (gate * chance)
    d_scanned_ref[...] = d_scanned
    d_gate_ref[...] = (
        grad * scanned_ref[...] * (chance * (1.0 + gate * (1.0 - chance)))
    ).astype(jnp.bfloat16)
    cumulative = cum_ref[...]
    decay = spread_heads(jnp.exp(cumulative + log_ref[...]), MIXER_HEAD_SIZE, z_ref.shape[1])
    state_ref[...] += dot_first(
        c_ref[...].astype(jnp.bfloat16), (d_scanned * decay).astype(jnp.bfloat16)
    )
    log_ref[...] += cumulative[-1:, :]


def scan_back_first(grads, at, scanned, cumulative):
    rows, width = scanned.shape
    state_size, lanes = (at["c"][2], cumulative.shape[1])
    by_chunk = pl.BlockSpec((BLOCK, width), lambda c: (c, 0))
    return run_scan(
        scan_back_first_kernel,
        rows // BLOCK,
        [
            part(grads, 0, grads.shape[1]),
            part(*at["z"]),
            part(scanned, 0, width),
            part(*at["c"]),
            part(cumulative, 0, lanes),
        ],
        (
            jax.ShapeDtypeStruct((rows, width), jnp.float32),
            jax.ShapeDtypeStruct((rows, width), jnp.bfloat16),
            jax.ShapeDtypeStruct((state_size, width), jnp.float32),
        ),
        (by_chunk, by_chunk, pl.BlockSpec((state_size, width), lambda c: (0, 0))),
        "scan_back_first",
        [pltpu.VMEM((1, lanes), jnp.float32)],
    )


def scan_back_kernel(
    x_ref,
    grad_ref,
    b_ref,
    c_ref,
    pre_ref,
    bias_ref,
    rate_ref,
    delta_ref,
    cum_ref,
    cum_row_ref,
    states_ref,
    near_ref,
    next_ref,
    far_ref,
    skip_ref,
    d_x_ref,
    d_b_ref,
    d_c_ref,
    d_pre_ref,
    sums_ref,
    state_ref,
):
    @pl.when(pl.program_id(0) == 0)
    def _():
        state_ref[...] = chained((near_ref, next_ref, far_ref), x_ref.shape[1])
        sums_ref[...] = jnp.zeros_like(sums_ref)

    head_size = MIXER_HEAD_SIZE
    pair = 2 * head_size
    size, width = x_ref.shape
    lanes = delta_ref.shape[1]
    low = jnp.bfloat16
    delta, cumulative, cum_row = (delta_ref[...], cum_ref[...], cum_row_ref[...])
    bmat, cmat = (b_ref[...].astype(low), c_ref[...].astype(low))
    x_all = x_ref[...].astype(low)
    x_single = x_all.astype(jnp.float32)
    grad = grad_ref[...]
    grad_low = grad.astype(low)
    state = states_ref[0]
    state_low = state.astype(low)
    after = state_ref[...]
    after_low = after.astype(low)
    ending = cumulative[-1:, :]
    row = lax.broadcasted_iota(jnp.int32, (size, size), 0)
    column = lax.broadcasted_iota(jnp.int32, (size, size), 1)
    later = column >= row
    before = (row > column).astype(low)
    onward = later.astype(low)
    lane = lax.broadcasted_iota(jnp.int32, (size, pair), 1)
    head_lane = lax.broadcasted_iota(jnp.int32, (size, lanes), 1)
    sum_heads = head_ones(width, head_size, lanes, low)

    inner = dot_last(bmat, cmat)
    from_after = mul(bmat, after_low)
    weight = jnp.exp(ending - cumulative)
    spread_weight = spread_heads(weight * delta, head_size, width)
    spread = spread_heads(jnp.exp(cumulative), head_size, width)
    to_end = mul((x_single * from_after).astype(low), sum_heads)
    through = jnp.exp(cumulative) * mul((grad * mul(cmat, state_low)).astype(low), sum_heads)
    carried = jnp.sum(state * after, axis=0, keepdims=True) * spread[-1:, :]
    carried = precise(carried, sum_heads.astype(jnp.float32))
    d_delta = weight * to_end
    d_log = (
        mul(onward, through.astype(low)) + mul(before, (d_delta * delta).astype(low)) + carried
    )

    d_inner = jnp.zeros((size, size), jnp.float32)
    for first in range(0, width // head_size, 2):
        here = slice(first * head_size, first * head_size + pair)
        x_pair, grad_pair = (x_all[:, here], grad_low[:, here])
        d_x = from_after[:, here] * spread_weight[:, here] + skip_ref[:, here] * grad[:, here]
        for head in (first, first + 1):
            mine = (lane >= head_size) == (head > first)
            gap = cum_row[head : head + 1, :] - cumulative[:, head : head + 1]
            decay = jnp.exp(jnp.where(later, gap, -1e30))
            delta_column = delta[:, head : head + 1]
            d_mixing = dot_last(jnp.where(mine, x_pair, 0.0).astype(low), grad_pair) * decay
            d_inner += d_mixing * delta_column
            flow = d_mixing * inner
            mixing = inner * decay * delta_column
            d_x += mul(mixing.astype(low), jnp.where(mine, grad_pair, 0.0).astype(low))
            d_delta_head = jnp.sum(flow, axis=1, keepdims=True)
            passing = mul(before, (flow * delta_column).astype(low))
            d_log_head = jnp.sum(jnp.where(later, passing, 0.0), axis=1, keepdims=True)
            d_delta += jnp.where(head_lane == head, d_delta_head, 0.0)
            d_log += jnp.where(head_lane == head, d_log_head, 0.0)
        d_x_ref[:, here] = d_x.astype(low)

    d_inner_low = d_inner.astype(low)
    scaled_grad = (grad * spread).astype(low)
    weighted = (x_single * spread_weight).astype(low)
    d_b_ref[...] = (mul(d_inner_low, cmat) + dot_last(weighted, after_low)).astype(low)
    d_c_ref[...] = (dot_first(d_inner_low, bmat) + dot_last(scaled_grad, state_low)).astype(low)
    state_ref[...] = after * spread[-1:, :] + dot_first(cmat, scaled_grad)
    rate = rate_ref[...]
    d_pre = (d_delta - d_log * rate) * jax.nn.sigmoid(pre_ref[...] + bias_ref[...])
    d_pre = jnp.where(head_lane < width // head_size, d_pre, 0.0)
    d_pre_ref[...] = d_pre.astype(low)
    skip_sum = precise(
        jnp.sum(grad * x_single, axis=0, keepdims=True), sum_heads.astype(jnp.float32)
    )
    sums_ref[0:1, :] += jnp.sum(d_pre, axis=0, keepdims=True)
    sums_ref[1:2, :] += jnp.sum(d_log * (-delta * rate), axis=0, keepdims=True)
    sums_ref[2:3, :] += skip_sum


def scan_back(
    at, d_scanned, bias, rate, delta, cumulative, cum_row, states, entry, skip, after
):
    rows, width = d_scanned.shape
    state_size, lanes = (at["b"][2], delta.shape[1])
    chunks = rows // BLOCK
    back = lambda c: chunks - 1 - c
    by_chunk = lambda columns: pl.BlockSpec((BLOCK, columns), lambda c: (back(c), 0))
    shape = lambda columns: jax.ShapeDtypeStruct((rows, columns), jnp.bfloat16)
    return run_scan(
        scan_back_kernel,
        chunks,
        [
            part(in_hbm(at["x"][0]), *at["x"][1:], back),
            part(in_hbm(d_scanned), 0, width, back),
            part(in_hbm(at["b"][0]), *at["b"][1:], back),
            part(in_hbm(at["c"][0]), *at["c"][1:], back),
            part(in_hbm(at["misc"][0]), *at["misc"][1:], back),
            whole(bias),
            whole(rate),
            part(in_hbm(delta), 0, lanes, back),
            part(in_hbm(cumulative), 0, lanes, back),
            (in_hbm(cum_row), pl.BlockSpec((8, BLOCK), lambda c: (0, back(c)))),
            (in_hbm(states), pl.BlockSpec((1, state_size, width), lambda c: (back(c), 0, 0))),
            *[whole(in_hbm(packed)) for packed in entry],
            whole(skip),
        ],
        (
            shape(width),
            shape(state_size),
            shape(state_size),
            shape(lanes),
            jax.ShapeDtypeStruct((8, lanes), jnp.float32),
        ),
        (
            by_chunk(width),
            by_chunk(state_size),
            by_chunk(state_size),
            by_chunk(lanes),
            pl.BlockSpec((8, lanes), lambda c: (0, 0)),
        ),
        "scan_back",
        [pltpu.VMEM((state_size, width), jnp.float32)],
        after,
        44,
    )


def on_heads(value, move):
    devices = lax.axis_size("heads")
    pairs = []
    for at in range(devices):
        z, core = move(at // 2, at % 2)
        pairs.append((at, 2 * (z % (devices // 2)) + core))
    return lax.ppermute(value, "heads", pairs)


def to_partner(value):
    return on_heads(value, lambda z, core: (z, 1 - core))


def along(value):
    return on_heads(value, lambda z, core: (z + 1 - 2 * core, core))


def against(value):
    return on_heads(value, lambda z, core: (z - 1 + 2 * core, core))


def chunk_ranks():
    devices = lax.axis_size("heads")
    z, core = (lax.axis_index("heads") // 2, lax.axis_index("heads") % 2)
    step, other = (1 - 2 * core, 1 - core)
    owners = (
        (z, core),
        (z + 2, core),
        (z - step, core),
        (z - step, other),
        (z, other),
        (z + 2, other),
        (z + step, other),
        (z + step, core),
    )
    return jnp.stack([2 * ((at + devices) % (devices // 2)) + side for at, side in owners])


def against_other(value):
    return on_heads(value, lambda z, core: (z - 1 + 2 * core, 1 - core))


def gather_rows(own, joined=False):
    partner = to_partner(own)
    near = along(own)
    near_other = along(partner)
    far = along(near)
    last = (to_partner(far), to_partner(near), to_partner(near_other))
    mine = (own, far, near, near_other)
    theirs = (partner,) + last
    rows = join(mine + theirs) if joined else jnp.concatenate(mine + theirs, axis=0)
    return rows, last


def scatter_rows(product, half, late=None):
    chunk = half // 4
    got = to_partner(product(slice(half, 2 * half)).astype(jnp.bfloat16))
    kept = lax.optimization_barrier(product(slice(0, half)))

    summed = kept + got.astype(jnp.float32)
    low = summed[chunk:].astype(jnp.bfloat16)
    far = against(low[:chunk])
    near_other = against_other(low[2 * chunk :])
    near = low[chunk : 2 * chunk].astype(jnp.float32) + far.astype(jnp.float32)
    near = against(near.astype(jnp.bfloat16))
    total = summed[:chunk] + near.astype(jnp.float32) + near_other.astype(jnp.float32)
    return total if late is None else total + late


def across(value, bit):
    devices = lax.axis_size("heads")
    return lax.ppermute(value, "heads", [(at, at ^ bit) for at in range(devices)])


def gather_small(value):
    for bit in (1, 2, 4):
        value = jnp.concatenate([value, across(value, bit)], axis=0)
    return value


def scatter_small(value):
    for bit in (4, 2, 1):
        half = value.shape[0] // 2
        got = across(value[half:].astype(jnp.bfloat16), bit)
        value = value[:half].astype(jnp.float32) + got.astype(jnp.float32)
    return value


def on_blocks(value, step):
    devices = lax.axis_size("blk")
    pairs = [(at, at + step) for at in range(devices) if 0 <= at + step < devices]
    return lax.ppermute(value, "blk", pairs)


def from_earlier(value, step=1):
    return tuple(on_blocks(value, distance * step) for distance in (1, 2, 3))


def pack_state(state, log_total):
    high = log_total.astype(jnp.bfloat16)
    rest = log_total - high.astype(jnp.float32)
    middle = rest.astype(jnp.bfloat16)
    low = (rest - middle.astype(jnp.float32)).astype(jnp.bfloat16)
    logs = jnp.concatenate([high, middle, low], axis=0)
    logs = jnp.pad(logs, ((0, 16 - logs.shape[0]), (0, state.shape[1] - logs.shape[1])))
    return jnp.concatenate([state.astype(jnp.bfloat16), logs], axis=0)


def sum_blocks(value):
    for axis in ("dp", "blk"):
        for bit in (1, 2):
            value = value + lax.ppermute(
                value, axis, [(at, at ^ bit) for at in range(lax.axis_size(axis))]
            )
    return value


def weight_sum(grads):
    return lax.psum_scatter(grads, ("dp", "blk"), scatter_dimension=0, tiled=True)


def split_columns(value_in, widths):
    pieces, start = [], 0
    for width in widths:
        pieces.append(value_in[:, start : start + width])
        start += width
    return pieces


def inverse_rms(rows_in):
    return lax.rsqrt(jnp.mean(rows_in * rows_in, axis=-1, keepdims=True) + norm_eps)


def norm_back(rows_in, gain_in, cotangent):
    inverse = inverse_rms(rows_in)
    scaled = rows_in * inverse
    weighted = cotangent * gain_in
    return inverse * (weighted - scaled * jnp.mean(weighted * scaled, axis=-1, keepdims=True))


def shards(
    x_in,
    out_grad,
    norm_one,
    w_query,
    w_key,
    w_value,
    output_gate_weight,
    mixer_input_weight,
    w_delta,
    w_bmat,
    w_cmat,
    delta_bias,
    decay_log,
    skip_gain,
    w_attn_out,
    mixer_output_weight,
    norm_two,
    w_gate,
    w_up,
    w_down,
):
    heads_count = lax.axis_size("heads")
    head_rank = lax.axis_index("heads")
    core = head_rank % 2
    block_rank = lax.axis_index("blk")
    rank = block_rank.astype(jnp.int32)[None]
    own_rows = x_in.shape[0]
    span_length = own_rows * heads_count
    half_span = span_length // 2
    span_start = block_rank * span_length
    query_width = w_query.shape[1]
    mixer_width = mixer_input_weight.shape[1]
    heads = mixer_width // MIXER_HEAD_SIZE
    state_size = w_bmat.shape[1]
    hidden_width = w_gate.shape[1]
    rows_of = w_query.shape[0]
    kv_index = head_rank * (query_width // HD) // (QH // KVH)
    kv_width = KVH * HD
    low = jnp.bfloat16
    ranks = chunk_ranks().astype(jnp.int32)
    turns = (head_rank ^ jnp.arange(heads_count)).astype(jnp.int32)

    gains = jnp.stack([norm_one, norm_two], axis=1)
    gains = jnp.pad(gains, ((0, 0), (heads, LANES - heads - 2)))
    shared = pack((w_key, w_value, w_bmat, w_cmat, gains), (False,) * 5)
    delta_wide = jnp.pad(w_delta, ((0, 0), (0, LANES - heads)))
    in_names = ("z", "x", "query", "b", "c", "misc", "key", "value")
    in_widths = (mixer_width, mixer_width, query_width, state_size, state_size, LANES, HD, HD)
    in_width = sum(in_widths)
    starts = [sum(in_widths[:k]) for k in range(len(in_widths))]
    at = dict(zip(in_names, zip(starts, in_widths)))
    mix_at = {
        "ssm_out": (in_width, mixer_width),
        "attn_out": (in_width + mixer_width, query_width),
    }
    first_own = pack_first(
        turns,
        kv_index.astype(jnp.int32)[None],
        gather_small(shared),
        delta_wide,
        [output_gate_weight, mixer_input_weight, w_query, mixer_output_weight, w_attn_out],
        at | mix_at,
    )
    gain_part = first_own[:, at["misc"][0] + heads : at["misc"][0] + heads + 2]
    first_full = lax.all_gather(first_own, ("dp", "blk"), axis=0, tiled=True)
    in_full, mix_t = (first_full[:, :in_width], first_full[:, in_width:])
    x_float = x_in.astype(jnp.float32)
    zero = 0.0 * first_own[0, 0]
    x_span, _ = gather_rows(x_in + zero, joined=True)
    ffn_grad, _ = gather_rows(out_grad + zero, joined=True)
    ffn_own = pack((w_gate, w_up, w_down), (False, False, True), [corner(x_span)])
    ffn_full = lax.all_gather(ffn_own, ("dp", "blk"), axis=0, tiled=True)
    mixed_width = query_width + mixer_width
    gate_full, up_full, down_t = split_columns(ffn_full, (hidden_width,) * 3)
    positions = (span_start + jnp.arange(span_length)).astype(jnp.float32)
    freqs = rope_base ** (-2.0 * jnp.arange(HD // 2, dtype=jnp.float32) / HD)
    angles = positions[:, None] * freqs[None, :]
    cosine, sine = (jnp.cos(angles), jnp.sin(angles))
    cosine = jnp.concatenate([cosine, cosine], axis=1)
    sine = jnp.concatenate([-sine, sine], axis=1)
    normed_ordered, queries, keys_values, gain_rows = enter(
        ranks, jnp.full((1,), heads, jnp.int32), x_span, first_full, at, cosine, sine, [corner(ffn_own), corner(ffn_grad)]
    )
    gain_one, gain_two = (gain_rows[0:1], gain_rows[1:2])
    mine = lax.dynamic_slice_in_dim(keys_values, core * half_span, half_span, 0)
    pieces = []
    for piece in from_earlier(mine):
        pieces += [piece, to_partner(piece)]
    gate_raw = simple_product(normed_ordered, in_full[:, :mixer_width])
    x_raw = simple_product(normed_ordered, in_full[:, mixer_width : 2 * mixer_width])
    state_raw = simple_product(normed_ordered, in_full[:, at["b"][0] : at["key"][0]])
    raw = {
        "z": (gate_raw, 0, mixer_width),
        "x": (x_raw, 0, mixer_width),
        "b": (state_raw, 0, state_size),
        "c": (state_raw, state_size, state_size),
        "misc": (state_raw, 2 * state_size, LANES),
    }

    pad_lanes = lambda vector: jnp.pad(vector, (0, LANES - heads))[None]
    bias, rate = (pad_lanes(delta_bias), pad_lanes(jnp.exp(decay_log)))
    skip = jnp.repeat(skip_gain, MIXER_HEAD_SIZE)[None]
    delta, cumulative, delta_row, cum_row, local_state, local_log = scan_first(raw, bias, rate)
    entry_states = from_earlier(pack_state(local_state, local_log))
    attended, attn_part, log_totals = attend(rank, queries, keys_values, pieces)
    scanned, gated, states = scan(
        raw, delta, cumulative, delta_row, cum_row, entry_states, skip, [corner(attn_part)]
    )
    mixers = reorder(ranks, [gated, attn_part])
    ffn_zero = 0.0 * ffn_full[0, 0].astype(jnp.float32)
    mixed = scatter_rows(lambda rows: dot_last(mixers[rows], mix_t), half_span, ffn_zero)
    middle = x_float + mixed
    middle_scaled = middle * inverse_rms(middle)
    normed_two, _ = gather_rows((middle_scaled * gain_two).astype(low))
    ffn_gate = simple_product(normed_two, gate_full)
    ffn_up = simple_product(normed_two, up_full)
    ffn_sig = jax.nn.sigmoid(ffn_gate)
    hidden = (ffn_gate * ffn_sig * ffn_up).astype(low)

    d_hidden = simple_product(ffn_grad, down_t)
    d_ffn_gate = (d_hidden * ffn_up * (ffn_sig * (1.0 + ffn_gate * (1.0 - ffn_sig)))).astype(low)
    d_ffn_up = (d_hidden * (ffn_gate * ffn_sig)).astype(low)
    ffn_grads = weight_grads(
        [(normed_two, [d_ffn_gate, d_ffn_up]), (ffn_grad, [hidden])],
        3 * hidden_width,
    )
    grads_zero = 0.0 * ffn_grads[0, 0].astype(jnp.float32)

    def d_normed_two_of(rows):
        value = dot_last(d_ffn_gate[rows], gate_full) + dot_last(d_ffn_up[rows], up_full)
        return value + grads_zero if rows.start == 0 else value

    d_normed_two = scatter_rows(d_normed_two_of, half_span)
    d_middle = out_grad.astype(jnp.float32) + norm_back(middle, gain_two, d_normed_two)
    mix_grad, _ = gather_rows(d_middle.astype(low))
    ffn_sums = weight_sum(ffn_grads).astype(jnp.float32)
    grad_gate, grad_up, grad_down_t = split_columns(ffn_sums, (hidden_width,) * 3)
    grad_two_part = jnp.sum(grad_gate * w_gate + grad_up * w_up, axis=1, keepdims=True)
    gain_own = gain_part.astype(jnp.float32)
    grad_two_part = grad_two_part / gain_own[:, 1:2]
    d_mixers = reorder(
        ranks, [simple_product(mix_grad, mix_t).astype(low)], inverse=True, after=[corner(ffn_grads)]
    )
    d_scanned, d_gate_z, d_entry = scan_back_first(d_mixers, raw, scanned, cumulative)
    d_entry = pack_state(d_entry, local_log)
    after_states = from_earlier(d_entry, -1)
    mix_width = mixed_width + mixer_width
    all_width = mixed_width + in_width
    mix_grads = weight_grads(
        [(mix_grad, [mixers]), (normed_ordered, [d_gate_z])], all_width, after=[corner(d_entry)]
    )
    d_query, d_own, d_far = attend_back(
        rank, queries, keys_values, pieces, attended, log_totals, d_mixers, cosine, sine, [corner(mix_grads), *map(corner, after_states)]
    )
    d_ssm_in, d_bmat, d_cmat, d_pre, sums = scan_back(
        raw,
        d_scanned,
        bias,
        rate,
        delta,
        cumulative,
        cum_row,
        states,
        after_states,
        skip,
        [corner(d_query)],
    )
    far_half = d_far.shape[0] // 2
    d_mine = lax.dynamic_slice_in_dim(d_own, core * half_span, half_span, 0)
    d_theirs = lax.dynamic_slice_in_dim(d_own, (1 - core) * half_span, half_span, 0)
    d_mine = d_mine + to_partner(d_theirs.astype(low)).astype(jnp.float32)
    d_far = d_far[:far_half].astype(jnp.float32) + to_partner(d_far[far_half:]).astype(jnp.float32)
    d_one, d_two, d_three = (
        d_far[k * half_span : (k + 1) * half_span] for k in range(d_far.shape[0] // half_span)
    )
    scan_zero = 0.0 * d_pre[0, 0].astype(jnp.float32)
    d_one = d_one + on_blocks(d_two.astype(low), -1).astype(jnp.float32) + scan_zero
    d_mine = d_mine + on_blocks(d_one.astype(low), -1).astype(jnp.float32)
    d_mine = d_mine + on_blocks(d_three.astype(low), -3).astype(jnp.float32)
    half_cos = lax.dynamic_slice_in_dim(cosine, core * half_span, half_span, 0)
    half_sin = lax.dynamic_slice_in_dim(sine, core * half_span, half_span, 0)
    d_key = d_mine[:, :HD]
    d_key = d_key * half_cos - jnp.roll(d_key, HD // 2, axis=1) * half_sin
    d_mine = jnp.concatenate([d_key, d_mine[:, HD:]], axis=1).astype(low)
    d_keys_values = lax.dynamic_update_slice_in_dim(
        jnp.zeros((span_length, 2 * HD), low), d_mine, core * half_span, 0
    )

    scan_rights = [d_ssm_in, d_bmat, d_cmat, d_pre]
    in_grads = weight_grads([(normed_ordered, scan_rights)], all_width, mix_width, mix_grads)
    late_rights = [d_keys_values, d_query]
    late_start = mix_width + sum(array.shape[1] for array in scan_rights)
    in_grads = weight_grads([(normed_ordered, late_rights)], all_width, late_start, in_grads)
    in_sums = weight_sum(in_grads)
    d_projected = reorder(
        ranks,
        [d_gate_z, d_ssm_in, d_query, d_bmat, d_cmat, d_pre, d_keys_values],
        after=[corner(in_grads)],
    )
    d_normed = scatter_rows(lambda rows: dot_last(d_projected[rows], in_full), half_span)
    input_grad = d_middle + norm_back(x_float, gain_one, d_normed)
    back_zero = 0.0 * d_query[0, 0].astype(jnp.float32)
    ffn_out = scatter_rows(
        lambda rows: dot_last(hidden[rows], down_t) + back_zero, half_span
    )
    activations = (middle + ffn_out).astype(low)
    sums_names = ("ssm_out", "attn_out", "z", "x", "b", "c", "misc", "key", "value", "query")
    sums_widths = [mixer_width, query_width] + [at[name][1] for name in sums_names[2:]]
    sums_starts = [sum(sums_widths[:k]) for k in range(len(sums_widths))]
    sums_at = dict(zip(sums_names, zip(sums_starts, sums_widths)))
    extra = jnp.concatenate([gain_own[:, 0:1], grad_two_part], axis=1)
    extra = jnp.pad(extra, ((0, 0), (0, LANES - 2)))
    grad_ssm_out, grad_attn_out, grad_gatez, grad_ssmx, grad_query, misc_sums, shared_parts = finish(
        turns,
        kv_index.astype(jnp.int32)[None],
        in_sums,
        first_own,
        extra,
        at,
        sums_at,
    )
    shared_sums = scatter_small(shared_parts)
    grad_key, grad_value, grad_bmat, grad_cmat, gain_sums = split_columns(
        shared_sums, (kv_width, kv_width, state_size, state_size, LANES)
    )
    small_sums = sum_blocks(sums)[:, :heads]
    return (
        activations,
        input_grad,
        gain_sums[:, 0],
        grad_query,
        grad_key,
        grad_value,
        grad_gatez,
        grad_ssmx,
        misc_sums[:, :heads],
        grad_bmat,
        grad_cmat,
        small_sums[0],
        small_sums[1],
        small_sums[2],
        grad_attn_out,
        grad_ssm_out,
        gain_sums[:, 1],
        grad_gate,
        grad_up,
        grad_down_t.T,
    )


def solution(mesh):
    placed = (
        P(("dp", "blk", "heads"), None),
        P(("dp", "blk", "heads"), None),
        P(("dp", "blk", "heads")),
        P(("dp", "blk"), "heads"),
        P(("dp", "blk", "heads"), None),
        P(("dp", "blk", "heads"), None),
        P(("dp", "blk"), "heads"),
        P(("dp", "blk"), "heads"),
        P(("dp", "blk"), "heads"),
        P(("dp", "blk", "heads"), None),
        P(("dp", "blk", "heads"), None),
        P("heads"),
        P("heads"),
        P("heads"),
        P("heads", ("dp", "blk")),
        P("heads", ("dp", "blk")),
        P(("dp", "blk", "heads")),
        P(("dp", "blk"), "heads"),
        P(("dp", "blk"), "heads"),
        P("heads", ("dp", "blk")),
    )
    return jax.shard_map(
        shards,
        mesh=mesh,
        in_specs=placed,
        out_specs=(
            P(("dp", "blk", "heads"), None),
            P(("dp", "blk", "heads"), None),
            P(("dp", "blk", "heads")),
            P(("dp", "blk"), "heads"),
            P(("dp", "blk", "heads"), None),
            P(("dp", "blk", "heads"), None),
            P(("dp", "blk"), "heads"),
            P(("dp", "blk"), "heads"),
            P(("dp", "blk"), "heads"),
            P(("dp", "blk", "heads"), None),
            P(("dp", "blk", "heads"), None),
            P("heads"),
            P("heads"),
            P("heads"),
            P("heads", ("dp", "blk")),
            P("heads", ("dp", "blk")),
            P(("dp", "blk", "heads")),
            P(("dp", "blk"), "heads"),
            P(("dp", "blk"), "heads"),
            P("heads", ("dp", "blk")),
        ),
        check_vma=False,
    )
```
